32 devices in a mesh: groups: 2 (over x), row: 8 (over z, y), col: 2 (over core).
Axes of the slice: x: 2, y: 2, z: 4, core: 2. Of those that a mesh axis runs over, the one named last changes fastest.
Arguments:
- snapshot: bfloat16 [2048, 32, 2048], P(('groups', 'row'), None, 'col'), parts along dimension 0, may hold values from -6 to 6
- mode2_factor: bfloat16 [4096, 64], P(('groups', 'col')), parts along dimension 0, may hold values from -0.125 to 0.125
- old_factor: bfloat16 [2048, 64], P(('groups', 'row')), parts along dimension 0, may hold values from -0.1875 to 0.1875
Outputs:
- new_factor: float32 [2048, 64], P(('groups', 'row', 'col')), parts along dimension 0
The draws below stay inside these ranges and needn't reach their ends.
There are 2 independent parts, one for each index of `groups`. The reference program is written for one: setup_inputs(seed, part) draws one part's arguments, and reference() takes and returns one part's arrays. A program takes and returns all parts, laid end to end along the dimension named above; each array names one. Nothing has to cross between parts.
All inputs are finite; a program needn't handle non-finite values.
Results may differ from the reference program's by a relative error of at most 0.01.
Values may be sent and summed in bfloat16 or wider, within the bound.
No kernel may reach another device: no remote copies, remote signals or barrier semaphores. Data moves between devices by JAX's collectives and lax.ppermute only.
A program may use at most 64 MiB of HBM per device.

```python
import jax
import jax.numpy as jnp
from jax import lax

RANK = 64
FIBERS = 32
I1 = 1024
I2 = 2048
N_COL = 2


def levels(stream_key, dims, split, smallest, top_value):
    loudness = 1.0
    for dim, parts in split:
        heights = jax.random.uniform(jax.random.fold_in(jax.random.fold_in(stream_key, 6), dim), (parts,), jnp.float32, smallest / len(split), top_value / len(split))
        loudness = loudness * jnp.repeat(jnp.exp(heights), dims[dim] // parts).reshape((-1,) + (1,) * (len(dims) - 1 - dim))
    return loudness


def gaussian(rng, shape, scale, bound, cuts=(), held_as=jnp.bfloat16):
    gain = levels(rng, shape, cuts, -0.22, 0.18) if cuts else 1.0
    drawn = jax.random.normal(rng, shape, jnp.float32) * scale * gain
    return jnp.minimum(jnp.maximum(drawn, -bound), bound).astype(held_as)


def setup_inputs(seed: int = 0, part: int = 0) -> dict:
    seeds = jax.random.split(jax.random.key(seed), 4)
    own_keys = jax.random.split(jax.random.fold_in(seeds[3], part), 4)
    return {
        "snapshot": gaussian(own_keys[0], (I1, FIBERS, I2), 1.0, 6.0, ((0, 8), (2, 2))),
        "mode2_factor": gaussian(own_keys[1], (I2, RANK), I2 ** -0.5, 0.125, ((0, 2),)),
        "old_factor": gaussian(own_keys[2], (I1, RANK), I1 ** -0.5, 0.1875, ((0, 8),)),
    }


def reference(snapshot, mode2_factor, old_factor):
    flat = snapshot.reshape(I1 * FIBERS, I2)
    width = I2 // N_COL
    core = jnp.zeros((I1 * FIBERS, RANK), jnp.float32)
    for block in range(N_COL):
        part = jnp.dot(flat[:, block * width:(block + 1) * width].astype(jnp.float32), mode2_factor[block * width:(block + 1) * width].astype(jnp.float32), preferred_element_type=jnp.float32)
        part = lax.optimization_barrier(part.astype(jnp.bfloat16))
        core = core + part.astype(jnp.float32)
    unfolded = core.reshape(I1, FIBERS * RANK)
    projected = jnp.dot(old_factor.astype(jnp.float32).T.astype(jnp.float32), unfolded.astype(jnp.float32), precision=lax.Precision.HIGHEST, preferred_element_type=jnp.float32).astype(jnp.bfloat16)
    product = jnp.dot(unfolded.astype(jnp.float32), projected.astype(jnp.float32).T.astype(jnp.float32), precision=lax.Precision.HIGHEST, preferred_element_type=jnp.float32)
    gram = jnp.dot(product.T.astype(jnp.float32), product.astype(jnp.float32), precision=lax.Precision.HIGHEST, preferred_element_type=jnp.float32)
    lower = jnp.linalg.cholesky(gram)
    solved = jax.scipy.linalg.solve_triangular(lower, product.T, lower=True)
    return solved.T * jnp.sqrt(jnp.float32(I1))
```

```python
import functools

import jax
import jax.numpy as jnp
from jax import lax
from jax.experimental import pallas as pl
from jax.experimental.pallas import tpu as pltpu
from jax.sharding import PartitionSpec as P

F32 = jnp.float32
BF16 = jnp.bfloat16
LANES = 128


def dot_f32(a, b, dims, precision=None):
    return lax.dot_general(a, b, (dims, ((), ())), precision=precision, preferred_element_type=F32)


def contract_kernel(fibers, rank, snapshot_ref, mode2_ref, send_ref, own_ref, wide_ref, core_ref):
    cells, _, depth = snapshot_ref.shape
    reps = LANES // rank

    @pl.when(pl.program_id(0) == 0)
    def _():
        wide_ref[...] = jnp.concatenate([mode2_ref[...]] * reps, axis=1)

    core_ref[...] = dot_f32(
        snapshot_ref[...].reshape(cells * fibers, depth), wide_ref[...], ((1,), (0,))
    )
    lane = lax.broadcasted_iota(jnp.int32, (cells, LANES), 1)
    first = lax.axis_index("col") == 0
    half = fibers // 2

    def columns(start):
        part = core_ref[pl.ds(start, cells, stride=fibers), :]
        for r in range(1, reps):
            other = core_ref[pl.ds(start + r, cells, stride=fibers), :]
            part = jnp.where(lane < r * rank, part, other)
        return part

    for block in range(half // reps):
        low = columns(block * reps)
        high = columns(half + block * reps)
        where = slice(block * LANES, (block + 1) * LANES)
        own_ref[:, where] = jnp.where(first, low, high).astype(BF16)
        send_ref[:, where] = jnp.where(first, high, low).astype(BF16)


def contract(snapshot, mode2):
    cells, fibers, depth = snapshot.shape
    rank = mode2.shape[1]
    step = 16
    width = fibers // 2 * rank
    out = jax.ShapeDtypeStruct((cells, width), BF16)
    return pl.pallas_call(
        functools.partial(contract_kernel, fibers, rank),
        grid=(cells // step,),
        in_specs=[
            pl.BlockSpec((step, fibers, depth), lambda i: (i, 0, 0)),
            pl.BlockSpec((depth, rank), lambda i: (0, 0)),
        ],
        out_specs=[pl.BlockSpec((step, width), lambda i: (i, 0))] * 2,
        out_shape=[out, out],
        scratch_shapes=[
            pltpu.VMEM((depth, LANES), BF16),
            pltpu.VMEM((step * fibers, LANES), F32),
        ],
        compiler_params=pltpu.CompilerParams(vmem_limit_bytes=32 * 2**20),
        name="contract",
    )(snapshot, mode2)


def project_kernel(own_ref, got_ref, factor_ref, out_ref):
    rank = factor_ref.shape[1]
    factor = factor_ref[...]
    total = dot_f32(factor, own_ref[...], ((0,), (0,))) + dot_f32(factor, got_ref[...], ((0,), (0,)))
    for block in range(total.shape[1] // LANES):
        out_ref[pl.ds(block * rank, rank), :] = total[:, block * LANES:(block + 1) * LANES].astype(BF16)


def project(own, got, factor):
    rank = factor.shape[1]
    rows = rank * own.shape[1] // LANES
    return pl.pallas_call(
        project_kernel,
        out_shape=jax.ShapeDtypeStruct((rows, LANES), BF16),
        name="project",
    )(own, got, factor)


def reduce_kernel(parts_ref, out_ref):
    total = jnp.sum(parts_ref[...].astype(F32), axis=0).astype(BF16)
    out_ref[...] = jnp.broadcast_to(total[None], out_ref.shape)


def reduce_parts(parts):
    return pl.pallas_call(
        reduce_kernel,
        out_shape=jax.ShapeDtypeStruct(parts.shape, BF16),
        name="reduce_parts",
    )(parts)


def product_kernel(own_ref, got_ref, projected_ref, out_ref):
    cells, width = own_ref.shape
    rank = projected_ref.shape[0] // (width // LANES)
    total = jnp.zeros((cells, rank), F32)
    for block in range(width // LANES):
        where = slice(block * LANES, (block + 1) * LANES)
        projected = projected_ref[pl.ds(block * rank, rank), :]
        total += dot_f32(own_ref[:, where], projected, ((1,), (1,)))
        total += dot_f32(got_ref[:, where], projected, ((1,), (1,)))
    half = cells // 2
    both = jnp.concatenate([total[:half], total[half:]], axis=1).astype(BF16)
    out_ref[...] = jnp.broadcast_to(both[None], out_ref.shape)


def product_terms(own, got, projected, copies):
    cells = own.shape[0]
    return pl.pallas_call(
        product_kernel,
        out_shape=jax.ShapeDtypeStruct((copies, cells // 2, LANES), BF16),
        name="product_terms",
    )(own, got, projected)


def finish_kernel(n_rows, n_cols, parts_ref, out_ref, prod_ref):
    half = parts_ref.shape[1]
    rank = LANES // 2
    highest = lax.Precision.HIGHEST
    for row in range(n_rows):
        total = parts_ref[row * n_cols].astype(F32)
        for col in range(1, n_cols):
            total += parts_ref[row * n_cols + col].astype(F32)
        prod_ref[pl.ds(row * half, half), :] = total
    prod = prod_ref[...]
    wide = dot_f32(prod, prod, ((0,), (0,)), highest)
    gram = wide[:rank, :rank] + wide[rank:, rank:]
    eye = (
        lax.broadcasted_iota(jnp.int32, (rank, rank), 0)
        == lax.broadcasted_iota(jnp.int32, (rank, rank), 1)
    ).astype(F32)
    both = jnp.concatenate([gram, eye], axis=1)
    row_index = lax.broadcasted_iota(jnp.int32, (rank, 1), 0)
    pivots = jnp.zeros((rank, 1), F32)
    for k in range(rank):
        pivot = both[k:k + 1, k:k + 1]
        pivots = jnp.where(row_index == k, pivot, pivots)
        factor = jnp.where(row_index > k, both[:, k:k + 1] / pivot, 0.0)
        both = both - factor * both[k:k + 1, :]
    total_rows = n_rows * half * 2
    inverse = both[:, rank:] * (lax.rsqrt(pivots) * (total_rows ** 0.5))
    row = lax.axis_index("row")
    mine = prod_ref[pl.ds(pl.multiple_of(row * half, half), half), :]
    mine = jnp.where(lax.axis_index("col") == 0, mine[:, :rank], mine[:, rank:])
    out_ref[...] = dot_f32(mine, inverse, ((1,), (1,)), highest)


def finish(parts, n_rows, n_cols):
    half = parts.shape[1]
    return pl.pallas_call(
        functools.partial(finish_kernel, n_rows, n_cols),
        out_shape=jax.ShapeDtypeStruct((half, LANES // 2), F32),
        scratch_shapes=[pltpu.VMEM((n_rows * half, LANES), F32)],
        name="finish",
    )(parts)


def per_device(snapshot, mode2_factor, old_factor):
    n_rows, n_cols = lax.axis_size("row"), lax.axis_size("col")
    send, own = contract(snapshot, mode2_factor)
    got = lax.ppermute(send, "col", [(c, (c + 1) % n_cols) for c in range(n_cols)])
    partial = project(own, got, old_factor)
    parts = lax.all_to_all(partial.reshape(n_rows, -1, LANES), "row", 0, 0, tiled=True)
    chunks = lax.all_to_all(reduce_parts(parts), "row", 0, 0, tiled=True)
    terms = product_terms(own, got, chunks.reshape(-1, LANES), n_rows * n_cols)
    gathered = lax.all_to_all(terms, ("row", "col"), 0, 0, tiled=True)
    return finish(gathered, n_rows, n_cols)


def solution(mesh):
    return jax.shard_map(
        per_device,
        mesh=mesh,
        in_specs=(
            P(("groups", "row"), None, "col"),
            P(("groups", "col"), None),
            P(("groups", "row"), None),
        ),
        out_specs=P(("groups", "row", "col"), None),
        check_vma=False,
    )
```

```python
import functools

import jax
import jax.numpy as jnp
from jax import lax
from jax.experimental import pallas as pl
from jax.experimental.pallas import tpu as pltpu
from jax.sharding import PartitionSpec as P

F32 = jnp.float32
BF16 = jnp.bfloat16
LANES = 128
MIB = 2**20


def dot_f32(a, b, dims, precision=None):
    return lax.dot_general(a, b, (dims, ((), ())), precision=precision, preferred_element_type=F32)


def params(mib):
    return pltpu.CompilerParams(vmem_limit_bytes=mib * MIB)


def contract_kernel(step, snapshot_ref, mode2_ref, send_ref, own_ref, slab_ref, core_ref, sems):
    cells, fibers, depth = snapshot_ref.shape
    rank = mode2_ref.shape[0]
    reps = LANES // rank
    half = fibers // 2
    chunks = cells // step

    def copy(chunk):
        where = pl.ds(chunk * step, step)
        return pltpu.make_async_copy(snapshot_ref.at[where], slab_ref.at[where], sems.at[chunk])

    for chunk in range(chunks):
        copy(chunk).start()
    wide = jnp.concatenate([mode2_ref[...]] * reps, axis=0).T
    lane = lax.broadcasted_iota(jnp.int32, (step, LANES), 1)
    first = lax.axis_index("col") == 0

    for chunk in range(chunks):
        copy(chunk).wait()
        core = core_ref.at[chunk % 2]
        rows = pl.ds(chunk * step, step)
        core[...] = dot_f32(slab_ref[rows].reshape(step * fibers, depth), wide, ((1,), (0,)))

        def columns(start):
            part = core[pl.ds(start, step, stride=fibers), :]
            for r in range(1, reps):
                other = core[pl.ds(start + r, step, stride=fibers), :]
                part = jnp.where(lane < r * rank, part, other)
            return part

        for block in range(half // reps):
            low = columns(block * reps)
            high = columns(half + block * reps)
            where = slice(block * LANES, (block + 1) * LANES)
            own_ref[rows, where] = jnp.where(first, low, high).astype(BF16)
            send_ref[rows, where] = jnp.where(first, high, low).astype(BF16)


def contract(snapshot, mode2_t):
    cells, fibers, depth = snapshot.shape
    rank = mode2_t.shape[0]
    step = 16
    out = jax.ShapeDtypeStruct((cells, fibers // 2 * rank), BF16)
    return pl.pallas_call(
        functools.partial(contract_kernel, step),
        in_specs=[
            pl.BlockSpec(memory_space=pltpu.HBM),
            pl.BlockSpec(memory_space=pltpu.VMEM),
        ],
        out_shape=[out, out],
        scratch_shapes=[
            pltpu.VMEM(snapshot.shape, BF16),
            pltpu.VMEM((2, step * fibers, LANES), F32),
            pltpu.SemaphoreType.DMA((cells // step,)),
        ],
        compiler_params=params(16),
        name="contract",
    )(snapshot, mode2_t)


def project_kernel(n_rows, own_ref, got_ref, factor_ref, *refs):
    outs, scratch_ref = refs[:-1], refs[-1]
    rank = factor_ref.shape[0]
    factor = factor_ref[...]
    total = dot_f32(factor, own_ref[...], ((1,), (0,))) + dot_f32(factor, got_ref[...], ((1,), (0,)))
    for block in range(total.shape[1] // LANES):
        scratch_ref[pl.ds(block * rank, rank), :] = total[:, block * LANES:(block + 1) * LANES]
    row = lax.axis_index("row")
    size = outs[0].shape[0]
    for m, out in enumerate(outs):
        piece = lax.rem(row + m, n_rows)
        out[...] = scratch_ref[pl.ds(pl.multiple_of(piece * size, size), size), :].astype(BF16)


def project(own, got, factor_t, n_rows):
    rank = factor_t.shape[0]
    rows = rank * own.shape[1] // LANES
    return pl.pallas_call(
        functools.partial(project_kernel, n_rows),
        out_shape=[jax.ShapeDtypeStruct((rows // n_rows, LANES), BF16)] * n_rows,
        scratch_shapes=[pltpu.VMEM((rows, LANES), F32)],
        compiler_params=params(4),
        name="project",
    )(own, got, factor_t)


def reduce_kernel(*refs):
    total = refs[0][...].astype(F32)
    for ref in refs[1:-1]:
        total += ref[...].astype(F32)
    refs[-1][...] = total.astype(BF16)


def reduce_parts(parts):
    return pl.pallas_call(
        reduce_kernel,
        out_shape=jax.ShapeDtypeStruct(parts[0].shape, BF16),
        compiler_params=params(4),
        name="reduce_parts",
    )(*parts)


def product_kernel(n_rows, own_ref, got_ref, *refs):
    pieces, out_ref, scratch_ref = refs[:-2], refs[-2], refs[-1]
    cells, width = own_ref.shape
    rank = scratch_ref.shape[0] // (width // LANES)
    row = lax.axis_index("row")
    size = pieces[0].shape[0]
    for m, ref in enumerate(pieces):
        piece = lax.rem(row - m + n_rows, n_rows)
        scratch_ref[pl.ds(pl.multiple_of(piece * size, size), size), :] = ref[...].astype(F32)
    total = jnp.zeros((cells, rank), F32)
    for block in range(width // LANES):
        where = slice(block * LANES, (block + 1) * LANES)
        projected = scratch_ref[pl.ds(block * rank, rank), :].astype(BF16)
        total += dot_f32(own_ref[:, where], projected, ((1,), (1,)))
        total += dot_f32(got_ref[:, where], projected, ((1,), (1,)))
    half = cells // 2
    out_ref[...] = jnp.concatenate([total[:half], total[half:]], axis=1).astype(BF16)


def product_terms(own, got, pieces):
    cells = own.shape[0]
    rows = len(pieces) * pieces[0].shape[0]
    return pl.pallas_call(
        functools.partial(product_kernel, len(pieces)),
        out_shape=jax.ShapeDtypeStruct((cells // 2, LANES), BF16),
        scratch_shapes=[pltpu.VMEM((rows, LANES), F32)],
        compiler_params=params(4),
        name="product_terms",
    )(own, got, *pieces)


def finish_kernel(n_rows, n_cols, *refs):
    terms, out_ref, prod_ref = refs[:-2], refs[-2], refs[-1]
    half = terms[0].shape[0]
    rank = LANES // 2
    highest = lax.Precision.HIGHEST
    col = lax.axis_index("col")
    for step in range(n_rows):
        total = terms[step * n_cols][...].astype(F32)
        for m in range(1, n_cols):
            total += terms[step * n_cols + m][...].astype(F32)
        prod_ref[pl.ds(step * half, half), :] = total
    prod = prod_ref[...]
    wide = dot_f32(prod, prod, ((0,), (0,)), highest)
    gram = wide[:rank, :rank] + wide[rank:, rank:]
    eye = (
        lax.broadcasted_iota(jnp.int32, (rank, rank), 0)
        == lax.broadcasted_iota(jnp.int32, (rank, rank), 1)
    ).astype(F32)
    both = jnp.concatenate([gram, eye], axis=1)
    row_index = lax.broadcasted_iota(jnp.int32, (rank, 1), 0)
    pivots = jnp.zeros((rank, 1), F32)
    for k in range(rank):
        pivot = both[k:k + 1, k:k + 1]
        pivots = jnp.where(row_index == k, pivot, pivots)
        factor = jnp.where(row_index > k, both[:, k:k + 1] / pivot, 0.0)
        both = both - factor * both[k:k + 1, :]
    total_rows = n_rows * half * 2
    inverse = both[:, rank:] * (lax.rsqrt(pivots) * (total_rows ** 0.5))
    mine = prod_ref[pl.ds(0, half), :]
    mine = jnp.where(col == 0, mine[:, :rank], mine[:, rank:])
    out_ref[...] = dot_f32(mine, inverse, ((1,), (1,)), highest)


def finish(terms, n_rows, n_cols):
    half = terms[0].shape[0]
    return pl.pallas_call(
        functools.partial(finish_kernel, n_rows, n_cols),
        out_shape=jax.ShapeDtypeStruct((half, LANES // 2), F32),
        scratch_shapes=[pltpu.VMEM((n_rows * half, LANES), F32)],
        compiler_params=params(16),
        name="finish",
    )(*terms)


def per_device(snapshot, mode2_factor, old_factor):
    n_rows, n_cols = lax.axis_size("row"), lax.axis_size("col")

    def shift(x, row_by, col_by):
        if row_by == 0 and col_by == 0:
            return x
        pairs = [
            (r * n_cols + c, (r + row_by) % n_rows * n_cols + (c + col_by) % n_cols)
            for r in range(n_rows)
            for c in range(n_cols)
        ]
        return lax.ppermute(x, ("row", "col"), pairs)

    send, own = contract(snapshot, mode2_factor.T)
    got = shift(send, 0, 1)
    pieces = project(own, got, old_factor.T, n_rows)
    mine = reduce_parts([shift(piece, m, 0) for m, piece in enumerate(pieces)])
    projected = [shift(mine, m, 0) for m in range(n_rows)]
    term = product_terms(own, got, projected)
    terms = [shift(term, r, c) for r in range(n_rows) for c in range(n_cols)]
    return finish(terms, n_rows, n_cols)


def solution(mesh):
    return jax.shard_map(
        per_device,
        mesh=mesh,
        in_specs=(
            P(("groups", "row"), None, "col"),
            P(("groups", "col"), None),
            P(("groups", "row"), None),
        ),
        out_specs=P(("groups", "row", "col"), None),
        check_vma=False,
    )
```

```python
import functools

import jax
import jax.numpy as jnp
from jax import lax
from jax.experimental import pallas as pl
from jax.experimental.pallas import tpu as pltpu
from jax.sharding import PartitionSpec as P

F32 = jnp.float32
BF16 = jnp.bfloat16
LANES = 128
MIB = 2**20


def dot_f32(a, b, dims, precision=None):
    return lax.dot_general(a, b, (dims, ((), ())), precision=precision, preferred_element_type=F32)


def params(mib):
    return pltpu.CompilerParams(vmem_limit_bytes=mib * MIB)


def contract_kernel(step, snapshot_ref, mode2_ref, send_ref, own_ref, slab_ref, core_ref, sems):
    cells, fibers, depth = snapshot_ref.shape
    rank = mode2_ref.shape[0]
    reps = LANES // rank
    half = fibers // 2
    chunks = cells // step

    def copy(chunk):
        where = pl.ds(chunk * step, step)
        return pltpu.make_async_copy(snapshot_ref.at[where], slab_ref.at[where], sems.at[chunk])

    for chunk in range(chunks):
        copy(chunk).start()
    wide = jnp.concatenate([mode2_ref[...]] * reps, axis=0).T
    lane = lax.broadcasted_iota(jnp.int32, (step, LANES), 1)
    first = lax.axis_index("col") == 0

    for chunk in range(chunks):
        copy(chunk).wait()
        core = core_ref.at[chunk % 2]
        rows = pl.ds(chunk * step, step)
        core[...] = dot_f32(slab_ref[rows].reshape(step * fibers, depth), wide, ((1,), (0,)))

        def columns(start):
            part = core[pl.ds(start, step, stride=fibers), :]
            for r in range(1, reps):
                other = core[pl.ds(start + r, step, stride=fibers), :]
                part = jnp.where(lane < r * rank, part, other)
            return part

        for block in range(half // reps):
            low = columns(block * reps)
            high = columns(half + block * reps)
            where = slice(block * LANES, (block + 1) * LANES)
            own_ref[rows, where] = jnp.where(first, low, high).astype(BF16)
            send_ref[rows, where] = jnp.where(first, high, low).astype(BF16)


def contract(snapshot, mode2_t):
    cells, fibers, depth = snapshot.shape
    rank = mode2_t.shape[0]
    step = 16
    out = jax.ShapeDtypeStruct((cells, fibers // 2 * rank), BF16)
    return pl.pallas_call(
        functools.partial(contract_kernel, step),
        in_specs=[
            pl.BlockSpec(memory_space=pltpu.HBM),
            pl.BlockSpec(memory_space=pltpu.VMEM),
        ],
        out_shape=[out, out],
        scratch_shapes=[
            pltpu.VMEM(snapshot.shape, BF16),
            pltpu.VMEM((2, step * fibers, LANES), F32),
            pltpu.SemaphoreType.DMA((cells // step,)),
        ],
        compiler_params=params(57),
        name="contract",
    )(snapshot, mode2_t)


def add_to(*refs):
    total = refs[0][...].astype(F32)
    for ref in refs[1:]:
        total += ref[...].astype(F32)
    return total


def project_kernel(own_ref, got_ref, factor_ref, keep_ref, send_ref):
    rank = factor_ref.shape[0]
    factor = factor_ref[...]
    total = dot_f32(factor, own_ref[...], ((1,), (0,))) + dot_f32(factor, got_ref[...], ((1,), (0,)))
    even = lax.rem(lax.axis_index("row"), 2) == 0
    blocks = total.shape[1] // LANES // 2
    for block in range(blocks):
        low = total[:, block * LANES:(block + 1) * LANES]
        high = total[:, (block + blocks) * LANES:(block + blocks + 1) * LANES]
        rows = pl.ds(block * rank, rank)
        keep_ref[rows, :] = jnp.where(even, low, high)
        send_ref[rows, :] = jnp.where(even, high, low).astype(BF16)


def project(own, got, factor_t):
    rank = factor_t.shape[0]
    shape = (rank * own.shape[1] // LANES // 2, LANES)
    return pl.pallas_call(
        project_kernel,
        out_shape=[jax.ShapeDtypeStruct(shape, F32), jax.ShapeDtypeStruct(shape, BF16)],
        compiler_params=params(4),
        name="project",
    )(own, got, factor_t)


def add_kernel(mine_ref, got_ref, out_ref):
    out_ref[...] = add_to(mine_ref, got_ref).astype(out_ref.dtype)


def add(mine, got):
    return pl.pallas_call(
        add_kernel,
        out_shape=jax.ShapeDtypeStruct(got.shape, got.dtype),
        compiler_params=params(4),
        name="add",
    )(mine, got)


def product_kernel(own_ref, got_ref, mine_ref, other_ref, out_ref):
    cells, width = own_ref.shape
    blocks = width // LANES // 2
    rank = mine_ref.shape[0] // blocks
    even = lax.rem(lax.axis_index("row"), 2) == 0
    total = jnp.zeros((cells, rank), F32)
    for block in range(blocks):
        rows = pl.ds(block * rank, rank)
        mine, other = mine_ref[rows, :], other_ref[rows, :]
        low = jnp.where(even, mine, other)
        high = jnp.where(even, other, mine)
        for at, projected in ((block, low), (block + blocks, high)):
            where = slice(at * LANES, (at + 1) * LANES)
            total += dot_f32(own_ref[:, where], projected, ((1,), (1,)))
            total += dot_f32(got_ref[:, where], projected, ((1,), (1,)))
    half = cells // 2
    out_ref[...] = jnp.concatenate([total[:half], total[half:]], axis=1).astype(BF16)


def product_terms(own, got, mine, other):
    return pl.pallas_call(
        product_kernel,
        out_shape=jax.ShapeDtypeStruct((own.shape[0] // 2, LANES), BF16),
        compiler_params=params(4),
        name="product_terms",
    )(own, got, mine, other)


def gram_kernel(term_ref, got_ref, out_ref):
    product = add_to(term_ref, got_ref)
    rank = LANES // 2
    wide = dot_f32(product, product, ((0,), (0,)), lax.Precision.HIGHEST)
    gram = wide[:rank, :rank] + wide[rank:, rank:]
    out_ref[...] = jnp.concatenate([gram[:rank // 2], gram[rank // 2:]], axis=1)


def local_gram(term, got):
    return pl.pallas_call(
        gram_kernel,
        out_shape=jax.ShapeDtypeStruct((LANES // 4, LANES), F32),
        compiler_params=params(4),
        name="local_gram",
    )(term, got)


def finish_kernel(total_rows, term_ref, got_term_ref, gram_ref, got_gram_ref, out_ref):
    rank = LANES // 2
    packed = gram_ref[...] + got_gram_ref[...]
    gram = jnp.concatenate([packed[:, :rank], packed[:, rank:]], axis=0)
    eye = (
        lax.broadcasted_iota(jnp.int32, (rank, rank), 0)
        == lax.broadcasted_iota(jnp.int32, (rank, rank), 1)
    ).astype(F32)
    both = jnp.concatenate([gram, eye], axis=1)
    row_index = lax.broadcasted_iota(jnp.int32, (rank, 1), 0)
    pivots = jnp.zeros((rank, 1), F32)
    for k in range(rank):
        pivot = both[k:k + 1, k:k + 1]
        pivots = jnp.where(row_index == k, pivot, pivots)
        factor = jnp.where(row_index > k, both[:, k:k + 1] / pivot, 0.0)
        both = both - factor * both[k:k + 1, :]
    inverse = both[:, rank:] * (lax.rsqrt(pivots) * (total_rows ** 0.5))
    product = add_to(term_ref, got_term_ref)
    mine = jnp.where(lax.axis_index("col") == 0, product[:, :rank], product[:, rank:])
    out_ref[...] = dot_f32(mine, inverse, ((1,), (1,)), lax.Precision.HIGHEST)


def finish(total_rows, term, got_term, gram, got_gram):
    return pl.pallas_call(
        functools.partial(finish_kernel, total_rows),
        out_shape=jax.ShapeDtypeStruct((term.shape[0], LANES // 2), F32),
        compiler_params=params(4),
        name="finish",
    )(term, got_term, gram, got_gram)


def swap(x, axis, mask):
    return lax.ppermute(x, axis, [(d, d ^ mask) for d in range(lax.axis_size(axis))])


def per_device(snapshot, mode2_factor, old_factor):
    n_rows = lax.axis_size("row")
    masks = [1 << bit for bit in range(n_rows.bit_length() - 1)]
    total_rows = snapshot.shape[0] * n_rows

    send, own = contract(snapshot, mode2_factor.T)
    got = swap(send, "col", 1)

    keep, send = project(own, got, old_factor.T)
    mine = add(keep, swap(send, "row", masks[0]))
    for mask in masks[1:]:
        mine = add(mine, swap(mine, "row", mask))
    other = swap(mine, "row", masks[0])

    term = product_terms(own, got, mine, other)
    got_term = swap(term, "col", 1)
    gram = local_gram(term, got_term)
    for mask in masks[:-1]:
        gram = add(gram, swap(gram, "row", mask))
    return finish(total_rows, term, got_term, gram, swap(gram, "row", masks[-1]))


def solution(mesh):
    return jax.shard_map(
        per_device,
        mesh=mesh,
        in_specs=(
            P(("groups", "row"), None, "col"),
            P(("groups", "col"), None),
            P(("groups", "row"), None),
        ),
        out_specs=P(("groups", "row", "col"), None),
        check_vma=False,
    )
```

```python
import functools

import jax
import jax.numpy as jnp
from jax import lax
from jax.experimental import pallas as pl
from jax.experimental.pallas import tpu as pltpu
from jax.sharding import PartitionSpec as P

F32 = jnp.float32
BF16 = jnp.bfloat16
LANES = 128
MIB = 2**20


def dot_f32(a, b, dims, precision=None):
    return lax.dot_general(a, b, (dims, ((), ())), precision=precision, preferred_element_type=F32)


def params(mib):
    return pltpu.CompilerParams(vmem_limit_bytes=mib * MIB)


def contract_kernel(
    step, ahead, snapshot_ref, mode2_ref, factor_ref, core_ref, projected_ref,
    slab_ref, wide_ref, even_ref, odd_ref, sems,
):
    cells, fibers, depth = snapshot_ref.shape
    rank = mode2_ref.shape[0]
    reps = LANES // rank
    chunks = cells // step
    flat = (even_ref, odd_ref)

    def copy(chunk):
        where = pl.ds(chunk * step, step)
        return pltpu.make_async_copy(snapshot_ref.at[where], slab_ref.at[where], sems.at[chunk])

    for chunk in range(ahead):
        copy(chunk).start()
    wide_ref[...] = jnp.concatenate([mode2_ref[...]] * reps, axis=0).T
    lane = lax.broadcasted_iota(jnp.int32, (step, LANES), 1)

    def multiply(chunk):
        x = slab_ref[pl.ds(chunk * step, step)].reshape(step * fibers, depth)
        flat[chunk % 2][...] = dot_f32(x, wide_ref[...], ((1,), (0,)))

    def spread(chunk):
        source = flat[chunk % 2]
        for block in range(fibers // reps):
            part = source[pl.ds(block * reps, step, stride=fibers), :]
            for r in range(1, reps):
                other = source[pl.ds(block * reps + r, step, stride=fibers), :]
                part = jnp.where(lane < r * rank, part, other)
            where = slice(block * LANES, (block + 1) * LANES)
            core_ref[pl.ds(chunk * step, step), where] = part.astype(BF16)

    for chunk in range(chunks):
        copy(chunk).wait()
        if chunk + ahead < chunks:
            copy(chunk + ahead).start()
        multiply(chunk)
        if chunk:
            spread(chunk - 1)
    spread(chunks - 1)

    total = dot_f32(factor_ref[...], core_ref[...], ((1,), (0,)))
    for block in range(total.shape[1] // LANES):
        where = slice(block * LANES, (block + 1) * LANES)
        projected_ref[pl.ds(block * rank, rank), :] = total[:, where].astype(BF16)


def contract(snapshot, mode2_t, factor_t):
    cells, fibers, depth = snapshot.shape
    rank = mode2_t.shape[0]
    step = 16
    width = fibers * rank
    return pl.pallas_call(
        functools.partial(contract_kernel, step, 3),
        in_specs=[
            pl.BlockSpec(memory_space=pltpu.HBM),
            pl.BlockSpec(memory_space=pltpu.VMEM),
            pl.BlockSpec(memory_space=pltpu.VMEM),
        ],
        out_shape=[
            jax.ShapeDtypeStruct((cells, width), BF16),
            jax.ShapeDtypeStruct((rank * width // LANES, LANES), BF16),
        ],
        scratch_shapes=[
            pltpu.VMEM(snapshot.shape, BF16),
            pltpu.VMEM((depth, LANES), BF16),
            pltpu.VMEM((step * fibers, LANES), F32),
            pltpu.VMEM((step * fibers, LANES), F32),
            pltpu.SemaphoreType.DMA((cells // step,)),
        ],
        compiler_params=params(57),
        name="contract",
    )(snapshot, mode2_t, factor_t)


def add_kernel(mine_ref, got_ref, out_ref):
    total = mine_ref[...].astype(F32) + got_ref[...].astype(F32)
    out_ref[...] = total.astype(out_ref.dtype)


def add(mine, got):
    return pl.pallas_call(
        add_kernel,
        out_shape=jax.ShapeDtypeStruct(got.shape, got.dtype),
        compiler_params=params(4),
        name="add",
    )(mine, got)


def halves_kernel(mine_ref, got_ref, low_ref, high_ref):
    half = low_ref.shape[0]
    for out, start in ((low_ref, 0), (high_ref, half)):
        rows = pl.ds(start, half)
        out[...] = (mine_ref[rows, :].astype(F32) + got_ref[rows, :].astype(F32)).astype(BF16)


def add_in_halves(mine, got):
    out = jax.ShapeDtypeStruct((mine.shape[0] // 2, LANES), BF16)
    return pl.pallas_call(
        halves_kernel, out_shape=[out, out], compiler_params=params(4), name="add_in_halves"
    )(mine, got)


def product_kernel(own_ref, got_ref, low_ref, high_ref, product_ref, gram_ref):
    cells, width = own_ref.shape
    blocks = width // LANES // 2
    rank = low_ref.shape[0] // blocks
    total = jnp.zeros((cells, rank), F32)
    for start, ref in ((0, low_ref), (blocks, high_ref)):
        for block in range(blocks):
            projected = ref[pl.ds(block * rank, rank), :]
            where = slice((start + block) * LANES, (start + block + 1) * LANES)
            total += dot_f32(own_ref[:, where], projected, ((1,), (1,)))
            total += dot_f32(got_ref[:, where], projected, ((1,), (1,)))
    half = cells // 2
    product_ref[...] = jnp.concatenate([total[:half], total[half:]], axis=1)
    gram = dot_f32(total, total, ((0,), (0,)), lax.Precision.HIGHEST)
    gram_ref[...] = jnp.concatenate([gram[:rank // 2], gram[rank // 2:]], axis=1)


def product_and_gram(own, got, low, high):
    return pl.pallas_call(
        product_kernel,
        out_shape=[
            jax.ShapeDtypeStruct((own.shape[0] // 2, LANES), F32),
            jax.ShapeDtypeStruct((LANES // 4, LANES), F32),
        ],
        compiler_params=params(8),
        name="product_and_gram",
    )(own, got, low, high)


def finish_kernel(total_rows, mine_ref, got_ref, gram_ref, got_gram_ref, out_ref):
    rank = LANES // 2
    hub = lax.axis_index("col") == 1
    packed = jnp.where(hub, gram_ref[...], got_gram_ref[...])
    gram = jnp.concatenate([packed[:, :rank], packed[:, rank:]], axis=0)
    eye = (
        lax.broadcasted_iota(jnp.int32, (rank, rank), 0)
        == lax.broadcasted_iota(jnp.int32, (rank, rank), 1)
    ).astype(F32)
    both = jnp.concatenate([gram, eye], axis=1)
    row_index = lax.broadcasted_iota(jnp.int32, (rank, 1), 0)
    pivots = jnp.zeros((rank, 1), F32)
    for k in range(rank):
        pivot = both[k:k + 1, k:k + 1]
        pivots = jnp.where(row_index == k, pivot, pivots)
        factor = jnp.where(row_index > k, both[:, k:k + 1] / pivot, 0.0)
        both = both - factor * both[k:k + 1, :]
    inverse = both[:, rank:] * (lax.rsqrt(pivots) * (total_rows ** 0.5))
    mine = jnp.where(hub, mine_ref[:, rank:], got_ref[:, :rank])
    out_ref[...] = dot_f32(mine, inverse, ((1,), (1,)), lax.Precision.HIGHEST)


def finish(total_rows, mine, got, gram, got_gram):
    return pl.pallas_call(
        functools.partial(finish_kernel, total_rows),
        out_shape=jax.ShapeDtypeStruct((mine.shape[0], LANES // 2), F32),
        compiler_params=params(4),
        name="finish",
    )(mine, got, gram, got_gram)


def per_device(snapshot, mode2_factor, old_factor):
    n_rows, n_cols = lax.axis_size("row"), lax.axis_size("col")
    masks = [1 << bit for bit in range(n_rows.bit_length() - 1)]
    total_rows = snapshot.shape[0] * n_rows

    def to_hub(x):
        return lax.ppermute(x, "col", [(0, 1)])

    def from_hub(x):
        return lax.ppermute(x, "col", [(1, 0)])

    def swap(x, mask):
        pairs = [(r * n_cols + 1, (r ^ mask) * n_cols + 1) for r in range(n_rows)]
        return lax.ppermute(x, ("row", "col"), pairs)

    core, projected = contract(snapshot, mode2_factor.T, old_factor.T)
    got_projected = to_hub(projected)
    got_core = to_hub(core)
    low, high = add_in_halves(projected, got_projected)
    for mask, turned in zip(masks, masks[1:] + masks[:1]):
        got_low, got_high = swap(low, mask), swap(high, turned)
        low, high = add(low, got_low), add(high, got_high)

    product, gram = product_and_gram(core, got_core, low, high)
    got_product = from_hub(product)
    for mask in masks:
        gram = add(gram, swap(gram, mask))
    return finish(total_rows, product, got_product, gram, from_hub(gram))


def solution(mesh):
    return jax.shard_map(
        per_device,
        mesh=mesh,
        in_specs=(
            P(("groups", "row"), None, "col"),
            P(("groups", "col"), None),
            P(("groups", "row"), None),
        ),
        out_specs=P(("groups", "row", "col"), None),
        check_vma=False,
    )
```

```python
import functools

import jax
import jax.numpy as jnp
from jax import lax
from jax.experimental import pallas as pl
from jax.experimental.pallas import tpu as pltpu
from jax.sharding import PartitionSpec as P

F32 = jnp.float32
BF16 = jnp.bfloat16
LANES = 128
MIB = 2**20


def dot_f32(a, b, dims, precision=None):
    return lax.dot_general(a, b, (dims, ((), ())), precision=precision, preferred_element_type=F32)


def params(mib):
    return pltpu.CompilerParams(vmem_limit_bytes=mib * MIB)


def contract_kernel(
    step, ahead, snapshot_ref, mode2_ref, factor_ref, core_ref, projected_ref,
    slab_ref, wide_ref, even_ref, odd_ref, sems,
):
    cells, fibers, depth = snapshot_ref.shape
    rank = mode2_ref.shape[0]
    reps = LANES // rank
    chunks = cells // step

    def copy(chunk):
        where = pl.ds(chunk * step, step)
        return pltpu.make_async_copy(snapshot_ref.at[where], slab_ref.at[where], sems.at[chunk])

    for chunk in range(ahead):
        copy(chunk).start()
    wide_ref[...] = jnp.concatenate([mode2_ref[...]] * reps, axis=0).T
    lane = lax.broadcasted_iota(jnp.int32, (step, LANES), 1)

    def multiply(chunk, flat_ref):
        copy(chunk).wait()

        @pl.when(chunk + ahead < chunks)
        def _():
            copy(chunk + ahead).start()

        x = slab_ref[pl.ds(chunk * step, step)].reshape(step * fibers, depth)
        flat_ref[...] = dot_f32(x, wide_ref[...], ((1,), (0,)))

    def spread(chunk, flat_ref):
        rows = pl.ds(pl.multiple_of(chunk * step, step), step)
        for block in range(fibers // reps):
            part = flat_ref[pl.ds(block * reps, step, stride=fibers), :]
            for r in range(1, reps):
                other = flat_ref[pl.ds(block * reps + r, step, stride=fibers), :]
                part = jnp.where(lane < r * rank, part, other)
            core_ref[rows, block * LANES:(block + 1) * LANES] = part.astype(BF16)

    def two_chunks(pair, _):
        multiply(2 * pair, even_ref)
        spread(jnp.maximum(2 * pair - 1, 0), odd_ref)
        multiply(2 * pair + 1, odd_ref)
        spread(2 * pair, even_ref)
        return _

    lax.fori_loop(0, chunks // 2, two_chunks, 0)
    spread(chunks - 1, odd_ref)

    total = dot_f32(factor_ref[...], core_ref[...], ((1,), (0,)))
    for block in range(total.shape[1] // LANES):
        where = slice(block * LANES, (block + 1) * LANES)
        projected_ref[pl.ds(block * rank, rank), :] = total[:, where].astype(BF16)


def contract(snapshot, mode2_t, factor_t):
    cells, fibers, depth = snapshot.shape
    rank = mode2_t.shape[0]
    step = 16
    width = fibers * rank
    return pl.pallas_call(
        functools.partial(contract_kernel, step, 3),
        in_specs=[
            pl.BlockSpec(memory_space=pltpu.HBM),
            pl.BlockSpec(memory_space=pltpu.VMEM),
            pl.BlockSpec(memory_space=pltpu.VMEM),
        ],
        out_shape=[
            jax.ShapeDtypeStruct((cells, width), BF16),
            jax.ShapeDtypeStruct((rank * width // LANES, LANES), BF16),
        ],
        scratch_shapes=[
            pltpu.VMEM(snapshot.shape, BF16),
            pltpu.VMEM((depth, LANES), BF16),
            pltpu.VMEM((step * fibers, LANES), F32),
            pltpu.VMEM((step * fibers, LANES), F32),
            pltpu.SemaphoreType.DMA((cells // step,)),
        ],
        compiler_params=params(57),
        name="contract",
    )(snapshot, mode2_t, factor_t)


def add_kernel(mine_ref, got_ref, out_ref):
    total = mine_ref[...].astype(F32) + got_ref[...].astype(F32)
    out_ref[...] = total.astype(out_ref.dtype)


def add(mine, got):
    return pl.pallas_call(
        add_kernel,
        out_shape=jax.ShapeDtypeStruct(got.shape, got.dtype),
        compiler_params=params(4),
        name="add",
    )(mine, got)


def halves_kernel(mine_ref, got_ref, low_ref, high_ref):
    half = low_ref.shape[0]
    for out, start in ((low_ref, 0), (high_ref, half)):
        rows = pl.ds(start, half)
        out[...] = (mine_ref[rows, :].astype(F32) + got_ref[rows, :].astype(F32)).astype(BF16)


def add_in_halves(mine, got):
    out = jax.ShapeDtypeStruct((mine.shape[0] // 2, LANES), BF16)
    return pl.pallas_call(
        halves_kernel, out_shape=[out, out], compiler_params=params(4), name="add_in_halves"
    )(mine, got)


def product_kernel(own_ref, got_ref, low_ref, high_ref, product_ref, gram_ref):
    cells, width = own_ref.shape
    blocks = width // LANES // 2
    rank = low_ref.shape[0] // blocks
    total = jnp.zeros((cells, rank), F32)
    for start, ref in ((0, low_ref), (blocks, high_ref)):
        for block in range(blocks):
            projected = ref[pl.ds(block * rank, rank), :]
            where = slice((start + block) * LANES, (start + block + 1) * LANES)
            total += dot_f32(own_ref[:, where], projected, ((1,), (1,)))
            total += dot_f32(got_ref[:, where], projected, ((1,), (1,)))
    half = cells // 2
    product_ref[...] = jnp.concatenate([total[:half], total[half:]], axis=1)
    gram = dot_f32(total, total, ((0,), (0,)), lax.Precision.HIGHEST)
    gram_ref[...] = jnp.concatenate([gram[:rank // 2], gram[rank // 2:]], axis=1)


def product_and_gram(own, got, low, high):
    return pl.pallas_call(
        product_kernel,
        out_shape=[
            jax.ShapeDtypeStruct((own.shape[0] // 2, LANES), F32),
            jax.ShapeDtypeStruct((LANES // 4, LANES), F32),
        ],
        compiler_params=params(8),
        name="product_and_gram",
    )(own, got, low, high)


def finish_kernel(total_rows, mine_ref, got_ref, gram_ref, got_gram_ref, out_ref):
    rank = LANES // 2
    hub = lax.axis_index("col") == 1
    packed = jnp.where(hub, gram_ref[...], got_gram_ref[...])
    gram = jnp.concatenate([packed[:, :rank], packed[:, rank:]], axis=0)
    eye = (
        lax.broadcasted_iota(jnp.int32, (rank, rank), 0)
        == lax.broadcasted_iota(jnp.int32, (rank, rank), 1)
    ).astype(F32)
    both = jnp.concatenate([gram, eye], axis=1)
    row_index = lax.broadcasted_iota(jnp.int32, (rank, 1), 0)
    pivots = jnp.zeros((rank, 1), F32)
    for k in range(rank):
        pivot = both[k:k + 1, k:k + 1]
        pivots = jnp.where(row_index == k, pivot, pivots)
        factor = jnp.where(row_index > k, both[:, k:k + 1] / pivot, 0.0)
        both = both - factor * both[k:k + 1, :]
    inverse = both[:, rank:] * (lax.rsqrt(pivots) * (total_rows ** 0.5))
    mine = jnp.where(hub, mine_ref[:, rank:], got_ref[:, :rank])
    out_ref[...] = dot_f32(mine, inverse, ((1,), (1,)), lax.Precision.HIGHEST)


def finish(total_rows, mine, got, gram, got_gram):
    return pl.pallas_call(
        functools.partial(finish_kernel, total_rows),
        out_shape=jax.ShapeDtypeStruct((mine.shape[0], LANES // 2), F32),
        compiler_params=params(4),
        name="finish",
    )(mine, got, gram, got_gram)


def per_device(snapshot, mode2_factor, old_factor):
    n_rows, n_cols = lax.axis_size("row"), lax.axis_size("col")
    masks = [1 << bit for bit in range(n_rows.bit_length() - 1)]
    total_rows = snapshot.shape[0] * n_rows

    def in_chip(x):
        return lax.ppermute(x, "col", [(c, (c + 1) % n_cols) for c in range(n_cols)])

    def swap(x, mask):
        pairs = [
            (r * n_cols + c, (r ^ (mask if c else 0)) * n_cols + c)
            for r in range(n_rows)
            for c in range(n_cols)
        ]
        return lax.ppermute(x, ("row", "col"), pairs)

    core, projected = contract(snapshot, mode2_factor.T, old_factor.T)
    got_projected = in_chip(projected)
    got_core = in_chip(core)
    low, high = add_in_halves(projected, got_projected)
    for mask, turned in zip(masks, masks[1:] + masks[:1]):
        got_low, got_high = swap(low, mask), swap(high, turned)
        low, high = add(low, got_low), add(high, got_high)

    product, gram = product_and_gram(core, got_core, low, high)
    got_product = in_chip(product)
    for mask in masks:
        gram = add(gram, swap(gram, mask))
    return finish(total_rows, product, got_product, gram, in_chip(gram))


def solution(mesh):
    return jax.shard_map(
        per_device,
        mesh=mesh,
        in_specs=(
            P(("groups", "row"), None, "col"),
            P(("groups", "col"), None),
            P(("groups", "row"), None),
        ),
        out_specs=P(("groups", "row", "col"), None),
        check_vma=False,
    )
```

```python
import functools

import jax
import jax.numpy as jnp
from jax import lax
from jax.experimental import pallas as pl
from jax.experimental.pallas import tpu as pltpu
from jax.sharding import PartitionSpec as P

F32 = jnp.float32
BF16 = jnp.bfloat16
LANES = 128
MIB = 2**20


def dot_f32(a, b, dims, precision=None):
    return lax.dot_general(a, b, (dims, ((), ())), precision=precision, preferred_element_type=F32)


def params(mib):
    return pltpu.CompilerParams(vmem_limit_bytes=mib * MIB)


def own_half():
    row = lax.axis_index("row")
    half = lax.axis_index("col")
    for bit in range(lax.axis_size("row").bit_length() - 1):
        half += lax.rem(lax.div(row, 1 << bit), 2)
    return lax.rem(half, 2)


def contract_kernel(
    step, parts, snapshot_ref, mode2_ref, send_ref, own_ref,
    slab_ref, wide_ref, even_ref, odd_ref, sems,
):
    cells, fibers, depth = snapshot_ref.shape
    rank = mode2_ref.shape[0]
    reps = LANES // rank
    half = fibers // 2
    chunks = cells // step

    def copy(start, size, chunk):
        where = pl.ds(start, size)
        return pltpu.make_async_copy(snapshot_ref.at[where], slab_ref.at[where], sems.at[chunk])

    def start(piece, _):
        size = step // parts
        copy(piece * size, size, piece // parts).start()
        return _

    lax.fori_loop(0, chunks * parts, start, 0)
    wide_ref[...] = jnp.concatenate([mode2_ref[...]] * reps, axis=0).T
    lane = lax.broadcasted_iota(jnp.int32, (step, LANES), 1)
    own_start = own_half() * half
    send_start = half - own_start

    def multiply(chunk, flat_ref):
        copy(chunk * step, step, chunk).wait()
        x = slab_ref[pl.ds(chunk * step, step)].reshape(step * fibers, depth)
        flat_ref[...] = dot_f32(x, wide_ref[...], ((1,), (0,)))

    def spread(chunk, flat_ref):
        rows = pl.ds(pl.multiple_of(chunk * step, step), step)
        for base, out_ref in ((own_start, own_ref), (send_start, send_ref)):
            for block in range(half // reps):
                part = flat_ref[pl.ds(base + block * reps, step, stride=fibers), :]
                for r in range(1, reps):
                    other = flat_ref[pl.ds(base + block * reps + r, step, stride=fibers), :]
                    part = jnp.where(lane < r * rank, part, other)
                out_ref[rows, block * LANES:(block + 1) * LANES] = part.astype(BF16)

    def two_chunks(pair, _):
        multiply(2 * pair, even_ref)
        spread(jnp.maximum(2 * pair - 1, 0), odd_ref)
        multiply(2 * pair + 1, odd_ref)
        spread(2 * pair, even_ref)
        return _

    lax.fori_loop(0, chunks // 2, two_chunks, 0)
    spread(chunks - 1, odd_ref)


def contract(snapshot, mode2_t):
    cells, fibers, depth = snapshot.shape
    rank = mode2_t.shape[0]
    step = 16
    out = jax.ShapeDtypeStruct((cells, fibers // 2 * rank), BF16)
    return pl.pallas_call(
        functools.partial(contract_kernel, step, 4),
        in_specs=[
            pl.BlockSpec(memory_space=pltpu.HBM),
            pl.BlockSpec(memory_space=pltpu.VMEM),
        ],
        out_shape=[out, out],
        scratch_shapes=[
            pltpu.VMEM(snapshot.shape, BF16),
            pltpu.VMEM((depth, LANES), BF16),
            pltpu.VMEM((step * fibers, LANES), F32),
            pltpu.VMEM((step * fibers, LANES), F32),
            pltpu.SemaphoreType.DMA((cells // step,)),
        ],
        compiler_params=params(50),
        name="contract",
    )(snapshot, mode2_t)


def add_to(*refs):
    total = refs[0][...].astype(F32)
    for ref in refs[1:]:
        total += ref[...].astype(F32)
    return total


def project_kernel(own_ref, got_ref, factor_ref, keep_ref, send_ref):
    rank = factor_ref.shape[0]
    factor = factor_ref[...]
    total = dot_f32(factor, own_ref[...], ((1,), (0,))) + dot_f32(factor, got_ref[...], ((1,), (0,)))
    even = lax.rem(lax.axis_index("row"), 2) == 0
    blocks = total.shape[1] // LANES // 2
    for block in range(blocks):
        low = total[:, block * LANES:(block + 1) * LANES]
        high = total[:, (block + blocks) * LANES:(block + blocks + 1) * LANES]
        rows = pl.ds(block * rank, rank)
        keep_ref[rows, :] = jnp.where(even, low, high)
        send_ref[rows, :] = jnp.where(even, high, low).astype(BF16)


def project(own, got, factor_t):
    rank = factor_t.shape[0]
    shape = (rank * own.shape[1] // LANES // 2, LANES)
    return pl.pallas_call(
        project_kernel,
        out_shape=[jax.ShapeDtypeStruct(shape, F32), jax.ShapeDtypeStruct(shape, BF16)],
        compiler_params=params(4),
        name="project",
    )(own, got, factor_t)


def add_kernel(mine_ref, got_ref, out_ref):
    out_ref[...] = add_to(mine_ref, got_ref).astype(out_ref.dtype)


def add(mine, got):
    return pl.pallas_call(
        add_kernel,
        out_shape=jax.ShapeDtypeStruct(got.shape, got.dtype),
        compiler_params=params(4),
        name="add",
    )(mine, got)


def product_kernel(own_ref, got_ref, mine_ref, other_ref, out_ref):
    cells, width = own_ref.shape
    blocks = width // LANES // 2
    rank = mine_ref.shape[0] // blocks
    even = lax.rem(lax.axis_index("row"), 2) == 0
    total = jnp.zeros((cells, rank), F32)
    for block in range(blocks):
        rows = pl.ds(block * rank, rank)
        mine, other = mine_ref[rows, :], other_ref[rows, :]
        low = jnp.where(even, mine, other)
        high = jnp.where(even, other, mine)
        for at, projected in ((block, low), (block + blocks, high)):
            where = slice(at * LANES, (at + 1) * LANES)
            total += dot_f32(own_ref[:, where], projected, ((1,), (1,)))
            total += dot_f32(got_ref[:, where], projected, ((1,), (1,)))
    half = cells // 2
    out_ref[...] = jnp.concatenate([total[:half], total[half:]], axis=1).astype(BF16)


def product_terms(own, got, mine, other):
    return pl.pallas_call(
        product_kernel,
        out_shape=jax.ShapeDtypeStruct((own.shape[0] // 2, LANES), BF16),
        compiler_params=params(4),
        name="product_terms",
    )(own, got, mine, other)


def gram_kernel(term_ref, got_ref, out_ref):
    product = add_to(term_ref, got_ref)
    rank = LANES // 2
    wide = dot_f32(product, product, ((0,), (0,)), lax.Precision.HIGHEST)
    gram = wide[:rank, :rank] + wide[rank:, rank:]
    out_ref[...] = jnp.concatenate([gram[:rank // 2], gram[rank // 2:]], axis=1)


def local_gram(term, got):
    return pl.pallas_call(
        gram_kernel,
        out_shape=jax.ShapeDtypeStruct((LANES // 4, LANES), F32),
        compiler_params=params(4),
        name="local_gram",
    )(term, got)


def finish_kernel(total_rows, term_ref, got_term_ref, gram_ref, got_gram_ref, out_ref):
    rank = LANES // 2
    packed = gram_ref[...] + got_gram_ref[...]
    gram = jnp.concatenate([packed[:, :rank], packed[:, rank:]], axis=0)
    eye = (
        lax.broadcasted_iota(jnp.int32, (rank, rank), 0)
        == lax.broadcasted_iota(jnp.int32, (rank, rank), 1)
    ).astype(F32)
    both = jnp.concatenate([gram, eye], axis=1)
    row_index = lax.broadcasted_iota(jnp.int32, (rank, 1), 0)
    pivots = jnp.zeros((rank, 1), F32)
    for k in range(rank):
        pivot = both[k:k + 1, k:k + 1]
        pivots = jnp.where(row_index == k, pivot, pivots)
        factor = jnp.where(row_index > k, both[:, k:k + 1] / pivot, 0.0)
        both = both - factor * both[k:k + 1, :]
    inverse = both[:, rank:] * (lax.rsqrt(pivots) * (total_rows ** 0.5))
    product = add_to(term_ref, got_term_ref)
    mine = jnp.where(lax.axis_index("col") == 0, product[:, :rank], product[:, rank:])
    out_ref[...] = dot_f32(mine, inverse, ((1,), (1,)), lax.Precision.HIGHEST)


def finish(total_rows, term, got_term, gram, got_gram):
    return pl.pallas_call(
        functools.partial(finish_kernel, total_rows),
        out_shape=jax.ShapeDtypeStruct((term.shape[0], LANES // 2), F32),
        compiler_params=params(4),
        name="finish",
    )(term, got_term, gram, got_gram)


def per_device(snapshot, mode2_factor, old_factor):
    n_rows, n_cols = lax.axis_size("row"), lax.axis_size("col")
    masks = [1 << bit for bit in range(n_rows.bit_length() - 1)]
    total_rows = snapshot.shape[0] * n_rows

    def swap(x, mask):
        pairs = [
            (r * n_cols + c, (r ^ mask) * n_cols + (c + 1) % n_cols)
            for r in range(n_rows)
            for c in range(n_cols)
        ]
        return lax.ppermute(x, ("row", "col"), pairs)

    send, own = contract(snapshot, mode2_factor.T)
    got = swap(send, 0)

    keep, send = project(own, got, old_factor.T)
    mine = add(keep, swap(send, masks[0]))
    for mask in masks[1:]:
        mine = add(mine, swap(mine, mask))
    other = swap(mine, masks[0])

    term = product_terms(own, got, mine, other)
    got_term = swap(term, 0)
    gram = local_gram(term, got_term)
    for mask in masks[:-1]:
        gram = add(gram, swap(gram, mask))
    return finish(total_rows, term, got_term, gram, swap(gram, masks[-1]))


def solution(mesh):
    return jax.shard_map(
        per_device,
        mesh=mesh,
        in_specs=(
            P(("groups", "row"), None, "col"),
            P(("groups", "col"), None),
            P(("groups", "row"), None),
        ),
        out_specs=P(("groups", "row", "col"), None),
        check_vma=False,
    )
```

```python
import functools

import jax
import jax.numpy as jnp
from jax import lax
from jax.experimental import pallas as pl
from jax.experimental.pallas import tpu as pltpu
from jax.sharding import PartitionSpec as P

F32 = jnp.float32
BF16 = jnp.bfloat16
LANES = 128
MIB = 2**20


def dot_f32(a, b, dims, precision=None):
    return lax.dot_general(a, b, (dims, ((), ())), precision=precision, preferred_element_type=F32)


def params(mib):
    return pltpu.CompilerParams(vmem_limit_bytes=mib * MIB)


def own_half():
    row = lax.axis_index("row")
    half = lax.axis_index("col")
    for bit in range(lax.axis_size("row").bit_length() - 1):
        half += lax.rem(lax.div(row, 1 << bit), 2)
    return lax.rem(half, 2)


def contract_kernel(
    step, parts, snapshot_ref, mode2_ref, send_ref, own_ref,
    slab_ref, wide_ref, even_ref, odd_ref, sems,
):
    cells, fibers, depth = snapshot_ref.shape
    rank = mode2_ref.shape[0]
    reps = LANES // rank
    half = fibers // 2
    chunks = cells // step

    def copy(start, size, chunk):
        where = pl.ds(start, size)
        return pltpu.make_async_copy(snapshot_ref.at[where], slab_ref.at[where], sems.at[chunk])

    def start(piece, _):
        size = step // parts
        copy(piece * size, size, piece // parts).start()
        return _

    lax.fori_loop(0, chunks * parts, start, 0)
    wide_ref[...] = jnp.concatenate([mode2_ref[...]] * reps, axis=0)
    lane = lax.broadcasted_iota(jnp.int32, (step, LANES), 1)
    own_start = own_half() * half
    send_start = half - own_start

    def multiply(chunk, flat_ref):
        copy(chunk * step, step, chunk).wait()
        x = slab_ref[pl.ds(chunk * step, step)].reshape(step * fibers, depth)
        flat_ref[...] = dot_f32(x, wide_ref[...], ((1,), (1,)))

    def spread(chunk, flat_ref):
        rows = pl.ds(pl.multiple_of(chunk * step, step), step)
        for base, out_ref in ((own_start, own_ref), (send_start, send_ref)):
            for block in range(half // reps):
                part = flat_ref[pl.ds(base + block * reps, step, stride=fibers), :]
                for r in range(1, reps):
                    other = flat_ref[pl.ds(base + block * reps + r, step, stride=fibers), :]
                    part = jnp.where(lane < r * rank, part, other)
                out_ref[rows, block * LANES:(block + 1) * LANES] = part.astype(BF16)

    def two_chunks(pair, _):
        multiply(2 * pair, even_ref)
        spread(jnp.maximum(2 * pair - 1, 0), odd_ref)
        multiply(2 * pair + 1, odd_ref)
        spread(2 * pair, even_ref)
        return _

    lax.fori_loop(0, chunks // 2, two_chunks, 0)
    spread(chunks - 1, odd_ref)


def contract(snapshot, mode2_t):
    cells, fibers, depth = snapshot.shape
    rank = mode2_t.shape[0]
    step = 16
    out = jax.ShapeDtypeStruct((cells, fibers // 2 * rank), BF16)
    return pl.pallas_call(
        functools.partial(contract_kernel, step, 4),
        in_specs=[
            pl.BlockSpec(memory_space=pltpu.HBM),
            pl.BlockSpec(memory_space=pltpu.VMEM),
        ],
        out_shape=[out, out],
        scratch_shapes=[
            pltpu.VMEM(snapshot.shape, BF16),
            pltpu.VMEM((LANES, depth), BF16),
            pltpu.VMEM((step * fibers, LANES), F32),
            pltpu.VMEM((step * fibers, LANES), F32),
            pltpu.SemaphoreType.DMA((cells // step,)),
        ],
        compiler_params=params(50),
        name="contract",
    )(snapshot, mode2_t)


def add_to(*refs):
    total = refs[0][...].astype(F32)
    for ref in refs[1:]:
        total += ref[...].astype(F32)
    return total


def project_kernel(own_ref, got_ref, factor_ref, keep_ref, send_ref):
    rank = factor_ref.shape[0]
    factor = factor_ref[...]
    total = dot_f32(factor, own_ref[...], ((1,), (0,))) + dot_f32(factor, got_ref[...], ((1,), (0,)))
    even = lax.rem(lax.axis_index("row"), 2) == 0
    blocks = total.shape[1] // LANES // 2
    for block in range(blocks):
        low = total[:, block * LANES:(block + 1) * LANES]
        high = total[:, (block + blocks) * LANES:(block + blocks + 1) * LANES]
        rows = pl.ds(block * rank, rank)
        keep_ref[rows, :] = jnp.where(even, low, high)
        send_ref[rows, :] = jnp.where(even, high, low).astype(BF16)


def project(own, got, factor_t):
    rank = factor_t.shape[0]
    shape = (rank * own.shape[1] // LANES // 2, LANES)
    return pl.pallas_call(
        project_kernel,
        out_shape=[jax.ShapeDtypeStruct(shape, F32), jax.ShapeDtypeStruct(shape, BF16)],
        compiler_params=params(4),
        name="project",
    )(own, got, factor_t)


def add_kernel(mine_ref, got_ref, out_ref):
    out_ref[...] = add_to(mine_ref, got_ref).astype(out_ref.dtype)


def add(mine, got):
    return pl.pallas_call(
        add_kernel,
        out_shape=jax.ShapeDtypeStruct(got.shape, got.dtype),
        compiler_params=params(4),
        name="add",
    )(mine, got)


def product_kernel(own_ref, got_ref, mine_ref, other_ref, out_ref):
    cells, width = own_ref.shape
    blocks = width // LANES // 2
    rank = mine_ref.shape[0] // blocks
    even = lax.rem(lax.axis_index("row"), 2) == 0
    total = jnp.zeros((cells, rank), F32)
    for block in range(blocks):
        rows = pl.ds(block * rank, rank)
        mine, other = mine_ref[rows, :], other_ref[rows, :]
        low = jnp.where(even, mine, other)
        high = jnp.where(even, other, mine)
        for at, projected in ((block, low), (block + blocks, high)):
            where = slice(at * LANES, (at + 1) * LANES)
            total += dot_f32(own_ref[:, where], projected, ((1,), (1,)))
            total += dot_f32(got_ref[:, where], projected, ((1,), (1,)))
    half = cells // 2
    out_ref[...] = jnp.concatenate([total[:half], total[half:]], axis=1).astype(BF16)


def product_terms(own, got, mine, other):
    return pl.pallas_call(
        product_kernel,
        out_shape=jax.ShapeDtypeStruct((own.shape[0] // 2, LANES), BF16),
        compiler_params=params(4),
        name="product_terms",
    )(own, got, mine, other)


def gram_kernel(term_ref, got_ref, out_ref):
    product = add_to(term_ref, got_ref)
    rank = LANES // 2
    wide = dot_f32(product, product, ((0,), (0,)), lax.Precision.HIGHEST)
    gram = wide[:rank, :rank] + wide[rank:, rank:]
    out_ref[...] = jnp.concatenate([gram[:rank // 2], gram[rank // 2:]], axis=1)


def local_gram(term, got):
    return pl.pallas_call(
        gram_kernel,
        out_shape=jax.ShapeDtypeStruct((LANES // 4, LANES), F32),
        compiler_params=params(4),
        name="local_gram",
    )(term, got)


def eliminate(gram):
    rank = gram.shape[0]
    tile = 8
    count = rank // tile
    wide = 2 * rank
    sublane = lax.broadcasted_iota(jnp.int32, (tile, wide), 0)
    lane = lax.broadcasted_iota(jnp.int32, (tile, wide), 1)
    full = lambda x: jnp.broadcast_to(x, (tile, wide))
    both = []
    for v in range(count):
        mine = gram[v * tile:(v + 1) * tile]
        both.append(jnp.where(lane < rank, jnp.concatenate([mine, mine], axis=1),
                              (lane - rank == sublane + v * tile).astype(F32)))
    pivots = []
    for p in range(count):
        cols = [
            {v: full(both[v][:, p * tile + j:p * tile + j + 1]) for v in range(p, count)}
            for j in range(tile)
        ]
        found = jnp.ones((tile, wide), F32)
        for j in range(tile):
            pivot = full(cols[j][p][j:j + 1])
            found = jnp.where(sublane == j, pivot, found)
            inverse = 1.0 / pivot
            row = full(both[p][j:j + 1]) * inverse
            heads = {k: full(cols[k][p][j:j + 1]) * inverse for k in range(j + 1, tile)}
            for v in range(p, count):
                factor = cols[j][v]
                if v == p:
                    factor = jnp.where(sublane > j, factor, 0.0)
                for k, head in heads.items():
                    cols[k][v] = cols[k][v] - factor * head
                both[v] = both[v] - factor * row
        pivots.append(found)
    return both, pivots


def finish_kernel(total_rows, term_ref, got_term_ref, gram_ref, got_gram_ref, out_ref):
    rank = LANES // 2
    packed = gram_ref[...] + got_gram_ref[...]
    gram = jnp.concatenate([packed[:, :rank], packed[:, rank:]], axis=0)
    both, pivots = eliminate(gram)
    scale = total_rows ** 0.5
    inverse = jnp.concatenate([b * (lax.rsqrt(p) * scale) for b, p in zip(both, pivots)], axis=0)
    inverse = inverse[:, rank:]
    product = add_to(term_ref, got_ref)
    rank = LANES // 2
    wide = dot_f32(product, product, ((0,), (0,)), lax.Precision.HIGHEST)
    gram = wide[:rank, :rank] + wide[rank:, rank:]
    out_ref[...] = jnp.concatenate([gram[:rank // 2], gram[rank // 2:]], axis=1)


def local_gram(term, got):
    return pl.pallas_call(
        gram_kernel,
        out_shape=jax.ShapeDtypeStruct((LANES // 4, LANES), F32),
        compiler_params=params(4),
        name="local_gram",
    )(term, got)


def finish_kernel(total_rows, term_ref, got_term_ref, gram_ref, got_gram_ref, out_ref):
    rank = LANES // 2
    packed = gram_ref[...] + got_gram_ref[...]
    gram = jnp.concatenate([packed[:, :rank], packed[:, rank:]], axis=0)
    eye = (
        lax.broadcasted_iota(jnp.int32, (rank, rank), 0)
        == lax.broadcasted_iota(jnp.int32, (rank, rank), 1)
    ).astype(F32)
    both = jnp.concatenate([gram, eye], axis=1)
    row_index = lax.broadcasted_iota(jnp.int32, (rank, 1), 0)
    pivots = jnp.zeros((rank, 1), F32)
    for k in range(rank):
        pivot = both[k:k + 1, k:k + 1]
        pivots = jnp.where(row_index == k, pivot, pivots)
        factor = jnp.where(row_index > k, both[:, k:k + 1] / pivot, 0.0)
        both = both - factor * both[k:k + 1, :]
    inverse = both[:, rank:] * (lax.rsqrt(pivots) * (total_rows ** 0.5))
    product = add_to(term_ref, got_term_ref)
    mine = jnp.where(lax.axis_index("col") == 0, product[:, :rank], product[:, rank:])
    out_ref[...] = dot_f32(mine, inverse, ((1,), (1,)), lax.Precision.HIGHEST)


def finish(total_rows, term, got_term, gram, got_gram):
    return pl.pallas_call(
        functools.partial(finish_kernel, total_rows),
        out_shape=jax.ShapeDtypeStruct((term.shape[0], LANES // 2), F32),
        compiler_params=params(4),
        name="finish",
    )(term, got_term, gram, got_gram)


def per_device(snapshot, mode2_factor, old_factor):
    n_rows, n_cols = lax.axis_size("row"), lax.axis_size("col")
    masks = [1 << bit for bit in range(n_rows.bit_length() - 1)]
    total_rows = snapshot.shape[0] * n_rows

    def swap(x, mask):
        pairs = [
            (r * n_cols + c, (r ^ mask) * n_cols + (c + 1) % n_cols)
            for r in range(n_rows)
            for c in range(n_cols)
        ]
        return lax.ppermute(x, ("row", "col"), pairs)

    send, own = contract(snapshot, mode2_factor.T)
    got = swap(send, 0)

    keep, send = project(own, got, old_factor.T)
    mine = add(keep, swap(send, masks[0]))
    for mask in masks[1:]:
        mine = add(mine, swap(mine, mask))
    other = swap(mine, masks[0])

    term = product_terms(own, got, mine, other)
    got_term = swap(term, 0)
    gram = local_gram(term, got_term)
    for mask in masks[:-1]:
        gram = add(gram, swap(gram, mask))
    return finish(total_rows, term, got_term, gram, swap(gram, masks[-1]))


def solution(mesh):
    return jax.shard_map(
        per_device,
        mesh=mesh,
        in_specs=(
            P(("groups", "row"), None, "col"),
            P(("groups", "col"), None),
            P(("groups", "row"), None),
        ),
        out_specs=P(("groups", "row", "col"), None),
        check_vma=False,
    )
```

```python
import functools

import jax
import jax.numpy as jnp
from jax import lax
from jax.experimental import pallas as pl
from jax.experimental.pallas import tpu as pltpu
from jax.sharding import PartitionSpec as P

F32 = jnp.float32
BF16 = jnp.bfloat16
LANES = 128
MIB = 2**20


def dot_f32(a, b, dims, precision=None):
    return lax.dot_general(a, b, (dims, ((), ())), precision=precision, preferred_element_type=F32)


def params(mib):
    return pltpu.CompilerParams(vmem_limit_bytes=mib * MIB)


def own_half():
    row = lax.axis_index("row")
    half = lax.axis_index("col")
    for bit in range(lax.axis_size("row").bit_length() - 1):
        half += lax.rem(lax.div(row, 1 << bit), 2)
    return lax.rem(half, 2)


def contract_kernel(
    step, parts, ahead, snapshot_ref, mode2_ref, send_ref, own_ref,
    slab_ref, wide_ref, even_ref, odd_ref, sems,
):
    cells, fibers, depth = snapshot_ref.shape
    rank = mode2_ref.shape[0]
    reps = LANES // rank
    half = fibers // 2
    chunks = cells // step

    def copy(start, size, chunk):
        where = pl.ds(start, size)
        return pltpu.make_async_copy(snapshot_ref.at[where], slab_ref.at[where], sems.at[chunk])

    def start(chunk):
        size = step // parts
        for part in range(parts):
            copy(chunk * step + part * size, size, chunk).start()

    for chunk in range(ahead):
        start(chunk)
    wide_ref[...] = jnp.concatenate([mode2_ref[...]] * reps, axis=0)
    lane = lax.broadcasted_iota(jnp.int32, (step, LANES), 1)
    own_start = own_half() * half
    send_start = half - own_start

    def multiply(chunk, flat_ref):
        copy(chunk * step, step, chunk).wait()

        @pl.when(chunk + ahead < chunks)
        def _():
            start(chunk + ahead)

        x = slab_ref[pl.ds(chunk * step, step)].reshape(step * fibers, depth)
        flat_ref[...] = dot_f32(x, wide_ref[...], ((1,), (1,)))

    def spread(chunk, flat_ref):
        rows = pl.ds(pl.multiple_of(chunk * step, step), step)
        for base, out_ref in ((own_start, own_ref), (send_start, send_ref)):
            for block in range(half // reps):
                part = flat_ref[pl.ds(base + block * reps, step, stride=fibers), :]
                for r in range(1, reps):
                    other = flat_ref[pl.ds(base + block * reps + r, step, stride=fibers), :]
                    part = jnp.where(lane < r * rank, part, other)
                out_ref[rows, block * LANES:(block + 1) * LANES] = part.astype(BF16)

    def two_chunks(pair, _):
        multiply(2 * pair, even_ref)
        spread(jnp.maximum(2 * pair - 1, 0), odd_ref)
        multiply(2 * pair + 1, odd_ref)
        spread(2 * pair, even_ref)
        return _

    lax.fori_loop(0, chunks // 2, two_chunks, 0)
    spread(chunks - 1, odd_ref)


def contract(snapshot, mode2_t):
    cells, fibers, depth = snapshot.shape
    rank = mode2_t.shape[0]
    step = 16
    out = jax.ShapeDtypeStruct((cells, fibers // 2 * rank), BF16)
    return pl.pallas_call(
        functools.partial(contract_kernel, step, 8, 2),
        in_specs=[
            pl.BlockSpec(memory_space=pltpu.HBM),
            pl.BlockSpec(memory_space=pltpu.VMEM),
        ],
        out_shape=[out, out],
        scratch_shapes=[
            pltpu.VMEM(snapshot.shape, BF16),
            pltpu.VMEM((LANES, depth), BF16),
            pltpu.VMEM((step * fibers, LANES), F32),
            pltpu.VMEM((step * fibers, LANES), F32),
            pltpu.SemaphoreType.DMA((cells // step,)),
        ],
        compiler_params=params(50),
        name="contract",
    )(snapshot, mode2_t)


def add_to(*refs):
    total = refs[0][...].astype(F32)
    for ref in refs[1:]:
        total += ref[...].astype(F32)
    return total


def project_kernel(own_ref, got_ref, factor_ref, keep_ref, send_ref):
    rank = factor_ref.shape[0]
    factor = factor_ref[...]
    total = dot_f32(factor, own_ref[...], ((1,), (0,))) + dot_f32(factor, got_ref[...], ((1,), (0,)))
    even = lax.rem(lax.axis_index("row"), 2) == 0
    blocks = total.shape[1] // LANES // 2
    for block in range(blocks):
        low = total[:, block * LANES:(block + 1) * LANES]
        high = total[:, (block + blocks) * LANES:(block + blocks + 1) * LANES]
        rows = pl.ds(block * rank, rank)
        keep_ref[rows, :] = jnp.where(even, low, high)
        send_ref[rows, :] = jnp.where(even, high, low).astype(BF16)


def project(own, got, factor_t):
    rank = factor_t.shape[0]
    shape = (rank * own.shape[1] // LANES // 2, LANES)
    return pl.pallas_call(
        project_kernel,
        out_shape=[jax.ShapeDtypeStruct(shape, F32), jax.ShapeDtypeStruct(shape, BF16)],
        compiler_params=params(4),
        name="project",
    )(own, got, factor_t)


def add_kernel(mine_ref, got_ref, out_ref):
    out_ref[...] = add_to(mine_ref, got_ref).astype(out_ref.dtype)


def add(mine, got):
    return pl.pallas_call(
        add_kernel,
        out_shape=jax.ShapeDtypeStruct(got.shape, got.dtype),
        compiler_params=params(4),
        name="add",
    )(mine, got)


def product_kernel(own_ref, got_ref, mine_ref, other_ref, out_ref):
    cells, width = own_ref.shape
    blocks = width // LANES // 2
    rank = mine_ref.shape[0] // blocks
    even = lax.rem(lax.axis_index("row"), 2) == 0
    total = jnp.zeros((cells, rank), F32)
    for block in range(blocks):
        rows = pl.ds(block * rank, rank)
        mine, other = mine_ref[rows, :], other_ref[rows, :]
        low = jnp.where(even, mine, other)
        high = jnp.where(even, other, mine)
        for at, projected in ((block, low), (block + blocks, high)):
            where = slice(at * LANES, (at + 1) * LANES)
            total += dot_f32(own_ref[:, where], projected, ((1,), (1,)))
            total += dot_f32(got_ref[:, where], projected, ((1,), (1,)))
    half = cells // 2
    out_ref[...] = jnp.concatenate([total[:half], total[half:]], axis=1).astype(BF16)


def product_terms(own, got, mine, other):
    return pl.pallas_call(
        product_kernel,
        out_shape=jax.ShapeDtypeStruct((own.shape[0] // 2, LANES), BF16),
        compiler_params=params(4),
        name="product_terms",
    )(own, got, mine, other)


def gram_kernel(term_ref, got_ref, out_ref):
    product = add_to(term_ref, got_ref)
    rank = LANES // 2
    wide = dot_f32(product, product, ((0,), (0,)), lax.Precision.HIGHEST)
    gram = wide[:rank, :rank] + wide[rank:, rank:]
    out_ref[...] = jnp.concatenate([gram[:rank // 2], gram[rank // 2:]], axis=1)


def local_gram(term, got):
    return pl.pallas_call(
        gram_kernel,
        out_shape=jax.ShapeDtypeStruct((LANES // 4, LANES), F32),
        compiler_params=params(4),
        name="local_gram",
    )(term, got)


def reciprocal(x):
    guess = pl.reciprocal(x, approx=True, full_range=False)
    for _ in range(2):
        guess = guess * (2.0 - x * guess)
    return guess


def eliminate(gram):
    rank = gram.shape[0]
    tile = 8
    count = rank // tile
    wide = 2 * rank
    sublane = lax.broadcasted_iota(jnp.int32, (tile, wide), 0)
    lane = lax.broadcasted_iota(jnp.int32, (tile, wide), 1)
    full = lambda x: jnp.broadcast_to(x, (tile, wide))
    both = []
    for v in range(count):
        mine = gram[v * tile:(v + 1) * tile]
        both.append(jnp.where(lane < rank, jnp.concatenate([mine, mine], axis=1),
                              (lane - rank == sublane + v * tile).astype(F32)))
    pivots = []
    for p in range(count):
        cols = [
            {v: full(both[v][:, p * tile + j:p * tile + j + 1]) for v in range(p, count)}
            for j in range(tile)
        ]
        rows = [full(both[p][j:j + 1]) for j in range(tile)]
        block = [[full(cols[k][p][j:j + 1]) for k in range(j + 1)] for j in range(tile)]
        found, kept = block[0][0], rows[0]
        for j in range(tile):
            if j:
                found = jnp.where(sublane == j, block[j][j], found)
                kept = jnp.where(sublane == j, rows[j], kept)
            inverse = reciprocal(block[j][j])
            scaled = {i: block[i][j] * inverse for i in range(j + 1, tile)}
            for i, factor in scaled.items():
                for k in range(j + 1, i + 1):
                    block[i][k] = block[i][k] - factor * block[k][j]
                rows[i] = rows[i] - factor * rows[j]
            row = rows[j] * inverse
            for v in range(p + 1, count):
                for i, factor in scaled.items():
                    cols[i][v] = cols[i][v] - factor * cols[j][v]
                both[v] = both[v] - cols[j][v] * row
        both[p] = kept
        pivots.append(found)
    return both, pivots


def finish_kernel(total_rows, term_ref, got_term_ref, gram_ref, got_gram_ref, out_ref):
    rank = LANES // 2
    packed = gram_ref[...] + got_gram_ref[...]
    gram = jnp.concatenate([packed[:, :rank], packed[:, rank:]], axis=0)
    both, pivots = eliminate(gram)
    scale = total_rows ** 0.5
    inverse = jnp.concatenate([b * (lax.rsqrt(p) * scale) for b, p in zip(both, pivots)], axis=0)
    inverse = inverse[:, rank:]
    product = add_to(term_ref, got_ref)
    rank = LANES // 2
    wide = dot_f32(product, product, ((0,), (0,)), lax.Precision.HIGHEST)
    gram = wide[:rank, :rank] + wide[rank:, rank:]
    out_ref[...] = jnp.concatenate([gram[:rank // 2], gram[rank // 2:]], axis=1)


def local_gram(term, got):
    return pl.pallas_call(
        gram_kernel,
        out_shape=jax.ShapeDtypeStruct((LANES // 4, LANES), F32),
        compiler_params=params(4),
        name="local_gram",
    )(term, got)


def finish_kernel(total_rows, term_ref, got_term_ref, gram_ref, got_gram_ref, out_ref):
    rank = LANES // 2
    packed = gram_ref[...] + got_gram_ref[...]
    gram = jnp.concatenate([packed[:, :rank], packed[:, rank:]], axis=0)
    eye = (
        lax.broadcasted_iota(jnp.int32, (rank, rank), 0)
        == lax.broadcasted_iota(jnp.int32, (rank, rank), 1)
    ).astype(F32)
    both = jnp.concatenate([gram, eye], axis=1)
    row_index = lax.broadcasted_iota(jnp.int32, (rank, 1), 0)
    pivots = jnp.zeros((rank, 1), F32)
    for k in range(rank):
        pivot = both[k:k + 1, k:k + 1]
        pivots = jnp.where(row_index == k, pivot, pivots)
        factor = jnp.where(row_index > k, both[:, k:k + 1] / pivot, 0.0)
        both = both - factor * both[k:k + 1, :]
    inverse = both[:, rank:] * (lax.rsqrt(pivots) * (total_rows ** 0.5))
    product = add_to(term_ref, got_term_ref)
    mine = jnp.where(lax.axis_index("col") == 0, product[:, :rank], product[:, rank:])
    out_ref[...] = dot_f32(mine, inverse, ((1,), (1,)), lax.Precision.HIGHEST)


def finish(total_rows, term, got_term, gram, got_gram):
    return pl.pallas_call(
        functools.partial(finish_kernel, total_rows),
        out_shape=jax.ShapeDtypeStruct((term.shape[0], LANES // 2), F32),
        compiler_params=params(4),
        name="finish",
    )(term, got_term, gram, got_gram)


def per_device(snapshot, mode2_factor, old_factor):
    n_rows, n_cols = lax.axis_size("row"), lax.axis_size("col")
    masks = [1 << bit for bit in range(n_rows.bit_length() - 1)]
    total_rows = snapshot.shape[0] * n_rows

    def swap(x, mask):
        pairs = [
            (r * n_cols + c, (r ^ mask) * n_cols + (c + 1) % n_cols)
            for r in range(n_rows)
            for c in range(n_cols)
        ]
        return lax.ppermute(x, ("row", "col"), pairs)

    send, own = contract(snapshot, mode2_factor.T)
    got = swap(send, 0)

    keep, send = project(own, got, old_factor.T)
    mine = add(keep, swap(send, masks[0]))
    for mask in masks[1:]:
        mine = add(mine, swap(mine, mask))
    other = swap(mine, masks[0])

    term = product_terms(own, got, mine, other)
    got_term = swap(term, 0)
    gram = local_gram(term, got_term)
    for mask in masks[:-1]:
        gram = add(gram, swap(gram, mask))
    return finish(total_rows, term, got_term, gram, swap(gram, masks[-1]))


def solution(mesh):
    return jax.shard_map(
        per_device,
        mesh=mesh,
        in_specs=(
            P(("groups", "row"), None, "col"),
            P(("groups", "col"), None),
            P(("groups", "row"), None),
        ),
        out_specs=P(("groups", "row", "col"), None),
        check_vma=False,
    )
```

```python
import functools

import jax
import jax.numpy as jnp
from jax import lax
from jax.experimental import pallas as pl
from jax.experimental.pallas import tpu as pltpu
from jax.sharding import PartitionSpec as P

F32 = jnp.float32
BF16 = jnp.bfloat16
LANES = 128
MIB = 2**20


def dot_f32(a, b, dims, precision=None):
    return lax.dot_general(a, b, (dims, ((), ())), precision=precision, preferred_element_type=F32)


def params(mib):
    return pltpu.CompilerParams(vmem_limit_bytes=mib * MIB)


def own_half():
    row = lax.axis_index("row")
    half = lax.axis_index("col")
    for bit in range(lax.axis_size("row").bit_length() - 1):
        half += lax.rem(lax.div(row, 1 << bit), 2)
    return lax.rem(half, 2)


def contract_kernel(
    step, fibers, snapshot_ref, mode2_ref, send_ref, own_ref,
    slab_ref, wide_ref, even_ref, odd_ref, sems,
):
    rank, depth = mode2_ref.shape
    reps = LANES // rank
    half = fibers // 2
    chunks = snapshot_ref.shape[0] // (step * fibers)

    def copy(chunk):
        where = pl.ds(chunk * step * fibers, step * fibers)
        return pltpu.make_async_copy(snapshot_ref.at[where], slab_ref.at[where], sems.at[chunk])

    for chunk in range(chunks):
        copy(chunk).start(priority=chunk % 2)
    wide_ref[...] = jnp.concatenate([mode2_ref[...]] * reps, axis=0)
    lane = lax.broadcasted_iota(jnp.int32, (step, LANES), 1)
    own_start = own_half() * half
    send_start = half - own_start

    def multiply(chunk, flat_ref):
        copy(chunk).wait()
        x = slab_ref[pl.ds(chunk * step * fibers, step * fibers), :]
        flat_ref[...] = dot_f32(x, wide_ref[...], ((1,), (1,)))

    def spread(chunk, flat_ref):
        rows = pl.ds(pl.multiple_of(chunk * step, step), step)
        for base, out_ref in ((own_start, own_ref), (send_start, send_ref)):
            for block in range(half // reps):
                part = flat_ref[pl.ds(base + block * reps, step, stride=fibers), :]
                for r in range(1, reps):
                    other = flat_ref[pl.ds(base + block * reps + r, step, stride=fibers), :]
                    part = jnp.where(lane < r * rank, part, other)
                out_ref[rows, block * LANES:(block + 1) * LANES] = part.astype(BF16)

    def two_chunks(pair, _):
        multiply(2 * pair, even_ref)
        spread(jnp.maximum(2 * pair - 1, 0), odd_ref)
        multiply(2 * pair + 1, odd_ref)
        spread(2 * pair, even_ref)
        return _

    lax.fori_loop(0, chunks // 2, two_chunks, 0)
    spread(chunks - 1, odd_ref)


def contract(snapshot, mode2_t):
    cells, fibers, depth = snapshot.shape
    rank = mode2_t.shape[0]
    step = 16
    out = jax.ShapeDtypeStruct((cells, fibers // 2 * rank), BF16)
    return pl.pallas_call(
        functools.partial(contract_kernel, step, fibers),
        in_specs=[
            pl.BlockSpec(memory_space=pltpu.HBM),
            pl.BlockSpec(memory_space=pltpu.VMEM),
        ],
        out_shape=[out, out],
        scratch_shapes=[
            pltpu.VMEM((cells * fibers, depth), BF16),
            pltpu.VMEM((LANES, depth), BF16),
            pltpu.VMEM((step * fibers, LANES), F32),
            pltpu.VMEM((step * fibers, LANES), F32),
            pltpu.SemaphoreType.DMA((cells // step,)),
        ],
        compiler_params=params(50),
        name="contract",
    )(snapshot.reshape(cells * fibers, depth), mode2_t)


def add_to(*refs):
    total = refs[0][...].astype(F32)
    for ref in refs[1:]:
        total += ref[...].astype(F32)
    return total


def project_kernel(own_ref, got_ref, factor_ref, keep_ref, send_ref):
    rank = factor_ref.shape[0]
    factor = factor_ref[...]
    total = dot_f32(factor, own_ref[...], ((1,), (0,))) + dot_f32(factor, got_ref[...], ((1,), (0,)))
    even = lax.rem(lax.axis_index("row"), 2) == 0
    blocks = total.shape[1] // LANES // 2
    for block in range(blocks):
        low = total[:, block * LANES:(block + 1) * LANES]
        high = total[:, (block + blocks) * LANES:(block + blocks + 1) * LANES]
        rows = pl.ds(block * rank, rank)
        keep_ref[rows, :] = jnp.where(even, low, high)
        send_ref[rows, :] = jnp.where(even, high, low).astype(BF16)


def project(own, got, factor_t):
    rank = factor_t.shape[0]
    shape = (rank * own.shape[1] // LANES // 2, LANES)
    return pl.pallas_call(
        project_kernel,
        out_shape=[jax.ShapeDtypeStruct(shape, F32), jax.ShapeDtypeStruct(shape, BF16)],
        compiler_params=params(4),
        name="project",
    )(own, got, factor_t)


def add_kernel(mine_ref, got_ref, out_ref):
    out_ref[...] = add_to(mine_ref, got_ref).astype(out_ref.dtype)


def add(mine, got):
    return pl.pallas_call(
        add_kernel,
        out_shape=jax.ShapeDtypeStruct(got.shape, got.dtype),
        compiler_params=params(4),
        name="add",
    )(mine, got)


def product_kernel(own_ref, got_ref, mine_ref, other_ref, out_ref):
    cells, width = own_ref.shape
    blocks = width // LANES // 2
    rank = mine_ref.shape[0] // blocks
    even = lax.rem(lax.axis_index("row"), 2) == 0
    total = jnp.zeros((cells, rank), F32)
    for block in range(blocks):
        rows = pl.ds(block * rank, rank)
        mine, other = mine_ref[rows, :], other_ref[rows, :]
        low = jnp.where(even, mine, other)
        high = jnp.where(even, other, mine)
        for at, projected in ((block, low), (block + blocks, high)):
            where = slice(at * LANES, (at + 1) * LANES)
            total += dot_f32(own_ref[:, where], projected, ((1,), (1,)))
            total += dot_f32(got_ref[:, where], projected, ((1,), (1,)))
    half = cells // 2
    out_ref[...] = jnp.concatenate([total[:half], total[half:]], axis=1).astype(BF16)


def product_terms(own, got, mine, other):
    return pl.pallas_call(
        product_kernel,
        out_shape=jax.ShapeDtypeStruct((own.shape[0] // 2, LANES), BF16),
        compiler_params=params(4),
        name="product_terms",
    )(own, got, mine, other)


def gram_kernel(term_ref, got_ref, out_ref):
    product = add_to(term_ref, got_ref)
    rank = LANES // 2
    wide = dot_f32(product, product, ((0,), (0,)), lax.Precision.HIGHEST)
    gram = wide[:rank, :rank] + wide[rank:, rank:]
    out_ref[...] = jnp.concatenate([gram[:rank // 2], gram[rank // 2:]], axis=1)


def local_gram(term, got):
    return pl.pallas_call(
        gram_kernel,
        out_shape=jax.ShapeDtypeStruct((LANES // 4, LANES), F32),
        compiler_params=params(4),
        name="local_gram",
    )(term, got)


def reciprocal(x):
    guess = pl.reciprocal(x, approx=True, full_range=False)
    for _ in range(2):
        guess = guess * (2.0 - x * guess)
    return guess


def eliminate(gram):
    rank = gram.shape[0]
    tile = 8
    count = rank // tile
    wide = 2 * rank
    sublane = lax.broadcasted_iota(jnp.int32, (tile, wide), 0)
    lane = lax.broadcasted_iota(jnp.int32, (tile, wide), 1)
    full = lambda x: jnp.broadcast_to(x, (tile, wide))
    both = []
    for v in range(count):
        mine = gram[v * tile:(v + 1) * tile]
        both.append(jnp.where(lane < rank, jnp.concatenate([mine, mine], axis=1),
                              (lane - rank == sublane + v * tile).astype(F32)))
    pivots = []
    for p in range(count):
        cols = [
            {v: full(both[v][:, p * tile + j:p * tile + j + 1]) for v in range(p, count)}
            for j in range(tile)
        ]
        rows = [full(both[p][j:j + 1]) for j in range(tile)]
        block = [[full(cols[k][p][j:j + 1]) for k in range(j + 1)] for j in range(tile)]
        found, kept = block[0][0], rows[0]
        for j in range(tile):
            if j:
                found = jnp.where(sublane == j, block[j][j], found)
                kept = jnp.where(sublane == j, rows[j], kept)
            inverse = reciprocal(block[j][j])
            scaled = {i: block[i][j] * inverse for i in range(j + 1, tile)}
            for i, factor in scaled.items():
                for k in range(j + 1, i + 1):
                    block[i][k] = block[i][k] - factor * block[k][j]
                rows[i] = rows[i] - factor * rows[j]
            row = rows[j] * inverse
            for v in range(p + 1, count):
                for i, factor in scaled.items():
                    cols[i][v] = cols[i][v] - factor * cols[j][v]
                both[v] = both[v] - cols[j][v] * row
        both[p] = kept
        pivots.append(found)
    return both, pivots


def finish_kernel(total_rows, term_ref, got_term_ref, gram_ref, got_gram_ref, out_ref):
    rank = LANES // 2
    packed = gram_ref[...] + got_gram_ref[...]
    gram = jnp.concatenate([packed[:, :rank], packed[:, rank:]], axis=0)
    both, pivots = eliminate(gram)
    scale = total_rows ** 0.5
    inverse = jnp.concatenate([b * (lax.rsqrt(p) * scale) for b, p in zip(both, pivots)], axis=0)
    inverse = inverse[:, rank:]
    product = add_to(term_ref, got_term_ref)
    mine = jnp.where(lax.axis_index("col") == 0, product[:, :rank], product[:, rank:])
    out_ref[...] = dot_f32(mine, inverse, ((1,), (1,)), lax.Precision.HIGHEST)


def finish(total_rows, term, got_term, gram, got_gram):
    return pl.pallas_call(
        functools.partial(finish_kernel, total_rows),
        out_shape=jax.ShapeDtypeStruct((term.shape[0], LANES // 2), F32),
        compiler_params=params(4),
        name="finish",
    )(term, got_term, gram, got_gram)


def per_device(snapshot, mode2_factor, old_factor):
    n_rows, n_cols = lax.axis_size("row"), lax.axis_size("col")
    masks = [1 << bit for bit in range(n_rows.bit_length() - 1)]
    total_rows = snapshot.shape[0] * n_rows

    def swap(x, mask):
        pairs = [
            (r * n_cols + c, (r ^ mask) * n_cols + (c + 1) % n_cols)
            for r in range(n_rows)
            for c in range(n_cols)
        ]
        return lax.ppermute(x, ("row", "col"), pairs)

    send, own = contract(snapshot, mode2_factor.T)
    got = swap(send, 0)

    keep, send = project(own, got, old_factor.T)
    mine = add(keep, swap(send, masks[0]))
    for mask in masks[1:]:
        mine = add(mine, swap(mine, mask))
    other = swap(mine, masks[0])

    term = product_terms(own, got, mine, other)
    got_term = swap(term, 0)
    gram = local_gram(term, got_term)
    for mask in masks[:-1]:
        gram = add(gram, swap(gram, mask))
    return finish(total_rows, term, got_term, gram, swap(gram, masks[-1]))


def solution(mesh):
    return jax.shard_map(
        per_device,
        mesh=mesh,
        in_specs=(
            P(("groups", "row"), None, "col"),
            P(("groups", "col"), None),
            P(("groups", "row"), None),
        ),
        out_specs=P(("groups", "row", "col"), None),
        check_vma=False,
    )
```

```python
import functools

import jax
import jax.numpy as jnp
from jax import lax
from jax.experimental import pallas as pl
from jax.experimental.pallas import tpu as pltpu
from jax.sharding import PartitionSpec as P

F32 = jnp.float32
BF16 = jnp.bfloat16
LANES = 128
MIB = 2**20


def dot_f32(a, b, dims, precision=None):
    return lax.dot_general(a, b, (dims, ((), ())), precision=precision, preferred_element_type=F32)


def params(mib):
    return pltpu.CompilerParams(vmem_limit_bytes=mib * MIB)


def own_half():
    row = lax.axis_index("row")
    half = lax.axis_index("col")
    for bit in range(lax.axis_size("row").bit_length() - 1):
        half += lax.rem(lax.div(row, 1 << bit), 2)
    return lax.rem(half, 2)


def contract_kernel(
    step, fibers, snapshot_ref, mode2_ref, send_ref, own_ref,
    wide_ref, even_ref, odd_ref,
):
    rank, depth = mode2_ref.shape
    reps = LANES // rank
    half = fibers // 2
    chunks = snapshot_ref.shape[0] // (step * fibers)

    wide_ref[...] = jnp.concatenate([mode2_ref[...]] * reps, axis=0)
    lane = lax.broadcasted_iota(jnp.int32, (step, LANES), 1)
    own_start = own_half() * half
    send_start = half - own_start

    def multiply(chunk, flat_ref):
        x = snapshot_ref[pl.ds(chunk * step * fibers, step * fibers), :]
        flat_ref[...] = dot_f32(x, wide_ref[...], ((1,), (1,)))

    def spread(chunk, flat_ref):
        rows = pl.ds(pl.multiple_of(chunk * step, step), step)
        for base, out_ref in ((own_start, own_ref), (send_start, send_ref)):
            for block in range(half // reps):
                part = flat_ref[pl.ds(base + block * reps, step, stride=fibers), :]
                for r in range(1, reps):
                    other = flat_ref[pl.ds(base + block * reps + r, step, stride=fibers), :]
                    part = jnp.where(lane < r * rank, part, other)
                out_ref[rows, block * LANES:(block + 1) * LANES] = part.astype(BF16)

    def two_chunks(pair, _):
        multiply(2 * pair, even_ref)
        spread(jnp.maximum(2 * pair - 1, 0), odd_ref)
        multiply(2 * pair + 1, odd_ref)
        spread(2 * pair, even_ref)
        return _

    lax.fori_loop(0, chunks // 2, two_chunks, 0)
    spread(chunks - 1, odd_ref)


def contract(snapshot, mode2_t):
    cells, fibers, depth = snapshot.shape
    rank = mode2_t.shape[0]
    step = 16
    out = jax.ShapeDtypeStruct((cells, fibers // 2 * rank), BF16)
    return pl.pallas_call(
        functools.partial(contract_kernel, step, fibers),
        in_specs=[
            pl.BlockSpec(memory_space=pltpu.VMEM),
            pl.BlockSpec(memory_space=pltpu.VMEM),
        ],
        out_shape=[out, out],
        scratch_shapes=[
            pltpu.VMEM((LANES, depth), BF16),
            pltpu.VMEM((step * fibers, LANES), F32),
            pltpu.VMEM((step * fibers, LANES), F32),
        ],
        compiler_params=params(24),
        name="contract",
    )(snapshot.reshape(cells * fibers, depth), mode2_t)


def add_to(*refs):
    total = refs[0][...].astype(F32)
    for ref in refs[1:]:
        total += ref[...].astype(F32)
    return total


def project_kernel(own_ref, got_ref, factor_ref, keep_ref, send_ref):
    rank = factor_ref.shape[0]
    factor = factor_ref[...]
    total = dot_f32(factor, own_ref[...], ((1,), (0,))) + dot_f32(factor, got_ref[...], ((1,), (0,)))
    even = lax.rem(lax.axis_index("row"), 2) == 0
    blocks = total.shape[1] // LANES // 2
    for block in range(blocks):
        low = total[:, block * LANES:(block + 1) * LANES]
        high = total[:, (block + blocks) * LANES:(block + blocks + 1) * LANES]
        rows = pl.ds(block * rank, rank)
        keep_ref[rows, :] = jnp.where(even, low, high)
        send_ref[rows, :] = jnp.where(even, high, low).astype(BF16)


def project(own, got, factor_t):
    rank = factor_t.shape[0]
    shape = (rank * own.shape[1] // LANES // 2, LANES)
    return pl.pallas_call(
        project_kernel,
        out_shape=[jax.ShapeDtypeStruct(shape, F32), jax.ShapeDtypeStruct(shape, BF16)],
        compiler_params=params(4),
        name="project",
    )(own, got, factor_t)


def add_kernel(mine_ref, got_ref, out_ref):
    out_ref[...] = add_to(mine_ref, got_ref).astype(out_ref.dtype)


def add(mine, got):
    return pl.pallas_call(
        add_kernel,
        out_shape=jax.ShapeDtypeStruct(got.shape, got.dtype),
        compiler_params=params(4),
        name="add",
    )(mine, got)


def product_kernel(own_ref, got_ref, mine_ref, other_ref, out_ref):
    cells, width = own_ref.shape
    blocks = width // LANES // 2
    rank = mine_ref.shape[0] // blocks
    even = lax.rem(lax.axis_index("row"), 2) == 0
    total = jnp.zeros((cells, rank), F32)
    for block in range(blocks):
        rows = pl.ds(block * rank, rank)
        mine, other = mine_ref[rows, :], other_ref[rows, :]
        low = jnp.where(even, mine, other)
        high = jnp.where(even, other, mine)
        for at, projected in ((block, low), (block + blocks, high)):
            where = slice(at * LANES, (at + 1) * LANES)
            total += dot_f32(own_ref[:, where], projected, ((1,), (1,)))
            total += dot_f32(got_ref[:, where], projected, ((1,), (1,)))
    half = cells // 2
    out_ref[...] = jnp.concatenate([total[:half], total[half:]], axis=1).astype(BF16)


def product_terms(own, got, mine, other):
    return pl.pallas_call(
        product_kernel,
        out_shape=jax.ShapeDtypeStruct((own.shape[0] // 2, LANES), BF16),
        compiler_params=params(4),
        name="product_terms",
    )(own, got, mine, other)


def gram_kernel(term_ref, got_ref, out_ref):
    product = add_to(term_ref, got_ref)
    rank = LANES // 2
    wide = dot_f32(product, product, ((0,), (0,)), lax.Precision.HIGHEST)
    gram = wide[:rank, :rank] + wide[rank:, rank:]
    out_ref[...] = jnp.concatenate([gram[:rank // 2], gram[rank // 2:]], axis=1)


def local_gram(term, got):
    return pl.pallas_call(
        gram_kernel,
        out_shape=jax.ShapeDtypeStruct((LANES // 4, LANES), F32),
        compiler_params=params(4),
        name="local_gram",
    )(term, got)


def reciprocal(x):
    guess = pl.reciprocal(x, approx=True, full_range=False)
    for _ in range(2):
        guess = guess * (2.0 - x * guess)
    return guess


def eliminate(gram):
    rank = gram.shape[0]
    tile = 8
    count = rank // tile
    wide = 2 * rank
    sublane = lax.broadcasted_iota(jnp.int32, (tile, wide), 0)
    lane = lax.broadcasted_iota(jnp.int32, (tile, wide), 1)
    full = lambda x: jnp.broadcast_to(x, (tile, wide))
    both = []
    for v in range(count):
        mine = gram[v * tile:(v + 1) * tile]
        both.append(jnp.where(lane < rank, jnp.concatenate([mine, mine], axis=1),
                              (lane - rank == sublane + v * tile).astype(F32)))
    pivots = []
    for p in range(count):
        cols = [
            {v: full(both[v][:, p * tile + j:p * tile + j + 1]) for v in range(p, count)}
            for j in range(tile)
        ]
        rows = [full(both[p][j:j + 1]) for j in range(tile)]
        block = [[full(cols[k][p][j:j + 1]) for k in range(j + 1)] for j in range(tile)]
        found, kept = block[0][0], rows[0]
        for j in range(tile):
            if j:
                found = jnp.where(sublane == j, block[j][j], found)
                kept = jnp.where(sublane == j, rows[j], kept)
            inverse = reciprocal(block[j][j])
            scaled = {i: block[i][j] * inverse for i in range(j + 1, tile)}
            for i, factor in scaled.items():
                for k in range(j + 1, i + 1):
                    block[i][k] = block[i][k] - factor * block[k][j]
                rows[i] = rows[i] - factor * rows[j]
            row = rows[j] * inverse
            for v in range(p + 1, count):
                for i, factor in scaled.items():
                    cols[i][v] = cols[i][v] - factor * cols[j][v]
                both[v] = both[v] - cols[j][v] * row
        both[p] = kept
        pivots.append(found)
    return both, pivots


def finish_kernel(total_rows, term_ref, got_term_ref, gram_ref, got_gram_ref, out_ref):
    rank = LANES // 2
    packed = gram_ref[...] + got_gram_ref[...]
    gram = jnp.concatenate([packed[:, :rank], packed[:, rank:]], axis=0)
    both, pivots = eliminate(gram)
    scale = total_rows ** 0.5
    inverse = jnp.concatenate([b * (lax.rsqrt(p) * scale) for b, p in zip(both, pivots)], axis=0)
    inverse = inverse[:, rank:]
    product = add_to(term_ref, got_term_ref)
    mine = jnp.where(lax.axis_index("col") == 0, product[:, :rank], product[:, rank:])
    out_ref[...] = dot_f32(mine, inverse, ((1,), (1,)), lax.Precision.HIGHEST)


def finish(total_rows, term, got_term, gram, got_gram):
    return pl.pallas_call(
        functools.partial(finish_kernel, total_rows),
        out_shape=jax.ShapeDtypeStruct((term.shape[0], LANES // 2), F32),
        compiler_params=params(4),
        name="finish",
    )(term, got_term, gram, got_gram)


def per_device(snapshot, mode2_factor, old_factor):
    n_rows, n_cols = lax.axis_size("row"), lax.axis_size("col")
    masks = [1 << bit for bit in range(n_rows.bit_length() - 1)]
    total_rows = snapshot.shape[0] * n_rows

    def swap(x, mask):
        pairs = [
            (r * n_cols + c, (r ^ mask) * n_cols + (c + 1) % n_cols)
            for r in range(n_rows)
            for c in range(n_cols)
        ]
        return lax.ppermute(x, ("row", "col"), pairs)

    send, own = contract(snapshot, mode2_factor.T)
    got = swap(send, 0)

    keep, send = project(own, got, old_factor.T)
    mine = add(keep, swap(send, masks[0]))
    for mask in masks[1:]:
        mine = add(mine, swap(mine, mask))
    other = swap(mine, masks[0])

    term = product_terms(own, got, mine, other)
    got_term = swap(term, 0)
    gram = local_gram(term, got_term)
    for mask in masks[:-1]:
        gram = add(gram, swap(gram, mask))
    return finish(total_rows, term, got_term, gram, swap(gram, masks[-1]))


def solution(mesh):
    return jax.shard_map(
        per_device,
        mesh=mesh,
        in_specs=(
            P(("groups", "row"), None, "col"),
            P(("groups", "col"), None),
            P(("groups", "row"), None),
        ),
        out_specs=P(("groups", "row", "col"), None),
        check_vma=False,
    )
```

```python
import functools

import jax
import jax.numpy as jnp
from jax import lax
from jax.experimental import pallas as pl
from jax.experimental.pallas import tpu as pltpu
from jax.sharding import PartitionSpec as P

F32 = jnp.float32
BF16 = jnp.bfloat16
LANES = 128
MIB = 2**20


def dot_f32(a, b, dims, precision=None):
    return lax.dot_general(a, b, (dims, ((), ())), precision=precision, preferred_element_type=F32)


def params(mib):
    return pltpu.CompilerParams(vmem_limit_bytes=mib * MIB)


def own_half():
    row = lax.axis_index("row")
    half = lax.axis_index("col")
    for bit in range(lax.axis_size("row").bit_length() - 1):
        half += lax.rem(lax.div(row, 1 << bit), 2)
    return lax.rem(half, 2)


def contract_kernel(step, fibers, snapshot_ref, mode2_ref, send_ref, own_ref, even_ref, odd_ref):
    rank, depth = mode2_ref.shape
    tile = 8
    reps = LANES // rank
    block = tile * fibers
    blocks = step // tile
    out_rows = block // reps
    chunks = snapshot_ref.shape[0] // (step * fibers)
    wide = jnp.concatenate([mode2_ref[...]] * reps, axis=0)
    lane = lax.broadcasted_iota(jnp.int32, (block, LANES), 1)
    to = lax.broadcasted_iota(jnp.int32, (out_rows, reps * block), 0)
    at = lax.broadcasted_iota(jnp.int32, (out_rows, reps * block), 1)
    cell = lax.div(lax.rem(at, block), fibers)
    fiber = lax.rem(at, fibers)
    wanted = lax.div(to, tile) * reps + lax.div(at, block)
    order = ((lax.rem(to, tile) == cell) & (wanted == fiber)).astype(F32).astype(BF16)
    first = own_half() == 0
    pairs = fibers // reps

    def multiply(chunk, flat_ref):
        x = snapshot_ref[pl.ds(chunk * step * fibers, step * fibers), :]
        flat_ref[...] = dot_f32(x, wide, ((1,), (1,))).astype(BF16)

    def spread(chunk, flat_ref):
        rows = pl.ds(pl.multiple_of(chunk * step, step), step)
        spreads = []
        for b in range(blocks):
            flat = flat_ref[pl.ds(b * block, block), :].astype(F32)
            groups = [
                jnp.where(lax.div(lane, rank) == r, flat, 0.0).astype(BF16) for r in range(reps)
            ]
            spreads.append(dot_f32(order, jnp.concatenate(groups, axis=0), ((1,), (0,))))
        for p in range(pairs // 2):
            low = jnp.concatenate([x[p * tile:(p + 1) * tile] for x in spreads], axis=0)
            q = p + pairs // 2
            high = jnp.concatenate([x[q * tile:(q + 1) * tile] for x in spreads], axis=0)
            where = slice(p * LANES, (p + 1) * LANES)
            own_ref[rows, where] = jnp.where(first, low, high).astype(BF16)
            send_ref[rows, where] = jnp.where(first, high, low).astype(BF16)

    def two_chunks(pair, _):
        multiply(2 * pair, even_ref)
        spread(jnp.maximum(2 * pair - 1, 0), odd_ref)
        multiply(2 * pair + 1, odd_ref)
        spread(2 * pair, even_ref)
        return _

    lax.fori_loop(0, chunks // 2, two_chunks, 0)
    spread(chunks - 1, odd_ref)


def contract(snapshot, mode2_t):
    cells, fibers, depth = snapshot.shape
    rank = mode2_t.shape[0]
    step = 16
    out = jax.ShapeDtypeStruct((cells, fibers // 2 * rank), BF16)
    return pl.pallas_call(
        functools.partial(contract_kernel, step, fibers),
        in_specs=[
            pl.BlockSpec(memory_space=pltpu.VMEM),
            pl.BlockSpec(memory_space=pltpu.VMEM),
        ],
        out_shape=[out, out],
        scratch_shapes=[pltpu.VMEM((step * fibers, LANES), BF16)] * 2,
        compiler_params=params(24),
        name="contract",
    )(snapshot.reshape(cells * fibers, depth), mode2_t)


def add_to(*refs):
    total = refs[0][...].astype(F32)
    for ref in refs[1:]:
        total += ref[...].astype(F32)
    return total


def project_kernel(own_ref, got_ref, factor_ref, keep_ref, send_ref):
    rank = factor_ref.shape[0]
    factor = factor_ref[...]
    total = dot_f32(factor, own_ref[...], ((1,), (0,))) + dot_f32(factor, got_ref[...], ((1,), (0,)))
    even = lax.rem(lax.axis_index("row"), 2) == 0
    blocks = total.shape[1] // LANES // 2
    for block in range(blocks):
        low = total[:, block * LANES:(block + 1) * LANES]
        high = total[:, (block + blocks) * LANES:(block + blocks + 1) * LANES]
        rows = pl.ds(block * rank, rank)
        keep_ref[rows, :] = jnp.where(even, low, high)
        send_ref[rows, :] = jnp.where(even, high, low).astype(BF16)


def project(own, got, factor_t):
    rank = factor_t.shape[0]
    shape = (rank * own.shape[1] // LANES // 2, LANES)
    return pl.pallas_call(
        project_kernel,
        out_shape=[jax.ShapeDtypeStruct(shape, F32), jax.ShapeDtypeStruct(shape, BF16)],
        compiler_params=params(4),
        name="project",
    )(own, got, factor_t)


def add_kernel(mine_ref, got_ref, out_ref):
    out_ref[...] = add_to(mine_ref, got_ref).astype(out_ref.dtype)


def add(mine, got):
    return pl.pallas_call(
        add_kernel,
        out_shape=jax.ShapeDtypeStruct(got.shape, got.dtype),
        compiler_params=params(4),
        name="add",
    )(mine, got)


def product_kernel(own_ref, got_ref, mine_ref, other_ref, out_ref):
    cells, width = own_ref.shape
    blocks = width // LANES // 2
    rank = mine_ref.shape[0] // blocks
    even = lax.rem(lax.axis_index("row"), 2) == 0
    total = jnp.zeros((cells, rank), F32)
    for block in range(blocks):
        rows = pl.ds(block * rank, rank)
        mine, other = mine_ref[rows, :], other_ref[rows, :]
        low = jnp.where(even, mine, other)
        high = jnp.where(even, other, mine)
        for at, projected in ((block, low), (block + blocks, high)):
            where = slice(at * LANES, (at + 1) * LANES)
            total += dot_f32(own_ref[:, where], projected, ((1,), (1,)))
            total += dot_f32(got_ref[:, where], projected, ((1,), (1,)))
    half = cells // 2
    out_ref[...] = jnp.concatenate([total[:half], total[half:]], axis=1).astype(BF16)


def product_terms(own, got, mine, other):
    return pl.pallas_call(
        product_kernel,
        out_shape=jax.ShapeDtypeStruct((own.shape[0] // 2, LANES), BF16),
        compiler_params=params(4),
        name="product_terms",
    )(own, got, mine, other)


def gram_kernel(term_ref, got_ref, out_ref):
    product = add_to(term_ref, got_ref)
    rank = LANES // 2
    wide = dot_f32(product, product, ((0,), (0,)), lax.Precision.HIGHEST)
    gram = wide[:rank, :rank] + wide[rank:, rank:]
    out_ref[...] = jnp.concatenate([gram[:rank // 2], gram[rank // 2:]], axis=1)


def local_gram(term, got):
    return pl.pallas_call(
        gram_kernel,
        out_shape=jax.ShapeDtypeStruct((LANES // 4, LANES), F32),
        compiler_params=params(4),
        name="local_gram",
    )(term, got)


def reciprocal(x):
    guess = pl.reciprocal(x, approx=True, full_range=False)
    for _ in range(2):
        guess = guess * (2.0 - x * guess)
    return guess


def eliminate(gram):
    rank = gram.shape[0]
    tile = 8
    count = rank // tile
    wide = 2 * rank
    sublane = lax.broadcasted_iota(jnp.int32, (tile, wide), 0)
    lane = lax.broadcasted_iota(jnp.int32, (tile, wide), 1)
    full = lambda x: jnp.broadcast_to(x, (tile, wide))
    both = []
    for v in range(count):
        mine = gram[v * tile:(v + 1) * tile]
        both.append(jnp.where(lane < rank, jnp.concatenate([mine, mine], axis=1),
                              (lane - rank == sublane + v * tile).astype(F32)))
    pivots = []
    for p in range(count):
        cols = [
            {v: full(both[v][:, p * tile + j:p * tile + j + 1]) for v in range(p, count)}
            for j in range(tile)
        ]
        rows = [full(both[p][j:j + 1]) for j in range(tile)]
        block = [[full(cols[k][p][j:j + 1]) for k in range(j + 1)] for j in range(tile)]
        found, kept = block[0][0], rows[0]
        for j in range(tile):
            if j:
                found = jnp.where(sublane == j, block[j][j], found)
                kept = jnp.where(sublane == j, rows[j], kept)
            inverse = reciprocal(block[j][j])
            scaled = {i: block[i][j] * inverse for i in range(j + 1, tile)}
            for i, factor in scaled.items():
                for k in range(j + 1, i + 1):
                    block[i][k] = block[i][k] - factor * block[k][j]
                rows[i] = rows[i] - factor * rows[j]
            row = rows[j] * inverse
            for v in range(p + 1, count):
                for i, factor in scaled.items():
                    cols[i][v] = cols[i][v] - factor * cols[j][v]
                both[v] = both[v] - cols[j][v] * row
        both[p] = kept
        pivots.append(found)
    return both, pivots


def finish_kernel(total_rows, term_ref, got_term_ref, gram_ref, got_gram_ref, out_ref):
    rank = LANES // 2
    packed = gram_ref[...] + got_gram_ref[...]
    gram = jnp.concatenate([packed[:, :rank], packed[:, rank:]], axis=0)
    both, pivots = eliminate(gram)
    scale = total_rows ** 0.5
    inverse = jnp.concatenate([b * (lax.rsqrt(p) * scale) for b, p in zip(both, pivots)], axis=0)
    inverse = inverse[:, rank:]
    product = add_to(term_ref, got_term_ref)
    mine = jnp.where(lax.axis_index("col") == 0, product[:, :rank], product[:, rank:])
    out_ref[...] = dot_f32(mine, inverse, ((1,), (1,)), lax.Precision.HIGHEST)


def finish(total_rows, term, got_term, gram, got_gram):
    return pl.pallas_call(
        functools.partial(finish_kernel, total_rows),
        out_shape=jax.ShapeDtypeStruct((term.shape[0], LANES // 2), F32),
        compiler_params=params(4),
        name="finish",
    )(term, got_term, gram, got_gram)


def per_device(snapshot, mode2_factor, old_factor):
    n_rows, n_cols = lax.axis_size("row"), lax.axis_size("col")
    masks = [1 << bit for bit in range(n_rows.bit_length() - 1)]
    total_rows = snapshot.shape[0] * n_rows

    def swap(x, mask):
        pairs = [
            (r * n_cols + c, (r ^ mask) * n_cols + (c + 1) % n_cols)
            for r in range(n_rows)
            for c in range(n_cols)
        ]
        return lax.ppermute(x, ("row", "col"), pairs)

    send, own = contract(snapshot, mode2_factor.T)
    got = swap(send, 0)

    keep, send = project(own, got, old_factor.T)
    mine = add(keep, swap(send, masks[0]))
    for mask in masks[1:]:
        mine = add(mine, swap(mine, mask))
    other = swap(mine, masks[0])

    term = product_terms(own, got, mine, other)
    got_term = swap(term, 0)
    gram = local_gram(term, got_term)
    for mask in masks[:-1]:
        gram = add(gram, swap(gram, mask))
    return finish(total_rows, term, got_term, gram, swap(gram, masks[-1]))


def solution(mesh):
    return jax.shard_map(
        per_device,
        mesh=mesh,
        in_specs=(
            P(("groups", "row"), None, "col"),
            P(("groups", "col"), None),
            P(("groups", "row"), None),
        ),
        out_specs=P(("groups", "row", "col"), None),
        check_vma=False,
    )
```

```python
import functools

import jax
import jax.numpy as jnp
from jax import lax
from jax.experimental import pallas as pl
from jax.experimental.pallas import tpu as pltpu
from jax.sharding import PartitionSpec as P

F32 = jnp.float32
BF16 = jnp.bfloat16
LANES = 128
MIB = 2**20


def dot_f32(a, b, dims, precision=None):
    return lax.dot_general(a, b, (dims, ((), ())), precision=precision, preferred_element_type=F32)


def params(mib):
    return pltpu.CompilerParams(vmem_limit_bytes=mib * MIB)


def own_half():
    row = lax.axis_index("row")
    half = lax.axis_index("col")
    for bit in range(lax.axis_size("row").bit_length() - 1):
        half += lax.rem(lax.div(row, 1 << bit), 2)
    return lax.rem(half, 2)


def contract_kernel(
    step, fibers, ahead, snapshot_ref, mode2_ref, send_ref, own_ref, slab_ref, even_ref, odd_ref, sems
):
    rank, depth = mode2_ref.shape
    tile = 8
    reps = LANES // rank
    block = tile * fibers
    blocks = step // tile
    out_rows = block // reps
    chunks = snapshot_ref.shape[0] // (step * fibers)

    def copy(chunk):
        where = pl.ds(chunk * step * fibers, step * fibers)
        return pltpu.make_async_copy(snapshot_ref.at[where], slab_ref.at[where], sems.at[chunk])

    for chunk in range(ahead):
        copy(chunk).start()
    wide = jnp.concatenate([mode2_ref[...]] * reps, axis=0)
    lane = lax.broadcasted_iota(jnp.int32, (block, LANES), 1)
    to = lax.broadcasted_iota(jnp.int32, (out_rows, reps * block), 0)
    at = lax.broadcasted_iota(jnp.int32, (out_rows, reps * block), 1)
    cell = lax.div(lax.rem(at, block), fibers)
    fiber = lax.rem(at, fibers)
    wanted = lax.div(to, tile) * reps + lax.div(at, block)
    order = ((lax.rem(to, tile) == cell) & (wanted == fiber)).astype(F32).astype(BF16)
    first = own_half() == 0
    pairs = fibers // reps

    def multiply(chunk, flat_ref):
        copy(chunk).wait()

        @pl.when(chunk + ahead < chunks)
        def _():
            copy(chunk + ahead).start()

        rows = pl.ds(chunk * step * fibers, step * fibers)
        low = dot_f32(slab_ref[rows, :depth // 2], wide[:, :depth // 2], ((1,), (1,)))
        high = dot_f32(slab_ref[rows, depth // 2:], wide[:, depth // 2:], ((1,), (1,)))
        flat_ref[...] = (low + high).astype(BF16)

    def spread(chunk, flat_ref):
        rows = pl.ds(pl.multiple_of(chunk * step, step), step)
        spreads = []
        for b in range(blocks):
            flat = flat_ref[pl.ds(b * block, block), :].astype(F32)
            groups = [
                jnp.where(lax.div(lane, rank) == r, flat, 0.0).astype(BF16) for r in range(reps)
            ]
            spreads.append(dot_f32(order, jnp.concatenate(groups, axis=0), ((1,), (0,))))
        for p in range(pairs // 2):
            low = jnp.concatenate([x[p * tile:(p + 1) * tile] for x in spreads], axis=0)
            q = p + pairs // 2
            high = jnp.concatenate([x[q * tile:(q + 1) * tile] for x in spreads], axis=0)
            where = slice(p * LANES, (p + 1) * LANES)
            own_ref[rows, where] = jnp.where(first, low, high).astype(BF16)
            send_ref[rows, where] = jnp.where(first, high, low).astype(BF16)

    def two_chunks(pair, _):
        multiply(2 * pair, even_ref)
        spread(jnp.maximum(2 * pair - 1, 0), odd_ref)
        multiply(2 * pair + 1, odd_ref)
        spread(2 * pair, even_ref)
        return _

    lax.fori_loop(0, chunks // 2, two_chunks, 0)
    spread(chunks - 1, odd_ref)


def contract(snapshot, mode2_t):
    cells, fibers, depth = snapshot.shape
    rank = mode2_t.shape[0]
    step = 16
    out = jax.ShapeDtypeStruct((cells, fibers // 2 * rank), BF16)
    return pl.pallas_call(
        functools.partial(contract_kernel, step, fibers, 3),
        in_specs=[
            pl.BlockSpec(memory_space=pltpu.HBM),
            pl.BlockSpec(memory_space=pltpu.VMEM),
        ],
        out_shape=[out, out],
        scratch_shapes=[
            pltpu.VMEM((cells * fibers, depth), BF16),
            pltpu.VMEM((step * fibers, LANES), BF16),
            pltpu.VMEM((step * fibers, LANES), BF16),
            pltpu.SemaphoreType.DMA((cells // step,)),
        ],
        compiler_params=params(50),
        name="contract",
    )(snapshot.reshape(cells * fibers, depth), mode2_t)


def add_to(*refs):
    total = refs[0][...].astype(F32)
    for ref in refs[1:]:
        total += ref[...].astype(F32)
    return total


def project_kernel(own_ref, got_ref, factor_ref, keep_ref, send_ref):
    rank = factor_ref.shape[0]
    factor = factor_ref[...]
    total = dot_f32(factor, own_ref[...], ((1,), (0,))) + dot_f32(factor, got_ref[...], ((1,), (0,)))
    even = lax.rem(lax.axis_index("row"), 2) == 0
    blocks = total.shape[1] // LANES // 2
    for block in range(blocks):
        low = total[:, block * LANES:(block + 1) * LANES]
        high = total[:, (block + blocks) * LANES:(block + blocks + 1) * LANES]
        rows = pl.ds(block * rank, rank)
        keep_ref[rows, :] = jnp.where(even, low, high)
        send_ref[rows, :] = jnp.where(even, high, low).astype(BF16)


def project(own, got, factor_t):
    rank = factor_t.shape[0]
    shape = (rank * own.shape[1] // LANES // 2, LANES)
    return pl.pallas_call(
        project_kernel,
        out_shape=[jax.ShapeDtypeStruct(shape, F32), jax.ShapeDtypeStruct(shape, BF16)],
        compiler_params=params(4),
        name="project",
    )(own, got, factor_t)


def add_kernel(mine_ref, got_ref, out_ref):
    out_ref[...] = add_to(mine_ref, got_ref).astype(out_ref.dtype)


def add(mine, got):
    return pl.pallas_call(
        add_kernel,
        out_shape=jax.ShapeDtypeStruct(got.shape, got.dtype),
        compiler_params=params(4),
        name="add",
    )(mine, got)


def product_kernel(own_ref, got_ref, mine_ref, other_ref, out_ref):
    cells, width = own_ref.shape
    blocks = width // LANES // 2
    rank = mine_ref.shape[0] // blocks
    even = lax.rem(lax.axis_index("row"), 2) == 0
    total = jnp.zeros((cells, rank), F32)
    for block in range(blocks):
        rows = pl.ds(block * rank, rank)
        mine, other = mine_ref[rows, :], other_ref[rows, :]
        low = jnp.where(even, mine, other)
        high = jnp.where(even, other, mine)
        for at, projected in ((block, low), (block + blocks, high)):
            where = slice(at * LANES, (at + 1) * LANES)
            total += dot_f32(own_ref[:, where], projected, ((1,), (1,)))
            total += dot_f32(got_ref[:, where], projected, ((1,), (1,)))
    half = cells // 2
    out_ref[...] = jnp.concatenate([total[:half], total[half:]], axis=1).astype(BF16)


def product_terms(own, got, mine, other):
    return pl.pallas_call(
        product_kernel,
        out_shape=jax.ShapeDtypeStruct((own.shape[0] // 2, LANES), BF16),
        compiler_params=params(4),
        name="product_terms",
    )(own, got, mine, other)


def gram_kernel(term_ref, got_ref, out_ref):
    product = add_to(term_ref, got_ref)
    rank = LANES // 2
    wide = dot_f32(product, product, ((0,), (0,)), lax.Precision.HIGHEST)
    gram = wide[:rank, :rank] + wide[rank:, rank:]
    out_ref[...] = jnp.concatenate([gram[:rank // 2], gram[rank // 2:]], axis=1)


def local_gram(term, got):
    return pl.pallas_call(
        gram_kernel,
        out_shape=jax.ShapeDtypeStruct((LANES // 4, LANES), F32),
        compiler_params=params(4),
        name="local_gram",
    )(term, got)


def reciprocal(x):
    guess = pl.reciprocal(x, approx=True, full_range=False)
    for _ in range(2):
        guess = guess * (2.0 - x * guess)
    return guess


def eliminate(gram):
    rank = gram.shape[0]
    tile = 8
    count = rank // tile
    wide = 2 * rank
    sublane = lax.broadcasted_iota(jnp.int32, (tile, wide), 0)
    lane = lax.broadcasted_iota(jnp.int32, (tile, wide), 1)
    full = lambda x: jnp.broadcast_to(x, (tile, wide))
    both = []
    for v in range(count):
        mine = gram[v * tile:(v + 1) * tile]
        both.append(jnp.where(lane < rank, jnp.concatenate([mine, mine], axis=1),
                              (lane - rank == sublane + v * tile).astype(F32)))
    pivots = []
    for p in range(count):
        cols = [
            {v: full(both[v][:, p * tile + j:p * tile + j + 1]) for v in range(p, count)}
            for j in range(tile)
        ]
        rows = [full(both[p][j:j + 1]) for j in range(tile)]
        block = [[full(cols[k][p][j:j + 1]) for k in range(j + 1)] for j in range(tile)]
        found, kept = block[0][0], rows[0]
        for j in range(tile):
            if j:
                found = jnp.where(sublane == j, block[j][j], found)
                kept = jnp.where(sublane == j, rows[j], kept)
            inverse = reciprocal(block[j][j])
            scaled = {i: block[i][j] * inverse for i in range(j + 1, tile)}
            for i, factor in scaled.items():
                for k in range(j + 1, i + 1):
                    block[i][k] = block[i][k] - factor * block[k][j]
                rows[i] = rows[i] - factor * rows[j]
            row = rows[j] * inverse
            for v in range(p + 1, count):
                for i, factor in scaled.items():
                    cols[i][v] = cols[i][v] - factor * cols[j][v]
                both[v] = both[v] - cols[j][v] * row
        both[p] = kept
        pivots.append(found)
    return both, pivots


def finish_kernel(total_rows, term_ref, got_term_ref, gram_ref, got_gram_ref, out_ref):
    rank = LANES // 2
    packed = gram_ref[...] + got_gram_ref[...]
    gram = jnp.concatenate([packed[:, :rank], packed[:, rank:]], axis=0)
    both, pivots = eliminate(gram)
    scale = total_rows ** 0.5
    inverse = jnp.concatenate([b * (lax.rsqrt(p) * scale) for b, p in zip(both, pivots)], axis=0)
    inverse = inverse[:, rank:]
    product = add_to(term_ref, got_term_ref)
    mine = jnp.where(lax.axis_index("col") == 0, product[:, :rank], product[:, rank:])
    out_ref[...] = dot_f32(mine, inverse, ((1,), (1,)), lax.Precision.HIGHEST)


def finish(total_rows, term, got_term, gram, got_gram):
    return pl.pallas_call(
        functools.partial(finish_kernel, total_rows),
        out_shape=jax.ShapeDtypeStruct((term.shape[0], LANES // 2), F32),
        compiler_params=params(4),
        name="finish",
    )(term, got_term, gram, got_gram)


def per_device(snapshot, mode2_factor, old_factor):
    n_rows, n_cols = lax.axis_size("row"), lax.axis_size("col")
    masks = [1 << bit for bit in range(n_rows.bit_length() - 1)]
    total_rows = snapshot.shape[0] * n_rows

    def swap(x, mask):
        pairs = [
            (r * n_cols + c, (r ^ mask) * n_cols + (c + 1) % n_cols)
            for r in range(n_rows)
            for c in range(n_cols)
        ]
        return lax.ppermute(x, ("row", "col"), pairs)

    send, own = contract(snapshot, mode2_factor.T)
    got = swap(send, 0)

    keep, send = project(own, got, old_factor.T)
    mine = add(keep, swap(send, masks[0]))
    for mask in masks[1:]:
        mine = add(mine, swap(mine, mask))
    other = swap(mine, masks[0])

    term = product_terms(own, got, mine, other)
    got_term = swap(term, 0)
    gram = local_gram(term, got_term)
    for mask in masks[:-1]:
        gram = add(gram, swap(gram, mask))
    return finish(total_rows, term, got_term, gram, swap(gram, masks[-1]))


def solution(mesh):
    return jax.shard_map(
        per_device,
        mesh=mesh,
        in_specs=(
            P(("groups", "row"), None, "col"),
            P(("groups", "col"), None),
            P(("groups", "row"), None),
        ),
        out_specs=P(("groups", "row", "col"), None),
        check_vma=False,
    )
```

```python
import functools

import jax
import jax.numpy as jnp
from jax import lax
from jax.experimental import pallas as pl
from jax.experimental.pallas import tpu as pltpu
from jax.sharding import PartitionSpec as P

F32 = jnp.float32
BF16 = jnp.bfloat16
LANES = 128
MIB = 2**20


def dot_f32(a, b, dims, precision=None):
    return lax.dot_general(a, b, (dims, ((), ())), precision=precision, preferred_element_type=F32)


def params(mib):
    return pltpu.CompilerParams(vmem_limit_bytes=mib * MIB)


def own_half():
    row = lax.axis_index("row")
    half = lax.axis_index("col")
    for bit in range(lax.axis_size("row").bit_length() - 1):
        half += lax.rem(lax.div(row, 1 << bit), 2)
    return lax.rem(half, 2)


def contract_kernel(
    step, fibers, ahead, snapshot_ref, mode2_ref, send_ref, own_ref, slab_ref, even_ref, odd_ref, sems
):
    rank, depth = mode2_ref.shape
    tile = 8
    reps = LANES // rank
    block = tile * fibers
    blocks = step // tile
    out_rows = block // reps
    chunks = snapshot_ref.shape[0] // (step * fibers)

    def copy(chunk):
        where = pl.ds(chunk * step * fibers, step * fibers)
        return pltpu.make_async_copy(snapshot_ref.at[where], slab_ref.at[where], sems.at[chunk])

    for chunk in range(ahead):
        copy(chunk).start()
    wide = jnp.concatenate([mode2_ref[...]] * reps, axis=0)
    lane = lax.broadcasted_iota(jnp.int32, (block, LANES), 1)
    to = lax.broadcasted_iota(jnp.int32, (out_rows, reps * block), 0)
    at = lax.broadcasted_iota(jnp.int32, (out_rows, reps * block), 1)
    cell = lax.div(lax.rem(at, block), fibers)
    fiber = lax.rem(at, fibers)
    wanted = lax.div(to, tile) * reps + lax.div(at, block)
    order = ((lax.rem(to, tile) == cell) & (wanted == fiber)).astype(F32).astype(BF16)
    first = own_half() == 0
    pairs = fibers // reps

    def multiply(chunk, flat_ref):
        copy(chunk).wait()

        @pl.when(chunk + ahead < chunks)
        def _():
            copy(chunk + ahead).start()

        rows = pl.ds(chunk * step * fibers, step * fibers)
        low = dot_f32(slab_ref[rows, :depth // 2], wide[:, :depth // 2], ((1,), (1,)))
        high = dot_f32(slab_ref[rows, depth // 2:], wide[:, depth // 2:], ((1,), (1,)))
        flat_ref[...] = (low + high).astype(BF16)

    def spread(chunk, flat_ref):
        rows = pl.ds(pl.multiple_of(chunk * step, step), step)
        spreads = []
        for b in range(blocks):
            flat = flat_ref[pl.ds(b * block, block), :].astype(F32)
            groups = [
                jnp.where(lax.div(lane, rank) == r, flat, 0.0).astype(BF16) for r in range(reps)
            ]
            spreads.append(dot_f32(order, jnp.concatenate(groups, axis=0), ((1,), (0,))))
        for p in range(pairs // 2):
            low = jnp.concatenate([x[p * tile:(p + 1) * tile] for x in spreads], axis=0)
            q = p + pairs // 2
            high = jnp.concatenate([x[q * tile:(q + 1) * tile] for x in spreads], axis=0)
            where = slice(p * LANES, (p + 1) * LANES)
            own_ref[rows, where] = jnp.where(first, low, high).astype(BF16)
            send_ref[rows, where] = jnp.where(first, high, low).astype(BF16)

    def two_chunks(pair, _):
        multiply(2 * pair, even_ref)
        spread(jnp.maximum(2 * pair - 1, 0), odd_ref)
        multiply(2 * pair + 1, odd_ref)
        spread(2 * pair, even_ref)
        return _

    lax.fori_loop(0, chunks // 2, two_chunks, 0)
    spread(chunks - 1, odd_ref)


def contract(snapshot, mode2_t):
    cells, fibers, depth = snapshot.shape
    rank = mode2_t.shape[0]
    step = 16
    out = jax.ShapeDtypeStruct((cells, fibers // 2 * rank), BF16)
    return pl.pallas_call(
        functools.partial(contract_kernel, step, fibers, 3),
        in_specs=[
            pl.BlockSpec(memory_space=pltpu.HBM),
            pl.BlockSpec(memory_space=pltpu.VMEM),
        ],
        out_shape=[out, out],
        scratch_shapes=[
            pltpu.VMEM((cells * fibers, depth), BF16),
            pltpu.VMEM((step * fibers, LANES), BF16),
            pltpu.VMEM((step * fibers, LANES), BF16),
            pltpu.SemaphoreType.DMA((cells // step,)),
        ],
        compiler_params=params(50),
        name="contract",
    )(snapshot.reshape(cells * fibers, depth), mode2_t)


def is_even():
    return lax.rem(lax.axis_index("row"), 2) == 0


def project_kernel(own_ref, got_ref, factor_ref, keep_ref, send_ref, mine_ref, give_ref):
    rank = factor_ref.shape[0]
    width = mine_ref.shape[1]
    even = is_even()
    halves = []
    for start in (0, width):
        where = slice(start, start + width)
        halves.append(own_ref[:, where].astype(F32) + got_ref[:, where].astype(F32))
    mine = jnp.where(even, halves[0], halves[1]).astype(BF16)
    give = jnp.where(even, halves[1], halves[0]).astype(BF16)
    mine_ref[...] = mine
    give_ref[...] = give
    keep = dot_f32(factor_ref[...], mine, ((1,), (0,)))
    send = dot_f32(factor_ref[...], give, ((1,), (0,)))
    for block in range(width // LANES):
        where = slice(block * LANES, (block + 1) * LANES)
        rows = pl.ds(block * rank, rank)
        keep_ref[rows, :] = keep[:, where]
        send_ref[rows, :] = send[:, where].astype(BF16)


def project(own, got, factor_t):
    cells, width = own.shape
    rows = factor_t.shape[0] * width // LANES // 2
    columns = jax.ShapeDtypeStruct((cells, width // 2), BF16)
    return pl.pallas_call(
        project_kernel,
        out_shape=[
            jax.ShapeDtypeStruct((rows, LANES), F32),
            jax.ShapeDtypeStruct((rows, LANES), BF16),
            columns,
            columns,
        ],
        compiler_params=params(8),
        name="project",
    )(own, got, factor_t)


def add_kernel(mine_ref, got_ref, out_ref):
    total = mine_ref[...].astype(F32) + got_ref[...].astype(F32)
    out_ref[...] = total.astype(out_ref.dtype)


def add(mine, got):
    return pl.pallas_call(
        add_kernel,
        out_shape=jax.ShapeDtypeStruct(got.shape, got.dtype),
        compiler_params=params(4),
        name="add",
    )(mine, got)


def product_kernel(mine_ref, got_ref, projected_ref, out_ref):
    blocks = mine_ref.shape[1] // LANES
    rank = projected_ref.shape[0] // blocks
    terms = []
    for ref in (mine_ref, got_ref):
        total = jnp.zeros((ref.shape[0], rank), F32)
        for block in range(blocks):
            projected = projected_ref[pl.ds(block * rank, rank), :]
            where = slice(block * LANES, (block + 1) * LANES)
            total += dot_f32(ref[:, where], projected, ((1,), (1,)))
        terms.append(total)
    even = is_even()
    low = jnp.where(even, terms[0], terms[1])
    high = jnp.where(even, terms[1], terms[0])
    out_ref[...] = jnp.concatenate([low, high], axis=1).astype(BF16)


def product_terms(mine, got, projected):
    return pl.pallas_call(
        product_kernel,
        out_shape=jax.ShapeDtypeStruct((mine.shape[0], LANES), BF16),
        compiler_params=params(4),
        name="product_terms",
    )(mine, got, projected)


def pair_product(term_ref, got_ref):
    return term_ref[...].astype(F32) + got_ref[...].astype(F32)


def gram_kernel(term_ref, got_ref, out_ref):
    product = pair_product(term_ref, got_ref)
    rank = LANES // 2
    wide = dot_f32(product, product, ((0,), (0,)), lax.Precision.HIGHEST)
    gram = wide[:rank, :rank] + wide[rank:, rank:]
    out_ref[...] = jnp.concatenate([gram[:rank // 2], gram[rank // 2:]], axis=1)


def local_gram(term, got):
    return pl.pallas_call(
        gram_kernel,
        out_shape=jax.ShapeDtypeStruct((LANES // 4, LANES), F32),
        compiler_params=params(4),
        name="local_gram",
    )(term, got)


def reciprocal(x):
    guess = pl.reciprocal(x, approx=True, full_range=False)
    for _ in range(2):
        guess = guess * (2.0 - x * guess)
    return guess


def eliminate(gram):
    rank = gram.shape[0]
    tile = 8
    count = rank // tile
    wide = 2 * rank
    sublane = lax.broadcasted_iota(jnp.int32, (tile, wide), 0)
    lane = lax.broadcasted_iota(jnp.int32, (tile, wide), 1)
    full = lambda x: jnp.broadcast_to(x, (tile, wide))
    both = []
    for v in range(count):
        mine = gram[v * tile:(v + 1) * tile]
        both.append(jnp.where(lane < rank, jnp.concatenate([mine, mine], axis=1),
                              (lane - rank == sublane + v * tile).astype(F32)))
    pivots = []
    for p in range(count):
        cols = [
            {v: full(both[v][:, p * tile + j:p * tile + j + 1]) for v in range(p, count)}
            for j in range(tile)
        ]
        rows = [full(both[p][j:j + 1]) for j in range(tile)]
        block = [[full(cols[k][p][j:j + 1]) for k in range(j + 1)] for j in range(tile)]
        found, kept = block[0][0], rows[0]
        for j in range(tile):
            if j:
                found = jnp.where(sublane == j, block[j][j], found)
                kept = jnp.where(sublane == j, rows[j], kept)
            inverse = reciprocal(block[j][j])
            scaled = {i: block[i][j] * inverse for i in range(j + 1, tile)}
            for i, factor in scaled.items():
                for k in range(j + 1, i + 1):
                    block[i][k] = block[i][k] - factor * block[k][j]
                rows[i] = rows[i] - factor * rows[j]
            row = rows[j] * inverse
            for v in range(p + 1, count):
                for i, factor in scaled.items():
                    cols[i][v] = cols[i][v] - factor * cols[j][v]
                both[v] = both[v] - cols[j][v] * row
        both[p] = kept
        pivots.append(found)
    return both, pivots


def finish_kernel(total_rows, term_ref, got_term_ref, gram_ref, got_gram_ref, out_ref):
    rank = LANES // 2
    packed = gram_ref[...] + got_gram_ref[...]
    gram = jnp.concatenate([packed[:, :rank], packed[:, rank:]], axis=0)
    both, pivots = eliminate(gram)
    scale = total_rows ** 0.5
    inverse = jnp.concatenate([b * (lax.rsqrt(p) * scale) for b, p in zip(both, pivots)], axis=0)
    inverse = inverse[:, rank:]
    half = term_ref.shape[0] // 2
    product = pair_product(term_ref, got_term_ref)
    product = jnp.where(lax.axis_index("col") == 0, product[:half], product[half:])
    mine = jnp.where(is_even(), product[:, :rank], product[:, rank:])
    out_ref[...] = dot_f32(mine, inverse, ((1,), (1,)), lax.Precision.HIGHEST)


def finish(total_rows, term, got_term, gram, got_gram):
    return pl.pallas_call(
        functools.partial(finish_kernel, total_rows),
        out_shape=jax.ShapeDtypeStruct((term.shape[0] // 2, LANES // 2), F32),
        compiler_params=params(4),
        name="finish",
    )(term, got_term, gram, got_gram)


def per_device(snapshot, mode2_factor, old_factor):
    n_rows, n_cols = lax.axis_size("row"), lax.axis_size("col")
    masks = [1 << bit for bit in range(n_rows.bit_length() - 1)]
    total_rows = snapshot.shape[0] * n_rows

    def swap(x, mask):
        pairs = [
            (r * n_cols + c, (r ^ mask) * n_cols + (c + 1) % n_cols)
            for r in range(n_rows)
            for c in range(n_cols)
        ]
        return lax.ppermute(x, ("row", "col"), pairs)

    send, own = contract(snapshot, mode2_factor.T)
    got = swap(send, 0)

    keep, send, columns, give = project(own, got, old_factor.T)
    mine = add(keep, swap(send, masks[0]))
    got_columns = swap(give, masks[0])
    for mask in masks[1:]:
        mine = add(mine, swap(mine, mask))

    term = product_terms(columns, got_columns, mine)
    term = add(term, swap(term, 0))
    got_term = swap(term, masks[0])
    gram = local_gram(term, got_term)
    for mask in masks[1:-1]:
        gram = add(gram, swap(gram, mask))
    return finish(total_rows, term, got_term, gram, swap(gram, masks[-1]))


def solution(mesh):
    return jax.shard_map(
        per_device,
        mesh=mesh,
        in_specs=(
            P(("groups", "row"), None, "col"),
            P(("groups", "col"), None),
            P(("groups", "row"), None),
        ),
        out_specs=P(("groups", "row", "col"), None),
        check_vma=False,
    )
```

```python
import functools

import jax
import jax.numpy as jnp
from jax import lax
from jax.experimental import pallas as pl
from jax.experimental.pallas import tpu as pltpu
from jax.sharding import PartitionSpec as P

F32 = jnp.float32
BF16 = jnp.bfloat16
LANES = 128
MIB = 2**20


def dot_f32(a, b, dims, precision=None):
    return lax.dot_general(a, b, (dims, ((), ())), precision=precision, preferred_element_type=F32)


def params(mib):
    return pltpu.CompilerParams(vmem_limit_bytes=mib * MIB)


def own_half():
    row = lax.axis_index("row")
    half = lax.axis_index("col")
    for bit in range(lax.axis_size("row").bit_length() - 1):
        half += lax.rem(lax.div(row, 1 << bit), 2)
    return lax.rem(half, 2)


TILE = 8


def prepare_kernel(fibers, mode2_ref, wide_ref, order_ref):
    rank = mode2_ref.shape[0]
    reps = LANES // rank
    wide_ref[...] = jnp.concatenate([mode2_ref[...]] * reps, axis=0)
    block = TILE * fibers
    to = lax.broadcasted_iota(jnp.int32, order_ref.shape, 0)
    at = lax.broadcasted_iota(jnp.int32, order_ref.shape, 1)
    cell = lax.div(lax.rem(at, block), fibers)
    wanted = lax.div(to, TILE) * reps + lax.div(at, block)
    same = (lax.rem(to, TILE) == cell) & (wanted == lax.rem(at, fibers))
    order_ref[...] = same.astype(F32).astype(BF16)


def prepare(mode2_t, fibers):
    rank, depth = mode2_t.shape
    reps = LANES // rank
    block = TILE * fibers
    return pl.pallas_call(
        functools.partial(prepare_kernel, fibers),
        out_shape=[
            jax.ShapeDtypeStruct((LANES, depth), BF16),
            jax.ShapeDtypeStruct((block // reps, block * reps), BF16),
        ],
        compiler_params=params(4),
        cost_estimate=pl.CostEstimate(flops=0, bytes_accessed=2**24, transcendentals=0),
        name="prepare",
    )(mode2_t)


def contract_kernel(step, own, snapshot_ref, wide_ref, order_ref, core_ref, even_ref, odd_ref):
    cells, fibers, depth = snapshot_ref.shape
    half = fibers // 2
    block = TILE * half
    reps = order_ref.shape[1] // block
    rank = LANES // reps
    chunks = cells // step
    lane = lax.broadcasted_iota(jnp.int32, (block, LANES), 1)
    start = own_half() if own else 1 - own_half()
    start = pl.multiple_of(start * half, half)

    def multiply(chunk, flat_ref):
        x = snapshot_ref[pl.ds(chunk * step, step), pl.ds(start, half), :]
        x = x.reshape(step * half, depth)
        low = dot_f32(x[:, :depth // 2], wide_ref[:, :depth // 2], ((1,), (1,)))
        high = dot_f32(x[:, depth // 2:], wide_ref[:, depth // 2:], ((1,), (1,)))
        flat_ref[...] = (low + high).astype(BF16)

    def spread(chunk, flat_ref):
        rows = pl.ds(pl.multiple_of(chunk * step, step), step)
        spreads = []
        for b in range(step // TILE):
            flat = flat_ref[pl.ds(b * block, block), :].astype(F32)
            groups = [
                jnp.where(lax.div(lane, rank) == r, flat, 0.0).astype(BF16) for r in range(reps)
            ]
            spreads.append(dot_f32(order_ref[...], jnp.concatenate(groups, axis=0), ((1,), (0,))))
        for p in range(half // reps):
            part = jnp.concatenate([x[p * TILE:(p + 1) * TILE] for x in spreads], axis=0)
            core_ref[rows, p * LANES:(p + 1) * LANES] = part.astype(BF16)

    def two_chunks(pair, _):
        multiply(2 * pair, even_ref)
        spread(jnp.maximum(2 * pair - 1, 0), odd_ref)
        multiply(2 * pair + 1, odd_ref)
        spread(2 * pair, even_ref)
        return _

    lax.fori_loop(0, chunks // 2, two_chunks, 0)
    spread(chunks - 1, odd_ref)


def contract(snapshot, wide, order, own):
    cells, fibers, depth = snapshot.shape
    step = 32
    reps = order.shape[1] // (TILE * fibers // 2)
    return pl.pallas_call(
        functools.partial(contract_kernel, step, own),
        out_shape=jax.ShapeDtypeStruct((cells, fibers // 2 // reps * LANES), BF16),
        scratch_shapes=[pltpu.VMEM((step * fibers // 2, LANES), BF16)] * 2,
        compiler_params=params(24),
        name="contract_own" if own else "contract_send",
    )(snapshot, wide, order)


def is_even():
    return lax.rem(lax.axis_index("row"), 2) == 0


def project_kernel(own_ref, got_ref, factor_ref, keep_ref, send_ref, mine_ref, give_ref):
    rank = factor_ref.shape[0]
    width = mine_ref.shape[1]
    even = is_even()
    halves = []
    for start in (0, width):
        where = slice(start, start + width)
        halves.append(own_ref[:, where].astype(F32) + got_ref[:, where].astype(F32))
    mine = jnp.where(even, halves[0], halves[1]).astype(BF16)
    give = jnp.where(even, halves[1], halves[0]).astype(BF16)
    mine_ref[...] = mine
    give_ref[...] = give
    keep = dot_f32(factor_ref[...], mine, ((1,), (0,)))
    send = dot_f32(factor_ref[...], give, ((1,), (0,)))
    for block in range(width // LANES):
        where = slice(block * LANES, (block + 1) * LANES)
        rows = pl.ds(block * rank, rank)
        keep_ref[rows, :] = keep[:, where]
        send_ref[rows, :] = send[:, where].astype(BF16)


def project(own, got, factor_t):
    cells, width = own.shape
    rows = factor_t.shape[0] * width // LANES // 2
    columns = jax.ShapeDtypeStruct((cells, width // 2), BF16)
    return pl.pallas_call(
        project_kernel,
        out_shape=[
            jax.ShapeDtypeStruct((rows, LANES), F32),
            jax.ShapeDtypeStruct((rows, LANES), BF16),
            columns,
            columns,
        ],
        compiler_params=params(8),
        name="project",
    )(own, got, factor_t)


def add_kernel(mine_ref, got_ref, *refs):
    total = mine_ref[...].astype(F32) + got_ref[...].astype(F32)
    refs[-1][...] = total.astype(refs[-1].dtype)


def add(mine, got, *after):
    whole = pl.BlockSpec(memory_space=pltpu.VMEM)
    return pl.pallas_call(
        add_kernel,
        in_specs=[whole, whole] + [pl.BlockSpec(memory_space=pl.ANY)] * len(after),
        out_shape=jax.ShapeDtypeStruct(got.shape, got.dtype),
        compiler_params=params(4),
        name="add",
    )(mine, got, *after)


def product_kernel(mine_ref, got_ref, projected_ref, out_ref):
    blocks = mine_ref.shape[1] // LANES
    rank = projected_ref.shape[0] // blocks
    terms = []
    for ref in (mine_ref, got_ref):
        total = jnp.zeros((ref.shape[0], rank), F32)
        for block in range(blocks):
            projected = projected_ref[pl.ds(block * rank, rank), :]
            where = slice(block * LANES, (block + 1) * LANES)
            total += dot_f32(ref[:, where], projected, ((1,), (1,)))
        terms.append(total)
    even = is_even()
    low = jnp.where(even, terms[0], terms[1])
    high = jnp.where(even, terms[1], terms[0])
    out_ref[...] = jnp.concatenate([low, high], axis=1).astype(BF16)


def product_terms(mine, got, projected):
    return pl.pallas_call(
        product_kernel,
        out_shape=jax.ShapeDtypeStruct((mine.shape[0], LANES), BF16),
        compiler_params=params(4),
        name="product_terms",
    )(mine, got, projected)


def pair_product(term_ref, got_ref):
    return term_ref[...].astype(F32) + got_ref[...].astype(F32)


def gram_kernel(term_ref, got_ref, out_ref):
    product = pair_product(term_ref, got_ref)
    rank = LANES // 2
    wide = dot_f32(product, product, ((0,), (0,)), lax.Precision.HIGHEST)
    gram = wide[:rank, :rank] + wide[rank:, rank:]
    out_ref[...] = jnp.concatenate([gram[:rank // 2], gram[rank // 2:]], axis=1)


def local_gram(term, got):
    return pl.pallas_call(
        gram_kernel,
        out_shape=jax.ShapeDtypeStruct((LANES // 4, LANES), F32),
        compiler_params=params(4),
        name="local_gram",
    )(term, got)


def reciprocal(x):
    guess = pl.reciprocal(x, approx=True, full_range=False)
    for _ in range(2):
        guess = guess * (2.0 - x * guess)
    return guess


def eliminate(gram):
    rank = gram.shape[0]
    tile = 8
    count = rank // tile
    wide = 2 * rank
    sublane = lax.broadcasted_iota(jnp.int32, (tile, wide), 0)
    lane = lax.broadcasted_iota(jnp.int32, (tile, wide), 1)
    full = lambda x: jnp.broadcast_to(x, (tile, wide))
    both = []
    for v in range(count):
        mine = gram[v * tile:(v + 1) * tile]
        both.append(jnp.where(lane < rank, jnp.concatenate([mine, mine], axis=1),
                              (lane - rank == sublane + v * tile).astype(F32)))
    pivots = []
    for p in range(count):
        cols = [
            {v: full(both[v][:, p * tile + j:p * tile + j + 1]) for v in range(p, count)}
            for j in range(tile)
        ]
        rows = [full(both[p][j:j + 1]) for j in range(tile)]
        block = [[full(cols[k][p][j:j + 1]) for k in range(j + 1)] for j in range(tile)]
        found, kept = block[0][0], rows[0]
        for j in range(tile):
            if j:
                found = jnp.where(sublane == j, block[j][j], found)
                kept = jnp.where(sublane == j, rows[j], kept)
            inverse = reciprocal(block[j][j])
            scaled = {i: block[i][j] * inverse for i in range(j + 1, tile)}
            for i, factor in scaled.items():
                for k in range(j + 1, i + 1):
                    block[i][k] = block[i][k] - factor * block[k][j]
                rows[i] = rows[i] - factor * rows[j]
            row = rows[j] * inverse
            for v in range(p + 1, count):
                for i, factor in scaled.items():
                    cols[i][v] = cols[i][v] - factor * cols[j][v]
                both[v] = both[v] - cols[j][v] * row
        both[p] = kept
        pivots.append(found)
    return both, pivots


def finish_kernel(total_rows, term_ref, got_term_ref, gram_ref, got_gram_ref, out_ref):
    rank = LANES // 2
    packed = gram_ref[...] + got_gram_ref[...]
    gram = jnp.concatenate([packed[:, :rank], packed[:, rank:]], axis=0)
    both, pivots = eliminate(gram)
    scale = total_rows ** 0.5
    inverse = jnp.concatenate([b * (lax.rsqrt(p) * scale) for b, p in zip(both, pivots)], axis=0)
    inverse = inverse[:, rank:]
    half = term_ref.shape[0] // 2
    product = pair_product(term_ref, got_term_ref)
    product = jnp.where(lax.axis_index("col") == 0, product[:half], product[half:])
    mine = jnp.where(is_even(), product[:, :rank], product[:, rank:])
    out_ref[...] = dot_f32(mine, inverse, ((1,), (1,)), lax.Precision.HIGHEST)


def finish(total_rows, term, got_term, gram, got_gram):
    return pl.pallas_call(
        functools.partial(finish_kernel, total_rows),
        out_shape=jax.ShapeDtypeStruct((term.shape[0] // 2, LANES // 2), F32),
        compiler_params=params(4),
        name="finish",
    )(term, got_term, gram, got_gram)


def per_device(snapshot, mode2_factor, old_factor):
    n_rows, n_cols = lax.axis_size("row"), lax.axis_size("col")
    masks = [1 << bit for bit in range(n_rows.bit_length() - 1)]
    total_rows = snapshot.shape[0] * n_rows

    def swap(x, mask):
        pairs = [
            (r * n_cols + c, (r ^ mask) * n_cols + (c + 1) % n_cols)
            for r in range(n_rows)
            for c in range(n_cols)
        ]
        return lax.ppermute(x, ("row", "col"), pairs)

    wide, order = prepare(mode2_factor.T, snapshot.shape[1] // 2)
    got = swap(contract(snapshot, wide, order, False), 0)
    own = contract(snapshot, wide, order, True)

    keep, send, columns, give = project(own, got, old_factor.T)
    mine = add(keep, swap(send, masks[0]))
    got_columns = swap(give, masks[0])
    for step, mask in enumerate(masks[1:]):
        after = [got_columns] if step == 0 else []
        mine = add(mine, swap(mine, mask), *after)

    term = product_terms(columns, got_columns, mine)
    term = add(term, swap(term, 0))
    got_term = swap(term, masks[0])
    gram = local_gram(term, got_term)
    for mask in masks[1:-1]:
        gram = add(gram, swap(gram, mask))
    return finish(total_rows, term, got_term, gram, swap(gram, masks[-1]))


def solution(mesh):
    return jax.shard_map(
        per_device,
        mesh=mesh,
        in_specs=(
            P(("groups", "row"), None, "col"),
            P(("groups", "col"), None),
            P(("groups", "row"), None),
        ),
        out_specs=P(("groups", "row", "col"), None),
        check_vma=False,
    )
```

```python
import functools

import jax
import jax.numpy as jnp
from jax import lax
from jax.experimental import pallas as pl
from jax.experimental.pallas import tpu as pltpu
from jax.sharding import PartitionSpec as P

F32 = jnp.float32
BF16 = jnp.bfloat16
LANES = 128
MIB = 2**20


def dot_f32(a, b, dims, precision=None):
    return lax.dot_general(a, b, (dims, ((), ())), precision=precision, preferred_element_type=F32)


def params(mib):
    return pltpu.CompilerParams(vmem_limit_bytes=mib * MIB)


def own_half():
    row = lax.axis_index("row")
    half = lax.axis_index("col")
    for bit in range(lax.axis_size("row").bit_length() - 1):
        half += lax.rem(lax.div(row, 1 << bit), 2)
    return lax.rem(half, 2)


TILE = 8


def contract_kernel(step, own, snapshot_ref, mode2_ref, core_ref, even_ref, odd_ref):
    cells, fibers, depth = snapshot_ref.shape
    rank = mode2_ref.shape[0]
    half = fibers // 2
    reps = LANES // rank
    block = TILE * half
    chunks = cells // step
    start = own_half() if own else 1 - own_half()
    start = pl.multiple_of(start * half, half)
    shape = (block // reps, block * reps)
    to = lax.broadcasted_iota(jnp.int32, shape, 0)
    at = lax.broadcasted_iota(jnp.int32, shape, 1)
    cell = lax.div(lax.rem(at, block), half)
    wanted = lax.div(to, TILE) * reps + lax.div(at, block)
    same = (lax.rem(to, TILE) == cell) & (wanted == lax.rem(at, half))
    order = same.astype(F32).astype(BF16)

    def multiply(chunk, flat_ref):
        x = snapshot_ref[pl.ds(chunk * step, step), pl.ds(start, half), :]
        x = x.reshape(step * half, depth)
        flat_ref[...] = dot_f32(mode2_ref[...], x, ((1,), (1,))).astype(BF16)

    def spread(chunk, flat_ref):
        rows = pl.ds(pl.multiple_of(chunk * step, step), step)
        spreads = []
        for b in range(step // TILE):
            flat = flat_ref[:, b * block:(b + 1) * block]
            none = jnp.zeros_like(flat)
            groups = [
                jnp.concatenate([flat if k == r else none for k in range(reps)], axis=1)
                for r in range(reps)
            ]
            spreads.append(dot_f32(order, jnp.concatenate(groups, axis=0), ((1,), (1,))))
        for p in range(half // reps):
            part = jnp.concatenate([x[p * TILE:(p + 1) * TILE] for x in spreads], axis=0)
            core_ref[rows, p * LANES:(p + 1) * LANES] = part.astype(BF16)

    def two_chunks(pair, _):
        multiply(2 * pair, even_ref)
        spread(jnp.maximum(2 * pair - 1, 0), odd_ref)
        multiply(2 * pair + 1, odd_ref)
        spread(2 * pair, even_ref)
        return _

    lax.fori_loop(0, chunks // 2, two_chunks, 0)
    spread(chunks - 1, odd_ref)


def contract(snapshot, mode2_t, own):
    cells, fibers, depth = snapshot.shape
    rank = mode2_t.shape[0]
    step = 32
    return pl.pallas_call(
        functools.partial(contract_kernel, step, own),
        out_shape=jax.ShapeDtypeStruct((cells, fibers // 2 * rank), BF16),
        scratch_shapes=[pltpu.VMEM((rank, step * fibers // 2), BF16)] * 2,
        compiler_params=params(24),
        name="contract_own" if own else "contract_send",
    )(snapshot, mode2_t)


def is_even():
    return lax.rem(lax.axis_index("row"), 2) == 0


def project_kernel(own_ref, got_ref, factor_ref, keep_ref, send_ref, mine_ref, give_ref):
    rank = factor_ref.shape[0]
    width = mine_ref.shape[1]
    even = is_even()
    halves = []
    for start in (0, width):
        where = slice(start, start + width)
        halves.append(own_ref[:, where].astype(F32) + got_ref[:, where].astype(F32))
    mine = jnp.where(even, halves[0], halves[1]).astype(BF16)
    give = jnp.where(even, halves[1], halves[0]).astype(BF16)
    mine_ref[...] = mine
    give_ref[...] = give
    keep = dot_f32(factor_ref[...], mine, ((1,), (0,)))
    send = dot_f32(factor_ref[...], give, ((1,), (0,)))
    for block in range(width // LANES):
        where = slice(block * LANES, (block + 1) * LANES)
        rows = pl.ds(block * rank, rank)
        keep_ref[rows, :] = keep[:, where]
        send_ref[rows, :] = send[:, where].astype(BF16)


def project(own, got, factor_t):
    cells, width = own.shape
    rows = factor_t.shape[0] * width // LANES // 2
    columns = jax.ShapeDtypeStruct((cells, width // 2), BF16)
    return pl.pallas_call(
        project_kernel,
        out_shape=[
            jax.ShapeDtypeStruct((rows, LANES), F32),
            jax.ShapeDtypeStruct((rows, LANES), BF16),
            columns,
            columns,
        ],
        compiler_params=params(8),
        name="project",
    )(own, got, factor_t)


def add_kernel(mine_ref, got_ref, *refs):
    total = mine_ref[...].astype(F32) + got_ref[...].astype(F32)
    refs[-1][...] = total.astype(refs[-1].dtype)


def add(mine, got, *after):
    whole = pl.BlockSpec(memory_space=pltpu.VMEM)
    return pl.pallas_call(
        add_kernel,
        in_specs=[whole, whole] + [pl.BlockSpec(memory_space=pl.ANY)] * len(after),
        out_shape=jax.ShapeDtypeStruct(got.shape, got.dtype),
        compiler_params=params(4),
        name="add",
    )(mine, got, *after)


def halves_kernel(mine_ref, got_ref, low_ref, high_ref):
    size = low_ref.shape[0]
    for start, ref in ((0, low_ref), (size, high_ref)):
        rows = pl.ds(start, size)
        ref[...] = (mine_ref[rows, :] + got_ref[rows, :].astype(F32)).astype(BF16)


def add_in_halves(mine, got):
    out = jax.ShapeDtypeStruct((got.shape[0] // 2, LANES), BF16)
    return pl.pallas_call(
        halves_kernel,
        out_shape=[out, out],
        compiler_params=params(4),
        name="add_in_halves",
    )(mine, got)


def product_kernel(mine_ref, got_ref, low_ref, high_ref, out_ref):
    blocks = mine_ref.shape[1] // LANES // 2
    rank = low_ref.shape[0] // blocks
    terms = []
    for ref in (mine_ref, got_ref):
        total = jnp.zeros((ref.shape[0], rank), F32)
        for block in range(2 * blocks):
            half_ref = low_ref if block < blocks else high_ref
            projected = half_ref[pl.ds(block % blocks * rank, rank), :]
            where = slice(block * LANES, (block + 1) * LANES)
            total += dot_f32(ref[:, where], projected, ((1,), (1,)))
        terms.append(total)
    even = is_even()
    low = jnp.where(even, terms[0], terms[1])
    high = jnp.where(even, terms[1], terms[0])
    out_ref[...] = jnp.concatenate([low, high], axis=1).astype(BF16)


def product_terms(mine, got, low, high):
    return pl.pallas_call(
        product_kernel,
        out_shape=jax.ShapeDtypeStruct((mine.shape[0], LANES), BF16),
        compiler_params=params(4),
        name="product_terms",
    )(mine, got, low, high)


def pair_product(term_ref, got_ref):
    return term_ref[...].astype(F32) + got_ref[...].astype(F32)


def gram_kernel(term_ref, got_ref, out_ref):
    product = pair_product(term_ref, got_ref)
    rank = LANES // 2
    wide = dot_f32(product, product, ((0,), (0,)), lax.Precision.HIGHEST)
    gram = wide[:rank, :rank] + wide[rank:, rank:]
    out_ref[...] = jnp.concatenate([gram[:rank // 2], gram[rank // 2:]], axis=1)


def local_gram(term, got):
    return pl.pallas_call(
        gram_kernel,
        out_shape=jax.ShapeDtypeStruct((LANES // 4, LANES), F32),
        compiler_params=params(4),
        name="local_gram",
    )(term, got)


def reciprocal(x):
    guess = pl.reciprocal(x, approx=True, full_range=False)
    for _ in range(2):
        guess = guess * (2.0 - x * guess)
    return guess


def eliminate(gram):
    rank = gram.shape[0]
    tile = 8
    count = rank // tile
    wide = 2 * rank
    sublane = lax.broadcasted_iota(jnp.int32, (tile, wide), 0)
    lane = lax.broadcasted_iota(jnp.int32, (tile, wide), 1)
    full = lambda x: jnp.broadcast_to(x, (tile, wide))
    both = []
    for v in range(count):
        mine = gram[v * tile:(v + 1) * tile]
        both.append(jnp.where(lane < rank, jnp.concatenate([mine, mine], axis=1),
                              (lane - rank == sublane + v * tile).astype(F32)))
    pivots = []
    for p in range(count):
        cols = [
            {v: full(both[v][:, p * tile + j:p * tile + j + 1]) for v in range(p, count)}
            for j in range(tile)
        ]
        rows = [full(both[p][j:j + 1]) for j in range(tile)]
        block = [[full(cols[k][p][j:j + 1]) for k in range(j + 1)] for j in range(tile)]
        found, kept = block[0][0], rows[0]
        for j in range(tile):
            if j:
                found = jnp.where(sublane == j, block[j][j], found)
                kept = jnp.where(sublane == j, rows[j], kept)
            inverse = reciprocal(block[j][j])
            scaled = {i: block[i][j] * inverse for i in range(j + 1, tile)}
            for i, factor in scaled.items():
                for k in range(j + 1, i + 1):
                    block[i][k] = block[i][k] - factor * block[k][j]
                rows[i] = rows[i] - factor * rows[j]
            row = rows[j] * inverse
            for v in range(p + 1, count):
                for i, factor in scaled.items():
                    cols[i][v] = cols[i][v] - factor * cols[j][v]
                both[v] = both[v] - cols[j][v] * row
        both[p] = kept
        pivots.append(found)
    return both, pivots


def finish_kernel(total_rows, term_ref, got_term_ref, gram_ref, got_gram_ref, out_ref):
    rank = LANES // 2
    packed = gram_ref[...] + got_gram_ref[...]
    gram = jnp.concatenate([packed[:, :rank], packed[:, rank:]], axis=0)
    both, pivots = eliminate(gram)
    scale = total_rows ** 0.5
    inverse = jnp.concatenate([b * (lax.rsqrt(p) * scale) for b, p in zip(both, pivots)], axis=0)
    inverse = inverse[:, rank:]
    half = term_ref.shape[0] // 2
    product = pair_product(term_ref, got_term_ref)
    product = jnp.where(lax.axis_index("col") == 0, product[:half], product[half:])
    mine = jnp.where(is_even(), product[:, :rank], product[:, rank:])
    out_ref[...] = dot_f32(mine, inverse, ((1,), (1,)), lax.Precision.HIGHEST)


def finish(total_rows, term, got_term, gram, got_gram):
    return pl.pallas_call(
        functools.partial(finish_kernel, total_rows),
        out_shape=jax.ShapeDtypeStruct((term.shape[0] // 2, LANES // 2), F32),
        compiler_params=params(4),
        name="finish",
    )(term, got_term, gram, got_gram)


def per_device(snapshot, mode2_factor, old_factor):
    n_rows, n_cols = lax.axis_size("row"), lax.axis_size("col")
    masks = [1 << bit for bit in range(n_rows.bit_length() - 1)]
    total_rows = snapshot.shape[0] * n_rows

    def swap(x, mask):
        pairs = [
            (r * n_cols + c, (r ^ mask) * n_cols + (c + 1) % n_cols)
            for r in range(n_rows)
            for c in range(n_cols)
        ]
        return lax.ppermute(x, ("row", "col"), pairs)

    mode2_t = mode2_factor.T
    got = swap(contract(snapshot, mode2_t, False), 0)
    own = contract(snapshot, mode2_t, True)

    keep, send, columns, give = project(own, got, old_factor.T)
    low, high = add_in_halves(keep, swap(send, masks[0]))
    got_columns = swap(give, masks[0])
    others = masks[1:]
    for step, (mask, turned) in enumerate(zip(others, others[1:] + others[:1])):
        after = [got_columns] if step == 1 else []
        got_low, got_high = swap(low, mask), swap(high, turned)
        low, high = add(low, got_low), add(high, got_high, *after)

    term = product_terms(columns, got_columns, low, high)
    term = add(term, swap(term, 0))
    got_term = swap(term, masks[0])
    gram = local_gram(term, got_term)
    for mask in masks[1:-1]:
        gram = add(gram, swap(gram, mask))
    return finish(total_rows, term, got_term, gram, swap(gram, masks[-1]))


def solution(mesh):
    return jax.shard_map(
        per_device,
        mesh=mesh,
        in_specs=(
            P(("groups", "row"), None, "col"),
            P(("groups", "col"), None),
            P(("groups", "row"), None),
        ),
        out_specs=P(("groups", "row", "col"), None),
        check_vma=False,
    )
```

```python
import functools

import jax
import jax.numpy as jnp
from jax import lax
from jax.experimental import pallas as pl
from jax.experimental.pallas import tpu as pltpu
from jax.sharding import PartitionSpec as P

F32 = jnp.float32
BF16 = jnp.bfloat16
LANES = 128
MIB = 2**20


def dot_f32(a, b, dims, precision=None):
    return lax.dot_general(a, b, (dims, ((), ())), precision=precision, preferred_element_type=F32)


def params(mib):
    return pltpu.CompilerParams(vmem_limit_bytes=mib * MIB)


def own_half():
    row = lax.axis_index("row")
    half = lax.axis_index("col")
    for bit in range(lax.axis_size("row").bit_length() - 1):
        half += lax.rem(lax.div(row, 1 << bit), 2)
    return lax.rem(half, 2)


TILE = 8


def fill_order(order_ref, half):
    block = TILE * half
    reps = order_ref.shape[1] // block
    to = lax.broadcasted_iota(jnp.int32, order_ref.shape, 0)
    at = lax.broadcasted_iota(jnp.int32, order_ref.shape, 1)
    cell = lax.div(lax.rem(at, block), half)
    wanted = lax.div(to, TILE) * reps + lax.div(at, block)
    same = (lax.rem(to, TILE) == cell) & (wanted == lax.rem(at, half))
    order_ref[...] = same.astype(F32).astype(BF16)


def contract_loop(step, slab_ref, wide_ref, order_ref, core_ref, even_ref, odd_ref, ready):
    cells, half, depth = slab_ref.shape
    block = TILE * half
    reps = order_ref.shape[1] // block
    rank = LANES // reps
    chunks = cells // step
    lane = lax.broadcasted_iota(jnp.int32, (block, LANES), 1)

    def multiply(chunk, flat_ref):
        ready(chunk)
        x = slab_ref[pl.ds(chunk * step, step)].reshape(step * half, depth)
        low = dot_f32(x[:, :depth // 2], wide_ref[:, :depth // 2], ((1,), (1,)))
        high = dot_f32(x[:, depth // 2:], wide_ref[:, depth // 2:], ((1,), (1,)))
        flat_ref[...] = (low + high).astype(BF16)

    def spread(chunk, flat_ref):
        rows = pl.ds(pl.multiple_of(chunk * step, step), step)
        spreads = []
        for b in range(step // TILE):
            flat = flat_ref[pl.ds(b * block, block), :].astype(F32)
            groups = [
                jnp.where(lax.div(lane, rank) == r, flat, 0.0).astype(BF16) for r in range(reps)
            ]
            spreads.append(dot_f32(order_ref[...], jnp.concatenate(groups, axis=0), ((1,), (0,))))
        for p in range(half // reps):
            part = jnp.concatenate([x[p * TILE:(p + 1) * TILE] for x in spreads], axis=0)
            core_ref[rows, p * LANES:(p + 1) * LANES] = part.astype(BF16)

    def two_chunks(pair, _):
        multiply(2 * pair, even_ref)
        spread(jnp.maximum(2 * pair - 1, 0), odd_ref)
        multiply(2 * pair + 1, odd_ref)
        spread(2 * pair, even_ref)
        return _

    lax.fori_loop(0, chunks // 2, two_chunks, 0)
    spread(chunks - 1, odd_ref)


STEP = 32


def send_kernel(
    snapshot_ref, mode2_ref, core_ref, kept_ref, wide_ref, order_ref,
    slab_ref, small_ref, even_ref, odd_ref, sems, kept_sem, small_sem,
):
    cells, half, _ = slab_ref.shape
    rank = mode2_ref.shape[0]
    chunks = cells // STEP
    keep_start = pl.multiple_of(own_half() * half, half)
    send_start = pl.multiple_of((1 - own_half()) * half, half)

    def send_copy(start, size, chunk):
        where = pl.ds(start, size)
        return pltpu.make_async_copy(
            snapshot_ref.at[where, pl.ds(send_start, half)], slab_ref.at[where], sems.at[chunk]
        )

    def kept_copy(start, size):
        where = pl.ds(start, size)
        return pltpu.make_async_copy(
            snapshot_ref.at[where, pl.ds(keep_start, half)], kept_ref.at[where], kept_sem
        )

    def start_send(chunk, parts):
        size = STEP // parts
        for part in range(parts):
            send_copy(chunk * STEP + part * size, size, chunk).start()

    def start_kept(chunk):
        for part in range(2):
            kept_copy(chunk * STEP + part * (STEP // 2), STEP // 2).start()

    small = pltpu.make_async_copy(mode2_ref, small_ref, small_sem)
    small.start()
    start_send(0, 4)
    for chunk in range(1, chunks - 1):
        start_send(chunk, 2)
    fill_order(order_ref, half)
    small.wait()
    wide_ref[...] = jnp.concatenate([small_ref[...]] * (LANES // rank), axis=0)

    def ready(chunk):
        send_copy(chunk * STEP, STEP, chunk).wait()
        for now in range(chunks):

            @pl.when(chunk == now)
            def _():
                if now == 0:
                    start_send(chunks - 1, 2)
                start_kept(now)

    contract_loop(STEP, slab_ref, wide_ref, order_ref, core_ref, even_ref, odd_ref, ready)
    kept_copy(0, cells).wait()


def contract_send(snapshot, mode2_t):
    cells, fibers, depth = snapshot.shape
    rank = mode2_t.shape[0]
    half = fibers // 2
    reps = LANES // rank
    block = TILE * half
    any_space = pl.BlockSpec(memory_space=pltpu.HBM)
    return pl.pallas_call(
        send_kernel,
        in_specs=[any_space, any_space],
        out_shape=[
            jax.ShapeDtypeStruct((cells, half * rank), BF16),
            jax.ShapeDtypeStruct((cells, half, depth), BF16),
            jax.ShapeDtypeStruct((LANES, depth), BF16),
            jax.ShapeDtypeStruct((block // reps, block * reps), BF16),
        ],
        scratch_shapes=[
            pltpu.VMEM((cells, half, depth), BF16),
            pltpu.VMEM((rank, depth), BF16),
            pltpu.VMEM((STEP * half, LANES), BF16),
            pltpu.VMEM((STEP * half, LANES), BF16),
            pltpu.SemaphoreType.DMA((cells // STEP,)),
            pltpu.SemaphoreType.DMA,
            pltpu.SemaphoreType.DMA,
        ],
        compiler_params=params(47),
        name="contract_send",
    )(snapshot, mode2_t)


def own_kernel(slab_ref, wide_ref, order_ref, core_ref, even_ref, odd_ref):
    contract_loop(
        STEP, slab_ref, wide_ref, order_ref, core_ref, even_ref, odd_ref, lambda chunk: None
    )


def contract_own(slab, wide, order):
    cells, half, _ = slab.shape
    reps = order.shape[1] // (TILE * half)
    return pl.pallas_call(
        own_kernel,
        out_shape=jax.ShapeDtypeStruct((cells, half // reps * LANES), BF16),
        scratch_shapes=[pltpu.VMEM((STEP * half, LANES), BF16)] * 2,
        compiler_params=params(24),
        name="contract_own",
    )(slab, wide, order)


def is_even():
    return lax.rem(lax.axis_index("row"), 2) == 0


def project_kernel(own_ref, got_ref, factor_ref, keep_ref, send_ref, mine_ref, give_ref):
    rank = factor_ref.shape[0]
    width = mine_ref.shape[1]
    even = is_even()
    halves = []
    for start in (0, width):
        where = slice(start, start + width)
        halves.append(own_ref[:, where].astype(F32) + got_ref[:, where].astype(F32))
    mine = jnp.where(even, halves[0], halves[1]).astype(BF16)
    give = jnp.where(even, halves[1], halves[0]).astype(BF16)
    mine_ref[...] = mine
    give_ref[...] = give
    keep = dot_f32(factor_ref[...], mine, ((1,), (0,)))
    send = dot_f32(factor_ref[...], give, ((1,), (0,)))
    for block in range(width // LANES):
        where = slice(block * LANES, (block + 1) * LANES)
        rows = pl.ds(block * rank, rank)
        keep_ref[rows, :] = keep[:, where]
        send_ref[rows, :] = send[:, where].astype(BF16)


def project(own, got, factor_t):
    cells, width = own.shape
    rows = factor_t.shape[0] * width // LANES // 2
    columns = jax.ShapeDtypeStruct((cells, width // 2), BF16)
    return pl.pallas_call(
        project_kernel,
        out_shape=[
            jax.ShapeDtypeStruct((rows, LANES), F32),
            jax.ShapeDtypeStruct((rows, LANES), BF16),
            columns,
            columns,
        ],
        compiler_params=params(8),
        name="project",
    )(own, got, factor_t)


def add_kernel(mine_ref, got_ref, *refs):
    total = mine_ref[...].astype(F32) + got_ref[...].astype(F32)
    refs[-1][...] = total.astype(refs[-1].dtype)


def add(mine, got, *after):
    whole = pl.BlockSpec(memory_space=pltpu.VMEM)
    return pl.pallas_call(
        add_kernel,
        in_specs=[whole, whole] + [pl.BlockSpec(memory_space=pl.ANY)] * len(after),
        out_shape=jax.ShapeDtypeStruct(got.shape, got.dtype),
        compiler_params=params(4),
        name="add",
    )(mine, got, *after)


def halves_kernel(mine_ref, got_ref, low_ref, high_ref):
    size = low_ref.shape[0]
    for start, ref in ((0, low_ref), (size, high_ref)):
        rows = pl.ds(start, size)
        ref[...] = (mine_ref[rows, :] + got_ref[rows, :].astype(F32)).astype(BF16)


def add_in_halves(mine, got):
    out = jax.ShapeDtypeStruct((got.shape[0] // 2, LANES), BF16)
    return pl.pallas_call(
        halves_kernel,
        out_shape=[out, out],
        compiler_params=params(4),
        name="add_in_halves",
    )(mine, got)


def product_kernel(mine_ref, got_ref, low_ref, high_ref, out_ref):
    blocks = mine_ref.shape[1] // LANES // 2
    rank = low_ref.shape[0] // blocks
    terms = []
    for ref in (mine_ref, got_ref):
        total = jnp.zeros((ref.shape[0], rank), F32)
        for block in range(2 * blocks):
            half_ref = low_ref if block < blocks else high_ref
            projected = half_ref[pl.ds(block % blocks * rank, rank), :]
            where = slice(block * LANES, (block + 1) * LANES)
            total += dot_f32(ref[:, where], projected, ((1,), (1,)))
        terms.append(total)
    even = is_even()
    low = jnp.where(even, terms[0], terms[1])
    high = jnp.where(even, terms[1], terms[0])
    out_ref[...] = jnp.concatenate([low, high], axis=1).astype(BF16)


def product_terms(mine, got, low, high):
    return pl.pallas_call(
        product_kernel,
        out_shape=jax.ShapeDtypeStruct((mine.shape[0], LANES), BF16),
        compiler_params=params(4),
        name="product_terms",
    )(mine, got, low, high)


def pair_product(term_ref, got_ref):
    return term_ref[...].astype(F32) + got_ref[...].astype(F32)


def gram_kernel(term_ref, got_ref, out_ref):
    product = pair_product(term_ref, got_ref)
    rank = LANES // 2
    wide = dot_f32(product, product, ((0,), (0,)), lax.Precision.HIGHEST)
    gram = wide[:rank, :rank] + wide[rank:, rank:]
    out_ref[...] = jnp.concatenate([gram[:rank // 2], gram[rank // 2:]], axis=1)


def local_gram(term, got):
    return pl.pallas_call(
        gram_kernel,
        out_shape=jax.ShapeDtypeStruct((LANES // 4, LANES), F32),
        compiler_params=params(4),
        name="local_gram",
    )(term, got)


def reciprocal(x):
    guess = pl.reciprocal(x, approx=True, full_range=False)
    for _ in range(2):
        guess = guess * (2.0 - x * guess)
    return guess


def eliminate(gram):
    rank = gram.shape[0]
    tile = 8
    count = rank // tile
    wide = 2 * rank
    sublane = lax.broadcasted_iota(jnp.int32, (tile, wide), 0)
    lane = lax.broadcasted_iota(jnp.int32, (tile, wide), 1)
    full = lambda x: jnp.broadcast_to(x, (tile, wide))
    both = []
    for v in range(count):
        mine = gram[v * tile:(v + 1) * tile]
        both.append(jnp.where(lane < rank, jnp.concatenate([mine, mine], axis=1),
                              (lane - rank == sublane + v * tile).astype(F32)))
    pivots = []
    for p in range(count):
        cols = [
            {v: full(both[v][:, p * tile + j:p * tile + j + 1]) for v in range(p, count)}
            for j in range(tile)
        ]
        rows = [full(both[p][j:j + 1]) for j in range(tile)]
        block = [[full(cols[k][p][j:j + 1]) for k in range(j + 1)] for j in range(tile)]
        found, kept = block[0][0], rows[0]
        for j in range(tile):
            if j:
                found = jnp.where(sublane == j, block[j][j], found)
                kept = jnp.where(sublane == j, rows[j], kept)
            inverse = reciprocal(block[j][j])
            scaled = {i: block[i][j] * inverse for i in range(j + 1, tile)}
            for i, factor in scaled.items():
                for k in range(j + 1, i + 1):
                    block[i][k] = block[i][k] - factor * block[k][j]
                rows[i] = rows[i] - factor * rows[j]
            row = rows[j] * inverse
            for v in range(p + 1, count):
                for i, factor in scaled.items():
                    cols[i][v] = cols[i][v] - factor * cols[j][v]
                both[v] = both[v] - cols[j][v] * row
        both[p] = kept
        pivots.append(found)
    return both, pivots


def finish_kernel(total_rows, term_ref, got_term_ref, gram_ref, got_gram_ref, out_ref):
    rank = LANES // 2
    packed = gram_ref[...] + got_gram_ref[...]
    gram = jnp.concatenate([packed[:, :rank], packed[:, rank:]], axis=0)
    both, pivots = eliminate(gram)
    scale = total_rows ** 0.5
    inverse = jnp.concatenate([b * (lax.rsqrt(p) * scale) for b, p in zip(both, pivots)], axis=0)
    inverse = inverse[:, rank:]
    half = term_ref.shape[0] // 2
    product = pair_product(term_ref, got_term_ref)
    product = jnp.where(lax.axis_index("col") == 0, product[:half], product[half:])
    mine = jnp.where(is_even(), product[:, :rank], product[:, rank:])
    out_ref[...] = dot_f32(mine, inverse, ((1,), (1,)), lax.Precision.HIGHEST)


def finish(total_rows, term, got_term, gram, got_gram):
    return pl.pallas_call(
        functools.partial(finish_kernel, total_rows),
        out_shape=jax.ShapeDtypeStruct((term.shape[0] // 2, LANES // 2), F32),
        compiler_params=params(4),
        name="finish",
    )(term, got_term, gram, got_gram)


def per_device(snapshot, mode2_factor, old_factor):
    n_rows, n_cols = lax.axis_size("row"), lax.axis_size("col")
    masks = [1 << bit for bit in range(n_rows.bit_length() - 1)]
    total_rows = snapshot.shape[0] * n_rows

    def swap(x, mask):
        pairs = [
            (r * n_cols + c, (r ^ mask) * n_cols + (c + 1) % n_cols)
            for r in range(n_rows)
            for c in range(n_cols)
        ]
        return lax.ppermute(x, ("row", "col"), pairs)

    send, kept, wide, order = contract_send(snapshot, mode2_factor.T)
    got = swap(send, 0)
    own = contract_own(kept, wide, order)

    keep, send, columns, give = project(own, got, old_factor.T)
    low, high = add_in_halves(keep, swap(send, masks[0]))
    got_columns = swap(give, masks[0])
    others = masks[1:]
    for step, (mask, turned) in enumerate(zip(others, others[1:] + others[:1])):
        after = [got_columns] if step == 1 else []
        got_low, got_high = swap(low, mask), swap(high, turned)
        low, high = add(low, got_low), add(high, got_high, *after)

    term = product_terms(columns, got_columns, low, high)
    term = add(term, swap(term, 0))
    got_term = swap(term, masks[0])
    gram = local_gram(term, got_term)
    for mask in masks[1:-1]:
        gram = add(gram, swap(gram, mask))
    return finish(total_rows, term, got_term, gram, swap(gram, masks[-1]))


def solution(mesh):
    return jax.shard_map(
        per_device,
        mesh=mesh,
        in_specs=(
            P(("groups", "row"), None, "col"),
            P(("groups", "col"), None),
            P(("groups", "row"), None),
        ),
        out_specs=P(("groups", "row", "col"), None),
        check_vma=False,
    )
```

```python
import functools

import jax
import jax.numpy as jnp
from jax import lax
from jax.experimental import pallas as pl
from jax.experimental.pallas import tpu as pltpu
from jax.sharding import PartitionSpec as P

F32 = jnp.float32
BF16 = jnp.bfloat16
LANES = 128
MIB = 2**20


def dot_f32(a, b, dims, precision=None):
    return lax.dot_general(a, b, (dims, ((), ())), precision=precision, preferred_element_type=F32)


def params(mib):
    return pltpu.CompilerParams(vmem_limit_bytes=mib * MIB)


def own_half():
    row = lax.axis_index("row")
    half = lax.axis_index("col")
    for bit in range(lax.axis_size("row").bit_length() - 1):
        half += lax.rem(lax.div(row, 1 << bit), 2)
    return lax.rem(half, 2)


TILE = 8


def prepare_kernel(fibers, mode2_ref, wide_ref, order_ref):
    rank = mode2_ref.shape[0]
    reps = LANES // rank
    wide_ref[...] = jnp.concatenate([mode2_ref[...]] * reps, axis=0)
    block = TILE * fibers
    to = lax.broadcasted_iota(jnp.int32, order_ref.shape, 0)
    at = lax.broadcasted_iota(jnp.int32, order_ref.shape, 1)
    cell = lax.div(lax.rem(at, block), fibers)
    wanted = lax.div(to, TILE) * reps + lax.div(at, block)
    same = (lax.rem(to, TILE) == cell) & (wanted == lax.rem(at, fibers))
    order_ref[...] = same.astype(F32).astype(BF16)


def prepare(mode2_t, fibers):
    rank, depth = mode2_t.shape
    reps = LANES // rank
    block = TILE * fibers
    return pl.pallas_call(
        functools.partial(prepare_kernel, fibers),
        out_shape=[
            jax.ShapeDtypeStruct((LANES, depth), BF16),
            jax.ShapeDtypeStruct((block // reps, block * reps), BF16),
        ],
        compiler_params=params(4),
        cost_estimate=pl.CostEstimate(flops=0, bytes_accessed=2**24, transcendentals=0),
        name="prepare",
    )(mode2_t)


def contract_kernel(step, own, snapshot_ref, wide_ref, order_ref, core_ref, even_ref, odd_ref):
    cells, fibers, depth = snapshot_ref.shape
    half = fibers // 2
    block = TILE * half
    reps = order_ref.shape[1] // block
    rank = LANES // reps
    chunks = cells // step
    lane = lax.broadcasted_iota(jnp.int32, (block, LANES), 1)
    start = own_half() if own else 1 - own_half()
    start = pl.multiple_of(start * half, half)

    def multiply(chunk, flat_ref):
        x = snapshot_ref[pl.ds(chunk * step, step), pl.ds(start, half), :]
        x = x.reshape(step * half, depth)
        low = dot_f32(x[:, :depth // 2], wide_ref[:, :depth // 2], ((1,), (1,)))
        high = dot_f32(x[:, depth // 2:], wide_ref[:, depth // 2:], ((1,), (1,)))
        flat_ref[...] = (low + high).astype(BF16)

    def spread(chunk, flat_ref):
        rows = pl.ds(pl.multiple_of(chunk * step, step), step)
        spreads = []
        for b in range(step // TILE):
            flat = flat_ref[pl.ds(b * block, block), :].astype(F32)
            groups = [
                jnp.where(lax.div(lane, rank) == r, flat, 0.0).astype(BF16) for r in range(reps)
            ]
            spreads.append(dot_f32(order_ref[...], jnp.concatenate(groups, axis=0), ((1,), (0,))))
        for p in range(half // reps):
            part = jnp.concatenate([x[p * TILE:(p + 1) * TILE] for x in spreads], axis=0)
            core_ref[rows, p * LANES:(p + 1) * LANES] = part.astype(BF16)

    def two_chunks(pair, _):
        multiply(2 * pair, even_ref)
        spread(jnp.maximum(2 * pair - 1, 0), odd_ref)
        multiply(2 * pair + 1, odd_ref)
        spread(2 * pair, even_ref)
        return _

    lax.fori_loop(0, chunks // 2, two_chunks, 0)
    spread(chunks - 1, odd_ref)


def contract(snapshot, wide, order, own):
    cells, fibers, depth = snapshot.shape
    step = 32
    reps = order.shape[1] // (TILE * fibers // 2)
    return pl.pallas_call(
        functools.partial(contract_kernel, step, own),
        out_shape=jax.ShapeDtypeStruct((cells, fibers // 2 // reps * LANES), BF16),
        scratch_shapes=[pltpu.VMEM((step * fibers // 2, LANES), BF16)] * 2,
        compiler_params=params(24),
        name="contract_own" if own else "contract_send",
    )(snapshot, wide, order)


def is_even():
    return lax.rem(lax.axis_index("row"), 2) == 0


def project_kernel(own_ref, got_ref, factor_ref, keep_ref, send_ref, mine_ref, give_ref):
    rank = factor_ref.shape[0]
    width = mine_ref.shape[1]
    even = is_even()
    halves = []
    for start in (0, width):
        where = slice(start, start + width)
        halves.append(own_ref[:, where].astype(F32) + got_ref[:, where].astype(F32))
    mine = jnp.where(even, halves[0], halves[1]).astype(BF16)
    give = jnp.where(even, halves[1], halves[0]).astype(BF16)
    mine_ref[...] = mine
    give_ref[...] = give
    keep = dot_f32(factor_ref[...], mine, ((1,), (0,)))
    send = dot_f32(factor_ref[...], give, ((1,), (0,)))
    for block in range(width // LANES):
        where = slice(block * LANES, (block + 1) * LANES)
        rows = pl.ds(block * rank, rank)
        keep_ref[rows, :] = keep[:, where]
        send_ref[rows, :] = send[:, where].astype(BF16)


def project(own, got, factor_t):
    cells, width = own.shape
    rows = factor_t.shape[0] * width // LANES // 2
    columns = jax.ShapeDtypeStruct((cells, width // 2), BF16)
    return pl.pallas_call(
        project_kernel,
        out_shape=[
            jax.ShapeDtypeStruct((rows, LANES), F32),
            jax.ShapeDtypeStruct((rows, LANES), BF16),
            columns,
            columns,
        ],
        compiler_params=params(8),
        name="project",
    )(own, got, factor_t)


def add_kernel(mine_ref, got_ref, *refs):
    total = mine_ref[...].astype(F32) + got_ref[...].astype(F32)
    refs[-1][...] = total.astype(refs[-1].dtype)


def add(mine, got, *after):
    whole = pl.BlockSpec(memory_space=pltpu.VMEM)
    return pl.pallas_call(
        add_kernel,
        in_specs=[whole, whole] + [pl.BlockSpec(memory_space=pl.ANY)] * len(after),
        out_shape=jax.ShapeDtypeStruct(got.shape, got.dtype),
        compiler_params=params(4),
        name="add",
    )(mine, got, *after)


def halves_kernel(mine_ref, got_ref, low_ref, high_ref):
    size = low_ref.shape[0]
    for start, ref in ((0, low_ref), (size, high_ref)):
        rows = pl.ds(start, size)
        ref[...] = (mine_ref[rows, :] + got_ref[rows, :].astype(F32)).astype(BF16)


def add_in_halves(mine, got):
    out = jax.ShapeDtypeStruct((got.shape[0] // 2, LANES), BF16)
    return pl.pallas_call(
        halves_kernel,
        out_shape=[out, out],
        compiler_params=params(4),
        name="add_in_halves",
    )(mine, got)


def product_kernel(mine_ref, got_ref, low_ref, high_ref, out_ref):
    blocks = mine_ref.shape[1] // LANES // 2
    rank = low_ref.shape[0] // blocks
    projected = jnp.concatenate(
        [
            ref[pl.ds(block * rank, rank), :]
            for ref in (low_ref, high_ref)
            for block in range(blocks)
        ],
        axis=1,
    )
    terms = [dot_f32(ref[...], projected, ((1,), (1,))) for ref in (mine_ref, got_ref)]
    even = is_even()
    low = jnp.where(even, terms[0], terms[1])
    high = jnp.where(even, terms[1], terms[0])
    out_ref[...] = jnp.concatenate([low, high], axis=1).astype(BF16)


def product_terms(mine, got, low, high):
    return pl.pallas_call(
        product_kernel,
        out_shape=jax.ShapeDtypeStruct((mine.shape[0], LANES), BF16),
        compiler_params=params(4),
        name="product_terms",
    )(mine, got, low, high)


def pair_product(term_ref, got_ref):
    return term_ref[...].astype(F32) + got_ref[...].astype(F32)


def gram_kernel(term_ref, got_ref, out_ref):
    product = pair_product(term_ref, got_ref)
    rank = LANES // 2
    wide = dot_parts(product, product, 0)
    gram = wide[:rank, :rank] + wide[rank:, rank:]
    out_ref[...] = jnp.concatenate([gram[:rank // 2], gram[rank // 2:]], axis=1)


def local_gram(term, got):
    return pl.pallas_call(
        gram_kernel,
        out_shape=jax.ShapeDtypeStruct((LANES // 4, LANES), F32),
        compiler_params=params(4),
        name="local_gram",
    )(term, got)


def parts(x):
    high = x.astype(BF16)
    return high, (x - high.astype(F32)).astype(BF16)


def dot_parts(a, b, axis):
    (ah, al), (bh, bl) = parts(a), parts(b)
    left = jnp.concatenate([ah, ah, al], axis=axis)
    right = jnp.concatenate([bh, bl, bh], axis=axis)
    return dot_f32(left, right, ((axis,), (axis,)))


def eliminate(gram):
    rank = gram.shape[0]
    tile = 8
    count = rank // tile
    wide = 2 * rank
    sublane = lax.broadcasted_iota(jnp.int32, (tile, wide), 0)
    lane = lax.broadcasted_iota(jnp.int32, (tile, wide), 1)
    full = lambda x: jnp.broadcast_to(x, (tile, wide))
    both = []
    for v in range(count):
        mine = gram[v * tile:(v + 1) * tile]
        both.append(jnp.where(lane < rank, jnp.concatenate([mine, mine], axis=1),
                              (lane - rank == sublane + v * tile).astype(F32)))
    pivots = []
    for p in range(count):
        cols = [
            {v: full(both[v][:, p * tile + j:p * tile + j + 1]) for v in range(p, count)}
            for j in range(tile)
        ]
        rows = [full(both[p][j:j + 1]) for j in range(tile)]
        block = [[full(cols[k][p][j:j + 1]) for k in range(j + 1)] for j in range(tile)]
        found, kept = block[0][0], rows[0]
        for j in range(tile):
            if j:
                found = jnp.where(sublane == j, block[j][j], found)
                kept = jnp.where(sublane == j, rows[j], kept)
            inverse = pl.reciprocal(block[j][j], approx=True, full_range=False)
            scaled = {i: block[i][j] * inverse for i in range(j + 1, tile)}
            for i, factor in scaled.items():
                for k in range(j + 1, i + 1):
                    block[i][k] = block[i][k] - factor * block[k][j]
                rows[i] = rows[i] - factor * rows[j]
            row = rows[j] * inverse
            for v in range(p + 1, count):
                for i, factor in scaled.items():
                    cols[i][v] = cols[i][v] - factor * cols[j][v]
                both[v] = both[v] - cols[j][v] * row
        both[p] = kept
        pivots.append(found)
    return both, pivots


def finish_kernel(total_rows, term_ref, got_term_ref, gram_ref, got_gram_ref, out_ref):
    rank = LANES // 2
    packed = gram_ref[...] + got_gram_ref[...]
    gram = jnp.concatenate([packed[:, :rank], packed[:, rank:]], axis=0)
    both, pivots = eliminate(gram)
    scale = total_rows ** 0.5
    inverse = jnp.concatenate([b * (lax.rsqrt(p) * scale) for b, p in zip(both, pivots)], axis=0)
    inverse = inverse[:, rank:]
    half = term_ref.shape[0] // 2
    product = pair_product(term_ref, got_term_ref)
    product = jnp.where(lax.axis_index("col") == 0, product[:half], product[half:])
    mine = jnp.where(is_even(), product[:, :rank], product[:, rank:])
    out_ref[...] = dot_parts(mine, inverse, 1)


def finish(total_rows, term, got_term, gram, got_gram):
    return pl.pallas_call(
        functools.partial(finish_kernel, total_rows),
        out_shape=jax.ShapeDtypeStruct((term.shape[0] // 2, LANES // 2), F32),
        compiler_params=params(4),
        name="finish",
    )(term, got_term, gram, got_gram)


def per_device(snapshot, mode2_factor, old_factor):
    n_rows, n_cols = lax.axis_size("row"), lax.axis_size("col")
    masks = [1 << bit for bit in range(n_rows.bit_length() - 1)]
    total_rows = snapshot.shape[0] * n_rows

    def swap(x, mask):
        pairs = [
            (r * n_cols + c, (r ^ mask) * n_cols + (c + 1) % n_cols)
            for r in range(n_rows)
            for c in range(n_cols)
        ]
        return lax.ppermute(x, ("row", "col"), pairs)

    wide, order = prepare(mode2_factor.T, snapshot.shape[1] // 2)
    got = swap(contract(snapshot, wide, order, False), 0)
    own = contract(snapshot, wide, order, True)

    keep, send, columns, give = project(own, got, old_factor.T)
    low, high = add_in_halves(keep, swap(send, masks[0]))
    got_columns = swap(give, masks[0])
    others = masks[1:]
    for step, (mask, turned) in enumerate(zip(others, others[1:] + others[:1])):
        after = [got_columns] if step == 1 else []
        got_low, got_high = swap(low, mask), swap(high, turned)
        low, high = add(low, got_low), add(high, got_high, *after)

    term = product_terms(columns, got_columns, low, high)
    term = add(term, swap(term, 0))
    got_term = swap(term, masks[0])
    gram = local_gram(term, got_term)
    for mask in masks[1:-1]:
        gram = add(gram, swap(gram, mask))
    return finish(total_rows, term, got_term, gram, swap(gram, masks[-1]))


def solution(mesh):
    return jax.shard_map(
        per_device,
        mesh=mesh,
        in_specs=(
            P(("groups", "row"), None, "col"),
            P(("groups", "col"), None),
            P(("groups", "row"), None),
        ),
        out_specs=P(("groups", "row", "col"), None),
        check_vma=False,
    )
```

```python
import functools

import jax
import jax.numpy as jnp
from jax import lax
from jax.experimental import pallas as pl
from jax.experimental.pallas import tpu as pltpu
from jax.sharding import PartitionSpec as P

F32 = jnp.float32
BF16 = jnp.bfloat16
LANES = 128
MIB = 2**20


def dot_f32(a, b, dims, precision=None):
    return lax.dot_general(a, b, (dims, ((), ())), precision=precision, preferred_element_type=F32)


def params(mib):
    return pltpu.CompilerParams(vmem_limit_bytes=mib * MIB)


def own_half():
    row = lax.axis_index("row")
    half = lax.axis_index("col")
    for bit in range(lax.axis_size("row").bit_length() - 1):
        half += lax.rem(lax.div(row, 1 << bit), 2)
    return lax.rem(half, 2)


TILE = 8


def fill_order(order_ref, half):
    block = TILE * half
    to = lax.broadcasted_iota(jnp.int32, order_ref.shape, 0)
    at = lax.broadcasted_iota(jnp.int32, order_ref.shape, 1)
    cell = lax.div(lax.rem(at, block), half)
    wanted = lax.div(to, TILE) * (order_ref.shape[1] // block) + lax.div(at, block)
    same = (lax.rem(to, TILE) == cell) & (wanted == lax.rem(at, half))
    order_ref[...] = same.astype(F32).astype(BF16)


def multiply(slab, wide_ref, flat_ref):
    cells, half, depth = slab.shape
    x = slab.reshape(cells * half, depth)
    low = dot_f32(x[:, :depth // 2], wide_ref[:, :depth // 2], ((1,), (1,)))
    high = dot_f32(x[:, depth // 2:], wide_ref[:, depth // 2:], ((1,), (1,)))
    flat_ref[...] = (low + high).astype(BF16)


def spread(half, flat_ref, order_ref, core_ref, start):
    block = TILE * half
    reps = order_ref.shape[1] // block
    step = flat_ref.shape[0] // half
    group = lax.div(lax.broadcasted_iota(jnp.int32, (block, LANES), 1), LANES // reps)
    spreads = []
    for b in range(step // TILE):
        flat = flat_ref[pl.ds(b * block, block), :].astype(F32)
        groups = [jnp.where(group == r, flat, 0.0).astype(BF16) for r in range(reps)]
        spreads.append(dot_f32(order_ref[...], jnp.concatenate(groups, axis=0), ((1,), (0,))))
    for p in range(half // reps):
        part = jnp.concatenate([x[p * TILE:(p + 1) * TILE] for x in spreads], axis=0)
        core_ref[pl.ds(start, step), p * LANES:(p + 1) * LANES] = part.astype(BF16)


STEP = 32


def slab_copies(snapshot_ref, first, slab_ref, half_index, sem):
    half = slab_ref.shape[1]
    fibers = pl.ds(pl.multiple_of(half_index * half, half), half)

    def copy(start, size):
        return pltpu.make_async_copy(
            snapshot_ref.at[pl.ds(start, size), fibers],
            slab_ref.at[pl.ds(start - first, size)],
            sem,
        )

    def start(begin, size, count):
        for part in range(count):
            copy(begin + part * (size // count), size // count).start()

    return start, lambda begin, size: copy(begin, size).wait()


def send_kernel(
    snapshot_ref, mode2_ref, core_ref, kept_ref, wide_ref, order_ref,
    slab_ref, small_ref, even_ref, odd_ref, sems, kept_sem, small_sem,
):
    cells, half, _ = slab_ref.shape
    rank = mode2_ref.shape[0]
    chunks = cells // STEP
    kept = kept_ref.shape[0]
    flat = (even_ref, odd_ref)
    sends = [
        slab_copies(snapshot_ref, 0, slab_ref, 1 - own_half(), sems.at[chunk])
        for chunk in range(chunks)
    ]
    start_kept, wait_kept = slab_copies(snapshot_ref, 0, kept_ref, own_half(), kept_sem)

    small = pltpu.make_async_copy(mode2_ref, small_ref, small_sem)
    small.start()
    for chunk in range(min(3, chunks)):
        sends[chunk][0](chunk * STEP, STEP, 2 if chunk else 4)
    fill_order(order_ref, half)
    small.wait()
    wide_ref[...] = jnp.concatenate([small_ref[...]] * (LANES // rank), axis=0)
    for chunk in range(chunks):
        sends[chunk][1](chunk * STEP, STEP)
        if chunk + 3 < chunks:
            sends[chunk + 3][0]((chunk + 3) * STEP, STEP, 2)
        if chunk * STEP < kept:
            start_kept(chunk * STEP, STEP, 2)
        multiply(slab_ref[pl.ds(chunk * STEP, STEP)], wide_ref, flat[chunk % 2])
        if chunk:
            spread(half, flat[(chunk - 1) % 2], order_ref, core_ref, (chunk - 1) * STEP)
    spread(half, flat[(chunks - 1) % 2], order_ref, core_ref, (chunks - 1) * STEP)
    wait_kept(0, kept)


def contract_send(snapshot, mode2_t):
    cells, fibers, depth = snapshot.shape
    rank = mode2_t.shape[0]
    half = fibers // 2
    reps = LANES // rank
    block = TILE * half
    pinned = pl.BlockSpec(memory_space=pltpu.HBM)
    return pl.pallas_call(
        send_kernel,
        in_specs=[pinned, pinned],
        out_shape=[
            jax.ShapeDtypeStruct((cells, half * rank), BF16),
            jax.ShapeDtypeStruct((cells // 2, half, depth), BF16),
            jax.ShapeDtypeStruct((LANES, depth), BF16),
            jax.ShapeDtypeStruct((block // reps, block * reps), BF16),
        ],
        scratch_shapes=[
            pltpu.VMEM((cells, half, depth), BF16),
            pltpu.VMEM((rank, depth), BF16),
            pltpu.VMEM((STEP * half, LANES), BF16),
            pltpu.VMEM((STEP * half, LANES), BF16),
            pltpu.SemaphoreType.DMA((cells // STEP,)),
            pltpu.SemaphoreType.DMA,
            pltpu.SemaphoreType.DMA,
        ],
        compiler_params=params(24),
        name="contract_send",
    )(snapshot, mode2_t)


def own_kernel(
    kept_ref, snapshot_ref, wide_ref, order_ref, core_ref, rest_ref, even_ref, odd_ref, sem
):
    kept, half, _ = kept_ref.shape
    rest = rest_ref.shape[0]
    start, wait = slab_copies(snapshot_ref, kept, rest_ref, own_half(), sem)
    start(kept, rest, 4)
    multiply(kept_ref[...], wide_ref, even_ref)
    wait(kept, rest)
    multiply(rest_ref[...], wide_ref, odd_ref)
    spread(half, even_ref, order_ref, core_ref, 0)
    spread(half, odd_ref, order_ref, core_ref, kept)


def contract_own(kept, snapshot, wide, order):
    cells = snapshot.shape[0]
    rows, half, depth = kept.shape
    reps = order.shape[1] // (TILE * half)
    whole = pl.BlockSpec(memory_space=pltpu.VMEM)
    return pl.pallas_call(
        own_kernel,
        in_specs=[whole, pl.BlockSpec(memory_space=pltpu.HBM), whole, whole],
        out_shape=jax.ShapeDtypeStruct((cells, half // reps * LANES), BF16),
        scratch_shapes=[
            pltpu.VMEM((cells - rows, half, depth), BF16),
            pltpu.VMEM((rows * half, LANES), BF16),
            pltpu.VMEM(((cells - rows) * half, LANES), BF16),
            pltpu.SemaphoreType.DMA,
        ],
        compiler_params=params(24),
        name="contract_own",
    )(kept, snapshot, wide, order)


def is_even():
    return lax.rem(lax.axis_index("row"), 2) == 0


def project_kernel(own_ref, got_ref, factor_ref, keep_ref, send_ref, mine_ref, give_ref):
    rank = factor_ref.shape[0]
    width = mine_ref.shape[1]
    even = is_even()
    halves = []
    for start in (0, width):
        where = slice(start, start + width)
        halves.append(own_ref[:, where].astype(F32) + got_ref[:, where].astype(F32))
    mine = jnp.where(even, halves[0], halves[1]).astype(BF16)
    give = jnp.where(even, halves[1], halves[0]).astype(BF16)
    mine_ref[...] = mine
    give_ref[...] = give
    keep = dot_f32(factor_ref[...], mine, ((1,), (0,)))
    send = dot_f32(factor_ref[...], give, ((1,), (0,)))
    for block in range(width // LANES):
        where = slice(block * LANES, (block + 1) * LANES)
        rows = pl.ds(block * rank, rank)
        keep_ref[rows, :] = keep[:, where]
        send_ref[rows, :] = send[:, where].astype(BF16)


def project(own, got, factor_t):
    cells, width = own.shape
    rows = factor_t.shape[0] * width // LANES // 2
    columns = jax.ShapeDtypeStruct((cells, width // 2), BF16)
    return pl.pallas_call(
        project_kernel,
        out_shape=[
            jax.ShapeDtypeStruct((rows, LANES), F32),
            jax.ShapeDtypeStruct((rows, LANES), BF16),
            columns,
            columns,
        ],
        compiler_params=params(8),
        name="project",
    )(own, got, factor_t)


def add_kernel(mine_ref, got_ref, *refs):
    total = mine_ref[...].astype(F32) + got_ref[...].astype(F32)
    refs[-1][...] = total.astype(refs[-1].dtype)


def add(mine, got, *after):
    whole = pl.BlockSpec(memory_space=pltpu.VMEM)
    return pl.pallas_call(
        add_kernel,
        in_specs=[whole, whole] + [pl.BlockSpec(memory_space=pl.ANY)] * len(after),
        out_shape=jax.ShapeDtypeStruct(got.shape, got.dtype),
        compiler_params=params(4),
        name="add",
    )(mine, got, *after)


def halves_kernel(mine_ref, got_ref, low_ref, high_ref):
    size = low_ref.shape[0]
    for start, ref in ((0, low_ref), (size, high_ref)):
        rows = pl.ds(start, size)
        ref[...] = (mine_ref[rows, :] + got_ref[rows, :].astype(F32)).astype(BF16)


def add_in_halves(mine, got):
    out = jax.ShapeDtypeStruct((got.shape[0] // 2, LANES), BF16)
    return pl.pallas_call(
        halves_kernel,
        out_shape=[out, out],
        compiler_params=params(4),
        name="add_in_halves",
    )(mine, got)


def product_kernel(mine_ref, got_ref, low_ref, high_ref, out_ref):
    blocks = mine_ref.shape[1] // LANES // 2
    rank = low_ref.shape[0] // blocks
    projected = jnp.concatenate(
        [
            ref[pl.ds(block * rank, rank), :]
            for ref in (low_ref, high_ref)
            for block in range(blocks)
        ],
        axis=1,
    )
    terms = [dot_f32(ref[...], projected, ((1,), (1,))) for ref in (mine_ref, got_ref)]
    even = is_even()
    low = jnp.where(even, terms[0], terms[1])
    high = jnp.where(even, terms[1], terms[0])
    out_ref[...] = jnp.concatenate([low, high], axis=1).astype(BF16)


def product_terms(mine, got, low, high):
    return pl.pallas_call(
        product_kernel,
        out_shape=jax.ShapeDtypeStruct((mine.shape[0], LANES), BF16),
        compiler_params=params(4),
        name="product_terms",
    )(mine, got, low, high)


def pair_product(term_ref, got_ref):
    return term_ref[...].astype(F32) + got_ref[...].astype(F32)


def gram_kernel(term_ref, got_ref, out_ref):
    product = pair_product(term_ref, got_ref)
    rank = LANES // 2
    wide = dot_parts(product, product, 0)
    gram = wide[:rank, :rank] + wide[rank:, rank:]
    out_ref[...] = jnp.concatenate([gram[:rank // 2], gram[rank // 2:]], axis=1)


def local_gram(term, got):
    return pl.pallas_call(
        gram_kernel,
        out_shape=jax.ShapeDtypeStruct((LANES // 4, LANES), F32),
        compiler_params=params(4),
        name="local_gram",
    )(term, got)


def parts(x):
    high = x.astype(BF16)
    return high, (x - high.astype(F32)).astype(BF16)


def dot_parts(a, b, axis):
    (ah, al), (bh, bl) = parts(a), parts(b)
    left = jnp.concatenate([ah, ah, al], axis=axis)
    right = jnp.concatenate([bh, bl, bh], axis=axis)
    return dot_f32(left, right, ((axis,), (axis,)))


def eliminate(gram):
    rank = gram.shape[0]
    tile = 8
    count = rank // tile
    wide = 2 * rank
    sublane = lax.broadcasted_iota(jnp.int32, (tile, wide), 0)
    lane = lax.broadcasted_iota(jnp.int32, (tile, wide), 1)
    full = lambda x: jnp.broadcast_to(x, (tile, wide))
    both = []
    for v in range(count):
        mine = gram[v * tile:(v + 1) * tile]
        both.append(jnp.where(lane < rank, jnp.concatenate([mine, mine], axis=1),
                              (lane - rank == sublane + v * tile).astype(F32)))
    pivots = []
    for p in range(count):
        cols = [
            {v: full(both[v][:, p * tile + j:p * tile + j + 1]) for v in range(p, count)}
            for j in range(tile)
        ]
        rows = [full(both[p][j:j + 1]) for j in range(tile)]
        block = [[full(cols[k][p][j:j + 1]) for k in range(j + 1)] for j in range(tile)]
        found, kept = block[0][0], rows[0]
        for j in range(tile):
            if j:
                found = jnp.where(sublane == j, block[j][j], found)
                kept = jnp.where(sublane == j, rows[j], kept)
            inverse = pl.reciprocal(block[j][j], approx=True, full_range=False)
            scaled = {i: block[i][j] * inverse for i in range(j + 1, tile)}
            for i, factor in scaled.items():
                for k in range(j + 1, i + 1):
                    block[i][k] = block[i][k] - factor * block[k][j]
                rows[i] = rows[i] - factor * rows[j]
            row = rows[j] * inverse
            for v in range(p + 1, count):
                for i, factor in scaled.items():
                    cols[i][v] = cols[i][v] - factor * cols[j][v]
                both[v] = both[v] - cols[j][v] * row
        both[p] = kept
        pivots.append(found)
    return both, pivots


def finish_kernel(total_rows, term_ref, got_term_ref, gram_ref, got_gram_ref, out_ref):
    rank = LANES // 2
    packed = gram_ref[...] + got_gram_ref[...]
    gram = jnp.concatenate([packed[:, :rank], packed[:, rank:]], axis=0)
    both, pivots = eliminate(gram)
    scale = total_rows ** 0.5
    inverse = jnp.concatenate([b * (lax.rsqrt(p) * scale) for b, p in zip(both, pivots)], axis=0)
    inverse = inverse[:, rank:]
    half = term_ref.shape[0] // 2
    product = pair_product(term_ref, got_term_ref)
    product = jnp.where(lax.axis_index("col") == 0, product[:half], product[half:])
    mine = jnp.where(is_even(), product[:, :rank], product[:, rank:])
    out_ref[...] = dot_parts(mine, inverse, 1)


def finish(total_rows, term, got_term, gram, got_gram):
    return pl.pallas_call(
        functools.partial(finish_kernel, total_rows),
        out_shape=jax.ShapeDtypeStruct((term.shape[0] // 2, LANES // 2), F32),
        compiler_params=params(4),
        name="finish",
    )(term, got_term, gram, got_gram)


def per_device(snapshot, mode2_factor, old_factor):
    n_rows, n_cols = lax.axis_size("row"), lax.axis_size("col")
    masks = [1 << bit for bit in range(n_rows.bit_length() - 1)]
    total_rows = snapshot.shape[0] * n_rows

    def swap(x, mask):
        pairs = [
            (r * n_cols + c, (r ^ mask) * n_cols + (c + 1) % n_cols)
            for r in range(n_rows)
            for c in range(n_cols)
        ]
        return lax.ppermute(x, ("row", "col"), pairs)

    snapshot = pltpu.with_memory_space_constraint(snapshot, pltpu.HBM)
    mode2_t = pltpu.with_memory_space_constraint(mode2_factor.T, pltpu.HBM)
    send, kept, wide, order = contract_send(snapshot, mode2_t)
    got = swap(send, 0)
    own = contract_own(kept, snapshot, wide, order)

    keep, send, columns, give = project(own, got, old_factor.T)
    low, high = add_in_halves(keep, swap(send, masks[0]))
    got_columns = swap(give, masks[0])
    others = masks[1:]
    for step, (mask, turned) in enumerate(zip(others, others[1:] + others[:1])):
        after = [got_columns] if step == 1 else []
        got_low, got_high = swap(low, mask), swap(high, turned)
        low, high = add(low, got_low), add(high, got_high, *after)

    term = product_terms(columns, got_columns, low, high)
    term = add(term, swap(term, 0))
    got_term = swap(term, masks[0])
    gram = local_gram(term, got_term)
    for mask in masks[1:-1]:
        gram = add(gram, swap(gram, mask))
    return finish(total_rows, term, got_term, gram, swap(gram, masks[-1]))


def solution(mesh):
    return jax.shard_map(
        per_device,
        mesh=mesh,
        in_specs=(
            P(("groups", "row"), None, "col"),
            P(("groups", "col"), None),
            P(("groups", "row"), None),
        ),
        out_specs=P(("groups", "row", "col"), None),
        check_vma=False,
    )
```

```python
import functools

import jax
import jax.numpy as jnp
from jax import lax
from jax.experimental import pallas as pl
from jax.experimental.pallas import tpu as pltpu
from jax.sharding import PartitionSpec as P

F32 = jnp.float32
BF16 = jnp.bfloat16
LANES = 128
MIB = 2**20


def dot_f32(a, b, dims, precision=None):
    return lax.dot_general(a, b, (dims, ((), ())), precision=precision, preferred_element_type=F32)


def params(mib):
    return pltpu.CompilerParams(vmem_limit_bytes=mib * MIB)


def own_half():
    row = lax.axis_index("row")
    half = lax.axis_index("col")
    for bit in range(lax.axis_size("row").bit_length() - 1):
        half += lax.rem(lax.div(row, 1 << bit), 2)
    return lax.rem(half, 2)


TILE = 8


def fill_order(order_ref, half):
    block = TILE * half
    to = lax.broadcasted_iota(jnp.int32, order_ref.shape, 0)
    at = lax.broadcasted_iota(jnp.int32, order_ref.shape, 1)
    cell = lax.div(lax.rem(at, block), half)
    wanted = lax.div(to, TILE) * (order_ref.shape[1] // block) + lax.div(at, block)
    same = (lax.rem(to, TILE) == cell) & (wanted == lax.rem(at, half))
    order_ref[...] = same.astype(F32).astype(BF16)


def multiply(slab, wide_ref, flat_ref):
    cells, half, depth = slab.shape
    x = slab.reshape(cells * half, depth)
    low = dot_f32(x[:, :depth // 2], wide_ref[:, :depth // 2], ((1,), (1,)))
    high = dot_f32(x[:, depth // 2:], wide_ref[:, depth // 2:], ((1,), (1,)))
    flat_ref[...] = (low + high).astype(BF16)


def spread(half, flat_ref, order_ref, core_ref, start):
    block = TILE * half
    reps = order_ref.shape[1] // block
    step = flat_ref.shape[0] // half
    group = lax.div(lax.broadcasted_iota(jnp.int32, (block, LANES), 1), LANES // reps)
    spreads = []
    for b in range(step // TILE):
        flat = flat_ref[pl.ds(b * block, block), :].astype(F32)
        groups = [jnp.where(group == r, flat, 0.0).astype(BF16) for r in range(reps)]
        spreads.append(dot_f32(order_ref[...], jnp.concatenate(groups, axis=0), ((1,), (0,))))
    for p in range(half // reps):
        part = jnp.concatenate([x[p * TILE:(p + 1) * TILE] for x in spreads], axis=0)
        core_ref[pl.ds(start, step), p * LANES:(p + 1) * LANES] = part.astype(BF16)


STEP = 32


def slab_copies(snapshot_ref, first, slab_ref, half_index, sem):
    half = slab_ref.shape[1]
    fibers = pl.ds(pl.multiple_of(half_index * half, half), half)

    def copy(start, size):
        return pltpu.make_async_copy(
            snapshot_ref.at[pl.ds(start, size), fibers],
            slab_ref.at[pl.ds(start - first, size)],
            sem,
        )

    def start(begin, size, count):
        for part in range(count):
            copy(begin + part * (size // count), size // count).start()

    return start, lambda begin, size: copy(begin, size).wait()


def send_kernel(
    snapshot_ref, mode2_ref, core_ref, kept_ref, wide_ref, order_ref,
    slab_ref, small_ref, even_ref, odd_ref, sems, kept_sem, small_sem,
):
    cells, half, _ = slab_ref.shape
    rank = mode2_ref.shape[0]
    chunks = cells // STEP
    flat = (even_ref, odd_ref)
    sends = [
        slab_copies(snapshot_ref, 0, slab_ref, 1 - own_half(), sems.at[chunk])
        for chunk in range(chunks)
    ]
    start_kept, wait_kept = slab_copies(snapshot_ref, 0, kept_ref, own_half(), kept_sem)

    small = pltpu.make_async_copy(mode2_ref, small_ref, small_sem)
    small.start()
    for chunk in range(chunks):
        sends[chunk][0](chunk * STEP, STEP, 2 if chunk else 4)
    fill_order(order_ref, half)
    small.wait()
    wide_ref[...] = jnp.concatenate([small_ref[...]] * (LANES // rank), axis=0)
    for chunk in range(chunks):
        sends[chunk][1](chunk * STEP, STEP)
        if chunk == 0:
            start_kept(0, cells, 2 * chunks)
        multiply(slab_ref[pl.ds(chunk * STEP, STEP)], wide_ref, flat[chunk % 2])
        if chunk:
            spread(half, flat[(chunk - 1) % 2], order_ref, core_ref, (chunk - 1) * STEP)
    spread(half, flat[(chunks - 1) % 2], order_ref, core_ref, (chunks - 1) * STEP)
    wait_kept(0, cells)


def contract_send(snapshot, mode2_t):
    cells, fibers, depth = snapshot.shape
    rank = mode2_t.shape[0]
    half = fibers // 2
    reps = LANES // rank
    block = TILE * half
    pinned = pl.BlockSpec(memory_space=pltpu.HBM)
    return pl.pallas_call(
        send_kernel,
        in_specs=[pinned, pinned],
        out_shape=[
            jax.ShapeDtypeStruct((cells, half * rank), BF16),
            jax.ShapeDtypeStruct((cells, half, depth), BF16),
            jax.ShapeDtypeStruct((LANES, depth), BF16),
            jax.ShapeDtypeStruct((block // reps, block * reps), BF16),
        ],
        scratch_shapes=[
            pltpu.VMEM((cells, half, depth), BF16),
            pltpu.VMEM((rank, depth), BF16),
            pltpu.VMEM((STEP * half, LANES), BF16),
            pltpu.VMEM((STEP * half, LANES), BF16),
            pltpu.SemaphoreType.DMA((cells // STEP,)),
            pltpu.SemaphoreType.DMA,
            pltpu.SemaphoreType.DMA,
        ],
        compiler_params=params(24),
        name="contract_send",
    )(snapshot, mode2_t)


def own_kernel(slab_ref, wide_ref, order_ref, core_ref, even_ref, odd_ref):
    cells, half, _ = slab_ref.shape
    flat = (even_ref, odd_ref)
    chunks = cells // STEP
    for chunk in range(chunks):
        multiply(slab_ref[pl.ds(chunk * STEP, STEP)], wide_ref, flat[chunk % 2])
        if chunk:
            spread(half, flat[(chunk - 1) % 2], order_ref, core_ref, (chunk - 1) * STEP)
    spread(half, flat[(chunks - 1) % 2], order_ref, core_ref, (chunks - 1) * STEP)


def contract_own(slab, wide, order):
    cells, half, _ = slab.shape
    reps = order.shape[1] // (TILE * half)
    return pl.pallas_call(
        own_kernel,
        out_shape=jax.ShapeDtypeStruct((cells, half // reps * LANES), BF16),
        scratch_shapes=[pltpu.VMEM((STEP * half, LANES), BF16)] * 2,
        compiler_params=params(24),
        name="contract_own",
    )(slab, wide, order)


def is_even():
    return lax.rem(lax.axis_index("row"), 2) == 0


def project_kernel(own_ref, got_ref, factor_ref, keep_ref, send_ref, mine_ref, give_ref):
    rank = factor_ref.shape[0]
    width = mine_ref.shape[1]
    even = is_even()
    halves = []
    for start in (0, width):
        where = slice(start, start + width)
        halves.append(own_ref[:, where].astype(F32) + got_ref[:, where].astype(F32))
    mine = jnp.where(even, halves[0], halves[1]).astype(BF16)
    give = jnp.where(even, halves[1], halves[0]).astype(BF16)
    mine_ref[...] = mine
    give_ref[...] = give
    keep = dot_f32(factor_ref[...], mine, ((1,), (0,)))
    send = dot_f32(factor_ref[...], give, ((1,), (0,)))
    for block in range(width // LANES):
        where = slice(block * LANES, (block + 1) * LANES)
        rows = pl.ds(block * rank, rank)
        keep_ref[rows, :] = keep[:, where]
        send_ref[rows, :] = send[:, where].astype(BF16)


def project(own, got, factor_t):
    cells, width = own.shape
    rows = factor_t.shape[0] * width // LANES // 2
    columns = jax.ShapeDtypeStruct((cells, width // 2), BF16)
    return pl.pallas_call(
        project_kernel,
        out_shape=[
            jax.ShapeDtypeStruct((rows, LANES), F32),
            jax.ShapeDtypeStruct((rows, LANES), BF16),
            columns,
            columns,
        ],
        compiler_params=params(8),
        name="project",
    )(own, got, factor_t)


def add_kernel(mine_ref, got_ref, *refs):
    total = mine_ref[...].astype(F32) + got_ref[...].astype(F32)
    refs[-1][...] = total.astype(refs[-1].dtype)


def add(mine, got, *after):
    whole = pl.BlockSpec(memory_space=pltpu.VMEM)
    return pl.pallas_call(
        add_kernel,
        in_specs=[whole, whole] + [pl.BlockSpec(memory_space=pl.ANY)] * len(after),
        out_shape=jax.ShapeDtypeStruct(got.shape, got.dtype),
        compiler_params=params(4),
        name="add",
    )(mine, got, *after)


def halves_kernel(mine_ref, got_ref, low_ref, high_ref):
    size = low_ref.shape[0]
    for start, ref in ((0, low_ref), (size, high_ref)):
        rows = pl.ds(start, size)
        ref[...] = (mine_ref[rows, :] + got_ref[rows, :].astype(F32)).astype(BF16)


def add_in_halves(mine, got):
    out = jax.ShapeDtypeStruct((got.shape[0] // 2, LANES), BF16)
    return pl.pallas_call(
        halves_kernel,
        out_shape=[out, out],
        compiler_params=params(4),
        name="add_in_halves",
    )(mine, got)


def product_kernel(mine_ref, got_ref, low_ref, high_ref, out_ref):
    blocks = mine_ref.shape[1] // LANES // 2
    rank = low_ref.shape[0] // blocks
    projected = jnp.concatenate(
        [
            ref[pl.ds(block * rank, rank), :]
            for ref in (low_ref, high_ref)
            for block in range(blocks)
        ],
        axis=1,
    )
    terms = [dot_f32(ref[...], projected, ((1,), (1,))) for ref in (mine_ref, got_ref)]
    even = is_even()
    low = jnp.where(even, terms[0], terms[1])
    high = jnp.where(even, terms[1], terms[0])
    out_ref[...] = jnp.concatenate([low, high], axis=1).astype(BF16)


def product_terms(mine, got, low, high):
    return pl.pallas_call(
        product_kernel,
        out_shape=jax.ShapeDtypeStruct((mine.shape[0], LANES), BF16),
        compiler_params=params(4),
        name="product_terms",
    )(mine, got, low, high)


def pair_product(term_ref, got_ref):
    return term_ref[...].astype(F32) + got_ref[...].astype(F32)


def gram_kernel(term_ref, got_ref, out_ref):
    product = pair_product(term_ref, got_ref)
    rank = LANES // 2
    wide = dot_parts(product, product, 0)
    gram = wide[:rank, :rank] + wide[rank:, rank:]
    out_ref[...] = jnp.concatenate([gram[:rank // 2], gram[rank // 2:]], axis=1)


def local_gram(term, got):
    return pl.pallas_call(
        gram_kernel,
        out_shape=jax.ShapeDtypeStruct((LANES // 4, LANES), F32),
        compiler_params=params(4),
        name="local_gram",
    )(term, got)


def parts(x):
    high = x.astype(BF16)
    return high, (x - high.astype(F32)).astype(BF16)


def dot_parts(a, b, axis):
    (ah, al), (bh, bl) = parts(a), parts(b)
    left = jnp.concatenate([ah, ah, al], axis=axis)
    right = jnp.concatenate([bh, bl, bh], axis=axis)
    return dot_f32(left, right, ((axis,), (axis,)))


def eliminate(gram):
    rank = gram.shape[0]
    tile = 8
    count = rank // tile
    wide = 2 * rank
    sublane = lax.broadcasted_iota(jnp.int32, (tile, wide), 0)
    lane = lax.broadcasted_iota(jnp.int32, (tile, wide), 1)
    full = lambda x: jnp.broadcast_to(x, (tile, wide))
    both = []
    for v in range(count):
        mine = gram[v * tile:(v + 1) * tile]
        both.append(jnp.where(lane < rank, jnp.concatenate([mine, mine], axis=1),
                              (lane - rank == sublane + v * tile).astype(F32)))
    pivots = []
    for p in range(count):
        cols = [
            {v: full(both[v][:, p * tile + j:p * tile + j + 1]) for v in range(p, count)}
            for j in range(tile)
        ]
        rows = [full(both[p][j:j + 1]) for j in range(tile)]
        block = [[full(cols[k][p][j:j + 1]) for k in range(j + 1)] for j in range(tile)]
        found, kept = block[0][0], rows[0]
        for j in range(tile):
            if j:
                found = jnp.where(sublane == j, block[j][j], found)
                kept = jnp.where(sublane == j, rows[j], kept)
            inverse = pl.reciprocal(block[j][j], approx=True, full_range=False)
            scaled = {i: block[i][j] * inverse for i in range(j + 1, tile)}
            for i, factor in scaled.items():
                for k in range(j + 1, i + 1):
                    block[i][k] = block[i][k] - factor * block[k][j]
                rows[i] = rows[i] - factor * rows[j]
            row = rows[j] * inverse
            for v in range(p + 1, count):
                for i, factor in scaled.items():
                    cols[i][v] = cols[i][v] - factor * cols[j][v]
                both[v] = both[v] - cols[j][v] * row
        both[p] = kept
        pivots.append(found)
    return both, pivots


def finish_kernel(total_rows, term_ref, got_term_ref, gram_ref, got_gram_ref, out_ref):
    rank = LANES // 2
    packed = gram_ref[...] + got_gram_ref[...]
    gram = jnp.concatenate([packed[:, :rank], packed[:, rank:]], axis=0)
    both, pivots = eliminate(gram)
    scale = total_rows ** 0.5
    inverse = jnp.concatenate([b * (lax.rsqrt(p) * scale) for b, p in zip(both, pivots)], axis=0)
    inverse = inverse[:, rank:]
    half = term_ref.shape[0] // 2
    product = pair_product(term_ref, got_term_ref)
    product = jnp.where(lax.axis_index("col") == 0, product[:half], product[half:])
    mine = jnp.where(is_even(), product[:, :rank], product[:, rank:])
    out_ref[...] = dot_parts(mine, inverse, 1)


def finish(total_rows, term, got_term, gram, got_gram):
    return pl.pallas_call(
        functools.partial(finish_kernel, total_rows),
        out_shape=jax.ShapeDtypeStruct((term.shape[0] // 2, LANES // 2), F32),
        compiler_params=params(4),
        name="finish",
    )(term, got_term, gram, got_gram)


def per_device(snapshot, mode2_factor, old_factor):
    n_rows, n_cols = lax.axis_size("row"), lax.axis_size("col")
    masks = [1 << bit for bit in range(n_rows.bit_length() - 1)]
    total_rows = snapshot.shape[0] * n_rows

    def swap(x, mask):
        pairs = [
            (r * n_cols + c, (r ^ mask) * n_cols + (c + 1) % n_cols)
            for r in range(n_rows)
            for c in range(n_cols)
        ]
        return lax.ppermute(x, ("row", "col"), pairs)

    snapshot = pltpu.with_memory_space_constraint(snapshot, pltpu.HBM)
    mode2_t = pltpu.with_memory_space_constraint(mode2_factor.T, pltpu.HBM)
    send, kept, wide, order = contract_send(snapshot, mode2_t)
    got = swap(send, 0)
    own = contract_own(kept, wide, order)

    keep, send, columns, give = project(own, got, old_factor.T)
    low, high = add_in_halves(keep, swap(send, masks[0]))
    got_columns = swap(give, masks[0])
    others = masks[1:]
    for step, (mask, turned) in enumerate(zip(others, others[1:] + others[:1])):
        after = [got_columns] if step == 1 else []
        got_low, got_high = swap(low, mask), swap(high, turned)
        low, high = add(low, got_low), add(high, got_high, *after)

    term = product_terms(columns, got_columns, low, high)
    term = add(term, swap(term, 0))
    got_term = swap(term, masks[0])
    gram = local_gram(term, got_term)
    for mask in masks[1:-1]:
        gram = add(gram, swap(gram, mask))
    return finish(total_rows, term, got_term, gram, swap(gram, masks[-1]))


def solution(mesh):
    return jax.shard_map(
        per_device,
        mesh=mesh,
        in_specs=(
            P(("groups", "row"), None, "col"),
            P(("groups", "col"), None),
            P(("groups", "row"), None),
        ),
        out_specs=P(("groups", "row", "col"), None),
        check_vma=False,
    )
```

```python
import functools

import jax
import jax.numpy as jnp
from jax import lax
from jax.experimental import pallas as pl
from jax.experimental.pallas import tpu as pltpu
from jax.sharding import PartitionSpec as P

F32 = jnp.float32
BF16 = jnp.bfloat16
LANES = 128
MIB = 2**20


def dot_f32(a, b, dims, precision=None):
    return lax.dot_general(a, b, (dims, ((), ())), precision=precision, preferred_element_type=F32)


def params(mib):
    return pltpu.CompilerParams(vmem_limit_bytes=mib * MIB)


def own_half():
    row = lax.axis_index("row")
    half = lax.axis_index("col")
    for bit in range(lax.axis_size("row").bit_length() - 1):
        half += lax.rem(lax.div(row, 1 << bit), 2)
    return lax.rem(half, 2)


TILE = 8


def fill_order(order_ref, half):
    block = TILE * half
    to = lax.broadcasted_iota(jnp.int32, order_ref.shape, 0)
    at = lax.broadcasted_iota(jnp.int32, order_ref.shape, 1)
    cell = lax.div(lax.rem(at, block), half)
    wanted = lax.div(to, TILE) * (order_ref.shape[1] // block) + lax.div(at, block)
    same = (lax.rem(to, TILE) == cell) & (wanted == lax.rem(at, half))
    order_ref[...] = same.astype(F32).astype(BF16)


def multiply(slab, wide_ref, flat_ref):
    cells, half, depth = slab.shape
    x = slab.reshape(cells * half, depth)
    low = dot_f32(x[:, :depth // 2], wide_ref[:, :depth // 2], ((1,), (1,)))
    high = dot_f32(x[:, depth // 2:], wide_ref[:, depth // 2:], ((1,), (1,)))
    flat_ref[...] = (low + high).astype(BF16)


def spread(half, flat_ref, order_ref, core_ref, start):
    block = TILE * half
    reps = order_ref.shape[1] // block
    step = flat_ref.shape[0] // half
    group = lax.div(lax.broadcasted_iota(jnp.int32, (block, LANES), 1), LANES // reps)
    spreads = []
    for b in range(step // TILE):
        flat = flat_ref[pl.ds(b * block, block), :].astype(F32)
        groups = [jnp.where(group == r, flat, 0.0).astype(BF16) for r in range(reps)]
        spreads.append(dot_f32(order_ref[...], jnp.concatenate(groups, axis=0), ((1,), (0,))))
    for p in range(half // reps):
        part = jnp.concatenate([x[p * TILE:(p + 1) * TILE] for x in spreads], axis=0)
        core_ref[pl.ds(start, step), p * LANES:(p + 1) * LANES] = part.astype(BF16)


STEP = 32


def slab_copies(snapshot_ref, first, slab_ref, half_index, sem):
    half = slab_ref.shape[1]
    fibers = pl.ds(pl.multiple_of(half_index * half, half), half)

    def copy(start, size):
        return pltpu.make_async_copy(
            snapshot_ref.at[pl.ds(start, size), fibers],
            slab_ref.at[pl.ds(start - first, size)],
            sem,
        )

    def start(begin, size, count):
        for part in range(count):
            copy(begin + part * (size // count), size // count).start()

    return start, lambda begin, size: copy(begin, size).wait()


def send_kernel(
    snapshot_ref, mode2_ref, core_ref, wide_ref, order_ref,
    slab_ref, small_ref, even_ref, odd_ref, sems, small_sem,
):
    cells, half, _ = slab_ref.shape
    rank = mode2_ref.shape[0]
    chunks = cells // STEP
    flat = (even_ref, odd_ref)
    sends = [
        slab_copies(snapshot_ref, 0, slab_ref, 1 - own_half(), sems.at[chunk])
        for chunk in range(chunks)
    ]

    small = pltpu.make_async_copy(mode2_ref, small_ref, small_sem)
    small.start()
    for chunk in range(chunks):
        sends[chunk][0](chunk * STEP, STEP, 2 if chunk else 4)
    fill_order(order_ref, half)
    small.wait()
    wide_ref[...] = jnp.concatenate([small_ref[...]] * (LANES // rank), axis=0)
    for chunk in range(chunks):
        sends[chunk][1](chunk * STEP, STEP)
        multiply(slab_ref[pl.ds(chunk * STEP, STEP)], wide_ref, flat[chunk % 2])
        if chunk:
            spread(half, flat[(chunk - 1) % 2], order_ref, core_ref, (chunk - 1) * STEP)
    spread(half, flat[(chunks - 1) % 2], order_ref, core_ref, (chunks - 1) * STEP)


def contract_send(snapshot, mode2_t):
    cells, fibers, depth = snapshot.shape
    rank = mode2_t.shape[0]
    half = fibers // 2
    reps = LANES // rank
    block = TILE * half
    pinned = pl.BlockSpec(memory_space=pltpu.HBM)
    return pl.pallas_call(
        send_kernel,
        in_specs=[pinned, pinned],
        out_shape=[
            jax.ShapeDtypeStruct((cells, half * rank), BF16),
            jax.ShapeDtypeStruct((LANES, depth), BF16),
            jax.ShapeDtypeStruct((block // reps, block * reps), BF16),
        ],
        scratch_shapes=[
            pltpu.VMEM((cells, half, depth), BF16),
            pltpu.VMEM((rank, depth), BF16),
            pltpu.VMEM((STEP * half, LANES), BF16),
            pltpu.VMEM((STEP * half, LANES), BF16),
            pltpu.SemaphoreType.DMA((cells // STEP,)),
            pltpu.SemaphoreType.DMA,
        ],
        compiler_params=params(24),
        name="contract_send",
    )(snapshot, mode2_t)


def own_kernel(slab_ref, wide_ref, order_ref, core_ref, even_ref, odd_ref):
    cells, fibers, _ = slab_ref.shape
    half = fibers // 2
    kept = pl.ds(pl.multiple_of(own_half() * half, half), half)
    flat = (even_ref, odd_ref)
    chunks = cells // STEP
    for chunk in range(chunks):
        multiply(slab_ref[pl.ds(chunk * STEP, STEP), kept], wide_ref, flat[chunk % 2])
        if chunk:
            spread(half, flat[(chunk - 1) % 2], order_ref, core_ref, (chunk - 1) * STEP)
    spread(half, flat[(chunks - 1) % 2], order_ref, core_ref, (chunks - 1) * STEP)


def contract_own(slab, wide, order):
    cells, fibers, _ = slab.shape
    half = fibers // 2
    reps = order.shape[1] // (TILE * half)
    return pl.pallas_call(
        own_kernel,
        out_shape=jax.ShapeDtypeStruct((cells, half // reps * LANES), BF16),
        scratch_shapes=[pltpu.VMEM((STEP * half, LANES), BF16)] * 2,
        compiler_params=params(24),
        name="contract_own",
    )(slab, wide, order)


def is_even():
    return lax.rem(lax.axis_index("row"), 2) == 0


def project_kernel(own_ref, got_ref, factor_ref, keep_ref, send_ref, mine_ref, give_ref):
    rank = factor_ref.shape[0]
    width = mine_ref.shape[1]
    even = is_even()
    halves = []
    for start in (0, width):
        where = slice(start, start + width)
        halves.append(own_ref[:, where].astype(F32) + got_ref[:, where].astype(F32))
    mine = jnp.where(even, halves[0], halves[1]).astype(BF16)
    give = jnp.where(even, halves[1], halves[0]).astype(BF16)
    mine_ref[...] = mine
    give_ref[...] = give
    keep = dot_f32(factor_ref[...], mine, ((1,), (0,)))
    send = dot_f32(factor_ref[...], give, ((1,), (0,)))
    for block in range(width // LANES):
        where = slice(block * LANES, (block + 1) * LANES)
        rows = pl.ds(block * rank, rank)
        keep_ref[rows, :] = keep[:, where]
        send_ref[rows, :] = send[:, where].astype(BF16)


def project(own, got, factor_t):
    cells, width = own.shape
    rows = factor_t.shape[0] * width // LANES // 2
    columns = jax.ShapeDtypeStruct((cells, width // 2), BF16)
    return pl.pallas_call(
        project_kernel,
        out_shape=[
            jax.ShapeDtypeStruct((rows, LANES), F32),
            jax.ShapeDtypeStruct((rows, LANES), BF16),
            columns,
            columns,
        ],
        compiler_params=params(8),
        name="project",
    )(own, got, factor_t)


def add_kernel(mine_ref, got_ref, *refs):
    total = mine_ref[...].astype(F32) + got_ref[...].astype(F32)
    refs[-1][...] = total.astype(refs[-1].dtype)


def add(mine, got, *after):
    whole = pl.BlockSpec(memory_space=pltpu.VMEM)
    return pl.pallas_call(
        add_kernel,
        in_specs=[whole, whole] + [pl.BlockSpec(memory_space=pl.ANY)] * len(after),
        out_shape=jax.ShapeDtypeStruct(got.shape, got.dtype),
        compiler_params=params(4),
        name="add",
    )(mine, got, *after)


def halves_kernel(mine_ref, got_ref, low_ref, high_ref):
    size = low_ref.shape[0]
    for start, ref in ((0, low_ref), (size, high_ref)):
        rows = pl.ds(start, size)
        ref[...] = (mine_ref[rows, :] + got_ref[rows, :].astype(F32)).astype(BF16)


def add_in_halves(mine, got):
    out = jax.ShapeDtypeStruct((got.shape[0] // 2, LANES), BF16)
    return pl.pallas_call(
        halves_kernel,
        out_shape=[out, out],
        compiler_params=params(4),
        name="add_in_halves",
    )(mine, got)


def product_kernel(mine_ref, got_ref, low_ref, high_ref, out_ref):
    blocks = mine_ref.shape[1] // LANES // 2
    rank = low_ref.shape[0] // blocks
    projected = jnp.concatenate(
        [
            ref[pl.ds(block * rank, rank), :]
            for ref in (low_ref, high_ref)
            for block in range(blocks)
        ],
        axis=1,
    )
    terms = [dot_f32(ref[...], projected, ((1,), (1,))) for ref in (mine_ref, got_ref)]
    even = is_even()
    low = jnp.where(even, terms[0], terms[1])
    high = jnp.where(even, terms[1], terms[0])
    out_ref[...] = jnp.concatenate([low, high], axis=1).astype(BF16)


def product_terms(mine, got, low, high):
    return pl.pallas_call(
        product_kernel,
        out_shape=jax.ShapeDtypeStruct((mine.shape[0], LANES), BF16),
        compiler_params=params(4),
        name="product_terms",
    )(mine, got, low, high)


def pair_product(term_ref, got_ref):
    return term_ref[...].astype(F32) + got_ref[...].astype(F32)


def gram_kernel(term_ref, got_ref, out_ref):
    product = pair_product(term_ref, got_ref)
    rank = LANES // 2
    wide = dot_parts(product, product, 0)
    gram = wide[:rank, :rank] + wide[rank:, rank:]
    out_ref[...] = jnp.concatenate([gram[:rank // 2], gram[rank // 2:]], axis=1)


def local_gram(term, got):
    return pl.pallas_call(
        gram_kernel,
        out_shape=jax.ShapeDtypeStruct((LANES // 4, LANES), F32),
        compiler_params=params(4),
        name="local_gram",
    )(term, got)


def parts(x):
    high = x.astype(BF16)
    return high, (x - high.astype(F32)).astype(BF16)


def dot_parts(a, b, axis):
    (ah, al), (bh, bl) = parts(a), parts(b)
    left = jnp.concatenate([ah, ah, al], axis=axis)
    right = jnp.concatenate([bh, bl, bh], axis=axis)
    return dot_f32(left, right, ((axis,), (axis,)))


def eliminate(gram):
    rank = gram.shape[0]
    tile = 8
    count = rank // tile
    wide = 2 * rank
    sublane = lax.broadcasted_iota(jnp.int32, (tile, wide), 0)
    lane = lax.broadcasted_iota(jnp.int32, (tile, wide), 1)
    full = lambda x: jnp.broadcast_to(x, (tile, wide))
    both = []
    for v in range(count):
        mine = gram[v * tile:(v + 1) * tile]
        both.append(jnp.where(lane < rank, jnp.concatenate([mine, mine], axis=1),
                              (lane - rank == sublane + v * tile).astype(F32)))
    pivots = []
    for p in range(count):
        cols = [
            {v: full(both[v][:, p * tile + j:p * tile + j + 1]) for v in range(p, count)}
            for j in range(tile)
        ]
        rows = [full(both[p][j:j + 1]) for j in range(tile)]
        block = [[full(cols[k][p][j:j + 1]) for k in range(j + 1)] for j in range(tile)]
        found, kept = block[0][0], rows[0]
        for j in range(tile):
            if j:
                found = jnp.where(sublane == j, block[j][j], found)
                kept = jnp.where(sublane == j, rows[j], kept)
            inverse = pl.reciprocal(block[j][j], approx=True, full_range=False)
            scaled = {i: block[i][j] * inverse for i in range(j + 1, tile)}
            for i, factor in scaled.items():
                for k in range(j + 1, i + 1):
                    block[i][k] = block[i][k] - factor * block[k][j]
                rows[i] = rows[i] - factor * rows[j]
            row = rows[j] * inverse
            for v in range(p + 1, count):
                for i, factor in scaled.items():
                    cols[i][v] = cols[i][v] - factor * cols[j][v]
                both[v] = both[v] - cols[j][v] * row
        both[p] = kept
        pivots.append(found)
    return both, pivots


def finish_kernel(total_rows, term_ref, got_term_ref, gram_ref, got_gram_ref, out_ref):
    rank = LANES // 2
    packed = gram_ref[...] + got_gram_ref[...]
    gram = jnp.concatenate([packed[:, :rank], packed[:, rank:]], axis=0)
    both, pivots = eliminate(gram)
    scale = total_rows ** 0.5
    inverse = jnp.concatenate([b * (lax.rsqrt(p) * scale) for b, p in zip(both, pivots)], axis=0)
    inverse = inverse[:, rank:]
    half = term_ref.shape[0] // 2
    product = pair_product(term_ref, got_term_ref)
    product = jnp.where(lax.axis_index("col") == 0, product[:half], product[half:])
    mine = jnp.where(is_even(), product[:, :rank], product[:, rank:])
    out_ref[...] = dot_parts(mine, inverse, 1)


def finish(total_rows, term, got_term, gram, got_gram):
    return pl.pallas_call(
        functools.partial(finish_kernel, total_rows),
        out_shape=jax.ShapeDtypeStruct((term.shape[0] // 2, LANES // 2), F32),
        compiler_params=params(4),
        name="finish",
    )(term, got_term, gram, got_gram)


def per_device(snapshot, mode2_factor, old_factor):
    n_rows, n_cols = lax.axis_size("row"), lax.axis_size("col")
    masks = [1 << bit for bit in range(n_rows.bit_length() - 1)]
    total_rows = snapshot.shape[0] * n_rows

    def swap(x, mask):
        pairs = [
            (r * n_cols + c, (r ^ mask) * n_cols + (c + 1) % n_cols)
            for r in range(n_rows)
            for c in range(n_cols)
        ]
        return lax.ppermute(x, ("row", "col"), pairs)

    pinned = pltpu.with_memory_space_constraint(snapshot, pltpu.HBM)
    mode2_t = pltpu.with_memory_space_constraint(mode2_factor.T, pltpu.HBM)
    send, wide, order = contract_send(pinned, mode2_t)
    got = swap(send, 0)
    own = contract_own(snapshot, wide, order)

    keep, send, columns, give = project(own, got, old_factor.T)
    low, high = add_in_halves(keep, swap(send, masks[0]))
    got_columns = swap(give, masks[0])
    others = masks[1:]
    for step, (mask, turned) in enumerate(zip(others, others[1:] + others[:1])):
        after = [got_columns] if step == 1 else []
        got_low, got_high = swap(low, mask), swap(high, turned)
        low, high = add(low, got_low), add(high, got_high, *after)

    term = product_terms(columns, got_columns, low, high)
    term = add(term, swap(term, 0))
    got_term = swap(term, masks[0])
    gram = local_gram(term, got_term)
    for mask in masks[1:-1]:
        gram = add(gram, swap(gram, mask))
    return finish(total_rows, term, got_term, gram, swap(gram, masks[-1]))


def solution(mesh):
    return jax.shard_map(
        per_device,
        mesh=mesh,
        in_specs=(
            P(("groups", "row"), None, "col"),
            P(("groups", "col"), None),
            P(("groups", "row"), None),
        ),
        out_specs=P(("groups", "row", "col"), None),
        check_vma=False,
    )
```

```python
import functools

import jax
import jax.numpy as jnp
from jax import lax
from jax.experimental import pallas as pl
from jax.experimental.pallas import tpu as pltpu
from jax.sharding import PartitionSpec as P

F32 = jnp.float32
BF16 = jnp.bfloat16
LANES = 128
MIB = 2**20


def dot_f32(a, b, dims, precision=None):
    return lax.dot_general(a, b, (dims, ((), ())), precision=precision, preferred_element_type=F32)


def params(mib):
    return pltpu.CompilerParams(vmem_limit_bytes=mib * MIB)


def own_half():
    row = lax.axis_index("row")
    half = lax.axis_index("col")
    for bit in range(lax.axis_size("row").bit_length() - 1):
        half += lax.rem(lax.div(row, 1 << bit), 2)
    return lax.rem(half, 2)


TILE = 8


def fill_order(order_ref, half):
    block = TILE * half
    to = lax.broadcasted_iota(jnp.int32, order_ref.shape, 0)
    at = lax.broadcasted_iota(jnp.int32, order_ref.shape, 1)
    cell = lax.div(lax.rem(at, block), half)
    wanted = lax.div(to, TILE) * (order_ref.shape[1] // block) + lax.div(at, block)
    same = (lax.rem(to, TILE) == cell) & (wanted == lax.rem(at, half))
    order_ref[...] = same.astype(F32).astype(BF16)


def multiply(slab, wide_ref, flat_ref):
    cells, half, depth = slab.shape
    x = slab.reshape(cells * half, depth)
    low = dot_f32(x[:, :depth // 2], wide_ref[:, :depth // 2], ((1,), (1,)))
    high = dot_f32(x[:, depth // 2:], wide_ref[:, depth // 2:], ((1,), (1,)))
    flat_ref[...] = (low + high).astype(BF16)


def spread(half, flat_ref, order_ref, core_ref, start):
    block = TILE * half
    reps = order_ref.shape[1] // block
    step = flat_ref.shape[0] // half
    group = lax.div(lax.broadcasted_iota(jnp.int32, (block, LANES), 1), LANES // reps)
    spreads = []
    for b in range(step // TILE):
        flat = flat_ref[pl.ds(b * block, block), :].astype(F32)
        groups = [jnp.where(group == r, flat, 0.0).astype(BF16) for r in range(reps)]
        spreads.append(dot_f32(order_ref[...], jnp.concatenate(groups, axis=0), ((1,), (0,))))
    for p in range(half // reps):
        part = jnp.concatenate([x[p * TILE:(p + 1) * TILE] for x in spreads], axis=0)
        core_ref[pl.ds(start, step), p * LANES:(p + 1) * LANES] = part.astype(BF16)


STEP = 32


def slab_copies(snapshot_ref, first, slab_ref, half_index, sem):
    half = slab_ref.shape[1]
    fibers = pl.ds(pl.multiple_of(half_index * half, half), half)

    def copy(start, size):
        return pltpu.make_async_copy(
            snapshot_ref.at[pl.ds(start, size), fibers],
            slab_ref.at[pl.ds(start - first, size)],
            sem,
        )

    def start(begin, size, count):
        for part in range(count):
            copy(begin + part * (size // count), size // count).start()

    return start, lambda begin, size: copy(begin, size).wait()


def send_kernel(
    snapshot_ref, mode2_ref, core_ref, kept_ref, wide_ref, order_ref,
    slab_ref, small_ref, even_ref, odd_ref, sems, kept_sem, small_sem,
):
    cells, half, _ = slab_ref.shape
    rank = mode2_ref.shape[0]
    chunks = cells // STEP
    flat = (even_ref, odd_ref)
    sends = [
        slab_copies(snapshot_ref, 0, slab_ref, 1 - own_half(), sems.at[chunk])
        for chunk in range(chunks)
    ]
    start_kept, wait_kept = slab_copies(snapshot_ref, 0, kept_ref, own_half(), kept_sem)

    small = pltpu.make_async_copy(mode2_ref, small_ref, small_sem)
    small.start()
    for chunk in range(chunks):
        sends[chunk][0](chunk * STEP, STEP, 2 if chunk else 4)
    fill_order(order_ref, half)
    small.wait()
    wide_ref[...] = jnp.concatenate([small_ref[...]] * (LANES // rank), axis=0)
    for chunk in range(chunks):
        sends[chunk][1](chunk * STEP, STEP)
        if chunk == 0:
            start_kept(0, cells, 2 * chunks)
        multiply(slab_ref[pl.ds(chunk * STEP, STEP)], wide_ref, flat[chunk % 2])
        if chunk:
            spread(half, flat[(chunk - 1) % 2], order_ref, core_ref, (chunk - 1) * STEP)
    spread(half, flat[(chunks - 1) % 2], order_ref, core_ref, (chunks - 1) * STEP)
    wait_kept(0, cells)


def contract_send(snapshot, mode2_t):
    cells, fibers, depth = snapshot.shape
    rank = mode2_t.shape[0]
    half = fibers // 2
    reps = LANES // rank
    block = TILE * half
    pinned = pl.BlockSpec(memory_space=pltpu.HBM)
    return pl.pallas_call(
        send_kernel,
        in_specs=[pinned, pinned],
        out_shape=[
            jax.ShapeDtypeStruct((cells, half * rank), BF16),
            jax.ShapeDtypeStruct((cells, half, depth), BF16),
            jax.ShapeDtypeStruct((LANES, depth), BF16),
            jax.ShapeDtypeStruct((block // reps, block * reps), BF16),
        ],
        scratch_shapes=[
            pltpu.VMEM((cells, half, depth), BF16),
            pltpu.VMEM((rank, depth), BF16),
            pltpu.VMEM((STEP * half, LANES), BF16),
            pltpu.VMEM((STEP * half, LANES), BF16),
            pltpu.SemaphoreType.DMA((cells // STEP,)),
            pltpu.SemaphoreType.DMA,
            pltpu.SemaphoreType.DMA,
        ],
        compiler_params=params(24),
        name="contract_send",
    )(snapshot, mode2_t)


def own_kernel(slab_ref, wide_ref, order_ref, core_ref, even_ref, odd_ref):
    cells, half, _ = slab_ref.shape
    flat = (even_ref, odd_ref)
    chunks = cells // STEP
    for chunk in range(chunks):
        multiply(slab_ref[pl.ds(chunk * STEP, STEP)], wide_ref, flat[chunk % 2])
        if chunk:
            spread(half, flat[(chunk - 1) % 2], order_ref, core_ref, (chunk - 1) * STEP)
    spread(half, flat[(chunks - 1) % 2], order_ref, core_ref, (chunks - 1) * STEP)


def contract_own(slab, wide, order):
    cells, half, _ = slab.shape
    reps = order.shape[1] // (TILE * half)
    return pl.pallas_call(
        own_kernel,
        out_shape=jax.ShapeDtypeStruct((cells, half // reps * LANES), BF16),
        scratch_shapes=[pltpu.VMEM((STEP * half, LANES), BF16)] * 2,
        compiler_params=params(24),
        name="contract_own",
    )(slab, wide, order)


def is_even():
    return lax.rem(lax.axis_index("row"), 2) == 0


def project_kernel(own_ref, got_ref, factor_ref, keep_ref, send_ref, mine_ref, give_ref):
    rank = factor_ref.shape[0]
    width = mine_ref.shape[1]
    even = is_even()
    halves = []
    for start in (0, width):
        where = slice(start, start + width)
        halves.append(own_ref[:, where].astype(F32) + got_ref[:, where].astype(F32))
    mine = jnp.where(even, halves[0], halves[1]).astype(BF16)
    give = jnp.where(even, halves[1], halves[0]).astype(BF16)
    mine_ref[...] = mine
    give_ref[...] = give
    keep = dot_f32(factor_ref[...], mine, ((1,), (0,)))
    send = dot_f32(factor_ref[...], give, ((1,), (0,)))
    for block in range(width // LANES):
        where = slice(block * LANES, (block + 1) * LANES)
        rows = pl.ds(block * rank, rank)
        keep_ref[rows, :] = keep[:, where]
        send_ref[rows, :] = send[:, where].astype(BF16)


def project(own, got, factor_t):
    cells, width = own.shape
    rows = factor_t.shape[0] * width // LANES // 2
    columns = jax.ShapeDtypeStruct((cells, width // 2), BF16)
    return pl.pallas_call(
        project_kernel,
        out_shape=[
            jax.ShapeDtypeStruct((rows, LANES), F32),
            jax.ShapeDtypeStruct((rows, LANES), BF16),
            columns,
            columns,
        ],
        compiler_params=params(8),
        name="project",
    )(own, got, factor_t)


def add_kernel(mine_ref, got_ref, *refs):
    total = mine_ref[...].astype(F32) + got_ref[...].astype(F32)
    refs[-1][...] = total.astype(refs[-1].dtype)


def add(mine, got, *after):
    whole = pl.BlockSpec(memory_space=pltpu.VMEM)
    return pl.pallas_call(
        add_kernel,
        in_specs=[whole, whole] + [pl.BlockSpec(memory_space=pl.ANY)] * len(after),
        out_shape=jax.ShapeDtypeStruct(got.shape, got.dtype),
        compiler_params=params(4),
        name="add",
    )(mine, got, *after)


def halves_kernel(mine_ref, got_ref, low_ref, high_ref):
    size = low_ref.shape[0]
    for start, ref in ((0, low_ref), (size, high_ref)):
        rows = pl.ds(start, size)
        ref[...] = (mine_ref[rows, :] + got_ref[rows, :].astype(F32)).astype(BF16)


def add_in_halves(mine, got):
    out = jax.ShapeDtypeStruct((got.shape[0] // 2, LANES), BF16)
    return pl.pallas_call(
        halves_kernel,
        out_shape=[out, out],
        compiler_params=params(4),
        name="add_in_halves",
    )(mine, got)


def product_kernel(mine_ref, got_ref, low_ref, high_ref, out_ref):
    blocks = mine_ref.shape[1] // LANES // 2
    rank = low_ref.shape[0] // blocks
    projected = jnp.concatenate(
        [
            ref[pl.ds(block * rank, rank), :]
            for ref in (low_ref, high_ref)
            for block in range(blocks)
        ],
        axis=1,
    )
    terms = [dot_f32(ref[...], projected, ((1,), (1,))) for ref in (mine_ref, got_ref)]
    even = is_even()
    low = jnp.where(even, terms[0], terms[1])
    high = jnp.where(even, terms[1], terms[0])
    out_ref[...] = jnp.concatenate([low, high], axis=1).astype(BF16)


def product_terms(mine, got, low, high):
    return pl.pallas_call(
        product_kernel,
        out_shape=jax.ShapeDtypeStruct((mine.shape[0], LANES), BF16),
        compiler_params=params(4),
        name="product_terms",
    )(mine, got, low, high)


def pair_product(term_ref, got_ref):
    return term_ref[...].astype(F32) + got_ref[...].astype(F32)


def gram_kernel(*refs):
    out_ref = refs[-1]
    rank = LANES // 2
    product = jnp.concatenate(
        [pair_product(refs[k], refs[k + 1]) for k in range(0, len(refs) - 1, 2)], axis=0
    )
    wide = dot_parts(product, product, 0)
    gram = wide[:rank, :rank] + wide[rank:, rank:]
    out_ref[...] = jnp.concatenate([gram[:rank // 2], gram[rank // 2:]], axis=1)


def local_gram(*terms):
    return pl.pallas_call(
        gram_kernel,
        out_shape=jax.ShapeDtypeStruct((LANES // 4, LANES), F32),
        compiler_params=params(4),
        name="local_gram",
    )(*terms)


def parts(x):
    high = x.astype(BF16)
    return high, (x - high.astype(F32)).astype(BF16)


def dot_parts(a, b, axis):
    (ah, al), (bh, bl) = parts(a), parts(b)
    left = jnp.concatenate([ah, ah, al], axis=axis)
    right = jnp.concatenate([bh, bl, bh], axis=axis)
    return dot_f32(left, right, ((axis,), (axis,)))


def eliminate(gram):
    rank = gram.shape[0]
    tile = 8
    count = rank // tile
    wide = 2 * rank
    sublane = lax.broadcasted_iota(jnp.int32, (tile, wide), 0)
    lane = lax.broadcasted_iota(jnp.int32, (tile, wide), 1)
    full = lambda x: jnp.broadcast_to(x, (tile, wide))
    both = []
    for v in range(count):
        mine = gram[v * tile:(v + 1) * tile]
        both.append(jnp.where(lane < rank, jnp.concatenate([mine, mine], axis=1),
                              (lane - rank == sublane + v * tile).astype(F32)))
    pivots = []
    for p in range(count):
        cols = [
            {v: full(both[v][:, p * tile + j:p * tile + j + 1]) for v in range(p, count)}
            for j in range(tile)
        ]
        rows = [full(both[p][j:j + 1]) for j in range(tile)]
        block = [[full(cols[k][p][j:j + 1]) for k in range(j + 1)] for j in range(tile)]
        found, kept = block[0][0], rows[0]
        for j in range(tile):
            if j:
                found = jnp.where(sublane == j, block[j][j], found)
                kept = jnp.where(sublane == j, rows[j], kept)
            inverse = pl.reciprocal(block[j][j], approx=True, full_range=False)
            scaled = {i: block[i][j] * inverse for i in range(j + 1, tile)}
            for i, factor in scaled.items():
                for k in range(j + 1, i + 1):
                    block[i][k] = block[i][k] - factor * block[k][j]
                rows[i] = rows[i] - factor * rows[j]
            row = rows[j] * inverse
            for v in range(p + 1, count):
                for i, factor in scaled.items():
                    cols[i][v] = cols[i][v] - factor * cols[j][v]
                both[v] = both[v] - cols[j][v] * row
        both[p] = kept
        pivots.append(found)
    return both, pivots


def finish_kernel(total_rows, term_ref, got_term_ref, gram_ref, got_gram_ref, out_ref):
    rank = LANES // 2
    packed = gram_ref[...] + got_gram_ref[...]
    gram = jnp.concatenate([packed[:, :rank], packed[:, rank:]], axis=0)
    both, pivots = eliminate(gram)
    scale = total_rows ** 0.5
    inverse = jnp.concatenate([b * (lax.rsqrt(p) * scale) for b, p in zip(both, pivots)], axis=0)
    inverse = inverse[:, rank:]
    half = term_ref.shape[0] // 2
    product = pair_product(term_ref, got_term_ref)
    product = jnp.where(lax.axis_index("col") == 0, product[:half], product[half:])
    mine = jnp.where(is_even(), product[:, :rank], product[:, rank:])
    out_ref[...] = dot_parts(mine, inverse, 1)


def finish(total_rows, term, got_term, gram, got_gram):
    return pl.pallas_call(
        functools.partial(finish_kernel, total_rows),
        out_shape=jax.ShapeDtypeStruct((term.shape[0] // 2, LANES // 2), F32),
        compiler_params=params(4),
        name="finish",
    )(term, got_term, gram, got_gram)


def per_device(snapshot, mode2_factor, old_factor):
    n_rows, n_cols = lax.axis_size("row"), lax.axis_size("col")
    masks = [1 << bit for bit in range(n_rows.bit_length() - 1)]
    total_rows = snapshot.shape[0] * n_rows

    def swap(x, mask):
        pairs = [
            (r * n_cols + c, (r ^ mask) * n_cols + (c + 1) % n_cols)
            for r in range(n_rows)
            for c in range(n_cols)
        ]
        return lax.ppermute(x, ("row", "col"), pairs)

    snapshot = pltpu.with_memory_space_constraint(snapshot, pltpu.HBM)
    mode2_t = pltpu.with_memory_space_constraint(mode2_factor.T, pltpu.HBM)
    send, kept, wide, order = contract_send(snapshot, mode2_t)
    got = swap(send, 0)
    own = contract_own(kept, wide, order)

    keep, send, columns, give = project(own, got, old_factor.T)
    low, high = add_in_halves(keep, swap(send, masks[0]))
    got_columns = swap(give, masks[0])
    others = masks[1:]
    for step, (mask, turned) in enumerate(zip(others, others[1:] + others[:1])):
        after = [got_columns] if step == 1 else []
        got_low, got_high = swap(low, mask), swap(high, turned)
        low, high = add(low, got_low), add(high, got_high, *after)

    term = product_terms(columns, got_columns, low, high)
    term = add(term, swap(term, 0))
    pair, next_pair = masks[:2]
    got_term = swap(term, pair)
    gram = local_gram(term, got_term, swap(term, next_pair), swap(term, pair | next_pair))
    for mask in masks[2:-1]:
        gram = add(gram, swap(gram, mask))
    return finish(total_rows, term, got_term, gram, swap(gram, masks[-1]))


def solution(mesh):
    return jax.shard_map(
        per_device,
        mesh=mesh,
        in_specs=(
            P(("groups", "row"), None, "col"),
            P(("groups", "col"), None),
            P(("groups", "row"), None),
        ),
        out_specs=P(("groups", "row", "col"), None),
        check_vma=False,
    )
```

```python
import functools

import jax
import jax.numpy as jnp
from jax import lax
from jax.experimental import pallas as pl
from jax.experimental.pallas import tpu as pltpu
from jax.sharding import PartitionSpec as P

F32 = jnp.float32
BF16 = jnp.bfloat16
LANES = 128
MIB = 2**20


def dot_f32(a, b, dims, precision=None):
    return lax.dot_general(a, b, (dims, ((), ())), precision=precision, preferred_element_type=F32)


def params(mib):
    return pltpu.CompilerParams(vmem_limit_bytes=mib * MIB)


def own_half():
    row = lax.axis_index("row")
    half = lax.axis_index("col")
    for bit in range(lax.axis_size("row").bit_length() - 1):
        half += lax.rem(lax.div(row, 1 << bit), 2)
    return lax.rem(half, 2)


TILE = 8


def fill_order(order_ref, half):
    block = TILE * half
    to = lax.broadcasted_iota(jnp.int32, order_ref.shape, 0)
    at = lax.broadcasted_iota(jnp.int32, order_ref.shape, 1)
    cell = lax.div(lax.rem(at, block), half)
    wanted = lax.div(to, TILE) * (order_ref.shape[1] // block) + lax.div(at, block)
    same = (lax.rem(to, TILE) == cell) & (wanted == lax.rem(at, half))
    order_ref[...] = same.astype(F32).astype(BF16)


def multiply(slab, wide_ref, flat_ref):
    cells, half, depth = slab.shape
    x = slab.reshape(cells * half, depth)
    low = dot_f32(x[:, :depth // 2], wide_ref[:, :depth // 2], ((1,), (1,)))
    high = dot_f32(x[:, depth // 2:], wide_ref[:, depth // 2:], ((1,), (1,)))
    flat_ref[...] = (low + high).astype(BF16)


def spread(half, flat_ref, order_ref, core_ref, start):
    block = TILE * half
    reps = order_ref.shape[1] // block
    step = flat_ref.shape[0] // half
    group = lax.div(lax.broadcasted_iota(jnp.int32, (block, LANES), 1), LANES // reps)
    spreads = []
    for b in range(step // TILE):
        flat = flat_ref[pl.ds(b * block, block), :].astype(F32)
        groups = [jnp.where(group == r, flat, 0.0).astype(BF16) for r in range(reps)]
        spreads.append(dot_f32(order_ref[...], jnp.concatenate(groups, axis=0), ((1,), (0,))))
    for p in range(half // reps):
        part = jnp.concatenate([x[p * TILE:(p + 1) * TILE] for x in spreads], axis=0)
        core_ref[pl.ds(start, step), p * LANES:(p + 1) * LANES] = part.astype(BF16)


STEP = 32


def slab_copies(snapshot_ref, first, slab_ref, half_index, sem):
    half = slab_ref.shape[1]
    fibers = pl.ds(pl.multiple_of(half_index * half, half), half)

    def copy(start, size):
        return pltpu.make_async_copy(
            snapshot_ref.at[pl.ds(start, size), fibers],
            slab_ref.at[pl.ds(start - first, size)],
            sem,
        )

    def start(begin, size, count):
        for part in range(count):
            copy(begin + part * (size // count), size // count).start()

    return start, lambda begin, size: copy(begin, size).wait()


def send_kernel(
    snapshot_ref, mode2_ref, core_ref, kept_ref, wide_ref, order_ref,
    slab_ref, small_ref, even_ref, odd_ref, sems, kept_sem, small_sem,
):
    cells, half, _ = slab_ref.shape
    rank = mode2_ref.shape[0]
    chunks = cells // STEP
    flat = (even_ref, odd_ref)
    sends = [
        slab_copies(snapshot_ref, 0, slab_ref, 1 - own_half(), sems.at[chunk])
        for chunk in range(chunks)
    ]
    start_kept, wait_kept = slab_copies(snapshot_ref, 0, kept_ref, own_half(), kept_sem)

    small = pltpu.make_async_copy(mode2_ref, small_ref, small_sem)
    small.start()
    for chunk in range(chunks):
        sends[chunk][0](chunk * STEP, STEP, 2 if chunk else 4)
    fill_order(order_ref, half)
    small.wait()
    wide_ref[...] = jnp.concatenate([small_ref[...]] * (LANES // rank), axis=0)
    for chunk in range(chunks):
        sends[chunk][1](chunk * STEP, STEP)
        if chunk == 0:
            start_kept(0, cells, 2 * chunks)
        multiply(slab_ref[pl.ds(chunk * STEP, STEP)], wide_ref, flat[chunk % 2])
        if chunk:
            spread(half, flat[(chunk - 1) % 2], order_ref, core_ref, (chunk - 1) * STEP)
    spread(half, flat[(chunks - 1) % 2], order_ref, core_ref, (chunks - 1) * STEP)
    wait_kept(0, cells)


def contract_send(snapshot, mode2_t):
    cells, fibers, depth = snapshot.shape
    rank = mode2_t.shape[0]
    half = fibers // 2
    reps = LANES // rank
    block = TILE * half
    pinned = pl.BlockSpec(memory_space=pltpu.HBM)
    return pl.pallas_call(
        send_kernel,
        in_specs=[pinned, pinned],
        out_shape=[
            jax.ShapeDtypeStruct((cells, half * rank), BF16),
            jax.ShapeDtypeStruct((cells, half, depth), BF16),
            jax.ShapeDtypeStruct((LANES, depth), BF16),
            jax.ShapeDtypeStruct((block // reps, block * reps), BF16),
        ],
        scratch_shapes=[
            pltpu.VMEM((cells, half, depth), BF16),
            pltpu.VMEM((rank, depth), BF16),
            pltpu.VMEM((STEP * half, LANES), BF16),
            pltpu.VMEM((STEP * half, LANES), BF16),
            pltpu.SemaphoreType.DMA((cells // STEP,)),
            pltpu.SemaphoreType.DMA,
            pltpu.SemaphoreType.DMA,
        ],
        compiler_params=params(24),
        name="contract_send",
    )(snapshot, mode2_t)


def own_kernel(slab_ref, wide_ref, order_ref, core_ref, even_ref, odd_ref):
    cells, half, _ = slab_ref.shape
    flat = (even_ref, odd_ref)
    chunks = cells // STEP
    for chunk in range(chunks):
        multiply(slab_ref[pl.ds(chunk * STEP, STEP)], wide_ref, flat[chunk % 2])
        if chunk:
            spread(half, flat[(chunk - 1) % 2], order_ref, core_ref, (chunk - 1) * STEP)
    spread(half, flat[(chunks - 1) % 2], order_ref, core_ref, (chunks - 1) * STEP)


def contract_own(slab, wide, order):
    cells, half, _ = slab.shape
    reps = order.shape[1] // (TILE * half)
    return pl.pallas_call(
        own_kernel,
        out_shape=jax.ShapeDtypeStruct((cells, half // reps * LANES), BF16),
        scratch_shapes=[pltpu.VMEM((STEP * half, LANES), BF16)] * 2,
        compiler_params=params(24),
        name="contract_own",
    )(slab, wide, order)


def is_even():
    return lax.rem(lax.axis_index("row"), 2) == 0


def project_kernel(own_ref, got_ref, factor_ref, keep_ref, send_ref, mine_ref, give_ref):
    rank = factor_ref.shape[0]
    width = mine_ref.shape[1]
    even = is_even()
    halves = []
    for start in (0, width):
        where = slice(start, start + width)
        halves.append(own_ref[:, where].astype(F32) + got_ref[:, where].astype(F32))
    mine = jnp.where(even, halves[0], halves[1]).astype(BF16)
    give = jnp.where(even, halves[1], halves[0]).astype(BF16)
    mine_ref[...] = mine
    give_ref[...] = give
    keep = dot_f32(factor_ref[...], mine, ((1,), (0,)))
    send = dot_f32(factor_ref[...], give, ((1,), (0,)))
    for block in range(width // LANES):
        where = slice(block * LANES, (block + 1) * LANES)
        rows = pl.ds(block * rank, rank)
        keep_ref[rows, :] = keep[:, where]
        send_ref[rows, :] = send[:, where].astype(BF16)


def project(own, got, factor_t):
    cells, width = own.shape
    rows = factor_t.shape[0] * width // LANES // 2
    columns = jax.ShapeDtypeStruct((cells, width // 2), BF16)
    return pl.pallas_call(
        project_kernel,
        out_shape=[
            jax.ShapeDtypeStruct((rows, LANES), F32),
            jax.ShapeDtypeStruct((rows, LANES), BF16),
            columns,
            columns,
        ],
        compiler_params=params(8),
        name="project",
    )(own, got, factor_t)


def add_kernel(mine_ref, got_ref, *refs):
    total = mine_ref[...].astype(F32) + got_ref[...].astype(F32)
    refs[-1][...] = total.astype(refs[-1].dtype)


def add(mine, got, *after):
    whole = pl.BlockSpec(memory_space=pltpu.VMEM)
    return pl.pallas_call(
        add_kernel,
        in_specs=[whole, whole] + [pl.BlockSpec(memory_space=pl.ANY)] * len(after),
        out_shape=jax.ShapeDtypeStruct(got.shape, got.dtype),
        compiler_params=params(4),
        name="add",
    )(mine, got, *after)


def product_kernel(mine_ref, got_ref, projected_ref, out_ref):
    blocks = mine_ref.shape[1] // LANES
    rank = projected_ref.shape[0] // blocks
    projected = jnp.concatenate(
        [projected_ref[pl.ds(block * rank, rank), :] for block in range(blocks)], axis=1
    )
    terms = [dot_f32(ref[...], projected, ((1,), (1,))) for ref in (mine_ref, got_ref)]
    even = is_even()
    low = jnp.where(even, terms[0], terms[1])
    high = jnp.where(even, terms[1], terms[0])
    out_ref[...] = jnp.concatenate([low, high], axis=1).astype(BF16)


def product_terms(mine, got, projected):
    return pl.pallas_call(
        product_kernel,
        out_shape=jax.ShapeDtypeStruct((mine.shape[0], LANES), BF16),
        compiler_params=params(4),
        name="product_terms",
    )(mine, got, projected)


def pair_product(term_ref, got_ref):
    return term_ref[...].astype(F32) + got_ref[...].astype(F32)


def gram_kernel(*refs):
    out_ref = refs[-1]
    rank = LANES // 2
    product = jnp.concatenate(
        [pair_product(refs[k], refs[k + 1]) for k in range(0, len(refs) - 1, 2)], axis=0
    )
    wide = dot_parts(product, product, 0)
    gram = wide[:rank, :rank] + wide[rank:, rank:]
    out_ref[...] = jnp.concatenate([gram[:rank // 2], gram[rank // 2:]], axis=1)


def local_gram(*terms):
    return pl.pallas_call(
        gram_kernel,
        out_shape=jax.ShapeDtypeStruct((LANES // 4, LANES), F32),
        compiler_params=params(4),
        name="local_gram",
    )(*terms)


def parts(x):
    high = x.astype(BF16)
    return high, (x - high.astype(F32)).astype(BF16)


def dot_parts(a, b, axis):
    (ah, al), (bh, bl) = parts(a), parts(b)
    left = jnp.concatenate([ah, ah, al], axis=axis)
    right = jnp.concatenate([bh, bl, bh], axis=axis)
    return dot_f32(left, right, ((axis,), (axis,)))


def eliminate(gram):
    rank = gram.shape[0]
    tile = 8
    count = rank // tile
    wide = 2 * rank
    sublane = lax.broadcasted_iota(jnp.int32, (tile, wide), 0)
    lane = lax.broadcasted_iota(jnp.int32, (tile, wide), 1)
    full = lambda x: jnp.broadcast_to(x, (tile, wide))
    both = []
    for v in range(count):
        mine = gram[v * tile:(v + 1) * tile]
        both.append(jnp.where(lane < rank, jnp.concatenate([mine, mine], axis=1),
                              (lane - rank == sublane + v * tile).astype(F32)))
    pivots = []
    for p in range(count):
        cols = [
            {v: full(both[v][:, p * tile + j:p * tile + j + 1]) for v in range(p, count)}
            for j in range(tile)
        ]
        rows = [full(both[p][j:j + 1]) for j in range(tile)]
        block = [[full(cols[k][p][j:j + 1]) for k in range(j + 1)] for j in range(tile)]
        found, kept = block[0][0], rows[0]
        for j in range(tile):
            if j:
                found = jnp.where(sublane == j, block[j][j], found)
                kept = jnp.where(sublane == j, rows[j], kept)
            inverse = pl.reciprocal(block[j][j], approx=True, full_range=False)
            scaled = {i: block[i][j] * inverse for i in range(j + 1, tile)}
            for i, factor in scaled.items():
                for k in range(j + 1, i + 1):
                    block[i][k] = block[i][k] - factor * block[k][j]
                rows[i] = rows[i] - factor * rows[j]
            row = rows[j] * inverse
            for v in range(p + 1, count):
                for i, factor in scaled.items():
                    cols[i][v] = cols[i][v] - factor * cols[j][v]
                both[v] = both[v] - cols[j][v] * row
        both[p] = kept
        pivots.append(found)
    return both, pivots


def finish_kernel(total_rows, term_ref, got_term_ref, gram_ref, got_gram_ref, out_ref):
    rank = LANES // 2
    packed = gram_ref[...] + got_gram_ref[...]
    gram = jnp.concatenate([packed[:, :rank], packed[:, rank:]], axis=0)
    both, pivots = eliminate(gram)
    scale = total_rows ** 0.5
    inverse = jnp.concatenate([b * (lax.rsqrt(p) * scale) for b, p in zip(both, pivots)], axis=0)
    inverse = inverse[:, rank:]
    half = term_ref.shape[0] // 2
    product = pair_product(term_ref, got_term_ref)
    product = jnp.where(lax.axis_index("col") == 0, product[:half], product[half:])
    mine = jnp.where(is_even(), product[:, :rank], product[:, rank:])
    out_ref[...] = dot_parts(mine, inverse, 1)


def finish(total_rows, term, got_term, gram, got_gram):
    return pl.pallas_call(
        functools.partial(finish_kernel, total_rows),
        out_shape=jax.ShapeDtypeStruct((term.shape[0] // 2, LANES // 2), F32),
        compiler_params=params(4),
        name="finish",
    )(term, got_term, gram, got_gram)


def per_device(snapshot, mode2_factor, old_factor):
    n_rows, n_cols = lax.axis_size("row"), lax.axis_size("col")
    masks = [1 << bit for bit in range(n_rows.bit_length() - 1)]
    total_rows = snapshot.shape[0] * n_rows

    def swap(x, mask, other=None):
        pairs = []
        for r in range(n_rows):
            for c in range(n_cols):
                second = (c + r.bit_count()) % 2 and other is not None
                to = r ^ (other if second else mask)
                pairs.append((r * n_cols + c, to * n_cols + (c + 1) % n_cols))
        return lax.ppermute(x, ("row", "col"), pairs)

    snapshot = pltpu.with_memory_space_constraint(snapshot, pltpu.HBM)
    mode2_t = pltpu.with_memory_space_constraint(mode2_factor.T, pltpu.HBM)
    send, kept, wide, order = contract_send(snapshot, mode2_t)
    got = swap(send, 0)
    own = contract_own(kept, wide, order)

    keep, send, columns, give = project(own, got, old_factor.T)
    mine = add(keep, swap(send, masks[0]))
    got_columns = swap(give, masks[0])
    others = masks[1:]
    turned = others[len(others) // 2:] + others[:len(others) // 2]
    for step, (mask, other) in enumerate(zip(others, turned)):
        after = [got_columns] if step == 1 else []
        mine = add(mine, swap(mine, mask, other), *after)

    term = product_terms(columns, got_columns, mine)
    term = add(term, swap(term, 0))
    pair, next_pair = masks[:2]
    got_term = swap(term, pair)
    gram = local_gram(term, got_term, swap(term, next_pair), swap(term, pair | next_pair))
    for mask in masks[2:-1]:
        gram = add(gram, swap(gram, mask))
    return finish(total_rows, term, got_term, gram, swap(gram, masks[-1]))


def solution(mesh):
    return jax.shard_map(
        per_device,
        mesh=mesh,
        in_specs=(
            P(("groups", "row"), None, "col"),
            P(("groups", "col"), None),
            P(("groups", "row"), None),
        ),
        out_specs=P(("groups", "row", "col"), None),
        check_vma=False,
    )
```

```python
import functools

import jax
import jax.numpy as jnp
from jax import lax
from jax.experimental import pallas as pl
from jax.experimental.pallas import tpu as pltpu
from jax.sharding import PartitionSpec as P

F32 = jnp.float32
BF16 = jnp.bfloat16
LANES = 128
MIB = 2**20


def dot_f32(a, b, dims, precision=None):
    return lax.dot_general(a, b, (dims, ((), ())), precision=precision, preferred_element_type=F32)


def params(mib):
    return pltpu.CompilerParams(vmem_limit_bytes=mib * MIB)


def own_half():
    row = lax.axis_index("row")
    half = lax.axis_index("col")
    for bit in range(lax.axis_size("row").bit_length() - 1):
        half += lax.rem(lax.div(row, 1 << bit), 2)
    return lax.rem(half, 2)


TILE = 8


def fill_order(order_ref, half):
    block = TILE * half
    to = lax.broadcasted_iota(jnp.int32, order_ref.shape, 0)
    at = lax.broadcasted_iota(jnp.int32, order_ref.shape, 1)
    cell = lax.div(lax.rem(at, block), half)
    wanted = lax.div(to, TILE) * (order_ref.shape[1] // block) + lax.div(at, block)
    same = (lax.rem(to, TILE) == cell) & (wanted == lax.rem(at, half))
    order_ref[...] = same.astype(F32).astype(BF16)


def multiply(slab, wide_ref, flat_ref):
    cells, half, depth = slab.shape
    x = slab.reshape(cells * half, depth)
    low = dot_f32(x[:, :depth // 2], wide_ref[:, :depth // 2], ((1,), (1,)))
    high = dot_f32(x[:, depth // 2:], wide_ref[:, depth // 2:], ((1,), (1,)))
    flat_ref[...] = (low + high).astype(BF16)


def spread(half, flat_ref, order_ref, core_ref, start):
    block = TILE * half
    reps = order_ref.shape[1] // block
    step = flat_ref.shape[0] // half
    group = lax.div(lax.broadcasted_iota(jnp.int32, (block, LANES), 1), LANES // reps)
    spreads = []
    for b in range(step // TILE):
        flat = flat_ref[pl.ds(b * block, block), :].astype(F32)
        groups = [jnp.where(group == r, flat, 0.0).astype(BF16) for r in range(reps)]
        spreads.append(dot_f32(order_ref[...], jnp.concatenate(groups, axis=0), ((1,), (0,))))
    for p in range(half // reps):
        part = jnp.concatenate([x[p * TILE:(p + 1) * TILE] for x in spreads], axis=0)
        core_ref[pl.ds(start, step), p * LANES:(p + 1) * LANES] = part.astype(BF16)


STEP = 32


def slab_copies(snapshot_ref, first, slab_ref, half_index, sem):
    half = slab_ref.shape[1]
    fibers = pl.ds(pl.multiple_of(half_index * half, half), half)

    def copy(start, size):
        return pltpu.make_async_copy(
            snapshot_ref.at[pl.ds(start, size), fibers],
            slab_ref.at[pl.ds(start - first, size)],
            sem,
        )

    def start(begin, size, count):
        for part in range(count):
            copy(begin + part * (size // count), size // count).start()

    return start, lambda begin, size: copy(begin, size).wait()


def send_kernel(
    snapshot_ref, mode2_ref, core_ref, kept_ref, wide_ref, order_ref,
    slab_ref, small_ref, even_ref, odd_ref, sems, kept_sem, small_sem,
):
    cells, half, _ = slab_ref.shape
    rank = mode2_ref.shape[0]
    chunks = cells // STEP
    flat = (even_ref, odd_ref)
    sends = [
        slab_copies(snapshot_ref, 0, slab_ref, 1 - own_half(), sems.at[chunk])
        for chunk in range(chunks)
    ]
    start_kept, wait_kept = slab_copies(snapshot_ref, 0, kept_ref, own_half(), kept_sem)

    small = pltpu.make_async_copy(mode2_ref, small_ref, small_sem)
    small.start()
    for chunk in range(chunks):
        sends[chunk][0](chunk * STEP, STEP, 2 if chunk else 4)
    fill_order(order_ref, half)
    small.wait()
    wide_ref[...] = jnp.concatenate([small_ref[...]] * (LANES // rank), axis=0)
    for chunk in range(chunks):
        sends[chunk][1](chunk * STEP, STEP)
        if chunk == 0:
            start_kept(0, cells, 2 * chunks)
        multiply(slab_ref[pl.ds(chunk * STEP, STEP)], wide_ref, flat[chunk % 2])
        if chunk:
            spread(half, flat[(chunk - 1) % 2], order_ref, core_ref, (chunk - 1) * STEP)
    spread(half, flat[(chunks - 1) % 2], order_ref, core_ref, (chunks - 1) * STEP)
    wait_kept(0, cells)


def contract_send(snapshot, mode2_t):
    cells, fibers, depth = snapshot.shape
    rank = mode2_t.shape[0]
    half = fibers // 2
    reps = LANES // rank
    block = TILE * half
    pinned = pl.BlockSpec(memory_space=pltpu.HBM)
    return pl.pallas_call(
        send_kernel,
        in_specs=[pinned, pinned],
        out_shape=[
            jax.ShapeDtypeStruct((cells, half * rank), BF16),
            jax.ShapeDtypeStruct((cells, half, depth), BF16),
            jax.ShapeDtypeStruct((LANES, depth), BF16),
            jax.ShapeDtypeStruct((block // reps, block * reps), BF16),
        ],
        scratch_shapes=[
            pltpu.VMEM((cells, half, depth), BF16),
            pltpu.VMEM((rank, depth), BF16),
            pltpu.VMEM((STEP * half, LANES), BF16),
            pltpu.VMEM((STEP * half, LANES), BF16),
            pltpu.SemaphoreType.DMA((cells // STEP,)),
            pltpu.SemaphoreType.DMA,
            pltpu.SemaphoreType.DMA,
        ],
        compiler_params=params(24),
        name="contract_send",
    )(snapshot, mode2_t)


def own_kernel(slab_ref, wide_ref, order_ref, core_ref, even_ref, odd_ref):
    cells, half, _ = slab_ref.shape
    flat = (even_ref, odd_ref)
    chunks = cells // STEP
    for chunk in range(chunks):
        multiply(slab_ref[pl.ds(chunk * STEP, STEP)], wide_ref, flat[chunk % 2])
        if chunk:
            spread(half, flat[(chunk - 1) % 2], order_ref, core_ref, (chunk - 1) * STEP)
    spread(half, flat[(chunks - 1) % 2], order_ref, core_ref, (chunks - 1) * STEP)


def contract_own(slab, wide, order):
    cells, half, _ = slab.shape
    reps = order.shape[1] // (TILE * half)
    return pl.pallas_call(
        own_kernel,
        out_shape=jax.ShapeDtypeStruct((cells, half // reps * LANES), BF16),
        scratch_shapes=[pltpu.VMEM((STEP * half, LANES), BF16)] * 2,
        compiler_params=params(24),
        name="contract_own",
    )(slab, wide, order)


def is_even():
    return lax.rem(lax.axis_index("row"), 2) == 0


def project_kernel(own_ref, got_ref, factor_ref, keep_ref, send_ref, mine_ref, give_ref):
    rank = factor_ref.shape[0]
    width = mine_ref.shape[1]
    even = is_even()
    halves = []
    for start in (0, width):
        where = slice(start, start + width)
        halves.append(own_ref[:, where].astype(F32) + got_ref[:, where].astype(F32))
    mine = jnp.where(even, halves[0], halves[1]).astype(BF16)
    give = jnp.where(even, halves[1], halves[0]).astype(BF16)
    mine_ref[...] = mine
    give_ref[...] = give
    keep = dot_f32(factor_ref[...], mine, ((1,), (0,)))
    send = dot_f32(factor_ref[...], give, ((1,), (0,)))
    for block in range(width // LANES):
        where = slice(block * LANES, (block + 1) * LANES)
        rows = pl.ds(block * rank, rank)
        keep_ref[rows, :] = keep[:, where]
        send_ref[rows, :] = send[:, where].astype(BF16)


def project(own, got, factor_t):
    cells, width = own.shape
    rows = factor_t.shape[0] * width // LANES // 2
    columns = jax.ShapeDtypeStruct((cells, width // 2), BF16)
    return pl.pallas_call(
        project_kernel,
        out_shape=[
            jax.ShapeDtypeStruct((rows, LANES), F32),
            jax.ShapeDtypeStruct((rows, LANES), BF16),
            columns,
            columns,
        ],
        compiler_params=params(8),
        name="project",
    )(own, got, factor_t)


def add_kernel(mine_ref, got_ref, *refs):
    total = mine_ref[...].astype(F32) + got_ref[...].astype(F32)
    refs[-1][...] = total.astype(refs[-1].dtype)


def add(mine, got, *after):
    whole = pl.BlockSpec(memory_space=pltpu.VMEM)
    return pl.pallas_call(
        add_kernel,
        in_specs=[whole, whole] + [pl.BlockSpec(memory_space=pl.ANY)] * len(after),
        out_shape=jax.ShapeDtypeStruct(got.shape, got.dtype),
        compiler_params=params(4),
        name="add",
    )(mine, got, *after)


def product_kernel(mine_ref, got_ref, projected_ref, out_ref):
    blocks = mine_ref.shape[1] // LANES
    rank = projected_ref.shape[0] // blocks
    projected = jnp.concatenate(
        [projected_ref[pl.ds(block * rank, rank), :] for block in range(blocks)], axis=1
    )
    terms = [dot_f32(ref[...], projected, ((1,), (1,))) for ref in (mine_ref, got_ref)]
    even = is_even()
    low = jnp.where(even, terms[0], terms[1])
    high = jnp.where(even, terms[1], terms[0])
    out_ref[...] = jnp.concatenate([low, high], axis=1).astype(BF16)


def product_terms(mine, got, projected):
    return pl.pallas_call(
        product_kernel,
        out_shape=jax.ShapeDtypeStruct((mine.shape[0], LANES), BF16),
        compiler_params=params(4),
        name="product_terms",
    )(mine, got, projected)


def pair_product(term_ref, got_ref):
    return term_ref[...].astype(F32) + got_ref[...].astype(F32)


def gram_kernel(*refs):
    out_ref = refs[-1]
    rank = LANES // 2
    product = jnp.concatenate(
        [pair_product(refs[k], refs[k + 1]) for k in range(0, len(refs) - 1, 2)], axis=0
    )
    wide = dot_parts(product, product, 0)
    gram = wide[:rank, :rank] + wide[rank:, rank:]
    out_ref[...] = jnp.concatenate([gram[:rank // 2], gram[rank // 2:]], axis=1)


def local_gram(*terms):
    return pl.pallas_call(
        gram_kernel,
        out_shape=jax.ShapeDtypeStruct((LANES // 4, LANES), F32),
        compiler_params=params(4),
        name="local_gram",
    )(*terms)


def parts(x):
    high = x.astype(BF16)
    return high, (x - high.astype(F32)).astype(BF16)


def dot_parts(a, b, axis):
    (ah, al), (bh, bl) = parts(a), parts(b)
    left = jnp.concatenate([ah, ah, al], axis=axis)
    right = jnp.concatenate([bh, bl, bh], axis=axis)
    return dot_f32(left, right, ((axis,), (axis,)))


def eliminate(gram):
    rank = gram.shape[0]
    tile = 8
    count = rank // tile
    wide = 2 * rank
    sublane = lax.broadcasted_iota(jnp.int32, (tile, wide), 0)
    lane = lax.broadcasted_iota(jnp.int32, (tile, wide), 1)
    full = lambda x: jnp.broadcast_to(x, (tile, wide))
    both = []
    for v in range(count):
        mine = gram[v * tile:(v + 1) * tile]
        both.append(jnp.where(lane < rank, jnp.concatenate([mine, mine], axis=1),
                              (lane - rank == sublane + v * tile).astype(F32)))
    pivots = []
    for p in range(count):
        cols = [
            {v: full(both[v][:, p * tile + j:p * tile + j + 1]) for v in range(p, count)}
            for j in range(tile)
        ]
        rows = [full(both[p][j:j + 1]) for j in range(tile)]
        block = [[full(cols[k][p][j:j + 1]) for k in range(j + 1)] for j in range(tile)]
        found, kept = block[0][0], rows[0]
        for j in range(tile):
            if j:
                found = jnp.where(sublane == j, block[j][j], found)
                kept = jnp.where(sublane == j, rows[j], kept)
            inverse = pl.reciprocal(block[j][j], approx=True, full_range=False)
            scaled = {i: block[i][j] * inverse for i in range(j + 1, tile)}
            for i, factor in scaled.items():
                for k in range(j + 1, i + 1):
                    block[i][k] = block[i][k] - factor * block[k][j]
                rows[i] = rows[i] - factor * rows[j]
            row = rows[j] * inverse
            for v in range(p + 1, count):
                for i, factor in scaled.items():
                    cols[i][v] = cols[i][v] - factor * cols[j][v]
                both[v] = both[v] - cols[j][v] * row
        both[p] = kept
        pivots.append(found)
    return both, pivots


def finish_kernel(total_rows, term_ref, got_term_ref, gram_ref, got_gram_ref, out_ref):
    rank = LANES // 2
    packed = gram_ref[...] + got_gram_ref[...]
    gram = jnp.concatenate([packed[:, :rank], packed[:, rank:]], axis=0)
    both, pivots = eliminate(gram)
    scale = total_rows ** 0.5
    inverse = jnp.concatenate([b * (lax.rsqrt(p) * scale) for b, p in zip(both, pivots)], axis=0)
    inverse = inverse[:, rank:]
    half = term_ref.shape[0] // 2
    product = pair_product(term_ref, got_term_ref)
    product = jnp.where(lax.axis_index("col") == 0, product[:half], product[half:])
    mine = jnp.where(is_even(), product[:, :rank], product[:, rank:])
    out_ref[...] = dot_parts(mine, inverse, 1)


def finish(total_rows, term, got_term, gram, got_gram):
    return pl.pallas_call(
        functools.partial(finish_kernel, total_rows),
        out_shape=jax.ShapeDtypeStruct((term.shape[0] // 2, LANES // 2), F32),
        compiler_params=params(4),
        name="finish",
    )(term, got_term, gram, got_gram)


def per_device(snapshot, mode2_factor, old_factor):
    n_rows, n_cols = lax.axis_size("row"), lax.axis_size("col")
    masks = [1 << bit for bit in range(n_rows.bit_length() - 1)]
    total_rows = snapshot.shape[0] * n_rows

    def swap(x, mask, other=None):
        pairs = []
        for r in range(n_rows):
            for c in range(n_cols):
                second = (c + r.bit_count()) % 2 and other is not None
                to = r ^ (other if second else mask)
                pairs.append((r * n_cols + c, to * n_cols + (c + 1) % n_cols))
        return lax.ppermute(x, ("row", "col"), pairs)

    snapshot = pltpu.with_memory_space_constraint(snapshot, pltpu.HBM)
    mode2_t = pltpu.with_memory_space_constraint(mode2_factor.T, pltpu.HBM)
    send, kept, wide, order = contract_send(snapshot, mode2_t)
    got = swap(send, 0)
    own = contract_own(kept, wide, order)

    keep, send, columns, give = project(own, got, old_factor.T)
    mine = add(keep, swap(send, masks[0]))
    got_columns = swap(give, masks[0])
    others = masks[1:]
    turned = others[len(others) // 2:] + others[:len(others) // 2]
    for step, (mask, other) in enumerate(zip(others, turned)):
        after = [got_columns] if step == 0 else []
        mine = add(mine, swap(mine, mask, other), *after)

    term = product_terms(columns, got_columns, mine)
    term = add(term, swap(term, 0))
    pair, next_pair = masks[:2]
    got_term = swap(term, pair)
    gram = local_gram(term, got_term, swap(term, next_pair), swap(term, pair | next_pair))
    for mask in masks[2:-1]:
        gram = add(gram, swap(gram, mask))
    return finish(total_rows, term, got_term, gram, swap(gram, masks[-1]))


def solution(mesh):
    return jax.shard_map(
        per_device,
        mesh=mesh,
        in_specs=(
            P(("groups", "row"), None, "col"),
            P(("groups", "col"), None),
            P(("groups", "row"), None),
        ),
        out_specs=P(("groups", "row", "col"), None),
        check_vma=False,
    )
```

```python
import functools

import jax
import jax.numpy as jnp
from jax import lax
from jax.experimental import pallas as pl
from jax.experimental.pallas import tpu as pltpu
from jax.sharding import PartitionSpec as P

F32 = jnp.float32
BF16 = jnp.bfloat16
LANES = 128
MIB = 2**20


def dot_f32(a, b, dims, precision=None):
    return lax.dot_general(a, b, (dims, ((), ())), precision=precision, preferred_element_type=F32)


def params(mib):
    return pltpu.CompilerParams(vmem_limit_bytes=mib * MIB)


def own_half():
    row = lax.axis_index("row")
    half = lax.axis_index("col")
    for bit in range(lax.axis_size("row").bit_length() - 1):
        half += lax.rem(lax.div(row, 1 << bit), 2)
    return lax.rem(half, 2)


TILE = 8


def fill_order(order_ref, half):
    block = TILE * half
    to = lax.broadcasted_iota(jnp.int32, order_ref.shape, 0)
    at = lax.broadcasted_iota(jnp.int32, order_ref.shape, 1)
    cell = lax.div(lax.rem(at, block), half)
    wanted = lax.div(to, TILE) * (order_ref.shape[1] // block) + lax.div(at, block)
    same = (lax.rem(to, TILE) == cell) & (wanted == lax.rem(at, half))
    order_ref[...] = same.astype(F32).astype(BF16)


def multiply(slab, wide_ref, flat_ref):
    cells, half, depth = slab.shape
    x = slab.reshape(cells * half, depth)
    low = dot_f32(x[:, :depth // 2], wide_ref[:, :depth // 2], ((1,), (1,)))
    high = dot_f32(x[:, depth // 2:], wide_ref[:, depth // 2:], ((1,), (1,)))
    flat_ref[...] = (low + high).astype(BF16)


def spread(half, flat_ref, order_ref, core_ref, start):
    block = TILE * half
    reps = order_ref.shape[1] // block
    step = flat_ref.shape[0] // half
    group = lax.div(lax.broadcasted_iota(jnp.int32, (block, LANES), 1), LANES // reps)
    spreads = []
    for b in range(step // TILE):
        flat = flat_ref[pl.ds(b * block, block), :].astype(F32)
        groups = [jnp.where(group == r, flat, 0.0).astype(BF16) for r in range(reps)]
        spreads.append(dot_f32(order_ref[...], jnp.concatenate(groups, axis=0), ((1,), (0,))))
    for p in range(half // reps):
        part = jnp.concatenate([x[p * TILE:(p + 1) * TILE] for x in spreads], axis=0)
        core_ref[pl.ds(start, step), p * LANES:(p + 1) * LANES] = part.astype(BF16)


STEP = 32


def slab_copies(snapshot_ref, first, slab_ref, half_index, sem):
    half = slab_ref.shape[1]
    fibers = pl.ds(pl.multiple_of(half_index * half, half), half)

    def copy(start, size):
        return pltpu.make_async_copy(
            snapshot_ref.at[pl.ds(start, size), fibers],
            slab_ref.at[pl.ds(start - first, size)],
            sem,
        )

    def start(begin, size, count):
        for part in range(count):
            copy(begin + part * (size // count), size // count).start()

    return start, lambda begin, size: copy(begin, size).wait()


def send_kernel(
    snapshot_ref, mode2_ref, core_ref, kept_ref, wide_ref, order_ref,
    slab_ref, small_ref, even_ref, odd_ref, sems, kept_sem, small_sem,
):
    cells, half, _ = slab_ref.shape
    rank = mode2_ref.shape[0]
    chunks = cells // STEP
    flat = (even_ref, odd_ref)
    sends = [
        slab_copies(snapshot_ref, 0, slab_ref, 1 - own_half(), sems.at[chunk])
        for chunk in range(chunks)
    ]
    start_kept, wait_kept = slab_copies(snapshot_ref, 0, kept_ref, own_half(), kept_sem)

    small = pltpu.make_async_copy(mode2_ref, small_ref, small_sem)
    small.start()
    for chunk in range(chunks):
        sends[chunk][0](chunk * STEP, STEP, 4)
    fill_order(order_ref, half)
    small.wait()
    wide_ref[...] = jnp.concatenate([small_ref[...]] * (LANES // rank), axis=0)
    for chunk in range(chunks):
        sends[chunk][1](chunk * STEP, STEP)
        if chunk < 2:
            start_kept(chunk * (cells // 2), cells // 2, 2 * chunks)
        multiply(slab_ref[pl.ds(chunk * STEP, STEP)], wide_ref, flat[chunk % 2])
        if chunk:
            spread(half, flat[(chunk - 1) % 2], order_ref, core_ref, (chunk - 1) * STEP)
    spread(half, flat[(chunks - 1) % 2], order_ref, core_ref, (chunks - 1) * STEP)
    wait_kept(0, cells)


def contract_send(snapshot, mode2_t):
    cells, fibers, depth = snapshot.shape
    rank = mode2_t.shape[0]
    half = fibers // 2
    reps = LANES // rank
    block = TILE * half
    pinned = pl.BlockSpec(memory_space=pltpu.HBM)
    return pl.pallas_call(
        send_kernel,
        in_specs=[pinned, pinned],
        out_shape=[
            jax.ShapeDtypeStruct((cells, half * rank), BF16),
            jax.ShapeDtypeStruct((cells, half, depth), BF16),
            jax.ShapeDtypeStruct((LANES, depth), BF16),
            jax.ShapeDtypeStruct((block // reps, block * reps), BF16),
        ],
        scratch_shapes=[
            pltpu.VMEM((cells, half, depth), BF16),
            pltpu.VMEM((rank, depth), BF16),
            pltpu.VMEM((STEP * half, LANES), BF16),
            pltpu.VMEM((STEP * half, LANES), BF16),
            pltpu.SemaphoreType.DMA((cells // STEP,)),
            pltpu.SemaphoreType.DMA,
            pltpu.SemaphoreType.DMA,
        ],
        compiler_params=params(24),
        name="contract_send",
    )(snapshot, mode2_t)


def own_kernel(slab_ref, wide_ref, order_ref, core_ref, even_ref, odd_ref):
    cells, half, _ = slab_ref.shape
    flat = (even_ref, odd_ref)
    chunks = cells // STEP
    for chunk in range(chunks):
        multiply(slab_ref[pl.ds(chunk * STEP, STEP)], wide_ref, flat[chunk % 2])
        if chunk:
            spread(half, flat[(chunk - 1) % 2], order_ref, core_ref, (chunk - 1) * STEP)
    spread(half, flat[(chunks - 1) % 2], order_ref, core_ref, (chunks - 1) * STEP)


def contract_own(slab, wide, order):
    cells, half, _ = slab.shape
    reps = order.shape[1] // (TILE * half)
    return pl.pallas_call(
        own_kernel,
        out_shape=jax.ShapeDtypeStruct((cells, half // reps * LANES), BF16),
        scratch_shapes=[pltpu.VMEM((STEP * half, LANES), BF16)] * 2,
        compiler_params=params(24),
        name="contract_own",
    )(slab, wide, order)


def is_even():
    return lax.rem(lax.axis_index("row"), 2) == 0


def project_kernel(own_ref, got_ref, factor_ref, keep_ref, send_ref, mine_ref, give_ref):
    rank = factor_ref.shape[0]
    width = mine_ref.shape[1]
    even = is_even()
    halves = []
    for start in (0, width):
        where = slice(start, start + width)
        halves.append(own_ref[:, where].astype(F32) + got_ref[:, where].astype(F32))
    mine = jnp.where(even, halves[0], halves[1]).astype(BF16)
    give = jnp.where(even, halves[1], halves[0]).astype(BF16)
    mine_ref[...] = mine
    give_ref[...] = give
    keep = dot_f32(factor_ref[...], mine, ((1,), (0,)))
    send = dot_f32(factor_ref[...], give, ((1,), (0,)))
    for block in range(width // LANES):
        where = slice(block * LANES, (block + 1) * LANES)
        rows = pl.ds(block * rank, rank)
        keep_ref[rows, :] = keep[:, where]
        send_ref[rows, :] = send[:, where].astype(BF16)


def project(own, got, factor_t):
    cells, width = own.shape
    rows = factor_t.shape[0] * width // LANES // 2
    columns = jax.ShapeDtypeStruct((cells, width // 2), BF16)
    return pl.pallas_call(
        project_kernel,
        out_shape=[
            jax.ShapeDtypeStruct((rows, LANES), F32),
            jax.ShapeDtypeStruct((rows, LANES), BF16),
            columns,
            columns,
        ],
        compiler_params=params(8),
        name="project",
    )(own, got, factor_t)


def add_kernel(mine_ref, got_ref, *refs):
    total = mine_ref[...].astype(F32) + got_ref[...].astype(F32)
    refs[-1][...] = total.astype(refs[-1].dtype)


def add(mine, got, *after):
    whole = pl.BlockSpec(memory_space=pltpu.VMEM)
    return pl.pallas_call(
        add_kernel,
        in_specs=[whole, whole] + [pl.BlockSpec(memory_space=pl.ANY)] * len(after),
        out_shape=jax.ShapeDtypeStruct(got.shape, got.dtype),
        compiler_params=params(4),
        name="add",
    )(mine, got, *after)


def product_kernel(mine_ref, got_ref, projected_ref, out_ref):
    blocks = mine_ref.shape[1] // LANES
    rank = projected_ref.shape[0] // blocks
    projected = jnp.concatenate(
        [projected_ref[pl.ds(block * rank, rank), :] for block in range(blocks)], axis=1
    )
    terms = [dot_f32(ref[...], projected, ((1,), (1,))) for ref in (mine_ref, got_ref)]
    even = is_even()
    low = jnp.where(even, terms[0], terms[1])
    high = jnp.where(even, terms[1], terms[0])
    out_ref[...] = jnp.concatenate([low, high], axis=1).astype(BF16)


def product_terms(mine, got, projected):
    return pl.pallas_call(
        product_kernel,
        out_shape=jax.ShapeDtypeStruct((mine.shape[0], LANES), BF16),
        compiler_params=params(4),
        name="product_terms",
    )(mine, got, projected)


def pair_product(term_ref, first_ref, second_ref):
    got = jnp.where(own_half() == 0, first_ref[...].astype(F32), second_ref[...].astype(F32))
    return term_ref[...].astype(F32) + got


def gram_kernel(term_ref, first_ref, second_ref, last_ref, out_ref):
    rank = LANES // 2
    product = jnp.concatenate(
        [
            pair_product(term_ref, first_ref, second_ref),
            pair_product(last_ref, second_ref, first_ref),
        ],
        axis=0,
    )
    wide = dot_parts(product, product, 0)
    gram = wide[:rank, :rank] + wide[rank:, rank:]
    out_ref[...] = jnp.concatenate([gram[:rank // 2], gram[rank // 2:]], axis=1)


def local_gram(*terms):
    return pl.pallas_call(
        gram_kernel,
        out_shape=jax.ShapeDtypeStruct((LANES // 4, LANES), F32),
        compiler_params=params(4),
        name="local_gram",
    )(*terms)


def parts(x):
    high = x.astype(BF16)
    return high, (x - high.astype(F32)).astype(BF16)


def dot_parts(a, b, axis):
    (ah, al), (bh, bl) = parts(a), parts(b)
    left = jnp.concatenate([ah, ah, al], axis=axis)
    right = jnp.concatenate([bh, bl, bh], axis=axis)
    return dot_f32(left, right, ((axis,), (axis,)))


def eliminate(gram):
    rank = gram.shape[0]
    tile = 8
    count = rank // tile
    wide = 2 * rank
    sublane = lax.broadcasted_iota(jnp.int32, (tile, wide), 0)
    lane = lax.broadcasted_iota(jnp.int32, (tile, wide), 1)
    full = lambda x: jnp.broadcast_to(x, (tile, wide))
    both = []
    for v in range(count):
        mine = gram[v * tile:(v + 1) * tile]
        both.append(jnp.where(lane < rank, jnp.concatenate([mine, mine], axis=1),
                              (lane - rank == sublane + v * tile).astype(F32)))
    pivots = []
    for p in range(count):
        cols = [
            {v: full(both[v][:, p * tile + j:p * tile + j + 1]) for v in range(p, count)}
            for j in range(tile)
        ]
        rows = [full(both[p][j:j + 1]) for j in range(tile)]
        block = [[full(cols[k][p][j:j + 1]) for k in range(j + 1)] for j in range(tile)]
        found, kept = block[0][0], rows[0]
        for j in range(tile):
            if j:
                found = jnp.where(sublane == j, block[j][j], found)
                kept = jnp.where(sublane == j, rows[j], kept)
            inverse = pl.reciprocal(block[j][j], approx=True, full_range=False)
            scaled = {i: block[i][j] * inverse for i in range(j + 1, tile)}
            for i, factor in scaled.items():
                for k in range(j + 1, i + 1):
                    block[i][k] = block[i][k] - factor * block[k][j]
                rows[i] = rows[i] - factor * rows[j]
            row = rows[j] * inverse
            for v in range(p + 1, count):
                for i, factor in scaled.items():
                    cols[i][v] = cols[i][v] - factor * cols[j][v]
                both[v] = both[v] - cols[j][v] * row
        both[p] = kept
        pivots.append(found)
    return both, pivots


def finish_kernel(
    total_rows, term_ref, first_ref, second_ref, gram_ref, got_gram_ref, out_ref
):
    rank = LANES // 2
    packed = gram_ref[...] + got_gram_ref[...]
    gram = jnp.concatenate([packed[:, :rank], packed[:, rank:]], axis=0)
    both, pivots = eliminate(gram)
    scale = total_rows ** 0.5
    inverse = jnp.concatenate([b * (lax.rsqrt(p) * scale) for b, p in zip(both, pivots)], axis=0)
    inverse = inverse[:, rank:]
    half = term_ref.shape[0] // 2
    product = pair_product(term_ref, first_ref, second_ref)
    product = jnp.where(lax.axis_index("col") == 0, product[:half], product[half:])
    mine = jnp.where(is_even(), product[:, :rank], product[:, rank:])
    out_ref[...] = dot_parts(mine, inverse, 1)


def finish(total_rows, term, first, second, gram, got_gram):
    return pl.pallas_call(
        functools.partial(finish_kernel, total_rows),
        out_shape=jax.ShapeDtypeStruct((term.shape[0] // 2, LANES // 2), F32),
        compiler_params=params(4),
        name="finish",
    )(term, first, second, gram, got_gram)


def per_device(snapshot, mode2_factor, old_factor):
    n_rows, n_cols = lax.axis_size("row"), lax.axis_size("col")
    masks = [1 << bit for bit in range(n_rows.bit_length() - 1)]
    total_rows = snapshot.shape[0] * n_rows

    def swap(x, mask, other=None):
        pairs = []
        for r in range(n_rows):
            for c in range(n_cols):
                second = (c + r.bit_count()) % 2 and other is not None
                to = r ^ (other if second else mask)
                pairs.append((r * n_cols + c, to * n_cols + (c + 1) % n_cols))
        return lax.ppermute(x, ("row", "col"), pairs)

    snapshot = pltpu.with_memory_space_constraint(snapshot, pltpu.HBM)
    mode2_t = pltpu.with_memory_space_constraint(mode2_factor.T, pltpu.HBM)
    send, kept, wide, order = contract_send(snapshot, mode2_t)
    got = swap(send, 0)
    own = contract_own(kept, wide, order)

    keep, send, columns, give = project(own, got, old_factor.T)
    mine = add(keep, swap(send, masks[0]))
    got_columns = swap(give, masks[0])
    others = masks[1:]
    turned = others[len(others) // 2:] + others[:len(others) // 2]
    for step, (mask, other) in enumerate(zip(others, turned)):
        after = [got_columns] if step == 1 else []
        mine = add(mine, swap(mine, mask, other), *after)

    term = product_terms(columns, got_columns, mine)
    term = add(term, swap(term, 0))
    pair, next_pair = masks[:2]
    first, second = swap(term, pair, next_pair), swap(term, next_pair, pair)
    gram = local_gram(term, first, second, swap(term, pair | next_pair))
    for mask in masks[2:-1]:
        gram = add(gram, swap(gram, mask))
    return finish(total_rows, term, first, second, gram, swap(gram, masks[-1]))


def solution(mesh):
    return jax.shard_map(
        per_device,
        mesh=mesh,
        in_specs=(
            P(("groups", "row"), None, "col"),
            P(("groups", "col"), None),
            P(("groups", "row"), None),
        ),
        out_specs=P(("groups", "row", "col"), None),
        check_vma=False,
    )
```

```python
import functools

import jax
import jax.numpy as jnp
from jax import lax
from jax.experimental import pallas as pl
from jax.experimental.pallas import tpu as pltpu
from jax.sharding import PartitionSpec as P

F32 = jnp.float32
BF16 = jnp.bfloat16
LANES = 128
MIB = 2**20


def dot_f32(a, b, dims, precision=None):
    return lax.dot_general(a, b, (dims, ((), ())), precision=precision, preferred_element_type=F32)


def params(mib):
    return pltpu.CompilerParams(vmem_limit_bytes=mib * MIB)


def own_half():
    row = lax.axis_index("row")
    half = lax.axis_index("col")
    for bit in range(lax.axis_size("row").bit_length() - 1):
        half += lax.rem(lax.div(row, 1 << bit), 2)
    return lax.rem(half, 2)


TILE = 8


def fill_order(order_ref, half):
    block = TILE * half
    to = lax.broadcasted_iota(jnp.int32, order_ref.shape, 0)
    at = lax.broadcasted_iota(jnp.int32, order_ref.shape, 1)
    cell = lax.div(lax.rem(at, block), half)
    wanted = lax.div(to, TILE) * (order_ref.shape[1] // block) + lax.div(at, block)
    same = (lax.rem(to, TILE) == cell) & (wanted == lax.rem(at, half))
    order_ref[...] = same.astype(F32).astype(BF16)


def multiply(slab, wide_ref, flat_ref):
    cells, half, depth = slab.shape
    x = slab.reshape(cells * half, depth)
    low = dot_f32(x[:, :depth // 2], wide_ref[:, :depth // 2], ((1,), (1,)))
    high = dot_f32(x[:, depth // 2:], wide_ref[:, depth // 2:], ((1,), (1,)))
    flat_ref[...] = (low + high).astype(BF16)


def spread(half, flat_ref, order_ref, core_ref, start):
    block = TILE * half
    reps = order_ref.shape[1] // block
    step = flat_ref.shape[0] // half
    group = lax.div(lax.broadcasted_iota(jnp.int32, (block, LANES), 1), LANES // reps)
    spreads = []
    for b in range(step // TILE):
        flat = flat_ref[pl.ds(b * block, block), :].astype(F32)
        groups = [jnp.where(group == r, flat, 0.0).astype(BF16) for r in range(reps)]
        spreads.append(dot_f32(order_ref[...], jnp.concatenate(groups, axis=0), ((1,), (0,))))
    for p in range(half // reps):
        part = jnp.concatenate([x[p * TILE:(p + 1) * TILE] for x in spreads], axis=0)
        core_ref[pl.ds(start, step), p * LANES:(p + 1) * LANES] = part.astype(BF16)


STEP = 32


def slab_copies(snapshot_ref, first, slab_ref, half_index, sem):
    half = slab_ref.shape[1]
    fibers = pl.ds(pl.multiple_of(half_index * half, half), half)

    def copy(start, size):
        return pltpu.make_async_copy(
            snapshot_ref.at[pl.ds(start, size), fibers],
            slab_ref.at[pl.ds(start - first, size)],
            sem,
        )

    def start(begin, size, count):
        for part in range(count):
            copy(begin + part * (size // count), size // count).start()

    return start, lambda begin, size: copy(begin, size).wait()


def send_kernel(
    snapshot_ref, mode2_ref, core_ref, kept_ref, wide_ref, order_ref,
    slab_ref, small_ref, even_ref, odd_ref, sems, kept_sem, small_sem,
):
    cells, half, _ = slab_ref.shape
    rank = mode2_ref.shape[0]
    chunks = cells // STEP
    flat = (even_ref, odd_ref)
    sends = [
        slab_copies(snapshot_ref, 0, slab_ref, 1 - own_half(), sems.at[chunk])
        for chunk in range(chunks)
    ]
    start_kept, wait_kept = slab_copies(snapshot_ref, 0, kept_ref, own_half(), kept_sem)

    small = pltpu.make_async_copy(mode2_ref, small_ref, small_sem)
    small.start()
    for chunk in range(chunks):
        sends[chunk][0](chunk * STEP, STEP, 2 if chunk else 4)
    fill_order(order_ref, half)
    small.wait()
    wide_ref[...] = jnp.concatenate([small_ref[...]] * (LANES // rank), axis=0)
    for chunk in range(chunks):
        sends[chunk][1](chunk * STEP, STEP)
        if chunk == 0:
            start_kept(0, cells, 2 * chunks)
        multiply(slab_ref[pl.ds(chunk * STEP, STEP)], wide_ref, flat[chunk % 2])
        if chunk:
            spread(half, flat[(chunk - 1) % 2], order_ref, core_ref, (chunk - 1) * STEP)
    spread(half, flat[(chunks - 1) % 2], order_ref, core_ref, (chunks - 1) * STEP)
    wait_kept(0, cells)


def contract_send(snapshot, mode2_t):
    cells, fibers, depth = snapshot.shape
    rank = mode2_t.shape[0]
    half = fibers // 2
    reps = LANES // rank
    block = TILE * half
    pinned = pl.BlockSpec(memory_space=pltpu.HBM)
    return pl.pallas_call(
        send_kernel,
        in_specs=[pinned, pinned],
        out_shape=[
            jax.ShapeDtypeStruct((cells, half * rank), BF16),
            jax.ShapeDtypeStruct((cells, half, depth), BF16),
            jax.ShapeDtypeStruct((LANES, depth), BF16),
            jax.ShapeDtypeStruct((block // reps, block * reps), BF16),
        ],
        scratch_shapes=[
            pltpu.VMEM((cells, half, depth), BF16),
            pltpu.VMEM((rank, depth), BF16),
            pltpu.VMEM((STEP * half, LANES), BF16),
            pltpu.VMEM((STEP * half, LANES), BF16),
            pltpu.SemaphoreType.DMA((cells // STEP,)),
            pltpu.SemaphoreType.DMA,
            pltpu.SemaphoreType.DMA,
        ],
        compiler_params=params(24),
        name="contract_send",
    )(snapshot, mode2_t)


def own_kernel(slab_ref, wide_ref, order_ref, core_ref, even_ref, odd_ref):
    cells, half, _ = slab_ref.shape
    flat = (even_ref, odd_ref)
    chunks = cells // STEP
    for chunk in range(chunks):
        multiply(slab_ref[pl.ds(chunk * STEP, STEP)], wide_ref, flat[chunk % 2])
        if chunk:
            spread(half, flat[(chunk - 1) % 2], order_ref, core_ref, (chunk - 1) * STEP)
    spread(half, flat[(chunks - 1) % 2], order_ref, core_ref, (chunks - 1) * STEP)


def contract_own(slab, wide, order):
    cells, half, _ = slab.shape
    reps = order.shape[1] // (TILE * half)
    return pl.pallas_call(
        own_kernel,
        out_shape=jax.ShapeDtypeStruct((cells, half // reps * LANES), BF16),
        scratch_shapes=[pltpu.VMEM((STEP * half, LANES), BF16)] * 2,
        compiler_params=params(24),
        name="contract_own",
    )(slab, wide, order)


def is_even():
    return lax.rem(lax.axis_index("row"), 2) == 0


def project_kernel(own_ref, got_ref, factor_ref, keep_ref, send_ref, mine_ref, give_ref):
    rank = factor_ref.shape[0]
    width = mine_ref.shape[1]
    odd = lax.rem(lax.axis_index("row"), 2)

    def columns(start):
        where = pl.ds(pl.multiple_of(start, width), width)
        return (own_ref[:, where].astype(F32) + got_ref[:, where].astype(F32)).astype(BF16)

    mine = columns(odd * width)
    give = columns((1 - odd) * width)
    mine_ref[...] = mine
    give_ref[...] = give
    keep = dot_f32(factor_ref[...], mine, ((1,), (0,)))
    send = dot_f32(factor_ref[...], give, ((1,), (0,)))
    for block in range(width // LANES):
        where = slice(block * LANES, (block + 1) * LANES)
        rows = pl.ds(block * rank, rank)
        keep_ref[rows, :] = keep[:, where]
        send_ref[rows, :] = send[:, where].astype(BF16)


def project(own, got, factor_t):
    cells, width = own.shape
    rows = factor_t.shape[0] * width // LANES // 2
    columns = jax.ShapeDtypeStruct((cells, width // 2), BF16)
    return pl.pallas_call(
        project_kernel,
        out_shape=[
            jax.ShapeDtypeStruct((rows, LANES), F32),
            jax.ShapeDtypeStruct((rows, LANES), BF16),
            columns,
            columns,
        ],
        compiler_params=params(8),
        name="project",
    )(own, got, factor_t)


def add_kernel(mine_ref, got_ref, *refs):
    total = mine_ref[...].astype(F32) + got_ref[...].astype(F32)
    refs[-1][...] = total.astype(refs[-1].dtype)


def add(mine, got, *after):
    whole = pl.BlockSpec(memory_space=pltpu.VMEM)
    return pl.pallas_call(
        add_kernel,
        in_specs=[whole, whole] + [pl.BlockSpec(memory_space=pl.ANY)] * len(after),
        out_shape=jax.ShapeDtypeStruct(got.shape, got.dtype),
        compiler_params=params(4),
        name="add",
    )(mine, got, *after)


def product_kernel(mine_ref, got_ref, projected_ref, out_ref):
    blocks = mine_ref.shape[1] // LANES
    rank = projected_ref.shape[0] // blocks
    projected = jnp.concatenate(
        [projected_ref[pl.ds(block * rank, rank), :] for block in range(blocks)], axis=1
    )
    terms = [dot_f32(projected, ref[...], ((1,), (1,))) for ref in (mine_ref, got_ref)]
    even = is_even()
    low = jnp.where(even, terms[0], terms[1])
    high = jnp.where(even, terms[1], terms[0])
    out_ref[...] = jnp.concatenate([low, high], axis=0).astype(BF16)


def product_terms(mine, got, projected):
    return pl.pallas_call(
        product_kernel,
        out_shape=jax.ShapeDtypeStruct((LANES, mine.shape[0]), BF16),
        compiler_params=params(4),
        name="product_terms",
    )(mine, got, projected)


def pair_product(term_ref, got_ref):
    return term_ref[...].astype(F32) + got_ref[...].astype(F32)


def gram_kernel(*refs):
    out_ref = refs[-1]
    rank = LANES // 2
    pairs = [pair_product(refs[k], refs[k + 1]) for k in range(0, len(refs) - 1, 2)]
    product = jnp.concatenate([x[k:k + rank] for x in pairs for k in (0, rank)], axis=1)
    gram = dot_parts(product, product, 1)
    out_ref[...] = jnp.concatenate([gram[:rank // 2], gram[rank // 2:]], axis=1)


def local_gram(*terms):
    return pl.pallas_call(
        gram_kernel,
        out_shape=jax.ShapeDtypeStruct((LANES // 4, LANES), F32),
        compiler_params=params(4),
        name="local_gram",
    )(*terms)


def parts(x):
    high = x.astype(BF16)
    return high, (x - high.astype(F32)).astype(BF16)


def dot_parts(a, b, axis):
    (ah, al), (bh, bl) = parts(a), parts(b)
    left = jnp.concatenate([ah, ah, al], axis=axis)
    right = jnp.concatenate([bh, bl, bh], axis=axis)
    return dot_f32(left, right, ((axis,), (axis,)))


def eliminate(packed):
    rank = packed.shape[1] // 2
    tile = 8
    count = rank // tile
    wide = 2 * rank
    sublane = lax.broadcasted_iota(jnp.int32, (tile, wide), 0)
    lane = lax.broadcasted_iota(jnp.int32, (tile, wide), 1)
    full = lambda x: jnp.broadcast_to(x, (tile, wide))
    both = []
    for v in range(count):
        at = v % (count // 2) * tile
        mine = packed[at:at + tile]
        if v >= count // 2:
            mine = jnp.concatenate([mine[:, rank:], mine[:, :rank]], axis=1)
        both.append(jnp.where(lane < rank, mine, (lane - rank == sublane + v * tile).astype(F32)))
    pivots = []
    for p in range(count):
        cols = [
            {v: full(both[v][:, p * tile + j:p * tile + j + 1]) for v in range(p, count)}
            for j in range(tile)
        ]
        rows = [full(both[p][j:j + 1]) for j in range(tile)]
        block = [[full(cols[k][p][j:j + 1]) for k in range(j + 1)] for j in range(tile)]
        found, kept = block[0][0], rows[0]
        for j in range(tile):
            if j:
                found = jnp.where(sublane == j, block[j][j], found)
                kept = jnp.where(sublane == j, rows[j], kept)
            inverse = pl.reciprocal(block[j][j], approx=True, full_range=False)
            scaled = {i: block[i][j] * inverse for i in range(j + 1, tile)}
            for i, factor in scaled.items():
                for k in range(j + 1, i + 1):
                    block[i][k] = block[i][k] - factor * block[k][j]
                rows[i] = rows[i] - factor * rows[j]
            row = rows[j] * inverse
            for v in range(p + 1, count):
                for i, factor in scaled.items():
                    cols[i][v] = cols[i][v] - factor * cols[j][v]
                both[v] = both[v] - cols[j][v] * row
        both[p] = kept
        pivots.append(found)
    return both, pivots


def finish_kernel(total_rows, term_ref, got_term_ref, gram_ref, got_gram_ref, out_ref):
    rank = LANES // 2
    both, pivots = eliminate(gram_ref[...] + got_gram_ref[...])
    scale = total_rows ** 0.5
    inverse = jnp.concatenate([b * (lax.rsqrt(p) * scale) for b, p in zip(both, pivots)], axis=0)
    inverse = inverse[:, rank:]
    half = term_ref.shape[1] // 2
    product = pair_product(term_ref, got_term_ref)
    product = jnp.where(is_even(), product[:rank], product[rank:])
    mine = jnp.where(lax.axis_index("col") == 0, product[:, :half], product[:, half:]).T
    out_ref[...] = dot_parts(mine, inverse, 1)


def finish(total_rows, term, got_term, gram, got_gram):
    return pl.pallas_call(
        functools.partial(finish_kernel, total_rows),
        out_shape=jax.ShapeDtypeStruct((term.shape[1] // 2, LANES // 2), F32),
        compiler_params=params(4),
        name="finish",
    )(term, got_term, gram, got_gram)


def per_device(snapshot, mode2_factor, old_factor):
    n_rows, n_cols = lax.axis_size("row"), lax.axis_size("col")
    masks = [1 << bit for bit in range(n_rows.bit_length() - 1)]
    total_rows = snapshot.shape[0] * n_rows

    def swap(x, mask, other=None):
        pairs = []
        for r in range(n_rows):
            for c in range(n_cols):
                second = (c + r.bit_count()) % 2 and other is not None
                to = r ^ (other if second else mask)
                pairs.append((r * n_cols + c, to * n_cols + (c + 1) % n_cols))
        return lax.ppermute(x, ("row", "col"), pairs)

    snapshot = pltpu.with_memory_space_constraint(snapshot, pltpu.HBM)
    mode2_t = pltpu.with_memory_space_constraint(mode2_factor.T, pltpu.HBM)
    send, kept, wide, order = contract_send(snapshot, mode2_t)
    got = swap(send, 0)
    own = contract_own(kept, wide, order)

    keep, send, columns, give = project(own, got, old_factor.T)
    mine = add(keep, swap(send, masks[0]))
    got_columns = swap(give, masks[0])
    others = masks[1:]
    turned = others[len(others) // 2:] + others[:len(others) // 2]
    for step, (mask, other) in enumerate(zip(others, turned)):
        after = [got_columns] if step == 1 else []
        mine = add(mine, swap(mine, mask, other), *after)

    term = product_terms(columns, got_columns, mine)
    term = add(term, swap(term, 0))
    pair, next_pair = masks[:2]
    got_term = swap(term, pair)
    gram = local_gram(term, got_term, swap(term, next_pair), swap(term, pair | next_pair))
    for mask in masks[2:-1]:
        gram = add(gram, swap(gram, mask))
    return finish(total_rows, term, got_term, gram, swap(gram, masks[-1]))


def solution(mesh):
    return jax.shard_map(
        per_device,
        mesh=mesh,
        in_specs=(
            P(("groups", "row"), None, "col"),
            P(("groups", "col"), None),
            P(("groups", "row"), None),
        ),
        out_specs=P(("groups", "row", "col"), None),
        check_vma=False,
    )
```

```python
import functools

import jax
import jax.numpy as jnp
from jax import lax
from jax.experimental import pallas as pl
from jax.experimental.pallas import tpu as pltpu
from jax.sharding import PartitionSpec as P

F32 = jnp.float32
BF16 = jnp.bfloat16
LANES = 128
MIB = 2**20


def dot_f32(a, b, dims, precision=None):
    return lax.dot_general(a, b, (dims, ((), ())), precision=precision, preferred_element_type=F32)


def params(mib):
    return pltpu.CompilerParams(vmem_limit_bytes=mib * MIB)


def own_half():
    row = lax.axis_index("row")
    half = lax.axis_index("col")
    for bit in range(lax.axis_size("row").bit_length() - 1):
        half += lax.rem(lax.div(row, 1 << bit), 2)
    return lax.rem(half, 2)


TILE = 8


def fill_order(order_ref, half):
    block = TILE * half
    to = lax.broadcasted_iota(jnp.int32, order_ref.shape, 0)
    at = lax.broadcasted_iota(jnp.int32, order_ref.shape, 1)
    cell = lax.div(lax.rem(at, block), half)
    wanted = lax.div(to, TILE) * (order_ref.shape[1] // block) + lax.div(at, block)
    same = (lax.rem(to, TILE) == cell) & (wanted == lax.rem(at, half))
    order_ref[...] = same.astype(F32).astype(BF16)


def multiply(slab, wide_ref, flat_ref):
    cells, half, depth = slab.shape
    x = slab.reshape(cells * half, depth)
    low = dot_f32(x[:, :depth // 2], wide_ref[:, :depth // 2], ((1,), (1,)))
    high = dot_f32(x[:, depth // 2:], wide_ref[:, depth // 2:], ((1,), (1,)))
    flat_ref[...] = (low + high).astype(BF16)


def spread(half, flat_ref, order_ref, core_ref, start):
    block = TILE * half
    reps = order_ref.shape[1] // block
    step = flat_ref.shape[0] // half
    group = lax.div(lax.broadcasted_iota(jnp.int32, (block, LANES), 1), LANES // reps)
    spreads = []
    for b in range(step // TILE):
        flat = flat_ref[pl.ds(b * block, block), :].astype(F32)
        groups = [jnp.where(group == r, flat, 0.0).astype(BF16) for r in range(reps)]
        spreads.append(dot_f32(order_ref[...], jnp.concatenate(groups, axis=0), ((1,), (0,))))
    for p in range(half // reps):
        part = jnp.concatenate([x[p * TILE:(p + 1) * TILE] for x in spreads], axis=0)
        core_ref[pl.ds(start, step), p * LANES:(p + 1) * LANES] = part.astype(BF16)


STEP = 32


def slab_copies(snapshot_ref, first, slab_ref, half_index, sem, priority):
    half = slab_ref.shape[1]
    fibers = pl.ds(pl.multiple_of(half_index * half, half), half)

    def copy(start, size):
        return pltpu.make_async_copy(
            snapshot_ref.at[pl.ds(start, size), fibers],
            slab_ref.at[pl.ds(start - first, size)],
            sem,
        )

    def start(begin, size, count):
        for part in range(count):
            copy(begin + part * (size // count), size // count).start(priority=priority)

    return start, lambda begin, size: copy(begin, size).wait()


def send_kernel(
    snapshot_ref, mode2_ref, core_ref, kept_ref, wide_ref, order_ref,
    slab_ref, small_ref, even_ref, odd_ref, sems, kept_sem, small_sem,
):
    cells, half, _ = slab_ref.shape
    rank = mode2_ref.shape[0]
    chunks = cells // STEP
    flat = (even_ref, odd_ref)
    sends = [
        slab_copies(snapshot_ref, 0, slab_ref, 1 - own_half(), sems.at[chunk], 1)
        for chunk in range(chunks)
    ]
    start_kept, wait_kept = slab_copies(snapshot_ref, 0, kept_ref, own_half(), kept_sem, 0)

    small = pltpu.make_async_copy(mode2_ref, small_ref, small_sem)
    small.start()
    for chunk in range(chunks):
        sends[chunk][0](chunk * STEP, STEP, 2 if chunk else 4)
    start_kept(0, cells, 2 * chunks)
    fill_order(order_ref, half)
    small.wait()
    wide_ref[...] = jnp.concatenate([small_ref[...]] * (LANES // rank), axis=0)
    for chunk in range(chunks):
        sends[chunk][1](chunk * STEP, STEP)
        multiply(slab_ref[pl.ds(chunk * STEP, STEP)], wide_ref, flat[chunk % 2])
        if chunk:
            spread(half, flat[(chunk - 1) % 2], order_ref, core_ref, (chunk - 1) * STEP)
    spread(half, flat[(chunks - 1) % 2], order_ref, core_ref, (chunks - 1) * STEP)
    wait_kept(0, cells)


def contract_send(snapshot, mode2_t):
    cells, fibers, depth = snapshot.shape
    rank = mode2_t.shape[0]
    half = fibers // 2
    reps = LANES // rank
    block = TILE * half
    pinned = pl.BlockSpec(memory_space=pltpu.HBM)
    return pl.pallas_call(
        send_kernel,
        in_specs=[pinned, pinned],
        out_shape=[
            jax.ShapeDtypeStruct((cells, half * rank), BF16),
            jax.ShapeDtypeStruct((cells, half, depth), BF16),
            jax.ShapeDtypeStruct((LANES, depth), BF16),
            jax.ShapeDtypeStruct((block // reps, block * reps), BF16),
        ],
        scratch_shapes=[
            pltpu.VMEM((cells, half, depth), BF16),
            pltpu.VMEM((rank, depth), BF16),
            pltpu.VMEM((STEP * half, LANES), BF16),
            pltpu.VMEM((STEP * half, LANES), BF16),
            pltpu.SemaphoreType.DMA((cells // STEP,)),
            pltpu.SemaphoreType.DMA,
            pltpu.SemaphoreType.DMA,
        ],
        compiler_params=params(24),
        name="contract_send",
    )(snapshot, mode2_t)


def own_kernel(slab_ref, wide_ref, order_ref, core_ref, even_ref, odd_ref):
    cells, half, _ = slab_ref.shape
    flat = (even_ref, odd_ref)
    chunks = cells // STEP
    for chunk in range(chunks):
        multiply(slab_ref[pl.ds(chunk * STEP, STEP)], wide_ref, flat[chunk % 2])
        if chunk:
            spread(half, flat[(chunk - 1) % 2], order_ref, core_ref, (chunk - 1) * STEP)
    spread(half, flat[(chunks - 1) % 2], order_ref, core_ref, (chunks - 1) * STEP)


def contract_own(slab, wide, order):
    cells, half, _ = slab.shape
    reps = order.shape[1] // (TILE * half)
    return pl.pallas_call(
        own_kernel,
        out_shape=jax.ShapeDtypeStruct((cells, half // reps * LANES), BF16),
        scratch_shapes=[pltpu.VMEM((STEP * half, LANES), BF16)] * 2,
        compiler_params=params(24),
        name="contract_own",
    )(slab, wide, order)


def is_even():
    return lax.rem(lax.axis_index("row"), 2) == 0


def project_kernel(kept, own_ref, got_ref, factor_ref, projected_ref, core_ref):
    rank = factor_ref.shape[0]
    width = core_ref.shape[1]
    odd = lax.rem(lax.axis_index("row"), 2)
    start = odd * width if kept else (1 - odd) * width
    where = pl.ds(pl.multiple_of(start, width), width)
    core = (own_ref[:, where].astype(F32) + got_ref[:, where].astype(F32)).astype(BF16)
    core_ref[...] = core
    projected = dot_f32(factor_ref[...], core, ((1,), (0,)))
    for block in range(width // LANES):
        part = projected[:, block * LANES:(block + 1) * LANES]
        projected_ref[pl.ds(block * rank, rank), :] = part.astype(projected_ref.dtype)


def project(own, got, factor_t, kept):
    cells, width = own.shape
    rows = factor_t.shape[0] * width // LANES // 2
    return pl.pallas_call(
        functools.partial(project_kernel, kept),
        out_shape=[
            jax.ShapeDtypeStruct((rows, LANES), F32 if kept else BF16),
            jax.ShapeDtypeStruct((cells, width // 2), BF16),
        ],
        compiler_params=params(8),
        name="project_kept" if kept else "project_sent",
    )(own, got, factor_t)


def add_kernel(mine_ref, got_ref, *refs):
    total = mine_ref[...].astype(F32) + got_ref[...].astype(F32)
    refs[-1][...] = total.astype(refs[-1].dtype)


def add(mine, got, *after):
    whole = pl.BlockSpec(memory_space=pltpu.VMEM)
    return pl.pallas_call(
        add_kernel,
        in_specs=[whole, whole] + [pl.BlockSpec(memory_space=pl.ANY)] * len(after),
        out_shape=jax.ShapeDtypeStruct(got.shape, got.dtype),
        compiler_params=params(4),
        name="add",
    )(mine, got, *after)


def product_kernel(mine_ref, got_ref, projected_ref, out_ref):
    blocks = mine_ref.shape[1] // LANES
    rank = projected_ref.shape[0] // blocks
    projected = jnp.concatenate(
        [projected_ref[pl.ds(block * rank, rank), :] for block in range(blocks)], axis=1
    )
    terms = [dot_f32(projected, ref[...], ((1,), (1,))) for ref in (mine_ref, got_ref)]
    even = is_even()
    low = jnp.where(even, terms[0], terms[1])
    high = jnp.where(even, terms[1], terms[0])
    out_ref[...] = jnp.concatenate([low, high], axis=0).astype(BF16)


def product_terms(mine, got, projected):
    return pl.pallas_call(
        product_kernel,
        out_shape=jax.ShapeDtypeStruct((LANES, mine.shape[0]), BF16),
        compiler_params=params(4),
        name="product_terms",
    )(mine, got, projected)


def pair_product(term_ref, got_ref):
    return term_ref[...].astype(F32) + got_ref[...].astype(F32)


def gram_kernel(*refs):
    out_ref = refs[-1]
    rank = LANES // 2
    pairs = [pair_product(refs[k], refs[k + 1]) for k in range(0, len(refs) - 1, 2)]
    product = jnp.concatenate([x[k:k + rank] for x in pairs for k in (0, rank)], axis=1)
    gram = dot_parts(product, product, 1)
    out_ref[...] = jnp.concatenate([gram[:rank // 2], gram[rank // 2:]], axis=1)


def local_gram(*terms):
    return pl.pallas_call(
        gram_kernel,
        out_shape=jax.ShapeDtypeStruct((LANES // 4, LANES), F32),
        compiler_params=params(4),
        name="local_gram",
    )(*terms)


def parts(x):
    high = x.astype(BF16)
    return high, (x - high.astype(F32)).astype(BF16)


def dot_parts(a, b, axis):
    (ah, al), (bh, bl) = parts(a), parts(b)
    left = jnp.concatenate([ah, ah, al], axis=axis)
    right = jnp.concatenate([bh, bl, bh], axis=axis)
    return dot_f32(left, right, ((axis,), (axis,)))


def eliminate(packed):
    rank = packed.shape[1] // 2
    tile = 8
    count = rank // tile
    wide = 2 * rank
    sublane = lax.broadcasted_iota(jnp.int32, (tile, wide), 0)
    lane = lax.broadcasted_iota(jnp.int32, (tile, wide), 1)
    full = lambda x: jnp.broadcast_to(x, (tile, wide))
    both = []
    for v in range(count):
        at = v % (count // 2) * tile
        mine = packed[at:at + tile]
        if v >= count // 2:
            mine = jnp.concatenate([mine[:, rank:], mine[:, :rank]], axis=1)
        both.append(jnp.where(lane < rank, mine, (lane - rank == sublane + v * tile).astype(F32)))
    pivots = []
    for p in range(count):
        cols = [
            {v: full(both[v][:, p * tile + j:p * tile + j + 1]) for v in range(p, count)}
            for j in range(tile)
        ]
        rows = [full(both[p][j:j + 1]) for j in range(tile)]
        block = [[full(cols[k][p][j:j + 1]) for k in range(j + 1)] for j in range(tile)]
        found, kept = block[0][0], rows[0]
        for j in range(tile):
            if j:
                found = jnp.where(sublane == j, block[j][j], found)
                kept = jnp.where(sublane == j, rows[j], kept)
            inverse = pl.reciprocal(block[j][j], approx=True, full_range=False)
            scaled = {i: block[i][j] * inverse for i in range(j + 1, tile)}
            for i, factor in scaled.items():
                for k in range(j + 1, i + 1):
                    block[i][k] = block[i][k] - factor * block[k][j]
                rows[i] = rows[i] - factor * rows[j]
            row = rows[j] * inverse
            for v in range(p + 1, count):
                for i, factor in scaled.items():
                    cols[i][v] = cols[i][v] - factor * cols[j][v]
                both[v] = both[v] - cols[j][v] * row
        both[p] = kept
        pivots.append(found)
    return both, pivots


def finish_kernel(total_rows, term_ref, got_term_ref, gram_ref, got_gram_ref, out_ref):
    rank = LANES // 2
    both, pivots = eliminate(gram_ref[...] + got_gram_ref[...])
    scale = total_rows ** 0.5
    inverse = jnp.concatenate([b * (lax.rsqrt(p) * scale) for b, p in zip(both, pivots)], axis=0)
    inverse = inverse[:, rank:]
    half = term_ref.shape[1] // 2
    product = pair_product(term_ref, got_term_ref)
    product = jnp.where(is_even(), product[:rank], product[rank:])
    mine = jnp.where(lax.axis_index("col") == 0, product[:, :half], product[:, half:]).T
    out_ref[...] = dot_parts(mine, inverse, 1)


def finish(total_rows, term, got_term, gram, got_gram):
    return pl.pallas_call(
        functools.partial(finish_kernel, total_rows),
        out_shape=jax.ShapeDtypeStruct((term.shape[1] // 2, LANES // 2), F32),
        compiler_params=params(4),
        name="finish",
    )(term, got_term, gram, got_gram)


def per_device(snapshot, mode2_factor, old_factor):
    n_rows, n_cols = lax.axis_size("row"), lax.axis_size("col")
    masks = [1 << bit for bit in range(n_rows.bit_length() - 1)]
    total_rows = snapshot.shape[0] * n_rows

    def swap(x, mask, other=None):
        pairs = []
        for r in range(n_rows):
            for c in range(n_cols):
                second = (c + r.bit_count()) % 2 and other is not None
                to = r ^ (other if second else mask)
                pairs.append((r * n_cols + c, to * n_cols + (c + 1) % n_cols))
        return lax.ppermute(x, ("row", "col"), pairs)

    snapshot = pltpu.with_memory_space_constraint(snapshot, pltpu.HBM)
    mode2_t = pltpu.with_memory_space_constraint(mode2_factor.T, pltpu.HBM)
    send, kept, wide, order = contract_send(snapshot, mode2_t)
    got = swap(send, 0)
    own = contract_own(kept, wide, order)

    send, give = project(own, got, old_factor.T, False)
    keep, columns = project(own, got, old_factor.T, True)
    mine = add(keep, swap(send, masks[0]))
    got_columns = swap(give, masks[0])
    others = masks[1:]
    turned = others[len(others) // 2:] + others[:len(others) // 2]
    for step, (mask, other) in enumerate(zip(others, turned)):
        after = [got_columns] if step == 1 else []
        mine = add(mine, swap(mine, mask, other), *after)

    term = product_terms(columns, got_columns, mine)
    term = add(term, swap(term, 0))
    pair, next_pair = masks[:2]
    got_term = swap(term, pair)
    gram = local_gram(term, got_term, swap(term, next_pair), swap(term, pair | next_pair))
    for mask in masks[2:-1]:
        gram = add(gram, swap(gram, mask))
    return finish(total_rows, term, got_term, gram, swap(gram, masks[-1]))


def solution(mesh):
    return jax.shard_map(
        per_device,
        mesh=mesh,
        in_specs=(
            P(("groups", "row"), None, "col"),
            P(("groups", "col"), None),
            P(("groups", "row"), None),
        ),
        out_specs=P(("groups", "row", "col"), None),
        check_vma=False,
    )
```

```python
import functools

import jax
import jax.numpy as jnp
from jax import lax
from jax.experimental import pallas as pl
from jax.experimental.pallas import tpu as pltpu
from jax.sharding import PartitionSpec as P

F32 = jnp.float32
BF16 = jnp.bfloat16
LANES = 128
MIB = 2**20


def dot_f32(a, b, dims, precision=None):
    return lax.dot_general(a, b, (dims, ((), ())), precision=precision, preferred_element_type=F32)


def params(mib):
    return pltpu.CompilerParams(vmem_limit_bytes=mib * MIB)


def row_masks(n_rows):
    masks = [1 << bit for bit in range(n_rows.bit_length() - 1)]
    return masks[:-1] + [masks[-1] | masks[-2]]


def half_of(row, col, n_rows):
    bits = n_rows.bit_length() - 2
    return (col + sum((row // (1 << bit)) % 2 for bit in range(bits))) % 2


def own_half():
    return half_of(lax.axis_index("row"), lax.axis_index("col"), lax.axis_size("row"))


TILE = 8


def fill_order(order_ref, half):
    block = TILE * half
    to = lax.broadcasted_iota(jnp.int32, order_ref.shape, 0)
    at = lax.broadcasted_iota(jnp.int32, order_ref.shape, 1)
    cell = lax.div(lax.rem(at, block), half)
    wanted = lax.div(to, TILE) * (order_ref.shape[1] // block) + lax.div(at, block)
    same = (lax.rem(to, TILE) == cell) & (wanted == lax.rem(at, half))
    order_ref[...] = same.astype(F32).astype(BF16)


def multiply(slab, wide_ref, flat_ref):
    cells, half, depth = slab.shape
    x = slab.reshape(cells * half, depth)
    low = dot_f32(x[:, :depth // 2], wide_ref[:, :depth // 2], ((1,), (1,)))
    high = dot_f32(x[:, depth // 2:], wide_ref[:, depth // 2:], ((1,), (1,)))
    flat_ref[...] = (low + high).astype(BF16)


def spread(half, flat_ref, order_ref, core_ref, start):
    block = TILE * half
    reps = order_ref.shape[1] // block
    step = flat_ref.shape[0] // half
    group = lax.div(lax.broadcasted_iota(jnp.int32, (block, LANES), 1), LANES // reps)
    spreads = []
    for b in range(step // TILE):
        flat = flat_ref[pl.ds(b * block, block), :].astype(F32)
        groups = [jnp.where(group == r, flat, 0.0).astype(BF16) for r in range(reps)]
        spreads.append(dot_f32(order_ref[...], jnp.concatenate(groups, axis=0), ((1,), (0,))))
    for p in range(half // reps):
        part = jnp.concatenate([x[p * TILE:(p + 1) * TILE] for x in spreads], axis=0)
        core_ref[pl.ds(start, step), p * LANES:(p + 1) * LANES] = part.astype(BF16)


STEP = 32


def slab_copies(snapshot_ref, first, slab_ref, half_index, sem):
    half = slab_ref.shape[1]
    fibers = pl.ds(pl.multiple_of(half_index * half, half), half)

    def copy(start, size):
        return pltpu.make_async_copy(
            snapshot_ref.at[pl.ds(start, size), fibers],
            slab_ref.at[pl.ds(start - first, size)],
            sem,
        )

    def start(begin, size, count):
        for part in range(count):
            copy(begin + part * (size // count), size // count).start()

    return start, lambda begin, size: copy(begin, size).wait()


def send_kernel(
    snapshot_ref, mode2_ref, core_ref, kept_ref, wide_ref, order_ref,
    slab_ref, small_ref, even_ref, odd_ref, sems, kept_sem, small_sem,
):
    cells, half, _ = slab_ref.shape
    rank = mode2_ref.shape[0]
    chunks = cells // STEP
    flat = (even_ref, odd_ref)
    sends = [
        slab_copies(snapshot_ref, 0, slab_ref, 1 - own_half(), sems.at[chunk])
        for chunk in range(chunks)
    ]
    start_kept, wait_kept = slab_copies(snapshot_ref, 0, kept_ref, own_half(), kept_sem)

    small = pltpu.make_async_copy(mode2_ref, small_ref, small_sem)
    small.start()
    for chunk in range(chunks):
        sends[chunk][0](chunk * STEP, STEP, 2 if chunk else 4)
    fill_order(order_ref, half)
    small.wait()
    wide_ref[...] = jnp.concatenate([small_ref[...]] * (LANES // rank), axis=0)
    for chunk in range(chunks):
        sends[chunk][1](chunk * STEP, STEP)
        if chunk == 0:
            start_kept(0, cells, 2 * chunks)
        multiply(slab_ref[pl.ds(chunk * STEP, STEP)], wide_ref, flat[chunk % 2])
        if chunk:
            spread(half, flat[(chunk - 1) % 2], order_ref, core_ref, (chunk - 1) * STEP)
    spread(half, flat[(chunks - 1) % 2], order_ref, core_ref, (chunks - 1) * STEP)
    wait_kept(0, cells)


def contract_send(snapshot, mode2_t):
    cells, fibers, depth = snapshot.shape
    rank = mode2_t.shape[0]
    half = fibers // 2
    reps = LANES // rank
    block = TILE * half
    pinned = pl.BlockSpec(memory_space=pltpu.HBM)
    return pl.pallas_call(
        send_kernel,
        in_specs=[pinned, pinned],
        out_shape=[
            jax.ShapeDtypeStruct((cells, half * rank), BF16),
            jax.ShapeDtypeStruct((cells, half, depth), BF16),
            jax.ShapeDtypeStruct((LANES, depth), BF16),
            jax.ShapeDtypeStruct((block // reps, block * reps), BF16),
        ],
        scratch_shapes=[
            pltpu.VMEM((cells, half, depth), BF16),
            pltpu.VMEM((rank, depth), BF16),
            pltpu.VMEM((STEP * half, LANES), BF16),
            pltpu.VMEM((STEP * half, LANES), BF16),
            pltpu.SemaphoreType.DMA((cells // STEP,)),
            pltpu.SemaphoreType.DMA,
            pltpu.SemaphoreType.DMA,
        ],
        compiler_params=params(24),
        name="contract_send",
    )(snapshot, mode2_t)


def own_kernel(slab_ref, wide_ref, order_ref, core_ref, even_ref, odd_ref):
    cells, half, _ = slab_ref.shape
    flat = (even_ref, odd_ref)
    chunks = cells // STEP
    for chunk in range(chunks):
        multiply(slab_ref[pl.ds(chunk * STEP, STEP)], wide_ref, flat[chunk % 2])
        if chunk:
            spread(half, flat[(chunk - 1) % 2], order_ref, core_ref, (chunk - 1) * STEP)
    spread(half, flat[(chunks - 1) % 2], order_ref, core_ref, (chunks - 1) * STEP)


def contract_own(slab, wide, order):
    cells, half, _ = slab.shape
    reps = order.shape[1] // (TILE * half)
    return pl.pallas_call(
        own_kernel,
        out_shape=jax.ShapeDtypeStruct((cells, half // reps * LANES), BF16),
        scratch_shapes=[pltpu.VMEM((STEP * half, LANES), BF16)] * 2,
        compiler_params=params(24),
        name="contract_own",
    )(slab, wide, order)


def is_even():
    return lax.rem(lax.axis_index("row"), 2) == 0


def project_kernel(own_ref, got_ref, factor_ref, keep_ref, send_ref, mine_ref, give_ref):
    rank = factor_ref.shape[0]
    width = mine_ref.shape[1]
    odd = lax.rem(lax.axis_index("row"), 2)

    def columns(start):
        where = pl.ds(pl.multiple_of(start, width), width)
        return (own_ref[:, where].astype(F32) + got_ref[:, where].astype(F32)).astype(BF16)

    mine = columns(odd * width)
    give = columns((1 - odd) * width)
    mine_ref[...] = mine
    give_ref[...] = give
    keep = dot_f32(factor_ref[...], mine, ((1,), (0,)))
    send = dot_f32(factor_ref[...], give, ((1,), (0,)))
    for block in range(width // LANES):
        where = slice(block * LANES, (block + 1) * LANES)
        rows = pl.ds(block * rank, rank)
        keep_ref[rows, :] = keep[:, where]
        send_ref[rows, :] = send[:, where].astype(BF16)


def project(own, got, factor_t):
    cells, width = own.shape
    rows = factor_t.shape[0] * width // LANES // 2
    columns = jax.ShapeDtypeStruct((cells, width // 2), BF16)
    return pl.pallas_call(
        project_kernel,
        out_shape=[
            jax.ShapeDtypeStruct((rows, LANES), F32),
            jax.ShapeDtypeStruct((rows, LANES), BF16),
            columns,
            columns,
        ],
        compiler_params=params(8),
        name="project",
    )(own, got, factor_t)


def add_kernel(mine_ref, got_ref, *refs):
    total = mine_ref[...].astype(F32) + got_ref[...].astype(F32)
    refs[-1][...] = total.astype(refs[-1].dtype)


def add(mine, got, *after):
    whole = pl.BlockSpec(memory_space=pltpu.VMEM)
    return pl.pallas_call(
        add_kernel,
        in_specs=[whole, whole] + [pl.BlockSpec(memory_space=pl.ANY)] * len(after),
        out_shape=jax.ShapeDtypeStruct(got.shape, got.dtype),
        compiler_params=params(4),
        name="add",
    )(mine, got, *after)


def product_kernel(mine_ref, got_ref, projected_ref, out_ref):
    blocks = mine_ref.shape[1] // LANES
    rank = projected_ref.shape[0] // blocks
    projected = jnp.concatenate(
        [projected_ref[pl.ds(block * rank, rank), :] for block in range(blocks)], axis=1
    )
    terms = [dot_f32(projected, ref[...], ((1,), (1,))) for ref in (mine_ref, got_ref)]
    even = is_even()
    low = jnp.where(even, terms[0], terms[1])
    high = jnp.where(even, terms[1], terms[0])
    out_ref[...] = jnp.concatenate([low, high], axis=0).astype(BF16)


def product_terms(mine, got, projected):
    return pl.pallas_call(
        product_kernel,
        out_shape=jax.ShapeDtypeStruct((LANES, mine.shape[0]), BF16),
        compiler_params=params(4),
        name="product_terms",
    )(mine, got, projected)


def pair_product(term_ref, got_ref):
    return term_ref[...].astype(F32) + got_ref[...].astype(F32)


def gram_kernel(*refs):
    out_ref = refs[-1]
    rank = LANES // 2
    pairs = [pair_product(refs[k], refs[k + 1]) for k in range(0, len(refs) - 1, 2)]
    product = jnp.concatenate([x[k:k + rank] for x in pairs for k in (0, rank)], axis=1)
    gram = dot_parts(product, product, 1)
    out_ref[...] = jnp.concatenate([gram[:rank // 2], gram[rank // 2:]], axis=1)


def local_gram(*terms):
    return pl.pallas_call(
        gram_kernel,
        out_shape=jax.ShapeDtypeStruct((LANES // 4, LANES), F32),
        compiler_params=params(4),
        name="local_gram",
    )(*terms)


def parts(x):
    high = x.astype(BF16)
    return high, (x - high.astype(F32)).astype(BF16)


def dot_parts(a, b, axis):
    (ah, al), (bh, bl) = parts(a), parts(b)
    left = jnp.concatenate([ah, ah, al], axis=axis)
    right = jnp.concatenate([bh, bl, bh], axis=axis)
    return dot_f32(left, right, ((axis,), (axis,)))


def eliminate(packed):
    rank = packed.shape[1] // 2
    tile = 8
    count = rank // tile
    wide = 2 * rank
    sublane = lax.broadcasted_iota(jnp.int32, (tile, wide), 0)
    lane = lax.broadcasted_iota(jnp.int32, (tile, wide), 1)
    full = lambda x: jnp.broadcast_to(x, (tile, wide))
    both = []
    for v in range(count):
        at = v % (count // 2) * tile
        mine = packed[at:at + tile]
        if v >= count // 2:
            mine = jnp.concatenate([mine[:, rank:], mine[:, :rank]], axis=1)
        both.append(jnp.where(lane < rank, mine, (lane - rank == sublane + v * tile).astype(F32)))
    pivots = []
    for p in range(count):
        cols = [
            {v: full(both[v][:, p * tile + j:p * tile + j + 1]) for v in range(p, count)}
            for j in range(tile)
        ]
        rows = [full(both[p][j:j + 1]) for j in range(tile)]
        block = [[full(cols[k][p][j:j + 1]) for k in range(j + 1)] for j in range(tile)]
        found, kept = block[0][0], rows[0]
        for j in range(tile):
            if j:
                found = jnp.where(sublane == j, block[j][j], found)
                kept = jnp.where(sublane == j, rows[j], kept)
            inverse = pl.reciprocal(block[j][j], approx=True, full_range=False)
            scaled = {i: block[i][j] * inverse for i in range(j + 1, tile)}
            for i, factor in scaled.items():
                for k in range(j + 1, i + 1):
                    block[i][k] = block[i][k] - factor * block[k][j]
                rows[i] = rows[i] - factor * rows[j]
            row = rows[j] * inverse
            for v in range(p + 1, count):
                for i, factor in scaled.items():
                    cols[i][v] = cols[i][v] - factor * cols[j][v]
                both[v] = both[v] - cols[j][v] * row
        both[p] = kept
        pivots.append(found)
    return both, pivots


def finish_kernel(total_rows, term_ref, got_term_ref, gram_ref, got_gram_ref, out_ref):
    rank = LANES // 2
    both, pivots = eliminate(gram_ref[...] + got_gram_ref[...])
    scale = total_rows ** 0.5
    inverse = jnp.concatenate([b * (lax.rsqrt(p) * scale) for b, p in zip(both, pivots)], axis=0)
    inverse = inverse[:, rank:]
    half = term_ref.shape[1] // 2
    product = pair_product(term_ref, got_term_ref)
    product = jnp.where(is_even(), product[:rank], product[rank:])
    mine = jnp.where(lax.axis_index("col") == 0, product[:, :half], product[:, half:]).T
    out_ref[...] = dot_parts(mine, inverse, 1)


def finish(total_rows, term, got_term, gram, got_gram):
    return pl.pallas_call(
        functools.partial(finish_kernel, total_rows),
        out_shape=jax.ShapeDtypeStruct((term.shape[1] // 2, LANES // 2), F32),
        compiler_params=params(4),
        name="finish",
    )(term, got_term, gram, got_gram)


def per_device(snapshot, mode2_factor, old_factor):
    n_rows, n_cols = lax.axis_size("row"), lax.axis_size("col")
    masks = row_masks(n_rows)
    total_rows = snapshot.shape[0] * n_rows

    def swap(x, mask, other=None):
        pairs = []
        for r in range(n_rows):
            for c in range(n_cols):
                second = half_of(r, c, n_rows) and other is not None
                to = r ^ (other if second else mask)
                pairs.append((r * n_cols + c, to * n_cols + (c + 1) % n_cols))
        return lax.ppermute(x, ("row", "col"), pairs)

    snapshot = pltpu.with_memory_space_constraint(snapshot, pltpu.HBM)
    mode2_t = pltpu.with_memory_space_constraint(mode2_factor.T, pltpu.HBM)
    send, kept, wide, order = contract_send(snapshot, mode2_t)
    got = swap(send, 0)
    own = contract_own(kept, wide, order)

    keep, send, columns, give = project(own, got, old_factor.T)
    mine = add(keep, swap(send, masks[0]))
    got_columns = swap(give, masks[0])
    others = masks[1:]
    turned = others[len(others) // 2:] + others[:len(others) // 2]
    for step, (mask, other) in enumerate(zip(others, turned)):
        after = [got_columns] if step == 1 else []
        mine = add(mine, swap(mine, mask, other), *after)

    term = product_terms(columns, got_columns, mine)
    term = add(term, swap(term, 0))
    pair, next_pair = masks[:2]
    got_term = swap(term, pair)
    gram = local_gram(term, got_term, swap(term, next_pair), swap(term, pair | next_pair))
    for mask in masks[2:-1]:
        gram = add(gram, swap(gram, mask))
    return finish(total_rows, term, got_term, gram, swap(gram, masks[-1]))


def solution(mesh):
    return jax.shard_map(
        per_device,
        mesh=mesh,
        in_specs=(
            P(("groups", "row"), None, "col"),
            P(("groups", "col"), None),
            P(("groups", "row"), None),
        ),
        out_specs=P(("groups", "row", "col"), None),
        check_vma=False,
    )
```

```python
import functools

import jax
import jax.numpy as jnp
from jax import lax
from jax.experimental import pallas as pl
from jax.experimental.pallas import tpu as pltpu
from jax.sharding import PartitionSpec as P

F32 = jnp.float32
BF16 = jnp.bfloat16
LANES = 128
MIB = 2**20


def dot_f32(a, b, dims, precision=None):
    return lax.dot_general(a, b, (dims, ((), ())), precision=precision, preferred_element_type=F32)


def params(mib):
    return pltpu.CompilerParams(vmem_limit_bytes=mib * MIB)


def own_half():
    row = lax.axis_index("row")
    half = lax.axis_index("col")
    for bit in range(lax.axis_size("row").bit_length() - 1):
        half += lax.rem(lax.div(row, 1 << bit), 2)
    return lax.rem(half, 2)


TILE = 8


def fill_order(order_ref, half):
    block = TILE * half
    to = lax.broadcasted_iota(jnp.int32, order_ref.shape, 0)
    at = lax.broadcasted_iota(jnp.int32, order_ref.shape, 1)
    cell = lax.div(lax.rem(at, block), half)
    wanted = lax.div(to, TILE) * (order_ref.shape[1] // block) + lax.div(at, block)
    same = (lax.rem(to, TILE) == cell) & (wanted == lax.rem(at, half))
    order_ref[...] = same.astype(F32).astype(BF16)


def multiply(slab, wide_ref, flat_ref):
    cells, half, depth = slab.shape
    x = slab.reshape(cells * half, depth)
    low = dot_f32(x[:, :depth // 2], wide_ref[:, :depth // 2], ((1,), (1,)))
    high = dot_f32(x[:, depth // 2:], wide_ref[:, depth // 2:], ((1,), (1,)))
    flat_ref[...] = (low + high).astype(BF16)


def spread(half, flat_ref, order_ref, core_ref, start):
    block = TILE * half
    reps = order_ref.shape[1] // block
    step = flat_ref.shape[0] // half
    group = lax.div(lax.broadcasted_iota(jnp.int32, (block, LANES), 1), LANES // reps)
    spreads = []
    for b in range(step // TILE):
        flat = flat_ref[pl.ds(b * block, block), :].astype(F32)
        groups = [jnp.where(group == r, flat, 0.0).astype(BF16) for r in range(reps)]
        spreads.append(dot_f32(order_ref[...], jnp.concatenate(groups, axis=0), ((1,), (0,))))
    for p in range(half // reps):
        part = jnp.concatenate([x[p * TILE:(p + 1) * TILE] for x in spreads], axis=0)
        core_ref[pl.ds(start, step), p * LANES:(p + 1) * LANES] = part.astype(BF16)


STEP = 32


def slab_copies(snapshot_ref, first, slab_ref, half_index, sem):
    half = slab_ref.shape[1]
    fibers = pl.ds(pl.multiple_of(half_index * half, half), half)

    def copy(start, size):
        return pltpu.make_async_copy(
            snapshot_ref.at[pl.ds(start, size), fibers],
            slab_ref.at[pl.ds(start - first, size)],
            sem,
        )

    def start(begin, size, count):
        for part in range(count):
            copy(begin + part * (size // count), size // count).start()

    return start, lambda begin, size: copy(begin, size).wait()


def send_kernel(
    snapshot_ref, mode2_ref, core_ref, kept_ref, wide_ref, order_ref,
    slab_ref, small_ref, even_ref, odd_ref, sems, kept_sem, small_sem,
):
    cells, half, _ = slab_ref.shape
    rank = mode2_ref.shape[0]
    chunks = cells // STEP
    flat = (even_ref, odd_ref)
    sends = [
        slab_copies(snapshot_ref, 0, slab_ref, 1 - own_half(), sems.at[chunk])
        for chunk in range(chunks)
    ]
    start_kept, wait_kept = slab_copies(snapshot_ref, 0, kept_ref, own_half(), kept_sem)

    small = pltpu.make_async_copy(mode2_ref, small_ref, small_sem)
    small.start()
    for chunk in range(chunks):
        sends[chunk][0](chunk * STEP, STEP, 2 if chunk else 4)
    fill_order(order_ref, half)
    small.wait()
    wide_ref[...] = jnp.concatenate([small_ref[...]] * (LANES // rank), axis=0)
    for chunk in range(chunks):
        sends[chunk][1](chunk * STEP, STEP)
        if chunk == 0:
            start_kept(0, cells, 2 * chunks)
        multiply(slab_ref[pl.ds(chunk * STEP, STEP)], wide_ref, flat[chunk % 2])
        if chunk:
            spread(half, flat[(chunk - 1) % 2], order_ref, core_ref, (chunk - 1) * STEP)
    spread(half, flat[(chunks - 1) % 2], order_ref, core_ref, (chunks - 1) * STEP)
    wait_kept(0, cells)


def contract_send(snapshot, mode2_t):
    cells, fibers, depth = snapshot.shape
    rank = mode2_t.shape[0]
    half = fibers // 2
    reps = LANES // rank
    block = TILE * half
    pinned = pl.BlockSpec(memory_space=pltpu.HBM)
    return pl.pallas_call(
        send_kernel,
        in_specs=[pinned, pinned],
        out_shape=[
            jax.ShapeDtypeStruct((cells, half * rank), BF16),
            jax.ShapeDtypeStruct((cells, half, depth), BF16),
            jax.ShapeDtypeStruct((LANES, depth), BF16),
            jax.ShapeDtypeStruct((block // reps, block * reps), BF16),
        ],
        scratch_shapes=[
            pltpu.VMEM((cells, half, depth), BF16),
            pltpu.VMEM((rank, depth), BF16),
            pltpu.VMEM((STEP * half, LANES), BF16),
            pltpu.VMEM((STEP * half, LANES), BF16),
            pltpu.SemaphoreType.DMA((cells // STEP,)),
            pltpu.SemaphoreType.DMA,
            pltpu.SemaphoreType.DMA,
        ],
        compiler_params=params(24),
        name="contract_send",
    )(snapshot, mode2_t)


def own_kernel(slab_ref, wide_ref, order_ref, core_ref, even_ref, odd_ref):
    cells, half, _ = slab_ref.shape
    flat = (even_ref, odd_ref)
    chunks = cells // STEP
    for chunk in range(chunks):
        multiply(slab_ref[pl.ds(chunk * STEP, STEP)], wide_ref, flat[chunk % 2])
        if chunk:
            spread(half, flat[(chunk - 1) % 2], order_ref, core_ref, (chunk - 1) * STEP)
    spread(half, flat[(chunks - 1) % 2], order_ref, core_ref, (chunks - 1) * STEP)


def contract_own(slab, wide, order):
    cells, half, _ = slab.shape
    reps = order.shape[1] // (TILE * half)
    return pl.pallas_call(
        own_kernel,
        out_shape=jax.ShapeDtypeStruct((cells, half // reps * LANES), BF16),
        scratch_shapes=[pltpu.VMEM((STEP * half, LANES), BF16)] * 2,
        compiler_params=params(24),
        name="contract_own",
    )(slab, wide, order)


def is_even():
    return lax.rem(lax.axis_index("row"), 2) == 0


def project_kernel(own_ref, got_ref, factor_ref, keep_ref, send_ref, mine_ref, give_ref):
    rank = factor_ref.shape[0]
    width = mine_ref.shape[1]
    odd = lax.rem(lax.axis_index("row"), 2)

    def columns(start):
        where = pl.ds(pl.multiple_of(start, width), width)
        return (own_ref[:, where].astype(F32) + got_ref[:, where].astype(F32)).astype(BF16)

    mine = columns(odd * width)
    give = columns((1 - odd) * width)
    mine_ref[...] = mine
    give_ref[...] = give
    keep = dot_f32(factor_ref[...], mine, ((1,), (0,)))
    send = dot_f32(factor_ref[...], give, ((1,), (0,)))
    for block in range(width // LANES):
        where = slice(block * LANES, (block + 1) * LANES)
        rows = pl.ds(block * rank, rank)
        keep_ref[rows, :] = keep[:, where]
        send_ref[rows, :] = send[:, where].astype(BF16)


def project(own, got, factor_t):
    cells, width = own.shape
    rows = factor_t.shape[0] * width // LANES // 2
    columns = jax.ShapeDtypeStruct((cells, width // 2), BF16)
    return pl.pallas_call(
        project_kernel,
        out_shape=[
            jax.ShapeDtypeStruct((rows, LANES), F32),
            jax.ShapeDtypeStruct((rows, LANES), BF16),
            columns,
            columns,
        ],
        compiler_params=params(8),
        name="project",
    )(own, got, factor_t)


def add_kernel(mine_ref, got_ref, *refs):
    total = mine_ref[...].astype(F32) + got_ref[...].astype(F32)
    refs[-1][...] = total.astype(refs[-1].dtype)


def add(mine, got, *after):
    whole = pl.BlockSpec(memory_space=pltpu.VMEM)
    return pl.pallas_call(
        add_kernel,
        in_specs=[whole, whole] + [pl.BlockSpec(memory_space=pl.ANY)] * len(after),
        out_shape=jax.ShapeDtypeStruct(got.shape, got.dtype),
        compiler_params=params(4),
        name="add",
    )(mine, got, *after)


def product_kernel(mine_ref, got_ref, projected_ref, out_ref):
    blocks = mine_ref.shape[1] // LANES
    rank = projected_ref.shape[0] // blocks
    projected = jnp.concatenate(
        [projected_ref[pl.ds(block * rank, rank), :] for block in range(blocks)], axis=1
    )
    terms = [dot_f32(projected, ref[...], ((1,), (1,))) for ref in (mine_ref, got_ref)]
    even = is_even()
    low = jnp.where(even, terms[0], terms[1])
    high = jnp.where(even, terms[1], terms[0])
    out_ref[...] = jnp.concatenate([low, high], axis=0).astype(BF16)


def product_terms(mine, got, projected):
    return pl.pallas_call(
        product_kernel,
        out_shape=jax.ShapeDtypeStruct((LANES, mine.shape[0]), BF16),
        compiler_params=params(4),
        name="product_terms",
    )(mine, got, projected)


def pair_product(term_ref, got_ref):
    return term_ref[...].astype(F32) + got_ref[...].astype(F32)


def gram_kernel(*refs):
    out_ref = refs[-1]
    rank = LANES // 2
    pairs = [pair_product(refs[k], refs[k + 1]) for k in range(0, len(refs) - 1, 2)]
    product = jnp.concatenate([x[k:k + rank] for x in pairs for k in (0, rank)], axis=1)
    gram = dot_parts(product, product, 1)
    out_ref[...] = jnp.concatenate([gram[:rank // 2], gram[rank // 2:]], axis=1)


def local_gram(*terms):
    return pl.pallas_call(
        gram_kernel,
        out_shape=jax.ShapeDtypeStruct((LANES // 4, LANES), F32),
        compiler_params=params(4),
        name="local_gram",
    )(*terms)


def parts(x):
    high = x.astype(BF16)
    return high, (x - high.astype(F32)).astype(BF16)


def dot_parts(a, b, axis):
    (ah, al), (bh, bl) = parts(a), parts(b)
    left = jnp.concatenate([ah, ah, al], axis=axis)
    right = jnp.concatenate([bh, bl, bh], axis=axis)
    return dot_f32(left, right, ((axis,), (axis,)))


def eliminate(packed, spread_ref):
    rank = packed.shape[1] // 2
    tile = 8
    count = rank // tile
    wide = 2 * rank
    sublane = lax.broadcasted_iota(jnp.int32, (tile, wide), 0)
    lane = lax.broadcasted_iota(jnp.int32, (tile, wide), 1)
    full = lambda x: jnp.broadcast_to(x, (tile, wide))
    both = []
    for v in range(count):
        at = v % (count // 2) * tile
        mine = packed[at:at + tile]
        if v >= count // 2:
            mine = jnp.concatenate([mine[:, rank:], mine[:, :rank]], axis=1)
        both.append(jnp.where(lane < rank, mine, (lane - rank == sublane + v * tile).astype(F32)))
    pivots = []
    for p in range(count):
        cols = [
            {v: full(both[v][:, p * tile + j:p * tile + j + 1]) for v in range(p, count)}
            for j in range(tile)
        ]
        base = p * (tile + 1) * tile
        spread_ref[pl.ds(base, tile), :] = both[p]
        for k in range(tile):
            spread_ref[pl.ds(base + (k + 1) * tile, tile), :] = cols[k][p]
        rows = [full(spread_ref[pl.ds(base + j, 1), :]) for j in range(tile)]
        block = [
            [full(spread_ref[pl.ds(base + (k + 1) * tile + j, 1), :]) for k in range(j + 1)]
            for j in range(tile)
        ]
        found, kept = block[0][0], rows[0]
        for j in range(tile):
            if j:
                found = jnp.where(sublane == j, block[j][j], found)
                kept = jnp.where(sublane == j, rows[j], kept)
            inverse = pl.reciprocal(block[j][j], approx=True, full_range=False)
            scaled = {i: block[i][j] * inverse for i in range(j + 1, tile)}
            for i, factor in scaled.items():
                for k in range(j + 1, i + 1):
                    block[i][k] = block[i][k] - factor * block[k][j]
                rows[i] = rows[i] - factor * rows[j]
            row = rows[j] * inverse
            for v in range(p + 1, count):
                for i, factor in scaled.items():
                    cols[i][v] = cols[i][v] - factor * cols[j][v]
                both[v] = both[v] - cols[j][v] * row
        both[p] = kept
        pivots.append(found)
    return both, pivots


def finish_kernel(
    total_rows, term_ref, got_term_ref, gram_ref, got_gram_ref, out_ref, spread_ref
):
    rank = LANES // 2
    both, pivots = eliminate(gram_ref[...] + got_gram_ref[...], spread_ref)
    scale = total_rows ** 0.5
    inverse = jnp.concatenate([b * (lax.rsqrt(p) * scale) for b, p in zip(both, pivots)], axis=0)
    inverse = inverse[:, rank:]
    half = term_ref.shape[1] // 2
    product = pair_product(term_ref, got_term_ref)
    product = jnp.where(is_even(), product[:rank], product[rank:])
    mine = jnp.where(lax.axis_index("col") == 0, product[:, :half], product[:, half:]).T
    out_ref[...] = dot_parts(mine, inverse, 1)


def finish(total_rows, term, got_term, gram, got_gram):
    return pl.pallas_call(
        functools.partial(finish_kernel, total_rows),
        out_shape=jax.ShapeDtypeStruct((term.shape[1] // 2, LANES // 2), F32),
        scratch_shapes=[pltpu.VMEM((LANES // 2 * 9, LANES), F32)],
        compiler_params=params(4),
        name="finish",
    )(term, got_term, gram, got_gram)


def per_device(snapshot, mode2_factor, old_factor):
    n_rows, n_cols = lax.axis_size("row"), lax.axis_size("col")
    masks = [1 << bit for bit in range(n_rows.bit_length() - 1)]
    total_rows = snapshot.shape[0] * n_rows

    def swap(x, mask, other=None):
        pairs = []
        for r in range(n_rows):
            for c in range(n_cols):
                second = (c + r.bit_count()) % 2 and other is not None
                to = r ^ (other if second else mask)
                pairs.append((r * n_cols + c, to * n_cols + (c + 1) % n_cols))
        return lax.ppermute(x, ("row", "col"), pairs)

    snapshot = pltpu.with_memory_space_constraint(snapshot, pltpu.HBM)
    mode2_t = pltpu.with_memory_space_constraint(mode2_factor.T, pltpu.HBM)
    send, kept, wide, order = contract_send(snapshot, mode2_t)
    got = swap(send, 0)
    own = contract_own(kept, wide, order)

    keep, send, columns, give = project(own, got, old_factor.T)
    mine = add(keep, swap(send, masks[0]))
    got_columns = swap(give, masks[0])
    others = masks[1:]
    turned = others[len(others) // 2:] + others[:len(others) // 2]
    for step, (mask, other) in enumerate(zip(others, turned)):
        after = [got_columns] if step == 1 else []
        mine = add(mine, swap(mine, mask, other), *after)

    term = product_terms(columns, got_columns, mine)
    term = add(term, swap(term, 0))
    pair, next_pair = masks[:2]
    got_term = swap(term, pair)
    gram = local_gram(term, got_term, swap(term, next_pair), swap(term, pair | next_pair))
    for mask in masks[2:-1]:
        gram = add(gram, swap(gram, mask))
    return finish(total_rows, term, got_term, gram, swap(gram, masks[-1]))


def solution(mesh):
    return jax.shard_map(
        per_device,
        mesh=mesh,
        in_specs=(
            P(("groups", "row"), None, "col"),
            P(("groups", "col"), None),
            P(("groups", "row"), None),
        ),
        out_specs=P(("groups", "row", "col"), None),
        check_vma=False,
    )
```

```python
import functools

import jax
import jax.numpy as jnp
from jax import lax
from jax.experimental import pallas as pl
from jax.experimental.pallas import tpu as pltpu
from jax.sharding import PartitionSpec as P

F32 = jnp.float32
BF16 = jnp.bfloat16
LANES = 128
MIB = 2**20


def dot_f32(a, b, dims, precision=None):
    return lax.dot_general(a, b, (dims, ((), ())), precision=precision, preferred_element_type=F32)


def params(mib):
    return pltpu.CompilerParams(vmem_limit_bytes=mib * MIB)


def own_half():
    row = lax.axis_index("row")
    half = lax.axis_index("col")
    for bit in range(lax.axis_size("row").bit_length() - 1):
        half += lax.rem(lax.div(row, 1 << bit), 2)
    return lax.rem(half, 2)


TILE = 8


def fill_order(order_ref, half):
    block = TILE * half
    to = lax.broadcasted_iota(jnp.int32, order_ref.shape, 0)
    at = lax.broadcasted_iota(jnp.int32, order_ref.shape, 1)
    cell = lax.div(lax.rem(at, block), half)
    wanted = lax.div(to, TILE) * (order_ref.shape[1] // block) + lax.div(at, block)
    same = (lax.rem(to, TILE) == cell) & (wanted == lax.rem(at, half))
    order_ref[...] = same.astype(F32).astype(BF16)


def multiply(slab, wide_ref, flat_ref):
    cells, half, depth = slab.shape
    x = slab.reshape(cells * half, depth)
    low = dot_f32(x[:, :depth // 2], wide_ref[:, :depth // 2], ((1,), (1,)))
    high = dot_f32(x[:, depth // 2:], wide_ref[:, depth // 2:], ((1,), (1,)))
    flat_ref[...] = (low + high).astype(BF16)


def spread(half, flat_ref, order_ref, core_ref, start):
    block = TILE * half
    reps = order_ref.shape[1] // block
    step = flat_ref.shape[0] // half
    group = lax.div(lax.broadcasted_iota(jnp.int32, (block, LANES), 1), LANES // reps)
    spreads = []
    for b in range(step // TILE):
        flat = flat_ref[pl.ds(b * block, block), :].astype(F32)
        groups = [jnp.where(group == r, flat, 0.0).astype(BF16) for r in range(reps)]
        spreads.append(dot_f32(order_ref[...], jnp.concatenate(groups, axis=0), ((1,), (0,))))
    for p in range(half // reps):
        part = jnp.concatenate([x[p * TILE:(p + 1) * TILE] for x in spreads], axis=0)
        core_ref[pl.ds(start, step), p * LANES:(p + 1) * LANES] = part.astype(BF16)


STEP = 32


def slab_copies(snapshot_ref, first, slab_ref, half_index, sem):
    half = slab_ref.shape[1]
    fibers = pl.ds(pl.multiple_of(half_index * half, half), half)

    def copy(start, size):
        return pltpu.make_async_copy(
            snapshot_ref.at[pl.ds(start, size), fibers],
            slab_ref.at[pl.ds(start - first, size)],
            sem,
        )

    def start(begin, size, count):
        for part in range(count):
            copy(begin + part * (size // count), size // count).start()

    return start, lambda begin, size: copy(begin, size).wait()


def send_kernel(
    snapshot_ref, mode2_ref, core_ref, kept_ref, wide_ref, order_ref,
    slab_ref, small_ref, even_ref, odd_ref, sems, kept_sem, small_sem,
):
    cells, half, _ = slab_ref.shape
    rank = mode2_ref.shape[0]
    chunks = cells // STEP
    flat = (even_ref, odd_ref)
    sends = [
        slab_copies(snapshot_ref, 0, slab_ref, 1 - own_half(), sems.at[chunk])
        for chunk in range(chunks)
    ]
    start_kept, wait_kept = slab_copies(snapshot_ref, 0, kept_ref, own_half(), kept_sem)

    small = pltpu.make_async_copy(mode2_ref, small_ref, small_sem)
    small.start()
    for chunk in range(chunks):
        sends[chunk][0](chunk * STEP, STEP, 2 if chunk else 4)
    fill_order(order_ref, half)
    small.wait()
    wide_ref[...] = jnp.concatenate([small_ref[...]] * (LANES // rank), axis=0)
    for chunk in range(chunks):
        sends[chunk][1](chunk * STEP, STEP)
        if chunk == 0:
            start_kept(0, cells, 2 * chunks)
        multiply(slab_ref[pl.ds(chunk * STEP, STEP)], wide_ref, flat[chunk % 2])
        if chunk:
            spread(half, flat[(chunk - 1) % 2], order_ref, core_ref, (chunk - 1) * STEP)
    spread(half, flat[(chunks - 1) % 2], order_ref, core_ref, (chunks - 1) * STEP)
    wait_kept(0, cells)


def contract_send(snapshot, mode2_t):
    cells, fibers, depth = snapshot.shape
    rank = mode2_t.shape[0]
    half = fibers // 2
    reps = LANES // rank
    block = TILE * half
    pinned = pl.BlockSpec(memory_space=pltpu.HBM)
    return pl.pallas_call(
        send_kernel,
        in_specs=[pinned, pinned],
        out_shape=[
            jax.ShapeDtypeStruct((cells, half * rank), BF16),
            jax.ShapeDtypeStruct((cells, half, depth), BF16),
            jax.ShapeDtypeStruct((LANES, depth), BF16),
            jax.ShapeDtypeStruct((block // reps, block * reps), BF16),
        ],
        scratch_shapes=[
            pltpu.VMEM((cells, half, depth), BF16),
            pltpu.VMEM((rank, depth), BF16),
            pltpu.VMEM((STEP * half, LANES), BF16),
            pltpu.VMEM((STEP * half, LANES), BF16),
            pltpu.SemaphoreType.DMA((cells // STEP,)),
            pltpu.SemaphoreType.DMA,
            pltpu.SemaphoreType.DMA,
        ],
        compiler_params=params(24),
        name="contract_send",
    )(snapshot, mode2_t)


def own_kernel(slab_ref, wide_ref, order_ref, core_ref, even_ref, odd_ref):
    cells, half, _ = slab_ref.shape
    flat = (even_ref, odd_ref)
    chunks = cells // STEP
    for chunk in range(chunks):
        multiply(slab_ref[pl.ds(chunk * STEP, STEP)], wide_ref, flat[chunk % 2])
        if chunk:
            spread(half, flat[(chunk - 1) % 2], order_ref, core_ref, (chunk - 1) * STEP)
    spread(half, flat[(chunks - 1) % 2], order_ref, core_ref, (chunks - 1) * STEP)


def contract_own(slab, wide, order):
    cells, half, _ = slab.shape
    reps = order.shape[1] // (TILE * half)
    return pl.pallas_call(
        own_kernel,
        out_shape=jax.ShapeDtypeStruct((cells, half // reps * LANES), BF16),
        scratch_shapes=[pltpu.VMEM((STEP * half, LANES), BF16)] * 2,
        compiler_params=params(24),
        name="contract_own",
    )(slab, wide, order)


def is_even():
    return lax.rem(lax.axis_index("row"), 2) == 0


def project_kernel(kept, own_ref, got_ref, factor_ref, projected_ref, core_ref):
    rank = factor_ref.shape[0]
    width = core_ref.shape[1]
    odd = lax.rem(lax.axis_index("row"), 2)
    start = odd * width if kept else (1 - odd) * width
    where = pl.ds(pl.multiple_of(start, width), width)
    core = (own_ref[:, where].astype(F32) + got_ref[:, where].astype(F32)).astype(BF16)
    core_ref[...] = core
    projected = dot_f32(factor_ref[...], core, ((1,), (0,)))
    for block in range(width // LANES):
        part = projected[:, block * LANES:(block + 1) * LANES]
        projected_ref[pl.ds(block * rank, rank), :] = part.astype(projected_ref.dtype)


def project(own, got, factor_t, kept):
    cells, width = own.shape
    rows = factor_t.shape[0] * width // LANES // 2
    return pl.pallas_call(
        functools.partial(project_kernel, kept),
        out_shape=[
            jax.ShapeDtypeStruct((rows, LANES), F32 if kept else BF16),
            jax.ShapeDtypeStruct((cells, width // 2), BF16),
        ],
        compiler_params=params(8),
        name="project_kept" if kept else "project_sent",
    )(own, got, factor_t)


def add_kernel(mine_ref, got_ref, *refs):
    total = mine_ref[...].astype(F32) + got_ref[...].astype(F32)
    refs[-1][...] = total.astype(refs[-1].dtype)


def add(mine, got, *after):
    whole = pl.BlockSpec(memory_space=pltpu.VMEM)
    return pl.pallas_call(
        add_kernel,
        in_specs=[whole, whole] + [pl.BlockSpec(memory_space=pl.ANY)] * len(after),
        out_shape=jax.ShapeDtypeStruct(got.shape, got.dtype),
        compiler_params=params(4),
        name="add",
    )(mine, got, *after)


def product_kernel(mine_ref, got_ref, projected_ref, out_ref):
    blocks = mine_ref.shape[1] // LANES
    rank = projected_ref.shape[0] // blocks
    projected = jnp.concatenate(
        [projected_ref[pl.ds(block * rank, rank), :] for block in range(blocks)], axis=1
    )
    terms = [dot_f32(projected, ref[...], ((1,), (1,))) for ref in (mine_ref, got_ref)]
    even = is_even()
    low = jnp.where(even, terms[0], terms[1])
    high = jnp.where(even, terms[1], terms[0])
    out_ref[...] = jnp.concatenate([low, high], axis=0).astype(BF16)


def product_terms(mine, got, projected):
    return pl.pallas_call(
        product_kernel,
        out_shape=jax.ShapeDtypeStruct((LANES, mine.shape[0]), BF16),
        compiler_params=params(4),
        name="product_terms",
    )(mine, got, projected)


def pair_product(term_ref, first_ref, second_ref):
    got = jnp.where(own_half() == 0, first_ref[...].astype(F32), second_ref[...].astype(F32))
    return term_ref[...].astype(F32) + got


def gram_kernel(term_ref, first_ref, second_ref, last_ref, out_ref):
    rank = LANES // 2
    pairs = [
        pair_product(term_ref, first_ref, second_ref),
        pair_product(last_ref, second_ref, first_ref),
    ]
    product = jnp.concatenate([x[k:k + rank] for x in pairs for k in (0, rank)], axis=1)
    gram = dot_parts(product, product, 1)
    out_ref[...] = jnp.concatenate([gram[:rank // 2], gram[rank // 2:]], axis=1)


def local_gram(*terms):
    return pl.pallas_call(
        gram_kernel,
        out_shape=jax.ShapeDtypeStruct((LANES // 4, LANES), F32),
        compiler_params=params(4),
        name="local_gram",
    )(*terms)


def parts(x):
    high = x.astype(BF16)
    return high, (x - high.astype(F32)).astype(BF16)


def dot_parts(a, b, axis):
    (ah, al), (bh, bl) = parts(a), parts(b)
    left = jnp.concatenate([ah, ah, al], axis=axis)
    right = jnp.concatenate([bh, bl, bh], axis=axis)
    return dot_f32(left, right, ((axis,), (axis,)))


def eliminate(packed, spread_ref):
    rank = packed.shape[1] // 2
    tile = 8
    count = rank // tile
    wide = 2 * rank
    sublane = lax.broadcasted_iota(jnp.int32, (tile, wide), 0)
    lane = lax.broadcasted_iota(jnp.int32, (tile, wide), 1)
    full = lambda x: jnp.broadcast_to(x, (tile, wide))
    both = []
    for v in range(count):
        at = v % (count // 2) * tile
        mine = packed[at:at + tile]
        if v >= count // 2:
            mine = jnp.concatenate([mine[:, rank:], mine[:, :rank]], axis=1)
        both.append(jnp.where(lane < rank, mine, (lane - rank == sublane + v * tile).astype(F32)))
    pivots = []
    for p in range(count):
        cols = [
            {v: full(both[v][:, p * tile + j:p * tile + j + 1]) for v in range(p, count)}
            for j in range(tile)
        ]
        base = p * (tile + 1) * tile
        spread_ref[pl.ds(base, tile), :] = both[p]
        for k in range(tile):
            spread_ref[pl.ds(base + (k + 1) * tile, tile), :] = cols[k][p]
        rows = [full(spread_ref[pl.ds(base + j, 1), :]) for j in range(tile)]
        block = [
            [full(spread_ref[pl.ds(base + (k + 1) * tile + j, 1), :]) for k in range(j + 1)]
            for j in range(tile)
        ]
        found, kept = block[0][0], rows[0]
        for j in range(tile):
            if j:
                found = jnp.where(sublane == j, block[j][j], found)
                kept = jnp.where(sublane == j, rows[j], kept)
            inverse = pl.reciprocal(block[j][j], approx=True, full_range=False)
            scaled = {i: block[i][j] * inverse for i in range(j + 1, tile)}
            for i, factor in scaled.items():
                for k in range(j + 1, i + 1):
                    block[i][k] = block[i][k] - factor * block[k][j]
                rows[i] = rows[i] - factor * rows[j]
            row = rows[j] * inverse
            for v in range(p + 1, count):
                for i, factor in scaled.items():
                    cols[i][v] = cols[i][v] - factor * cols[j][v]
                both[v] = both[v] - cols[j][v] * row
        both[p] = kept
        pivots.append(found)
    return both, pivots


def finish_kernel(
    total_rows, term_ref, first_ref, second_ref, gram_ref, got_gram_ref, out_ref, spread_ref
):
    rank = LANES // 2
    both, pivots = eliminate(gram_ref[...] + got_gram_ref[...], spread_ref)
    scale = total_rows ** 0.5
    inverse = jnp.concatenate([b * (lax.rsqrt(p) * scale) for b, p in zip(both, pivots)], axis=0)
    inverse = inverse[:, rank:]
    half = term_ref.shape[1] // 2
    product = pair_product(term_ref, first_ref, second_ref)
    product = jnp.where(is_even(), product[:rank], product[rank:])
    mine = jnp.where(lax.axis_index("col") == 0, product[:, :half], product[:, half:]).T
    out_ref[...] = dot_parts(mine, inverse, 1)


def finish(total_rows, term, first, second, gram, got_gram):
    return pl.pallas_call(
        functools.partial(finish_kernel, total_rows),
        out_shape=jax.ShapeDtypeStruct((term.shape[1] // 2, LANES // 2), F32),
        scratch_shapes=[pltpu.VMEM((LANES // 2 * 9, LANES), F32)],
        compiler_params=params(4),
        name="finish",
    )(term, first, second, gram, got_gram)


def per_device(snapshot, mode2_factor, old_factor):
    n_rows, n_cols = lax.axis_size("row"), lax.axis_size("col")
    masks = [1 << bit for bit in range(n_rows.bit_length() - 1)]
    total_rows = snapshot.shape[0] * n_rows

    def swap(x, mask, other=None):
        pairs = []
        for r in range(n_rows):
            for c in range(n_cols):
                second = (c + r.bit_count()) % 2 and other is not None
                to = r ^ (other if second else mask)
                pairs.append((r * n_cols + c, to * n_cols + (c + 1) % n_cols))
        return lax.ppermute(x, ("row", "col"), pairs)

    snapshot = pltpu.with_memory_space_constraint(snapshot, pltpu.HBM)
    mode2_t = pltpu.with_memory_space_constraint(mode2_factor.T, pltpu.HBM)
    send, kept, wide, order = contract_send(snapshot, mode2_t)
    got = swap(send, 0)
    own = contract_own(kept, wide, order)

    send, give = project(own, got, old_factor.T, False)
    keep, columns = project(own, got, old_factor.T, True)
    mine = add(keep, swap(send, masks[0]))
    got_columns = swap(give, masks[0])
    others = masks[1:]
    turned = others[len(others) // 2:] + others[:len(others) // 2]
    for step, (mask, other) in enumerate(zip(others, turned)):
        after = [got_columns] if step == 1 else []
        mine = add(mine, swap(mine, mask, other), *after)

    term = product_terms(columns, got_columns, mine)
    term = add(term, swap(term, 0))
    pair, next_pair = masks[:2]
    first, second = swap(term, pair, next_pair), swap(term, next_pair, pair)
    gram = local_gram(term, first, second, swap(term, pair | next_pair))
    for mask in masks[2:-1]:
        gram = add(gram, swap(gram, mask))
    return finish(total_rows, term, first, second, gram, swap(gram, masks[-1]))


def solution(mesh):
    return jax.shard_map(
        per_device,
        mesh=mesh,
        in_specs=(
            P(("groups", "row"), None, "col"),
            P(("groups", "col"), None),
            P(("groups", "row"), None),
        ),
        out_specs=P(("groups", "row", "col"), None),
        check_vma=False,
    )
```

```python
import functools

import jax
import jax.numpy as jnp
from jax import lax
from jax.experimental import pallas as pl
from jax.experimental.pallas import tpu as pltpu
from jax.sharding import PartitionSpec as P

F32 = jnp.float32
BF16 = jnp.bfloat16
LANES = 128
MIB = 2**20


def dot_f32(a, b, dims, precision=None):
    return lax.dot_general(a, b, (dims, ((), ())), precision=precision, preferred_element_type=F32)


def params(mib):
    return pltpu.CompilerParams(vmem_limit_bytes=mib * MIB)


def own_half():
    row = lax.axis_index("row")
    half = lax.axis_index("col")
    for bit in range(lax.axis_size("row").bit_length() - 1):
        half += lax.rem(lax.div(row, 1 << bit), 2)
    return lax.rem(half, 2)


TILE = 8


def fill_order(order_ref, half):
    block = TILE * half
    to = lax.broadcasted_iota(jnp.int32, order_ref.shape, 0)
    at = lax.broadcasted_iota(jnp.int32, order_ref.shape, 1)
    cell = lax.div(lax.rem(at, block), half)
    wanted = lax.div(to, TILE) * (order_ref.shape[1] // block) + lax.div(at, block)
    same = (lax.rem(to, TILE) == cell) & (wanted == lax.rem(at, half))
    order_ref[...] = same.astype(F32).astype(BF16)


def multiply(slab, wide_ref, flat_ref):
    cells, half, depth = slab.shape
    x = slab.reshape(cells * half, depth)
    low = dot_f32(x[:, :depth // 2], wide_ref[:, :depth // 2], ((1,), (1,)))
    high = dot_f32(x[:, depth // 2:], wide_ref[:, depth // 2:], ((1,), (1,)))
    flat_ref[...] = (low + high).astype(BF16)


def spread(half, flat_ref, order_ref, core_ref, start):
    block = TILE * half
    reps = order_ref.shape[1] // block
    step = flat_ref.shape[0] // half
    group = lax.div(lax.broadcasted_iota(jnp.int32, (block, LANES), 1), LANES // reps)
    spreads = []
    for b in range(step // TILE):
        flat = flat_ref[pl.ds(b * block, block), :].astype(F32)
        groups = [jnp.where(group == r, flat, 0.0).astype(BF16) for r in range(reps)]
        spreads.append(dot_f32(order_ref[...], jnp.concatenate(groups, axis=0), ((1,), (0,))))
    for p in range(half // reps):
        part = jnp.concatenate([x[p * TILE:(p + 1) * TILE] for x in spreads], axis=0)
        core_ref[pl.ds(start, step), p * LANES:(p + 1) * LANES] = part.astype(BF16)


STEP = 32


def slab_copies(snapshot_ref, first, slab_ref, half_index, sem):
    half = slab_ref.shape[1]
    fibers = pl.ds(pl.multiple_of(half_index * half, half), half)

    def copy(start, size):
        return pltpu.make_async_copy(
            snapshot_ref.at[pl.ds(start, size), fibers],
            slab_ref.at[pl.ds(start - first, size)],
            sem,
        )

    def start(begin, size, count):
        for part in range(count):
            copy(begin + part * (size // count), size // count).start()

    return start, lambda begin, size: copy(begin, size).wait()


def send_kernel(
    snapshot_ref, mode2_ref, core_ref, kept_ref, wide_ref, order_ref,
    slab_ref, small_ref, even_ref, odd_ref, sems, kept_sem, small_sem,
):
    cells, half, _ = slab_ref.shape
    rank = mode2_ref.shape[0]
    chunks = cells // STEP
    flat = (even_ref, odd_ref)
    sends = [
        slab_copies(snapshot_ref, 0, slab_ref, 1 - own_half(), sems.at[chunk])
        for chunk in range(chunks)
    ]
    start_kept, wait_kept = slab_copies(snapshot_ref, 0, kept_ref, own_half(), kept_sem)

    small = pltpu.make_async_copy(mode2_ref, small_ref, small_sem)
    small.start()
    for chunk in range(chunks):
        sends[chunk][0](chunk * STEP, STEP, 2 if chunk else 4)
    fill_order(order_ref, half)
    small.wait()
    wide_ref[...] = jnp.concatenate([small_ref[...]] * (LANES // rank), axis=0)
    for chunk in range(chunks):
        sends[chunk][1](chunk * STEP, STEP)
        if chunk == 0:
            start_kept(0, cells, 2 * chunks)
        multiply(slab_ref[pl.ds(chunk * STEP, STEP)], wide_ref, flat[chunk % 2])
        if chunk:
            spread(half, flat[(chunk - 1) % 2], order_ref, core_ref, (chunk - 1) * STEP)
    spread(half, flat[(chunks - 1) % 2], order_ref, core_ref, (chunks - 1) * STEP)
    wait_kept(0, cells)


def contract_send(snapshot, mode2_t):
    cells, fibers, depth = snapshot.shape
    rank = mode2_t.shape[0]
    half = fibers // 2
    reps = LANES // rank
    block = TILE * half
    pinned = pl.BlockSpec(memory_space=pltpu.HBM)
    return pl.pallas_call(
        send_kernel,
        in_specs=[pinned, pinned],
        out_shape=[
            jax.ShapeDtypeStruct((cells, half * rank), BF16),
            jax.ShapeDtypeStruct((cells, half, depth), BF16),
            jax.ShapeDtypeStruct((LANES, depth), BF16),
            jax.ShapeDtypeStruct((block // reps, block * reps), BF16),
        ],
        scratch_shapes=[
            pltpu.VMEM((cells, half, depth), BF16),
            pltpu.VMEM((rank, depth), BF16),
            pltpu.VMEM((STEP * half, LANES), BF16),
            pltpu.VMEM((STEP * half, LANES), BF16),
            pltpu.SemaphoreType.DMA((cells // STEP,)),
            pltpu.SemaphoreType.DMA,
            pltpu.SemaphoreType.DMA,
        ],
        compiler_params=params(24),
        name="contract_send",
    )(snapshot, mode2_t)


def own_kernel(slab_ref, wide_ref, order_ref, core_ref, even_ref, odd_ref):
    cells, half, _ = slab_ref.shape
    flat = (even_ref, odd_ref)
    chunks = cells // STEP
    for chunk in range(chunks):
        multiply(slab_ref[pl.ds(chunk * STEP, STEP)], wide_ref, flat[chunk % 2])
        if chunk:
            spread(half, flat[(chunk - 1) % 2], order_ref, core_ref, (chunk - 1) * STEP)
    spread(half, flat[(chunks - 1) % 2], order_ref, core_ref, (chunks - 1) * STEP)


def contract_own(slab, wide, order):
    cells, half, _ = slab.shape
    reps = order.shape[1] // (TILE * half)
    return pl.pallas_call(
        own_kernel,
        out_shape=jax.ShapeDtypeStruct((cells, half // reps * LANES), BF16),
        scratch_shapes=[pltpu.VMEM((STEP * half, LANES), BF16)] * 2,
        compiler_params=params(24),
        name="contract_own",
    )(slab, wide, order)


def is_even():
    return lax.rem(lax.axis_index("row"), 2) == 0


def project_kernel(kept, own_ref, got_ref, factor_ref, projected_ref, core_ref):
    rank = factor_ref.shape[0]
    width = core_ref.shape[1]
    odd = lax.rem(lax.axis_index("row"), 2)
    start = odd * width if kept else (1 - odd) * width
    where = pl.ds(pl.multiple_of(start, width), width)
    core = (own_ref[:, where].astype(F32) + got_ref[:, where].astype(F32)).astype(BF16)
    core_ref[...] = core
    projected = dot_f32(factor_ref[...], core, ((1,), (0,)))
    for block in range(width // LANES):
        part = projected[:, block * LANES:(block + 1) * LANES]
        projected_ref[pl.ds(block * rank, rank), :] = part.astype(projected_ref.dtype)


def project(own, got, factor_t, kept):
    cells, width = own.shape
    rows = factor_t.shape[0] * width // LANES // 2
    return pl.pallas_call(
        functools.partial(project_kernel, kept),
        out_shape=[
            jax.ShapeDtypeStruct((rows, LANES), F32 if kept else BF16),
            jax.ShapeDtypeStruct((cells, width // 2), BF16),
        ],
        compiler_params=params(8),
        name="project_kept" if kept else "project_sent",
    )(own, got, factor_t)


def add_kernel(mine_ref, got_ref, *refs):
    total = mine_ref[...].astype(F32) + got_ref[...].astype(F32)
    refs[-1][...] = total.astype(refs[-1].dtype)


def add(mine, got, *after):
    whole = pl.BlockSpec(memory_space=pltpu.VMEM)
    return pl.pallas_call(
        add_kernel,
        in_specs=[whole, whole] + [pl.BlockSpec(memory_space=pl.ANY)] * len(after),
        out_shape=jax.ShapeDtypeStruct(got.shape, got.dtype),
        compiler_params=params(4),
        name="add",
    )(mine, got, *after)


def product_kernel(mine_ref, got_ref, projected_ref, out_ref):
    blocks = mine_ref.shape[1] // LANES
    rank = projected_ref.shape[0] // blocks
    projected = jnp.concatenate(
        [projected_ref[pl.ds(block * rank, rank), :] for block in range(blocks)], axis=1
    )
    terms = [dot_f32(projected, ref[...], ((1,), (1,))) for ref in (mine_ref, got_ref)]
    even = is_even()
    low = jnp.where(even, terms[0], terms[1])
    high = jnp.where(even, terms[1], terms[0])
    out_ref[...] = jnp.concatenate([low, high], axis=0).astype(BF16)


def product_terms(mine, got, projected):
    return pl.pallas_call(
        product_kernel,
        out_shape=jax.ShapeDtypeStruct((LANES, mine.shape[0]), BF16),
        compiler_params=params(4),
        name="product_terms",
    )(mine, got, projected)


def pair_product(term_ref, first_ref, second_ref):
    got = jnp.where(own_half() == 0, first_ref[...].astype(F32), second_ref[...].astype(F32))
    return term_ref[...].astype(F32) + got


def gram_kernel(term_ref, first_ref, second_ref, last_ref, out_ref):
    rank = LANES // 2
    pairs = [
        pair_product(term_ref, first_ref, second_ref),
        pair_product(last_ref, second_ref, first_ref),
    ]
    product = jnp.concatenate([x[k:k + rank] for x in pairs for k in (0, rank)], axis=1)
    gram = dot_parts(product, product, 1)
    out_ref[...] = jnp.concatenate([gram[:rank // 2], gram[rank // 2:]], axis=1)


def local_gram(*terms):
    return pl.pallas_call(
        gram_kernel,
        out_shape=jax.ShapeDtypeStruct((LANES // 4, LANES), F32),
        compiler_params=params(4),
        name="local_gram",
    )(*terms)


def parts(x):
    high = x.astype(BF16)
    return high, (x - high.astype(F32)).astype(BF16)


def dot_parts(a, b, axis):
    (ah, al), (bh, bl) = parts(a), parts(b)
    left = jnp.concatenate([ah, ah, al], axis=axis)
    right = jnp.concatenate([bh, bl, bh], axis=axis)
    return dot_f32(left, right, ((axis,), (axis,)))


def eliminate(packed, spread_ref):
    rank = packed.shape[1] // 2
    tile = 8
    count = rank // tile
    wide = 2 * rank
    sublane = lax.broadcasted_iota(jnp.int32, (tile, wide), 0)
    lane = lax.broadcasted_iota(jnp.int32, (tile, wide), 1)
    full = lambda x: jnp.broadcast_to(x, (tile, wide))
    both = []
    for v in range(count):
        at = v % (count // 2) * tile
        mine = packed[at:at + tile]
        if v >= count // 2:
            mine = jnp.concatenate([mine[:, rank:], mine[:, :rank]], axis=1)
        both.append(jnp.where(lane < rank, mine, (lane - rank == sublane + v * tile).astype(F32)))
    def lanes(v, p):
        return [full(both[v][:, p * tile + k:p * tile + k + 1]) for k in range(tile)]

    slots = [0]

    def spread(x, count):
        at = slots[0] * tile
        slots[0] += 1
        spread_ref[pl.ds(at, tile), :] = x
        return [full(spread_ref[pl.ds(at + j, 1), :]) for j in range(count)]

    pivots = []
    diagonal = lanes(0, 0)
    for p in range(count):
        columns = [spread(diagonal[k], tile) for k in range(tile)]
        block = [[columns[k][j] for k in range(j + 1)] for j in range(tile)]
        rows = spread(both[p], tile)
        below = range(p + 1, count)
        cols = {v: lanes(v, p) for v in below}
        diagonal = lanes(p + 1, p + 1) if below else []
        found, kept = block[0][0], rows[0]
        for j in range(tile):
            if j:
                found = jnp.where(sublane == j, block[j][j], found)
                kept = jnp.where(sublane == j, rows[j], kept)
            inverse = pl.reciprocal(block[j][j], approx=True, full_range=False)
            scaled = {i: block[i][j] * inverse for i in range(j + 1, tile)}
            for i, factor in scaled.items():
                for k in range(j + 1, i + 1):
                    block[i][k] = block[i][k] - factor * block[k][j]
                rows[i] = rows[i] - factor * rows[j]
            if below:
                column = cols[p + 1][j]
                entries = spread(column, tile)
                diagonal = [x - column * (e * inverse) for x, e in zip(diagonal, entries)]
            row = rows[j] * inverse
            for v in below:
                for i, factor in scaled.items():
                    cols[v][i] = cols[v][i] - factor * cols[v][j]
                both[v] = both[v] - cols[v][j] * row
        both[p] = kept
        pivots.append(found)
    return both, pivots


def finish_kernel(
    total_rows, term_ref, first_ref, second_ref, gram_ref, got_gram_ref, out_ref, spread_ref
):
    rank = LANES // 2
    both, pivots = eliminate(gram_ref[...] + got_gram_ref[...], spread_ref)
    scale = total_rows ** 0.5
    inverse = jnp.concatenate([b * (lax.rsqrt(p) * scale) for b, p in zip(both, pivots)], axis=0)
    inverse = inverse[:, rank:]
    half = term_ref.shape[1] // 2
    product = pair_product(term_ref, first_ref, second_ref)
    product = jnp.where(is_even(), product[:rank], product[rank:])
    mine = jnp.where(lax.axis_index("col") == 0, product[:, :half], product[:, half:]).T
    out_ref[...] = dot_parts(mine, inverse, 1)


def finish(total_rows, term, first, second, gram, got_gram):
    return pl.pallas_call(
        functools.partial(finish_kernel, total_rows),
        out_shape=jax.ShapeDtypeStruct((term.shape[1] // 2, LANES // 2), F32),
        scratch_shapes=[pltpu.VMEM((LANES // 2 * 17, LANES), F32)],
        compiler_params=params(4),
        name="finish",
    )(term, first, second, gram, got_gram)


def per_device(snapshot, mode2_factor, old_factor):
    n_rows, n_cols = lax.axis_size("row"), lax.axis_size("col")
    masks = [1 << bit for bit in range(n_rows.bit_length() - 1)]
    total_rows = snapshot.shape[0] * n_rows

    def swap(x, mask, other=None):
        pairs = []
        for r in range(n_rows):
            for c in range(n_cols):
                second = (c + r.bit_count()) % 2 and other is not None
                to = r ^ (other if second else mask)
                pairs.append((r * n_cols + c, to * n_cols + (c + 1) % n_cols))
        return lax.ppermute(x, ("row", "col"), pairs)

    snapshot = pltpu.with_memory_space_constraint(snapshot, pltpu.HBM)
    mode2_t = pltpu.with_memory_space_constraint(mode2_factor.T, pltpu.HBM)
    send, kept, wide, order = contract_send(snapshot, mode2_t)
    got = swap(send, 0)
    own = contract_own(kept, wide, order)

    send, give = project(own, got, old_factor.T, False)
    keep, columns = project(own, got, old_factor.T, True)
    mine = add(keep, swap(send, masks[0]))
    got_columns = swap(give, masks[0])
    others = masks[1:]
    turned = others[len(others) // 2:] + others[:len(others) // 2]
    for step, (mask, other) in enumerate(zip(others, turned)):
        after = [got_columns] if step == 1 else []
        mine = add(mine, swap(mine, mask, other), *after)

    term = product_terms(columns, got_columns, mine)
    term = add(term, swap(term, 0))
    pair, next_pair = masks[:2]
    first, second = swap(term, pair, next_pair), swap(term, next_pair, pair)
    gram = local_gram(term, first, second, swap(term, pair | next_pair))
    for mask in masks[2:-1]:
        gram = add(gram, swap(gram, mask))
    return finish(total_rows, term, first, second, gram, swap(gram, masks[-1]))


def solution(mesh):
    return jax.shard_map(
        per_device,
        mesh=mesh,
        in_specs=(
            P(("groups", "row"), None, "col"),
            P(("groups", "col"), None),
            P(("groups", "row"), None),
        ),
        out_specs=P(("groups", "row", "col"), None),
        check_vma=False,
    )
```

```python
import functools

import jax
import jax.numpy as jnp
from jax import lax
from jax.experimental import pallas as pl
from jax.experimental.pallas import tpu as pltpu
from jax.sharding import PartitionSpec as P

F32 = jnp.float32
BF16 = jnp.bfloat16
LANES = 128
MIB = 2**20


def dot_f32(a, b, dims, precision=None):
    return lax.dot_general(a, b, (dims, ((), ())), precision=precision, preferred_element_type=F32)


def params(mib):
    return pltpu.CompilerParams(vmem_limit_bytes=mib * MIB)


def own_half():
    row = lax.axis_index("row")
    half = lax.axis_index("col")
    for bit in range(lax.axis_size("row").bit_length() - 1):
        half += lax.rem(lax.div(row, 1 << bit), 2)
    return lax.rem(half, 2)


TILE = 8


def fill_order(order_ref, half):
    block = TILE * half
    to = lax.broadcasted_iota(jnp.int32, order_ref.shape, 0)
    at = lax.broadcasted_iota(jnp.int32, order_ref.shape, 1)
    cell = lax.div(lax.rem(at, block), half)
    wanted = lax.div(to, TILE) * (order_ref.shape[1] // block) + lax.div(at, block)
    same = (lax.rem(to, TILE) == cell) & (wanted == lax.rem(at, half))
    order_ref[...] = same.astype(F32).astype(BF16)


def multiply(slab, wide_ref, flat_ref):
    cells, half, depth = slab.shape
    x = slab.reshape(cells * half, depth)
    low = dot_f32(x[:, :depth // 2], wide_ref[:, :depth // 2], ((1,), (1,)))
    high = dot_f32(x[:, depth // 2:], wide_ref[:, depth // 2:], ((1,), (1,)))
    flat_ref[...] = (low + high).astype(BF16)


def spread(half, flat_ref, order_ref, core_ref, start):
    block = TILE * half
    reps = order_ref.shape[1] // block
    step = flat_ref.shape[0] // half
    group = lax.div(lax.broadcasted_iota(jnp.int32, (block, LANES), 1), LANES // reps)
    spreads = []
    for b in range(step // TILE):
        flat = flat_ref[pl.ds(b * block, block), :].astype(F32)
        groups = [jnp.where(group == r, flat, 0.0).astype(BF16) for r in range(reps)]
        spreads.append(dot_f32(order_ref[...], jnp.concatenate(groups, axis=0), ((1,), (0,))))
    for p in range(half // reps):
        part = jnp.concatenate([x[p * TILE:(p + 1) * TILE] for x in spreads], axis=0)
        core_ref[pl.ds(start, step), p * LANES:(p + 1) * LANES] = part.astype(BF16)


STEP = 32


def slab_copies(snapshot_ref, first, slab_ref, half_index, sem):
    half = slab_ref.shape[1]
    fibers = pl.ds(pl.multiple_of(half_index * half, half), half)

    def copy(start, size):
        return pltpu.make_async_copy(
            snapshot_ref.at[pl.ds(start, size), fibers],
            slab_ref.at[pl.ds(start - first, size)],
            sem,
        )

    def start(begin, size, count):
        for part in range(count):
            copy(begin + part * (size // count), size // count).start()

    return start, lambda begin, size: copy(begin, size).wait()


def send_kernel(
    snapshot_ref, mode2_ref, core_ref, kept_ref, wide_ref, order_ref,
    slab_ref, small_ref, even_ref, odd_ref, sems, kept_sem, small_sem,
):
    cells, half, _ = slab_ref.shape
    rank = mode2_ref.shape[0]
    chunks = cells // STEP
    flat = (even_ref, odd_ref)
    sends = [
        slab_copies(snapshot_ref, 0, slab_ref, 1 - own_half(), sems.at[chunk])
        for chunk in range(chunks)
    ]
    start_kept, wait_kept = slab_copies(snapshot_ref, 0, kept_ref, own_half(), kept_sem)

    small = pltpu.make_async_copy(mode2_ref, small_ref, small_sem)
    small.start()
    for chunk in range(chunks):
        sends[chunk][0](chunk * STEP, STEP, 2 if chunk else 4)
    fill_order(order_ref, half)
    small.wait()
    wide_ref[...] = jnp.concatenate([small_ref[...]] * (LANES // rank), axis=0)
    for chunk in range(chunks):
        sends[chunk][1](chunk * STEP, STEP)
        if chunk == 0:
            start_kept(0, cells, 2 * chunks)
        multiply(slab_ref[pl.ds(chunk * STEP, STEP)], wide_ref, flat[chunk % 2])
        if chunk:
            spread(half, flat[(chunk - 1) % 2], order_ref, core_ref, (chunk - 1) * STEP)
    spread(half, flat[(chunks - 1) % 2], order_ref, core_ref, (chunks - 1) * STEP)
    wait_kept(0, cells)


def contract_send(snapshot, mode2_t):
    cells, fibers, depth = snapshot.shape
    rank = mode2_t.shape[0]
    half = fibers // 2
    reps = LANES // rank
    block = TILE * half
    pinned = pl.BlockSpec(memory_space=pltpu.HBM)
    return pl.pallas_call(
        send_kernel,
        in_specs=[pinned, pinned],
        out_shape=[
            jax.ShapeDtypeStruct((cells, half * rank), BF16),
            jax.ShapeDtypeStruct((cells, half, depth), BF16),
            jax.ShapeDtypeStruct((LANES, depth), BF16),
            jax.ShapeDtypeStruct((block // reps, block * reps), BF16),
        ],
        scratch_shapes=[
            pltpu.VMEM((cells, half, depth), BF16),
            pltpu.VMEM((rank, depth), BF16),
            pltpu.VMEM((STEP * half, LANES), BF16),
            pltpu.VMEM((STEP * half, LANES), BF16),
            pltpu.SemaphoreType.DMA((cells // STEP,)),
            pltpu.SemaphoreType.DMA,
            pltpu.SemaphoreType.DMA,
        ],
        compiler_params=params(24),
        name="contract_send",
    )(snapshot, mode2_t)


def own_kernel(slab_ref, wide_ref, order_ref, core_ref, even_ref, odd_ref):
    cells, half, _ = slab_ref.shape
    flat = (even_ref, odd_ref)
    chunks = cells // STEP
    for chunk in range(chunks):
        multiply(slab_ref[pl.ds(chunk * STEP, STEP)], wide_ref, flat[chunk % 2])
        if chunk:
            spread(half, flat[(chunk - 1) % 2], order_ref, core_ref, (chunk - 1) * STEP)
    spread(half, flat[(chunks - 1) % 2], order_ref, core_ref, (chunks - 1) * STEP)


def contract_own(slab, wide, order):
    cells, half, _ = slab.shape
    reps = order.shape[1] // (TILE * half)
    return pl.pallas_call(
        own_kernel,
        out_shape=jax.ShapeDtypeStruct((cells, half // reps * LANES), BF16),
        scratch_shapes=[pltpu.VMEM((STEP * half, LANES), BF16)] * 2,
        compiler_params=params(24),
        name="contract_own",
    )(slab, wide, order)


def is_even():
    return lax.rem(lax.axis_index("row"), 2) == 0


def project_kernel(kept, own_ref, got_ref, factor_ref, projected_ref, core_ref):
    rank = factor_ref.shape[0]
    width = core_ref.shape[1]
    odd = lax.rem(lax.axis_index("row"), 2)
    start = odd * width if kept else (1 - odd) * width
    where = pl.ds(pl.multiple_of(start, width), width)
    core = (own_ref[:, where].astype(F32) + got_ref[:, where].astype(F32)).astype(BF16)
    core_ref[...] = core
    projected = dot_f32(factor_ref[...], core, ((1,), (0,)))
    for block in range(width // LANES):
        part = projected[:, block * LANES:(block + 1) * LANES]
        projected_ref[pl.ds(block * rank, rank), :] = part.astype(projected_ref.dtype)


def project(own, got, factor_t, kept):
    cells, width = own.shape
    rows = factor_t.shape[0] * width // LANES // 2
    return pl.pallas_call(
        functools.partial(project_kernel, kept),
        out_shape=[
            jax.ShapeDtypeStruct((rows, LANES), F32 if kept else BF16),
            jax.ShapeDtypeStruct((cells, width // 2), BF16),
        ],
        compiler_params=params(8),
        name="project_kept" if kept else "project_sent",
    )(own, got, factor_t)


def add_kernel(mine_ref, got_ref, *refs):
    total = mine_ref[...].astype(F32) + got_ref[...].astype(F32)
    refs[-1][...] = total.astype(refs[-1].dtype)


def add(mine, got, *after):
    whole = pl.BlockSpec(memory_space=pltpu.VMEM)
    return pl.pallas_call(
        add_kernel,
        in_specs=[whole, whole] + [pl.BlockSpec(memory_space=pl.ANY)] * len(after),
        out_shape=jax.ShapeDtypeStruct(got.shape, got.dtype),
        compiler_params=params(4),
        name="add",
    )(mine, got, *after)


def product_kernel(mine_ref, got_ref, projected_ref, out_ref):
    blocks = mine_ref.shape[1] // LANES
    rank = projected_ref.shape[0] // blocks
    projected = jnp.concatenate(
        [projected_ref[pl.ds(block * rank, rank), :] for block in range(blocks)], axis=1
    )
    terms = [dot_f32(projected, ref[...], ((1,), (1,))) for ref in (mine_ref, got_ref)]
    even = is_even()
    low = jnp.where(even, terms[0], terms[1])
    high = jnp.where(even, terms[1], terms[0])
    out_ref[...] = jnp.concatenate([low, high], axis=0).astype(BF16)


def product_terms(mine, got, projected):
    return pl.pallas_call(
        product_kernel,
        out_shape=jax.ShapeDtypeStruct((LANES, mine.shape[0]), BF16),
        compiler_params=params(4),
        name="product_terms",
    )(mine, got, projected)


def pair_product(term_ref, first_ref, second_ref):
    got = jnp.where(own_half() == 0, first_ref[...].astype(F32), second_ref[...].astype(F32))
    return term_ref[...].astype(F32) + got


def gram_kernel(term_ref, first_ref, second_ref, last_ref, out_ref):
    rank = LANES // 2
    pairs = [
        pair_product(term_ref, first_ref, second_ref),
        pair_product(last_ref, second_ref, first_ref),
    ]
    product = jnp.concatenate([x[k:k + rank] for x in pairs for k in (0, rank)], axis=1)
    gram = dot_parts(product, product, 1)
    out_ref[...] = jnp.concatenate([gram[:rank // 2], gram[rank // 2:]], axis=1)


def local_gram(*terms):
    return pl.pallas_call(
        gram_kernel,
        out_shape=jax.ShapeDtypeStruct((LANES // 4, LANES), F32),
        compiler_params=params(4),
        name="local_gram",
    )(*terms)


def parts(x):
    high = x.astype(BF16)
    return high, (x - high.astype(F32)).astype(BF16)


def dot_parts(a, b, axis):
    (ah, al), (bh, bl) = parts(a), parts(b)
    left = jnp.concatenate([ah, ah, al], axis=axis)
    right = jnp.concatenate([bh, bl, bh], axis=axis)
    return dot_f32(left, right, ((axis,), (axis,)))


def eliminate(packed, spread_ref):
    rank = packed.shape[1] // 2
    tile = 8
    count = rank // tile
    wide = 2 * rank
    sublane = lax.broadcasted_iota(jnp.int32, (tile, wide), 0)
    lane = lax.broadcasted_iota(jnp.int32, (tile, wide), 1)
    full = lambda x: jnp.broadcast_to(x, (tile, wide))
    both = []
    for v in range(count):
        at = v % (count // 2) * tile
        mine = packed[at:at + tile]
        if v >= count // 2:
            mine = jnp.concatenate([mine[:, rank:], mine[:, :rank]], axis=1)
        both.append(jnp.where(lane < rank, mine, (lane - rank == sublane + v * tile).astype(F32)))
    def lanes(v, p):
        return [full(both[v][:, p * tile + k:p * tile + k + 1]) for k in range(tile)]

    slots = [0]

    def spread(x, count):
        at = slots[0] * tile
        slots[0] += 1
        spread_ref[pl.ds(at, tile), :] = x
        return [full(spread_ref[pl.ds(at + j, 1), :]) for j in range(count)]

    pivots = []
    diagonal = lanes(0, 0)
    for p in range(count):
        columns = [spread(diagonal[k], tile) for k in range(tile)]
        block = [[columns[k][j] for k in range(j + 1)] for j in range(tile)]
        rows = spread(both[p], tile)
        below = range(p + 1, count)
        cols = {v: lanes(v, p) for v in below}
        diagonal = lanes(p + 1, p + 1) if below else []
        found, kept = block[0][0], rows[0]
        for j in range(tile):
            if j:
                found = jnp.where(sublane == j, block[j][j], found)
                kept = jnp.where(sublane == j, rows[j], kept)
            inverse = pl.reciprocal(block[j][j], approx=True, full_range=False)
            scaled = {i: block[i][j] * inverse for i in range(j + 1, tile)}
            for i, factor in scaled.items():
                for k in range(j + 1, i + 1):
                    if i == j + 1:
                        update = block[i][j] * block[k][j] * inverse
                    else:
                        update = factor * block[k][j]
                    block[i][k] = block[i][k] - update
                rows[i] = rows[i] - factor * rows[j]
            if below:
                column = cols[p + 1][j]
                entries = spread(column, tile)
                diagonal = [x - column * e * inverse for x, e in zip(diagonal, entries)]
            row = rows[j] * inverse
            for v in below:
                for i, factor in scaled.items():
                    cols[v][i] = cols[v][i] - factor * cols[v][j]
                both[v] = both[v] - cols[v][j] * row
        both[p] = kept
        pivots.append(found)
    return both, pivots


def finish_kernel(
    total_rows, term_ref, first_ref, second_ref, gram_ref, got_gram_ref, out_ref, spread_ref
):
    rank = LANES // 2
    both, pivots = eliminate(gram_ref[...] + got_gram_ref[...], spread_ref)
    scale = total_rows ** 0.5
    inverse = jnp.concatenate([b * (lax.rsqrt(p) * scale) for b, p in zip(both, pivots)], axis=0)
    inverse = inverse[:, rank:]
    half = term_ref.shape[1] // 2
    product = pair_product(term_ref, first_ref, second_ref)
    product = jnp.where(is_even(), product[:rank], product[rank:])
    mine = jnp.where(lax.axis_index("col") == 0, product[:, :half], product[:, half:]).T
    out_ref[...] = dot_parts(mine, inverse, 1)


def finish(total_rows, term, first, second, gram, got_gram):
    return pl.pallas_call(
        functools.partial(finish_kernel, total_rows),
        out_shape=jax.ShapeDtypeStruct((term.shape[1] // 2, LANES // 2), F32),
        scratch_shapes=[pltpu.VMEM((LANES // 2 * 17, LANES), F32)],
        compiler_params=params(4),
        name="finish",
    )(term, first, second, gram, got_gram)


def per_device(snapshot, mode2_factor, old_factor):
    n_rows, n_cols = lax.axis_size("row"), lax.axis_size("col")
    masks = [1 << bit for bit in range(n_rows.bit_length() - 1)]
    total_rows = snapshot.shape[0] * n_rows

    def swap(x, mask, other=None):
        pairs = []
        for r in range(n_rows):
            for c in range(n_cols):
                second = (c + r.bit_count()) % 2 and other is not None
                to = r ^ (other if second else mask)
                pairs.append((r * n_cols + c, to * n_cols + (c + 1) % n_cols))
        return lax.ppermute(x, ("row", "col"), pairs)

    snapshot = pltpu.with_memory_space_constraint(snapshot, pltpu.HBM)
    mode2_t = pltpu.with_memory_space_constraint(mode2_factor.T, pltpu.HBM)
    send, kept, wide, order = contract_send(snapshot, mode2_t)
    got = swap(send, 0)
    own = contract_own(kept, wide, order)

    send, give = project(own, got, old_factor.T, False)
    keep, columns = project(own, got, old_factor.T, True)
    mine = add(keep, swap(send, masks[0]))
    got_columns = swap(give, masks[0])
    others = masks[1:]
    turned = others[len(others) // 2:] + others[:len(others) // 2]
    for step, (mask, other) in enumerate(zip(others, turned)):
        after = [got_columns] if step == 1 else []
        mine = add(mine, swap(mine, mask, other), *after)

    term = product_terms(columns, got_columns, mine)
    term = add(term, swap(term, 0))
    pair, next_pair = masks[:2]
    first, second = swap(term, pair, next_pair), swap(term, next_pair, pair)
    gram = local_gram(term, first, second, swap(term, pair | next_pair))
    for mask in masks[2:-1]:
        gram = add(gram, swap(gram, mask))
    return finish(total_rows, term, first, second, gram, swap(gram, masks[-1]))


def solution(mesh):
    return jax.shard_map(
        per_device,
        mesh=mesh,
        in_specs=(
            P(("groups", "row"), None, "col"),
            P(("groups", "col"), None),
            P(("groups", "row"), None),
        ),
        out_specs=P(("groups", "row", "col"), None),
        check_vma=False,
    )
```

```python
import functools

import jax
import jax.numpy as jnp
from jax import lax
from jax.experimental import pallas as pl
from jax.experimental.pallas import tpu as pltpu
from jax.sharding import PartitionSpec as P

F32 = jnp.float32
BF16 = jnp.bfloat16
LANES = 128
MIB = 2**20


def dot_f32(a, b, dims, precision=None):
    return lax.dot_general(a, b, (dims, ((), ())), precision=precision, preferred_element_type=F32)


def params(mib):
    return pltpu.CompilerParams(vmem_limit_bytes=mib * MIB)


def own_half():
    row = lax.axis_index("row")
    half = lax.axis_index("col")
    for bit in range(lax.axis_size("row").bit_length() - 1):
        half += lax.rem(lax.div(row, 1 << bit), 2)
    return lax.rem(half, 2)


TILE = 8


def fill_order(order_ref, half):
    block = TILE * half
    to = lax.broadcasted_iota(jnp.int32, order_ref.shape, 0)
    at = lax.broadcasted_iota(jnp.int32, order_ref.shape, 1)
    cell = lax.div(lax.rem(at, block), half)
    wanted = lax.div(to, TILE) * (order_ref.shape[1] // block) + lax.div(at, block)
    same = (lax.rem(to, TILE) == cell) & (wanted == lax.rem(at, half))
    order_ref[...] = same.astype(F32).astype(BF16)


def multiply(slab, wide_ref, flat_ref):
    cells, half, depth = slab.shape
    x = slab.reshape(cells * half, depth)
    low = dot_f32(x[:, :depth // 2], wide_ref[:, :depth // 2], ((1,), (1,)))
    high = dot_f32(x[:, depth // 2:], wide_ref[:, depth // 2:], ((1,), (1,)))
    flat_ref[...] = (low + high).astype(BF16)


def spread(half, flat_ref, order_ref, core_ref, start):
    block = TILE * half
    reps = order_ref.shape[1] // block
    step = flat_ref.shape[0] // half
    group = lax.div(lax.broadcasted_iota(jnp.int32, (block, LANES), 1), LANES // reps)
    spreads = []
    for b in range(step // TILE):
        flat = flat_ref[pl.ds(b * block, block), :].astype(F32)
        groups = [jnp.where(group == r, flat, 0.0).astype(BF16) for r in range(reps)]
        spreads.append(dot_f32(order_ref[...], jnp.concatenate(groups, axis=0), ((1,), (0,))))
    for p in range(half // reps):
        part = jnp.concatenate([x[p * TILE:(p + 1) * TILE] for x in spreads], axis=0)
        core_ref[pl.ds(start, step), p * LANES:(p + 1) * LANES] = part.astype(BF16)


STEP = 32


def slab_copies(snapshot_ref, first, slab_ref, half_index, sem):
    half = slab_ref.shape[1]
    fibers = pl.ds(pl.multiple_of(half_index * half, half), half)

    def copy(start, size):
        return pltpu.make_async_copy(
            snapshot_ref.at[pl.ds(start, size), fibers],
            slab_ref.at[pl.ds(start - first, size)],
            sem,
        )

    def start(begin, size, count):
        for part in range(count):
            copy(begin + part * (size // count), size // count).start()

    return start, lambda begin, size: copy(begin, size).wait()


def send_kernel(
    snapshot_ref, mode2_ref, core_ref, kept_ref, part_ref, wide_ref, order_ref,
    slab_ref, small_ref, even_ref, odd_ref, sems, kept_sems, small_sem,
):
    cells, half, _ = slab_ref.shape
    rank = mode2_ref.shape[0]
    chunks = cells // STEP
    flat = (even_ref, odd_ref)
    sends = [
        slab_copies(snapshot_ref, 0, slab_ref, 1 - own_half(), sems.at[chunk])
        for chunk in range(chunks)
    ]
    (start_first, wait_first), (start_rest, wait_rest) = (
        slab_copies(snapshot_ref, 0, kept_ref, own_half(), kept_sems.at[k]) for k in range(2)
    )

    small = pltpu.make_async_copy(mode2_ref, small_ref, small_sem)
    small.start()
    for chunk in range(chunks):
        sends[chunk][0](chunk * STEP, STEP, 2 if chunk else 4)
    fill_order(order_ref, half)
    small.wait()
    wide_ref[...] = jnp.concatenate([small_ref[...]] * (LANES // rank), axis=0)
    for chunk in range(chunks):
        sends[chunk][1](chunk * STEP, STEP)
        if chunk == 0:
            start_first(0, STEP, 4)
            start_rest(STEP, cells - STEP, 2 * (chunks - 1))
        multiply(slab_ref[pl.ds(chunk * STEP, STEP)], wide_ref, flat[chunk % 2])
        if chunk:
            spread(half, flat[(chunk - 1) % 2], order_ref, core_ref, (chunk - 1) * STEP)
    spread(half, flat[(chunks - 1) % 2], order_ref, core_ref, (chunks - 1) * STEP)
    wait_first(0, STEP)
    multiply(kept_ref[pl.ds(0, STEP)], wide_ref, flat[chunks % 2])
    spread(half, flat[chunks % 2], order_ref, part_ref, 0)
    wait_rest(STEP, cells - STEP)


def contract_send(snapshot, mode2_t):
    cells, fibers, depth = snapshot.shape
    rank = mode2_t.shape[0]
    half = fibers // 2
    reps = LANES // rank
    block = TILE * half
    pinned = pl.BlockSpec(memory_space=pltpu.HBM)
    return pl.pallas_call(
        send_kernel,
        in_specs=[pinned, pinned],
        out_shape=[
            jax.ShapeDtypeStruct((cells, half * rank), BF16),
            jax.ShapeDtypeStruct((cells, half, depth), BF16),
            jax.ShapeDtypeStruct((STEP, half * rank), BF16),
            jax.ShapeDtypeStruct((LANES, depth), BF16),
            jax.ShapeDtypeStruct((block // reps, block * reps), BF16),
        ],
        scratch_shapes=[
            pltpu.VMEM((cells, half, depth), BF16),
            pltpu.VMEM((rank, depth), BF16),
            pltpu.VMEM((STEP * half, LANES), BF16),
            pltpu.VMEM((STEP * half, LANES), BF16),
            pltpu.SemaphoreType.DMA((cells // STEP,)),
            pltpu.SemaphoreType.DMA((2,)),
            pltpu.SemaphoreType.DMA,
        ],
        compiler_params=params(24),
        name="contract_send",
    )(snapshot, mode2_t)


def own_kernel(slab_ref, part_ref, wide_ref, order_ref, core_ref, even_ref, odd_ref):
    cells, half, _ = slab_ref.shape
    flat = (even_ref, odd_ref)
    chunks = cells // STEP
    core_ref[pl.ds(0, STEP), :] = part_ref[...]
    for chunk in range(1, chunks):
        multiply(slab_ref[pl.ds(chunk * STEP, STEP)], wide_ref, flat[chunk % 2])
        if chunk > 1:
            spread(half, flat[(chunk - 1) % 2], order_ref, core_ref, (chunk - 1) * STEP)
    spread(half, flat[(chunks - 1) % 2], order_ref, core_ref, (chunks - 1) * STEP)


def contract_own(slab, part, wide, order):
    cells, half, _ = slab.shape
    reps = order.shape[1] // (TILE * half)
    return pl.pallas_call(
        own_kernel,
        out_shape=jax.ShapeDtypeStruct((cells, half // reps * LANES), BF16),
        scratch_shapes=[pltpu.VMEM((STEP * half, LANES), BF16)] * 2,
        compiler_params=params(24),
        name="contract_own",
    )(slab, part, wide, order)


def is_even():
    return lax.rem(lax.axis_index("row"), 2) == 0


def project_kernel(kept, own_ref, got_ref, factor_ref, projected_ref, core_ref):
    rank = factor_ref.shape[0]
    width = core_ref.shape[1]
    odd = lax.rem(lax.axis_index("row"), 2)
    start = odd * width if kept else (1 - odd) * width
    where = pl.ds(pl.multiple_of(start, width), width)
    core = (own_ref[:, where].astype(F32) + got_ref[:, where].astype(F32)).astype(BF16)
    core_ref[...] = core
    projected = dot_f32(factor_ref[...], core, ((1,), (0,)))
    for block in range(width // LANES):
        part = projected[:, block * LANES:(block + 1) * LANES]
        projected_ref[pl.ds(block * rank, rank), :] = part.astype(projected_ref.dtype)


def project(own, got, factor_t, kept):
    cells, width = own.shape
    rows = factor_t.shape[0] * width // LANES // 2
    return pl.pallas_call(
        functools.partial(project_kernel, kept),
        out_shape=[
            jax.ShapeDtypeStruct((rows, LANES), F32 if kept else BF16),
            jax.ShapeDtypeStruct((cells, width // 2), BF16),
        ],
        compiler_params=params(8),
        name="project_kept" if kept else "project_sent",
    )(own, got, factor_t)


def add_kernel(mine_ref, got_ref, *refs):
    total = mine_ref[...].astype(F32) + got_ref[...].astype(F32)
    refs[-1][...] = total.astype(refs[-1].dtype)


def add(mine, got, *after):
    whole = pl.BlockSpec(memory_space=pltpu.VMEM)
    return pl.pallas_call(
        add_kernel,
        in_specs=[whole, whole] + [pl.BlockSpec(memory_space=pl.ANY)] * len(after),
        out_shape=jax.ShapeDtypeStruct(got.shape, got.dtype),
        compiler_params=params(4),
        name="add",
    )(mine, got, *after)


def product_kernel(mine_ref, got_ref, projected_ref, out_ref):
    blocks = mine_ref.shape[1] // LANES
    rank = projected_ref.shape[0] // blocks
    projected = jnp.concatenate(
        [projected_ref[pl.ds(block * rank, rank), :] for block in range(blocks)], axis=1
    )
    terms = [dot_f32(projected, ref[...], ((1,), (1,))) for ref in (mine_ref, got_ref)]
    even = is_even()
    low = jnp.where(even, terms[0], terms[1])
    high = jnp.where(even, terms[1], terms[0])
    out_ref[...] = jnp.concatenate([low, high], axis=0).astype(BF16)


def product_terms(mine, got, projected):
    return pl.pallas_call(
        product_kernel,
        out_shape=jax.ShapeDtypeStruct((LANES, mine.shape[0]), BF16),
        compiler_params=params(4),
        name="product_terms",
    )(mine, got, projected)


def pair_product(term_ref, first_ref, second_ref):
    got = jnp.where(own_half() == 0, first_ref[...].astype(F32), second_ref[...].astype(F32))
    return term_ref[...].astype(F32) + got


def gram_kernel(term_ref, first_ref, second_ref, last_ref, out_ref):
    rank = LANES // 2
    pairs = [
        pair_product(term_ref, first_ref, second_ref),
        pair_product(last_ref, second_ref, first_ref),
    ]
    product = jnp.concatenate([x[k:k + rank] for x in pairs for k in (0, rank)], axis=1)
    gram = dot_parts(product, product, 1)
    out_ref[...] = jnp.concatenate([gram[:rank // 2], gram[rank // 2:]], axis=1)


def local_gram(*terms):
    return pl.pallas_call(
        gram_kernel,
        out_shape=jax.ShapeDtypeStruct((LANES // 4, LANES), F32),
        compiler_params=params(4),
        name="local_gram",
    )(*terms)


def parts(x):
    high = x.astype(BF16)
    return high, (x - high.astype(F32)).astype(BF16)


def dot_parts(a, b, axis):
    (ah, al), (bh, bl) = parts(a), parts(b)
    left = jnp.concatenate([ah, ah, al], axis=axis)
    right = jnp.concatenate([bh, bl, bh], axis=axis)
    return dot_f32(left, right, ((axis,), (axis,)))


def eliminate(packed, spread_ref):
    rank = packed.shape[1] // 2
    tile = 8
    count = rank // tile
    wide = 2 * rank
    sublane = lax.broadcasted_iota(jnp.int32, (tile, wide), 0)
    lane = lax.broadcasted_iota(jnp.int32, (tile, wide), 1)
    full = lambda x: jnp.broadcast_to(x, (tile, wide))
    both = []
    for v in range(count):
        at = v % (count // 2) * tile
        mine = packed[at:at + tile]
        if v >= count // 2:
            mine = jnp.concatenate([mine[:, rank:], mine[:, :rank]], axis=1)
        both.append(jnp.where(lane < rank, mine, (lane - rank == sublane + v * tile).astype(F32)))
    def lanes(v, p):
        return [full(both[v][:, p * tile + k:p * tile + k + 1]) for k in range(tile)]

    slots = [0]

    def spread(x, count):
        at = slots[0] * tile
        slots[0] += 1
        spread_ref[pl.ds(at, tile), :] = x
        return [full(spread_ref[pl.ds(at + j, 1), :]) for j in range(count)]

    pivots = []
    diagonal = lanes(0, 0)
    for p in range(count):
        columns = [spread(diagonal[k], tile) for k in range(tile)]
        block = [[columns[k][j] for k in range(j + 1)] for j in range(tile)]
        rows = spread(both[p], tile)
        below = range(p + 1, count)
        cols = {v: lanes(v, p) for v in below}
        diagonal = lanes(p + 1, p + 1) if below else []
        found, kept = block[0][0], rows[0]
        for j in range(tile):
            if j:
                found = jnp.where(sublane == j, block[j][j], found)
                kept = jnp.where(sublane == j, rows[j], kept)
            inverse = pl.reciprocal(block[j][j], approx=True, full_range=False)
            scaled = {i: block[i][j] * inverse for i in range(j + 1, tile)}
            for i, factor in scaled.items():
                for k in range(j + 1, i + 1):
                    block[i][k] = block[i][k] - factor * block[k][j]
                rows[i] = rows[i] - factor * rows[j]
            if below:
                column = cols[p + 1][j]
                entries = spread(column, tile)
                diagonal = [x - column * (e * inverse) for x, e in zip(diagonal, entries)]
            row = rows[j] * inverse
            for v in below:
                for i, factor in scaled.items():
                    cols[v][i] = cols[v][i] - factor * cols[v][j]
                both[v] = both[v] - cols[v][j] * row
        both[p] = kept
        pivots.append(found)
    return both, pivots


def finish_kernel(
    total_rows, term_ref, first_ref, second_ref, gram_ref, got_gram_ref, out_ref, spread_ref
):
    rank = LANES // 2
    both, pivots = eliminate(gram_ref[...] + got_gram_ref[...], spread_ref)
    scale = total_rows ** 0.5
    inverse = jnp.concatenate([b * (lax.rsqrt(p) * scale) for b, p in zip(both, pivots)], axis=0)
    inverse = inverse[:, rank:]
    half = term_ref.shape[1] // 2
    product = pair_product(term_ref, first_ref, second_ref)
    product = jnp.where(is_even(), product[:rank], product[rank:])
    mine = jnp.where(lax.axis_index("col") == 0, product[:, :half], product[:, half:]).T
    out_ref[...] = dot_parts(mine, inverse, 1)


def finish(total_rows, term, first, second, gram, got_gram):
    return pl.pallas_call(
        functools.partial(finish_kernel, total_rows),
        out_shape=jax.ShapeDtypeStruct((term.shape[1] // 2, LANES // 2), F32),
        scratch_shapes=[pltpu.VMEM((LANES // 2 * 17, LANES), F32)],
        compiler_params=params(4),
        name="finish",
    )(term, first, second, gram, got_gram)


def per_device(snapshot, mode2_factor, old_factor):
    n_rows, n_cols = lax.axis_size("row"), lax.axis_size("col")
    masks = [1 << bit for bit in range(n_rows.bit_length() - 1)]
    total_rows = snapshot.shape[0] * n_rows

    def swap(x, mask, other=None):
        pairs = []
        for r in range(n_rows):
            for c in range(n_cols):
                second = (c + r.bit_count()) % 2 and other is not None
                to = r ^ (other if second else mask)
                pairs.append((r * n_cols + c, to * n_cols + (c + 1) % n_cols))
        return lax.ppermute(x, ("row", "col"), pairs)

    snapshot = pltpu.with_memory_space_constraint(snapshot, pltpu.HBM)
    mode2_t = pltpu.with_memory_space_constraint(mode2_factor.T, pltpu.HBM)
    send, kept, part, wide, order = contract_send(snapshot, mode2_t)
    got = swap(send, 0)
    own = contract_own(kept, part, wide, order)

    send, give = project(own, got, old_factor.T, False)
    keep, columns = project(own, got, old_factor.T, True)
    mine = add(keep, swap(send, masks[0]))
    got_columns = swap(give, masks[0])
    others = masks[1:]
    turned = others[len(others) // 2:] + others[:len(others) // 2]
    for step, (mask, other) in enumerate(zip(others, turned)):
        after = [got_columns] if step == 1 else []
        mine = add(mine, swap(mine, mask, other), *after)

    term = product_terms(columns, got_columns, mine)
    term = add(term, swap(term, 0))
    pair, next_pair = masks[:2]
    first, second = swap(term, pair, next_pair), swap(term, next_pair, pair)
    gram = local_gram(term, first, second, swap(term, pair | next_pair))
    for mask in masks[2:-1]:
        gram = add(gram, swap(gram, mask))
    return finish(total_rows, term, first, second, gram, swap(gram, masks[-1]))


def solution(mesh):
    return jax.shard_map(
        per_device,
        mesh=mesh,
        in_specs=(
            P(("groups", "row"), None, "col"),
            P(("groups", "col"), None),
            P(("groups", "row"), None),
        ),
        out_specs=P(("groups", "row", "col"), None),
        check_vma=False,
    )
```

```python
import functools

import jax
import jax.numpy as jnp
from jax import lax
from jax.experimental import pallas as pl
from jax.experimental.pallas import tpu as pltpu
from jax.sharding import PartitionSpec as P

F32 = jnp.float32
BF16 = jnp.bfloat16
LANES = 128
MIB = 2**20


def dot_f32(a, b, dims, precision=None):
    return lax.dot_general(a, b, (dims, ((), ())), precision=precision, preferred_element_type=F32)


def params(mib):
    return pltpu.CompilerParams(vmem_limit_bytes=mib * MIB)


def own_half():
    row = lax.axis_index("row")
    half = lax.axis_index("col")
    for bit in range(lax.axis_size("row").bit_length() - 1):
        half += lax.rem(lax.div(row, 1 << bit), 2)
    return lax.rem(half, 2)


TILE = 8


def fill_order(order_ref, half):
    block = TILE * half
    to = lax.broadcasted_iota(jnp.int32, order_ref.shape, 0)
    at = lax.broadcasted_iota(jnp.int32, order_ref.shape, 1)
    cell = lax.div(lax.rem(at, block), half)
    wanted = lax.div(to, TILE) * (order_ref.shape[1] // block) + lax.div(at, block)
    same = (lax.rem(to, TILE) == cell) & (wanted == lax.rem(at, half))
    order_ref[...] = same.astype(F32).astype(BF16)


def multiply(slab, wide_ref, flat_ref):
    cells, half, depth = slab.shape
    x = slab.reshape(cells * half, depth)
    low = dot_f32(x[:, :depth // 2], wide_ref[:, :depth // 2], ((1,), (1,)))
    high = dot_f32(x[:, depth // 2:], wide_ref[:, depth // 2:], ((1,), (1,)))
    flat_ref[...] = (low + high).astype(BF16)


def spread(half, flat_ref, order_ref, core_ref, start):
    block = TILE * half
    reps = order_ref.shape[1] // block
    step = flat_ref.shape[0] // half
    group = lax.div(lax.broadcasted_iota(jnp.int32, (block, LANES), 1), LANES // reps)
    spreads = []
    for b in range(step // TILE):
        flat = flat_ref[pl.ds(b * block, block), :].astype(F32)
        groups = [jnp.where(group == r, flat, 0.0).astype(BF16) for r in range(reps)]
        spreads.append(dot_f32(order_ref[...], jnp.concatenate(groups, axis=0), ((1,), (0,))))
    for p in range(half // reps):
        part = jnp.concatenate([x[p * TILE:(p + 1) * TILE] for x in spreads], axis=0)
        core_ref[pl.ds(start, step), p * LANES:(p + 1) * LANES] = part.astype(BF16)


STEP = 32


def slab_copies(snapshot_ref, first, slab_ref, half_index, sem):
    half = slab_ref.shape[1]
    fibers = pl.ds(pl.multiple_of(half_index * half, half), half)

    def copy(start, size):
        return pltpu.make_async_copy(
            snapshot_ref.at[pl.ds(start, size), fibers],
            slab_ref.at[pl.ds(start - first, size)],
            sem,
        )

    def start(begin, size, count):
        for part in range(count):
            copy(begin + part * (size // count), size // count).start()

    return start, lambda begin, size: copy(begin, size).wait()


def send_kernel(
    snapshot_ref, mode2_ref, core_ref, kept_ref, wide_ref, order_ref,
    slab_ref, small_ref, even_ref, odd_ref, sems, kept_sem, small_sem,
):
    cells, half, _ = slab_ref.shape
    rank = mode2_ref.shape[0]
    chunks = cells // STEP
    flat = (even_ref, odd_ref)
    sends = [
        slab_copies(snapshot_ref, 0, slab_ref, 1 - own_half(), sems.at[chunk])
        for chunk in range(chunks)
    ]
    start_kept, wait_kept = slab_copies(snapshot_ref, 0, kept_ref, own_half(), kept_sem)

    small = pltpu.make_async_copy(mode2_ref, small_ref, small_sem)
    small.start()
    sends[0][0](0, STEP, 8)
    sends[1][0](STEP, STEP, 2)
    fill_order(order_ref, half)
    small.wait()
    wide_ref[...] = jnp.concatenate([small_ref[...]] * (LANES // rank), axis=0)
    for chunk in range(chunks):
        sends[chunk][1](chunk * STEP, STEP)
        if chunk == 0:
            for later in range(2, chunks):
                sends[later][0](later * STEP, STEP, 2)
        if chunk < 2:
            start_kept(chunk * (cells // 2), cells // 2, chunks)
        multiply(slab_ref[pl.ds(chunk * STEP, STEP)], wide_ref, flat[chunk % 2])
        if chunk:
            spread(half, flat[(chunk - 1) % 2], order_ref, core_ref, (chunk - 1) * STEP)
    spread(half, flat[(chunks - 1) % 2], order_ref, core_ref, (chunks - 1) * STEP)
    wait_kept(0, cells)


def contract_send(snapshot, mode2_t):
    cells, fibers, depth = snapshot.shape
    rank = mode2_t.shape[0]
    half = fibers // 2
    reps = LANES // rank
    block = TILE * half
    pinned = pl.BlockSpec(memory_space=pltpu.HBM)
    return pl.pallas_call(
        send_kernel,
        in_specs=[pinned, pinned],
        out_shape=[
            jax.ShapeDtypeStruct((cells, half * rank), BF16),
            jax.ShapeDtypeStruct((cells, half, depth), BF16),
            jax.ShapeDtypeStruct((LANES, depth), BF16),
            jax.ShapeDtypeStruct((block // reps, block * reps), BF16),
        ],
        scratch_shapes=[
            pltpu.VMEM((cells, half, depth), BF16),
            pltpu.VMEM((rank, depth), BF16),
            pltpu.VMEM((STEP * half, LANES), BF16),
            pltpu.VMEM((STEP * half, LANES), BF16),
            pltpu.SemaphoreType.DMA((cells // STEP,)),
            pltpu.SemaphoreType.DMA,
            pltpu.SemaphoreType.DMA,
        ],
        compiler_params=params(24),
        name="contract_send",
    )(snapshot, mode2_t)


def own_kernel(slab_ref, wide_ref, order_ref, core_ref, even_ref, odd_ref):
    cells, half, _ = slab_ref.shape
    flat = (even_ref, odd_ref)
    chunks = cells // STEP
    for chunk in range(chunks):
        multiply(slab_ref[pl.ds(chunk * STEP, STEP)], wide_ref, flat[chunk % 2])
        if chunk:
            spread(half, flat[(chunk - 1) % 2], order_ref, core_ref, (chunk - 1) * STEP)
    spread(half, flat[(chunks - 1) % 2], order_ref, core_ref, (chunks - 1) * STEP)


def contract_own(slab, wide, order):
    cells, half, _ = slab.shape
    reps = order.shape[1] // (TILE * half)
    return pl.pallas_call(
        own_kernel,
        out_shape=jax.ShapeDtypeStruct((cells, half // reps * LANES), BF16),
        scratch_shapes=[pltpu.VMEM((STEP * half, LANES), BF16)] * 2,
        compiler_params=params(24),
        name="contract_own",
    )(slab, wide, order)


def is_even():
    return lax.rem(lax.axis_index("row"), 2) == 0


def project_kernel(kept, own_ref, got_ref, factor_ref, projected_ref, core_ref):
    rank = factor_ref.shape[0]
    width = core_ref.shape[1]
    odd = lax.rem(lax.axis_index("row"), 2)
    start = odd * width if kept else (1 - odd) * width
    where = pl.ds(pl.multiple_of(start, width), width)
    core = (own_ref[:, where].astype(F32) + got_ref[:, where].astype(F32)).astype(BF16)
    core_ref[...] = core
    projected = dot_f32(factor_ref[...], core, ((1,), (0,)))
    for block in range(width // LANES):
        part = projected[:, block * LANES:(block + 1) * LANES]
        projected_ref[pl.ds(block * rank, rank), :] = part.astype(projected_ref.dtype)


def project(own, got, factor_t, kept):
    cells, width = own.shape
    rows = factor_t.shape[0] * width // LANES // 2
    return pl.pallas_call(
        functools.partial(project_kernel, kept),
        out_shape=[
            jax.ShapeDtypeStruct((rows, LANES), F32 if kept else BF16),
            jax.ShapeDtypeStruct((cells, width // 2), BF16),
        ],
        compiler_params=params(8),
        name="project_kept" if kept else "project_sent",
    )(own, got, factor_t)


def add_kernel(mine_ref, got_ref, *refs):
    total = mine_ref[...].astype(F32) + got_ref[...].astype(F32)
    refs[-1][...] = total.astype(refs[-1].dtype)


def add(mine, got, *after):
    whole = pl.BlockSpec(memory_space=pltpu.VMEM)
    return pl.pallas_call(
        add_kernel,
        in_specs=[whole, whole] + [pl.BlockSpec(memory_space=pl.ANY)] * len(after),
        out_shape=jax.ShapeDtypeStruct(got.shape, got.dtype),
        compiler_params=params(4),
        name="add",
    )(mine, got, *after)


def product_kernel(mine_ref, got_ref, projected_ref, out_ref):
    blocks = mine_ref.shape[1] // LANES
    rank = projected_ref.shape[0] // blocks
    projected = jnp.concatenate(
        [projected_ref[pl.ds(block * rank, rank), :] for block in range(blocks)], axis=1
    )
    terms = [dot_f32(projected, ref[...], ((1,), (1,))) for ref in (mine_ref, got_ref)]
    even = is_even()
    low = jnp.where(even, terms[0], terms[1])
    high = jnp.where(even, terms[1], terms[0])
    out_ref[...] = jnp.concatenate([low, high], axis=0).astype(BF16)


def product_terms(mine, got, projected):
    return pl.pallas_call(
        product_kernel,
        out_shape=jax.ShapeDtypeStruct((LANES, mine.shape[0]), BF16),
        compiler_params=params(4),
        name="product_terms",
    )(mine, got, projected)


def pair_product(term_ref, first_ref, second_ref):
    got = jnp.where(own_half() == 0, first_ref[...].astype(F32), second_ref[...].astype(F32))
    return term_ref[...].astype(F32) + got


def gram_kernel(term_ref, first_ref, second_ref, last_ref, out_ref):
    rank = LANES // 2
    pairs = [
        pair_product(term_ref, first_ref, second_ref),
        pair_product(last_ref, second_ref, first_ref),
    ]
    product = jnp.concatenate([x[k:k + rank] for x in pairs for k in (0, rank)], axis=1)
    gram = dot_parts(product, product, 1)
    out_ref[...] = jnp.concatenate([gram[:rank // 2], gram[rank // 2:]], axis=1)


def local_gram(*terms):
    return pl.pallas_call(
        gram_kernel,
        out_shape=jax.ShapeDtypeStruct((LANES // 4, LANES), F32),
        compiler_params=params(4),
        name="local_gram",
    )(*terms)


def parts(x):
    high = x.astype(BF16)
    return high, (x - high.astype(F32)).astype(BF16)


def dot_parts(a, b, axis):
    (ah, al), (bh, bl) = parts(a), parts(b)
    left = jnp.concatenate([ah, ah, al], axis=axis)
    right = jnp.concatenate([bh, bl, bh], axis=axis)
    return dot_f32(left, right, ((axis,), (axis,)))


def eliminate(packed, spread_ref):
    rank = packed.shape[1] // 2
    tile = 8
    count = rank // tile
    wide = 2 * rank
    sublane = lax.broadcasted_iota(jnp.int32, (tile, wide), 0)
    lane = lax.broadcasted_iota(jnp.int32, (tile, wide), 1)
    full = lambda x: jnp.broadcast_to(x, (tile, wide))
    both = []
    for v in range(count):
        at = v % (count // 2) * tile
        mine = packed[at:at + tile]
        if v >= count // 2:
            mine = jnp.concatenate([mine[:, rank:], mine[:, :rank]], axis=1)
        both.append(jnp.where(lane < rank, mine, (lane - rank == sublane + v * tile).astype(F32)))
    def lanes(v, p):
        return [full(both[v][:, p * tile + k:p * tile + k + 1]) for k in range(tile)]

    slots = [0]

    def spread(x, count):
        at = slots[0] * tile
        slots[0] += 1
        spread_ref[pl.ds(at, tile), :] = x
        return [full(spread_ref[pl.ds(at + j, 1), :]) for j in range(count)]

    pivots = []
    diagonal = lanes(0, 0)
    for p in range(count):
        columns = [spread(diagonal[k], tile) for k in range(tile)]
        block = [[columns[k][j] for k in range(j + 1)] for j in range(tile)]
        rows = spread(both[p], tile)
        below = range(p + 1, count)
        cols = {v: lanes(v, p) for v in below}
        diagonal = lanes(p + 1, p + 1) if below else []
        found, kept = block[0][0], rows[0]
        for j in range(tile):
            if j:
                found = jnp.where(sublane == j, block[j][j], found)
                kept = jnp.where(sublane == j, rows[j], kept)
            inverse = pl.reciprocal(block[j][j], approx=True, full_range=False)
            scaled = {i: block[i][j] * inverse for i in range(j + 1, tile)}
            for i, factor in scaled.items():
                for k in range(j + 1, i + 1):
                    block[i][k] = block[i][k] - factor * block[k][j]
                rows[i] = rows[i] - factor * rows[j]
            if below:
                column = cols[p + 1][j]
                entries = spread(column, tile)
                diagonal = [x - column * (e * inverse) for x, e in zip(diagonal, entries)]
            row = rows[j] * inverse
            for v in below:
                for i, factor in scaled.items():
                    cols[v][i] = cols[v][i] - factor * cols[v][j]
                both[v] = both[v] - cols[v][j] * row
        both[p] = kept
        pivots.append(found)
    return both, pivots


def finish_kernel(
    total_rows, term_ref, first_ref, second_ref, gram_ref, got_gram_ref, out_ref, spread_ref
):
    rank = LANES // 2
    both, pivots = eliminate(gram_ref[...] + got_gram_ref[...], spread_ref)
    scale = total_rows ** 0.5
    inverse = jnp.concatenate([b * (lax.rsqrt(p) * scale) for b, p in zip(both, pivots)], axis=0)
    inverse = inverse[:, rank:]
    half = term_ref.shape[1] // 2
    product = pair_product(term_ref, first_ref, second_ref)
    product = jnp.where(is_even(), product[:rank], product[rank:])
    mine = jnp.where(lax.axis_index("col") == 0, product[:, :half], product[:, half:]).T
    out_ref[...] = dot_parts(mine, inverse, 1)


def finish(total_rows, term, first, second, gram, got_gram):
    return pl.pallas_call(
        functools.partial(finish_kernel, total_rows),
        out_shape=jax.ShapeDtypeStruct((term.shape[1] // 2, LANES // 2), F32),
        scratch_shapes=[pltpu.VMEM((LANES // 2 * 17, LANES), F32)],
        compiler_params=params(4),
        name="finish",
    )(term, first, second, gram, got_gram)


def per_device(snapshot, mode2_factor, old_factor):
    n_rows, n_cols = lax.axis_size("row"), lax.axis_size("col")
    masks = [1 << bit for bit in range(n_rows.bit_length() - 1)]
    total_rows = snapshot.shape[0] * n_rows

    def swap(x, mask, other=None):
        pairs = []
        for r in range(n_rows):
            for c in range(n_cols):
                second = (c + r.bit_count()) % 2 and other is not None
                to = r ^ (other if second else mask)
                pairs.append((r * n_cols + c, to * n_cols + (c + 1) % n_cols))
        return lax.ppermute(x, ("row", "col"), pairs)

    snapshot = pltpu.with_memory_space_constraint(snapshot, pltpu.HBM)
    mode2_t = pltpu.with_memory_space_constraint(mode2_factor.T, pltpu.HBM)
    send, kept, wide, order = contract_send(snapshot, mode2_t)
    got = swap(send, 0)
    own = contract_own(kept, wide, order)

    send, give = project(own, got, old_factor.T, False)
    keep, columns = project(own, got, old_factor.T, True)
    mine = add(keep, swap(send, masks[0]))
    got_columns = swap(give, masks[0])
    others = masks[1:]
    turned = others[len(others) // 2:] + others[:len(others) // 2]
    for step, (mask, other) in enumerate(zip(others, turned)):
        after = [got_columns] if step == 1 else []
        mine = add(mine, swap(mine, mask, other), *after)

    term = product_terms(columns, got_columns, mine)
    term = add(term, swap(term, 0))
    pair, next_pair = masks[:2]
    first, second = swap(term, pair, next_pair), swap(term, next_pair, pair)
    gram = local_gram(term, first, second, swap(term, pair | next_pair))
    for mask in masks[2:-1]:
        gram = add(gram, swap(gram, mask))
    return finish(total_rows, term, first, second, gram, swap(gram, masks[-1]))


def solution(mesh):
    return jax.shard_map(
        per_device,
        mesh=mesh,
        in_specs=(
            P(("groups", "row"), None, "col"),
            P(("groups", "col"), None),
            P(("groups", "row"), None),
        ),
        out_specs=P(("groups", "row", "col"), None),
        check_vma=False,
    )
```

```python
import functools

import jax
import jax.numpy as jnp
from jax import lax
from jax.experimental import pallas as pl
from jax.experimental.pallas import tpu as pltpu
from jax.sharding import PartitionSpec as P

F32 = jnp.float32
BF16 = jnp.bfloat16
LANES = 128
MIB = 2**20


def dot_f32(a, b, dims, precision=None):
    return lax.dot_general(a, b, (dims, ((), ())), precision=precision, preferred_element_type=F32)


def params(mib):
    return pltpu.CompilerParams(vmem_limit_bytes=mib * MIB)


def own_half():
    row = lax.axis_index("row")
    half = lax.axis_index("col")
    for bit in range(lax.axis_size("row").bit_length() - 1):
        half += lax.rem(lax.div(row, 1 << bit), 2)
    return lax.rem(half, 2)


TILE = 8


def fill_order(order_ref, half):
    block = TILE * half
    to = lax.broadcasted_iota(jnp.int32, order_ref.shape, 0)
    at = lax.broadcasted_iota(jnp.int32, order_ref.shape, 1)
    cell = lax.div(lax.rem(at, block), half)
    wanted = lax.div(to, TILE) * (order_ref.shape[1] // block) + lax.div(at, block)
    same = (lax.rem(to, TILE) == cell) & (wanted == lax.rem(at, half))
    order_ref[...] = same.astype(F32).astype(BF16)


def multiply(slab, wide_ref, flat_ref):
    cells, half, depth = slab.shape
    x = slab.reshape(cells * half, depth)
    low = dot_f32(x[:, :depth // 2], wide_ref[:, :depth // 2], ((1,), (1,)))
    high = dot_f32(x[:, depth // 2:], wide_ref[:, depth // 2:], ((1,), (1,)))
    flat_ref[...] = (low + high).astype(BF16)


def spread(half, flat_ref, order_ref, core_ref, start):
    block = TILE * half
    reps = order_ref.shape[1] // block
    step = flat_ref.shape[0] // half
    group = lax.div(lax.broadcasted_iota(jnp.int32, (block, LANES), 1), LANES // reps)
    spreads = []
    for b in range(step // TILE):
        flat = flat_ref[pl.ds(b * block, block), :].astype(F32)
        groups = [jnp.where(group == r, flat, 0.0).astype(BF16) for r in range(reps)]
        spreads.append(dot_f32(order_ref[...], jnp.concatenate(groups, axis=0), ((1,), (0,))))
    for p in range(half // reps):
        part = jnp.concatenate([x[p * TILE:(p + 1) * TILE] for x in spreads], axis=0)
        core_ref[pl.ds(start, step), p * LANES:(p + 1) * LANES] = part.astype(BF16)


STEP = 32


def slab_copies(snapshot_ref, first, slab_ref, half_index, sem):
    half = slab_ref.shape[1]
    fibers = pl.ds(pl.multiple_of(half_index * half, half), half)

    def copy(start, size):
        return pltpu.make_async_copy(
            snapshot_ref.at[pl.ds(start, size), fibers],
            slab_ref.at[pl.ds(start - first, size)],
            sem,
        )

    def start(begin, size, count):
        for part in range(count):
            copy(begin + part * (size // count), size // count).start()

    return start, lambda begin, size: copy(begin, size).wait()


def send_kernel(
    snapshot_ref, mode2_ref, core_ref, kept_ref, part_ref, wide_ref, order_ref,
    slab_ref, small_ref, even_ref, odd_ref, sems, kept_sems, small_sem,
):
    cells, half, _ = slab_ref.shape
    rank = mode2_ref.shape[0]
    chunks = cells // STEP
    flat = (even_ref, odd_ref)
    sends = [
        slab_copies(snapshot_ref, 0, slab_ref, 1 - own_half(), sems.at[chunk])
        for chunk in range(chunks)
    ]
    (start_first, wait_first), (start_rest, wait_rest) = (
        slab_copies(snapshot_ref, 0, kept_ref, own_half(), kept_sems.at[k]) for k in range(2)
    )

    small = pltpu.make_async_copy(mode2_ref, small_ref, small_sem)
    small.start()
    sends[0][0](0, STEP, 8)
    sends[1][0](STEP, STEP, 2)
    fill_order(order_ref, half)
    small.wait()
    wide_ref[...] = jnp.concatenate([small_ref[...]] * (LANES // rank), axis=0)
    for chunk in range(chunks):
        sends[chunk][1](chunk * STEP, STEP)
        if chunk == 0:
            for later in range(2, chunks):
                sends[later][0](later * STEP, STEP, 2)
            start_first(0, STEP, 2)
            start_rest(STEP, STEP, 2)
        if chunk == 1:
            start_rest(2 * STEP, cells - 2 * STEP, chunks)
        multiply(slab_ref[pl.ds(chunk * STEP, STEP)], wide_ref, flat[chunk % 2])
        if chunk:
            spread(half, flat[(chunk - 1) % 2], order_ref, core_ref, (chunk - 1) * STEP)
    spread(half, flat[(chunks - 1) % 2], order_ref, core_ref, (chunks - 1) * STEP)
    wait_first(0, STEP)
    multiply(kept_ref[pl.ds(0, STEP)], wide_ref, flat[chunks % 2])
    spread(half, flat[chunks % 2], order_ref, part_ref, 0)
    wait_rest(STEP, cells - STEP)


def contract_send(snapshot, mode2_t):
    cells, fibers, depth = snapshot.shape
    rank = mode2_t.shape[0]
    half = fibers // 2
    reps = LANES // rank
    block = TILE * half
    pinned = pl.BlockSpec(memory_space=pltpu.HBM)
    return pl.pallas_call(
        send_kernel,
        in_specs=[pinned, pinned],
        out_shape=[
            jax.ShapeDtypeStruct((cells, half * rank), BF16),
            jax.ShapeDtypeStruct((cells, half, depth), BF16),
            jax.ShapeDtypeStruct((STEP, half * rank), BF16),
            jax.ShapeDtypeStruct((LANES, depth), BF16),
            jax.ShapeDtypeStruct((block // reps, block * reps), BF16),
        ],
        scratch_shapes=[
            pltpu.VMEM((cells, half, depth), BF16),
            pltpu.VMEM((rank, depth), BF16),
            pltpu.VMEM((STEP * half, LANES), BF16),
            pltpu.VMEM((STEP * half, LANES), BF16),
            pltpu.SemaphoreType.DMA((cells // STEP,)),
            pltpu.SemaphoreType.DMA((2,)),
            pltpu.SemaphoreType.DMA,
        ],
        compiler_params=params(24),
        name="contract_send",
    )(snapshot, mode2_t)


def own_kernel(slab_ref, part_ref, wide_ref, order_ref, core_ref, even_ref, odd_ref):
    cells, half, _ = slab_ref.shape
    flat = (even_ref, odd_ref)
    chunks = cells // STEP
    core_ref[pl.ds(0, STEP), :] = part_ref[...]
    for chunk in range(1, chunks):
        multiply(slab_ref[pl.ds(chunk * STEP, STEP)], wide_ref, flat[chunk % 2])
        if chunk > 1:
            spread(half, flat[(chunk - 1) % 2], order_ref, core_ref, (chunk - 1) * STEP)
    spread(half, flat[(chunks - 1) % 2], order_ref, core_ref, (chunks - 1) * STEP)


def contract_own(slab, part, wide, order):
    cells, half, _ = slab.shape
    reps = order.shape[1] // (TILE * half)
    return pl.pallas_call(
        own_kernel,
        out_shape=jax.ShapeDtypeStruct((cells, half // reps * LANES), BF16),
        scratch_shapes=[pltpu.VMEM((STEP * half, LANES), BF16)] * 2,
        compiler_params=params(24),
        name="contract_own",
    )(slab, part, wide, order)


def is_even():
    return lax.rem(lax.axis_index("row"), 2) == 0


def project_kernel(kept, own_ref, got_ref, factor_ref, projected_ref, core_ref):
    rank = factor_ref.shape[0]
    width = core_ref.shape[1]
    odd = lax.rem(lax.axis_index("row"), 2)
    start = odd * width if kept else (1 - odd) * width
    where = pl.ds(pl.multiple_of(start, width), width)
    core = (own_ref[:, where].astype(F32) + got_ref[:, where].astype(F32)).astype(BF16)
    core_ref[...] = core
    projected = dot_f32(factor_ref[...], core, ((1,), (0,)))
    for block in range(width // LANES):
        part = projected[:, block * LANES:(block + 1) * LANES]
        projected_ref[pl.ds(block * rank, rank), :] = part.astype(projected_ref.dtype)


def project(own, got, factor_t, kept):
    cells, width = own.shape
    rows = factor_t.shape[0] * width // LANES // 2
    return pl.pallas_call(
        functools.partial(project_kernel, kept),
        out_shape=[
            jax.ShapeDtypeStruct((rows, LANES), F32 if kept else BF16),
            jax.ShapeDtypeStruct((cells, width // 2), BF16),
        ],
        compiler_params=params(8),
        name="project_kept" if kept else "project_sent",
    )(own, got, factor_t)


def add_kernel(mine_ref, got_ref, *refs):
    total = mine_ref[...].astype(F32) + got_ref[...].astype(F32)
    refs[-1][...] = total.astype(refs[-1].dtype)


def add(mine, got, *after):
    whole = pl.BlockSpec(memory_space=pltpu.VMEM)
    return pl.pallas_call(
        add_kernel,
        in_specs=[whole, whole] + [pl.BlockSpec(memory_space=pl.ANY)] * len(after),
        out_shape=jax.ShapeDtypeStruct(got.shape, got.dtype),
        compiler_params=params(4),
        name="add",
    )(mine, got, *after)


def product_kernel(mine_ref, got_ref, projected_ref, out_ref):
    blocks = mine_ref.shape[1] // LANES
    rank = projected_ref.shape[0] // blocks
    projected = jnp.concatenate(
        [projected_ref[pl.ds(block * rank, rank), :] for block in range(blocks)], axis=1
    )
    terms = [dot_f32(projected, ref[...], ((1,), (1,))) for ref in (mine_ref, got_ref)]
    even = is_even()
    low = jnp.where(even, terms[0], terms[1])
    high = jnp.where(even, terms[1], terms[0])
    out_ref[...] = jnp.concatenate([low, high], axis=0).astype(BF16)


def product_terms(mine, got, projected):
    return pl.pallas_call(
        product_kernel,
        out_shape=jax.ShapeDtypeStruct((LANES, mine.shape[0]), BF16),
        compiler_params=params(4),
        name="product_terms",
    )(mine, got, projected)


def pair_product(term_ref, first_ref, second_ref):
    got = jnp.where(own_half() == 0, first_ref[...].astype(F32), second_ref[...].astype(F32))
    return term_ref[...].astype(F32) + got


def gram_kernel(term_ref, first_ref, second_ref, last_ref, out_ref):
    rank = LANES // 2
    pairs = [
        pair_product(term_ref, first_ref, second_ref),
        pair_product(last_ref, second_ref, first_ref),
    ]
    product = jnp.concatenate([x[k:k + rank] for x in pairs for k in (0, rank)], axis=1)
    gram = dot_parts(product, product, 1)
    out_ref[...] = jnp.concatenate([gram[:rank // 2], gram[rank // 2:]], axis=1)


def local_gram(*terms):
    return pl.pallas_call(
        gram_kernel,
        out_shape=jax.ShapeDtypeStruct((LANES // 4, LANES), F32),
        compiler_params=params(4),
        name="local_gram",
    )(*terms)


def parts(x):
    high = x.astype(BF16)
    return high, (x - high.astype(F32)).astype(BF16)


def dot_parts(a, b, axis):
    (ah, al), (bh, bl) = parts(a), parts(b)
    left = jnp.concatenate([ah, ah, al], axis=axis)
    right = jnp.concatenate([bh, bl, bh], axis=axis)
    return dot_f32(left, right, ((axis,), (axis,)))


def eliminate(packed, spread_ref):
    rank = packed.shape[1] // 2
    tile = 8
    count = rank // tile
    wide = 2 * rank
    sublane = lax.broadcasted_iota(jnp.int32, (tile, wide), 0)
    lane = lax.broadcasted_iota(jnp.int32, (tile, wide), 1)
    full = lambda x: jnp.broadcast_to(x, (tile, wide))
    both = []
    for v in range(count):
        at = v % (count // 2) * tile
        mine = packed[at:at + tile]
        if v >= count // 2:
            mine = jnp.concatenate([mine[:, rank:], mine[:, :rank]], axis=1)
        both.append(jnp.where(lane < rank, mine, (lane - rank == sublane + v * tile).astype(F32)))
    def lanes(v, p):
        return [full(both[v][:, p * tile + k:p * tile + k + 1]) for k in range(tile)]

    slots = [0]

    def spread(x, count):
        at = slots[0] * tile
        slots[0] += 1
        spread_ref[pl.ds(at, tile), :] = x
        return [full(spread_ref[pl.ds(at + j, 1), :]) for j in range(count)]

    pivots = []
    diagonal = lanes(0, 0)
    for p in range(count):
        columns = [spread(diagonal[k], tile) for k in range(tile)]
        block = [[columns[k][j] for k in range(j + 1)] for j in range(tile)]
        rows = spread(both[p], tile)
        below = range(p + 1, count)
        cols = {v: lanes(v, p) for v in below}
        diagonal = lanes(p + 1, p + 1) if below else []
        found, kept = block[0][0], rows[0]
        for j in range(tile):
            if j:
                found = jnp.where(sublane == j, block[j][j], found)
                kept = jnp.where(sublane == j, rows[j], kept)
            inverse = pl.reciprocal(block[j][j], approx=True, full_range=False)
            scaled = {i: block[i][j] * inverse for i in range(j + 1, tile)}
            for i, factor in scaled.items():
                for k in range(j + 1, i + 1):
                    block[i][k] = block[i][k] - factor * block[k][j]
                rows[i] = rows[i] - factor * rows[j]
            if below:
                column = cols[p + 1][j]
                entries = spread(column, tile)
                diagonal = [x - column * (e * inverse) for x, e in zip(diagonal, entries)]
            row = rows[j] * inverse
            for v in below:
                for i, factor in scaled.items():
                    cols[v][i] = cols[v][i] - factor * cols[v][j]
                both[v] = both[v] - cols[v][j] * row
        both[p] = kept
        pivots.append(found)
    return both, pivots


def finish_kernel(
    total_rows, term_ref, first_ref, second_ref, gram_ref, got_gram_ref, out_ref, spread_ref
):
    rank = LANES // 2
    both, pivots = eliminate(gram_ref[...] + got_gram_ref[...], spread_ref)
    scale = total_rows ** 0.5
    inverse = jnp.concatenate([b * (lax.rsqrt(p) * scale) for b, p in zip(both, pivots)], axis=0)
    inverse = inverse[:, rank:]
    half = term_ref.shape[1] // 2
    product = pair_product(term_ref, first_ref, second_ref)
    product = jnp.where(is_even(), product[:rank], product[rank:])
    mine = jnp.where(lax.axis_index("col") == 0, product[:, :half], product[:, half:]).T
    out_ref[...] = dot_parts(mine, inverse, 1)


def finish(total_rows, term, first, second, gram, got_gram):
    return pl.pallas_call(
        functools.partial(finish_kernel, total_rows),
        out_shape=jax.ShapeDtypeStruct((term.shape[1] // 2, LANES // 2), F32),
        scratch_shapes=[pltpu.VMEM((LANES // 2 * 17, LANES), F32)],
        compiler_params=params(4),
        name="finish",
    )(term, first, second, gram, got_gram)


def per_device(snapshot, mode2_factor, old_factor):
    n_rows, n_cols = lax.axis_size("row"), lax.axis_size("col")
    masks = [1 << bit for bit in range(n_rows.bit_length() - 1)]
    total_rows = snapshot.shape[0] * n_rows

    def swap(x, mask, other=None):
        pairs = []
        for r in range(n_rows):
            for c in range(n_cols):
                second = (c + r.bit_count()) % 2 and other is not None
                to = r ^ (other if second else mask)
                pairs.append((r * n_cols + c, to * n_cols + (c + 1) % n_cols))
        return lax.ppermute(x, ("row", "col"), pairs)

    snapshot = pltpu.with_memory_space_constraint(snapshot, pltpu.HBM)
    mode2_t = pltpu.with_memory_space_constraint(mode2_factor.T, pltpu.HBM)
    send, kept, part, wide, order = contract_send(snapshot, mode2_t)
    got = swap(send, 0)
    own = contract_own(kept, part, wide, order)

    send, give = project(own, got, old_factor.T, False)
    keep, columns = project(own, got, old_factor.T, True)
    mine = add(keep, swap(send, masks[0]))
    got_columns = swap(give, masks[0])
    others = masks[1:]
    turned = others[len(others) // 2:] + others[:len(others) // 2]
    for step, (mask, other) in enumerate(zip(others, turned)):
        after = [got_columns] if step == 1 else []
        mine = add(mine, swap(mine, mask, other), *after)

    term = product_terms(columns, got_columns, mine)
    term = add(term, swap(term, 0))
    pair, next_pair = masks[:2]
    first, second = swap(term, pair, next_pair), swap(term, next_pair, pair)
    gram = local_gram(term, first, second, swap(term, pair | next_pair))
    for mask in masks[2:-1]:
        gram = add(gram, swap(gram, mask))
    return finish(total_rows, term, first, second, gram, swap(gram, masks[-1]))


def solution(mesh):
    return jax.shard_map(
        per_device,
        mesh=mesh,
        in_specs=(
            P(("groups", "row"), None, "col"),
            P(("groups", "col"), None),
            P(("groups", "row"), None),
        ),
        out_specs=P(("groups", "row", "col"), None),
        check_vma=False,
    )
```
